32 devices in a mesh: ens: 2 (over y), gz: 4 (over z), ta: 2 (over x), gy: 2 (over core).
Axes of the slice: x: 2, y: 2, z: 4, core: 2. Of those that a mesh axis runs over, the one named last changes fastest.
Arguments:
- pole_vectors: float32 [8, 2, 3, 4, 16, 128], P('ens', None, None, 'ta', ('gz', 'gy')), parts along dimension 0, may hold values from -6 to 6
- gauge_links: bfloat16 [8, 2, 3, 3, 4, 16, 128], P('ens', None, None, None, 'ta', ('gz', 'gy')), parts along dimension 0, may hold values from -2.5 to 2.5
- pole_coeff: float32 [4], replicated, may hold values from 0.2 to 1
- naik_coeff: float32 [4], replicated, may hold values from 0.1 to 0.5
- staple_weight: float32 [4], replicated, may hold values from 0.1 to 0.4
Outputs:
- force: float32 [8, 2, 3, 3, 4, 16, 128], P('ens', None, None, None, 'ta', ('gz', 'gy')), parts along dimension 0
The draws below stay inside these ranges and needn't reach their ends.
There are 2 independent parts, one for each index of `ens`. The reference program is written for one: setup_inputs(seed, part) draws one part's arguments, and reference() takes and returns one part's arrays. A program takes and returns all parts, laid end to end along the dimension named above; an argument that names none is the same for every part. Nothing has to cross between parts.
All inputs are finite; a program needn't handle non-finite values.
Results may differ from the reference program's by a relative error of at most 0.0003.
Values sent between devices are 32-bit elements; how exact they have to be, the bound alone decides.
No kernel may reach another device: no remote copies, remote signals or barrier semaphores. Data moves between devices by JAX's collectives and lax.ppermute only.
A program may use at most 64 MiB of HBM per device.

```python
import math
import jax
import jax.numpy as jnp

NX = 8
NY = 16
NP = 4
NZ = 16
NT = 4


def block_levels(rng, shape, cuts, least, top_value):
    loudness, own = 1.0, jax.random.fold_in(rng, 6)
    for position, blocks in cuts:
        heights = jnp.exp(jax.random.uniform(jax.random.fold_in(own, position), (blocks,), jnp.float32, least / len(cuts), top_value / len(cuts)))
        loudness = loudness * jnp.repeat(heights, shape[position] // blocks).reshape([-1 if axis == position else 1 for axis in range(len(shape))])
    return loudness


def centred(rng, dims, width, limit, shards=(), held_as=jnp.bfloat16):
    entries = jax.random.normal(rng, dims, jnp.float32) * width
    if len(shards) > 0:
        entries = block_levels(rng, dims, shards, -0.22, 0.18) * entries
    return jnp.clip(entries, min=-limit, max=limit).astype(held_as)


def setup_inputs(seed: int = 0, part: int = 0) -> dict:
    key_list = jax.random.split(jax.random.key(seed), 6)
    own_keys = jax.random.split(jax.random.fold_in(key_list[5], part), 6)
    return {
        "pole_vectors": centred(own_keys[0], (NP, 2, 3, NT, NZ, NY * NX), 1.0, 6.0, ((3, 2), (4, 8)), jnp.float32),
        "gauge_links": centred(own_keys[1], (4, 2, 3, 3, NT, NZ, NY * NX), 0.41, 2.5, ((4, 2), (5, 8))),
        "pole_coeff": jnp.clip(jnp.exp(jax.random.uniform(key_list[2], (NP,), jnp.float32, math.log(0.2), math.log(1.0))), 0.2, 1.0),
        "naik_coeff": jnp.clip(jnp.exp(jax.random.uniform(key_list[3], (NP,), jnp.float32, math.log(0.1), math.log(0.5))), 0.1, 0.5),
        "staple_weight": jnp.clip(jnp.exp(jax.random.uniform(key_list[4], (4,), jnp.float32, math.log(0.1), math.log(0.4))), 0.1, 0.4),
    }


def real_product(left_mat, right_mat):
    return jnp.sum(left_mat[:, :, None] * right_mat[None, :, :], axis=1)


def mat_mul(left_mat, right_mat):
    real_part = real_product(left_mat[0], right_mat[0]) - real_product(left_mat[1], right_mat[1])
    imag_part = real_product(left_mat[0], right_mat[1]) + real_product(left_mat[1], right_mat[0])
    return jnp.stack([real_part, imag_part])


def dagger(matrix):
    return jnp.stack([jnp.swapaxes(matrix[0], 0, 1), -jnp.swapaxes(matrix[1], 0, 1)])


def outer_product(column, row_vec):
    real_part = column[0][:, None] * row_vec[0][None] + column[1][:, None] * row_vec[1][None]
    imag_part = column[1][:, None] * row_vec[0][None] - column[0][:, None] * row_vec[1][None]
    return jnp.stack([real_part, imag_part])


def ahead_of(values, direction, offset):
    return jnp.roll(values, -offset, axis=values.ndim - 1 - direction)


def reference(pole_vectors, gauge_links, pole_coeff, naik_coeff, staple_weight):
    lattice = (NT, NZ, NY, NX)
    vectors = pole_vectors.reshape((NP, 2, 3) + lattice)
    gauge = gauge_links.astype(jnp.float32).reshape((4, 2, 3, 3) + lattice)
    one_link = []
    three_link = []
    for direction in range(4):
        near_sum = jnp.zeros((2, 3, 3) + lattice, jnp.float32)
        far_sum = jnp.zeros((2, 3, 3) + lattice, jnp.float32)
        for pole in range(NP):
            near_sum = near_sum + pole_coeff[pole] * outer_product(ahead_of(vectors[pole], direction, 1), vectors[pole])
            far_sum = far_sum + naik_coeff[pole] * outer_product(ahead_of(vectors[pole], direction, 3), vectors[pole])
        one_link.append(near_sum)
        three_link.append(far_sum)
    forces = []
    for direction in range(4):
        staple_sum = jnp.zeros((2, 3, 3) + lattice, jnp.float32)
        for across in range(4):
            if across == direction:
                continue
            link_here = gauge[across]
            link_moved = ahead_of(gauge[across], direction, 1)
            forward_term = mat_mul(mat_mul(link_here, ahead_of(one_link[direction], across, 1)), dagger(link_moved))
            staple_sum = staple_sum + forward_term
            backward_term = mat_mul(mat_mul(dagger(link_here), one_link[direction]), link_moved)
            staple_sum = staple_sum + ahead_of(backward_term, across, -1)
        forces.append(one_link[direction] + three_link[direction] + staple_weight[direction] * staple_sum)
    return jnp.stack(forces).reshape((4, 2, 3, 3, NT, NZ, NY * NX))
```

```python
import collections
import functools

import jax
import jax.numpy as jnp
from jax import lax
from jax.experimental import pallas as pl
from jax.experimental.pallas import tpu as pltpu
from jax.sharding import PartitionSpec as P

NX = 8
NY = 16
LANES = NX * NY
NP = 4
VEC = NP * 6
MAT = 18
SLOT = 24
TILE = 8 * SLOT
PAIRS = ((0, 1), (2, 3))
CROSS = (((1, 0), (2, 2), (3, 3)), ((0, 0), (1, 1), (3, 2)))
UNIT = ((1, 0, 0, 0), (0, 1, 0, 0), (0, 0, 1, 0), (0, 0, 0, 1))
CHUNKS = {"x": (8, 8, 8), "u": (8, 8, 2)}
F32 = jnp.float32


def plus(left, right, scale=1):
    return tuple(a + scale * b for a, b in zip(left, right))


def halo_plan(t_size):
    both = ((0, 0), (0, 1), (1, 0), (1, 1))
    t_low, t_high = ((0, 0), (0, 1)), ((1, 0), (1, 1))
    z_low, z_high = ((0, 0), (1, 0)), ((0, 1), (1, 1))

    def blocks(vec_at, links, link_at):
        found = [("x", 0) + at for at in vec_at]
        return found + [("u", n) + at for n in links for at in link_at]

    wanted = {
        (0, 1): blocks(both, (0, 1, 3), z_low),
        (0, 2): blocks(z_low, (), ()),
        (0, -1): blocks(z_high, (2,), z_high),
        (1, 0): blocks(both, (0, 1, 2), t_low),
        (2, 0): blocks(t_low, (), ()),
        (-1, 0): blocks(t_high, (3,), t_high),
        (1, 1): blocks(((0, 0),), (), ()),
        (-1, 1): blocks(((1, 0),), (3,), ((1, 0),)),
        (1, -1): blocks(((0, 1),), (2,), ((0, 1),)),
    }
    sends = collections.OrderedDict()
    for (dt, dz), items in wanted.items():
        to = (dt % t_size, dz)
        if to == (0, 0):
            continue
        held = sends.setdefault(to, [])
        held.extend(item for item in items if item not in held)
    return [(to, items) for to, items in sends.items()]


def block_rows(items):
    offsets, row = {}, 0
    for item in items:
        offsets[item] = row
        row += VEC if item[0] == "x" else MAT
    return offsets, -(-row // 8) * 8


def local_row(item):
    kind, n, t, z = item
    r = 2 * t + z
    return r * VEC if kind == "x" else (r * 4 + n) * SLOT


def copy_block(kind, src, src_row, dst, dst_rows, change=None):
    done = 0
    for size in CHUNKS[kind]:
        value = src[pl.ds(src_row + done, size), :]
        if change is not None:
            value = change(value)
        for dst_row in dst_rows:
            dst[pl.ds(dst_row + done, size), :] = value
        done += size


def pack_kernel(plan, x_ref, u_ref, xl_ref, ul_ref, *rest):
    outs, wide = rest[:-1], rest[-1]
    wide[...] = u_ref[...].astype(F32)
    for r in range(4):
        for k in range(3):
            xl_ref[pl.ds(r * VEC + 8 * k, 8), :] = x_ref[pl.ds(r + 32 * k, 8, stride=4), :]
        for n in range(4):
            done = 0
            for size in CHUNKS["u"]:
                value = wide[pl.ds((MAT * n + done) * 4 + r, size, stride=4), :]
                ul_ref[pl.ds((r * 4 + n) * SLOT + done, size), :] = value
                done += size
    for out, (_, items) in zip(outs, plan):
        offsets, _ = block_rows(items)
        for item, row in offsets.items():
            copy_block(item[0], xl_ref if item[0] == "x" else ul_ref, local_row(item), out, (row,))


def tile_fields():
    x_fields, u_fields = [], []
    zero = (0, 0, 0, 0)
    for pair, crosses in zip(PAIRS, CROSS):
        for cross in crosses:
            for sign in (1, -1):
                start = [plus(zero, UNIT[n], sign) for n in cross]
                x_fields.append([("x", 0, start[h]) for h in range(2)])
                x_fields.append([("x", 0, plus(start[h], UNIT[pair[h]])) for h in range(2)])
                base = [zero if sign > 0 else start[h] for h in range(2)]
                u_fields.append([("u", cross[h], base[h]) for h in range(2)])
                u_fields.append([("u", cross[h], plus(base[h], UNIT[pair[h]])) for h in range(2)])
    x_fields.append([("x", 0, zero)] * 2)
    for pair in PAIRS:
        x_fields.append([("x", 0, UNIT[m]) for m in pair])
        x_fields.append([("x", 0, plus(zero, UNIT[m], 3)) for m in pair])
    return x_fields, u_fields


def find_block(where, t_size, kind, n, t, z):
    dt, t_in = divmod(t, 2)
    dz, z_in = divmod(z, 2)
    to = (dt % t_size, dz)
    item = (kind, n, t_in, z_in)
    if to == (0, 0):
        return ("local", kind), local_row(item)
    return to, where[to][item]


def lane_shifted(value, dx, dy):
    if dx != 0:
        x_at = lax.broadcasted_iota(jnp.int32, value.shape, 1) % NX
        beyond = (x_at + dx >= NX) | (x_at + dx < 0)
        main = pltpu.roll(value, (-dx) % LANES, 1)
        wrapped = pltpu.roll(value, (NX - dx if dx > 0 else -NX - dx) % LANES, 1)
        value = jnp.where(beyond, wrapped, main)
    if dy != 0:
        value = pltpu.roll(value, (-dy * NX) % LANES, 1)
    return value


def build_fields(buffers, where, t_size, x_tiles, u_tiles):
    x_fields, u_fields = tile_fields()
    copies = collections.OrderedDict()
    for target, fields in ((0, x_fields), (1, u_fields)):
        for index, halves in enumerate(fields):
            for half, (kind, n, disp) in enumerate(halves):
                for r in range(4):
                    source = find_block(where, t_size, kind, n, r // 2 + disp[3], r % 2 + disp[2])
                    row = index * TILE + (4 * half + r) * SLOT
                    group = copies.setdefault((kind,) + source, collections.OrderedDict())
                    group.setdefault((disp[0], disp[1]), []).append(row)
    for (kind, name, src_row), shifts in copies.items():
        target = x_tiles if kind == "x" else u_tiles
        for (dx, dy), rows in shifts.items():
            change = functools.partial(lane_shifted, dx=dx, dy=dy)
            copy_block(kind, buffers[name], src_row, target, rows, change)


def tile_of(ref, base, component):
    return ref[pl.ds(base + component, 8, stride=SLOT), :]


def vector_tiles(ref, base, pole):
    return [[tile_of(ref, base, pole * 6 + part * 3 + i) for i in range(3)] for part in range(2)]


def pole_sum(ref, here, ahead, scales):
    total = None
    for pole in range(NP):
        h = [[scales[pole] * v for v in part] for part in vector_tiles(ref, here, pole)]
        a = vector_tiles(ref, ahead, pole)
        real = [[a[0][i] * h[0][j] + a[1][i] * h[1][j] for j in range(3)] for i in range(3)]
        imag = [[a[1][i] * h[0][j] - a[0][i] * h[1][j] for j in range(3)] for i in range(3)]
        if total is None:
            total = [real, imag]
        else:
            total = [
                [[total[c][i][j] + new[i][j] for j in range(3)] for i in range(3)]
                for c, new in enumerate((real, imag))
            ]
    return total


def matrix_tiles(ref, base):
    return [
        [[tile_of(ref, base, part * 9 + i * 3 + j) for j in range(3)] for i in range(3)]
        for part in range(2)
    ]


def conj(matrix, transposed=True):
    return [[[matrix[part][j][i] for j in range(3)] for i in range(3)] for part in range(2)]


def row_times(row, right, row_sign, right_sign):
    result = [[], []]
    for j in range(3):
        real = imag = None
        for k in range(3):
            rr = row[0][k] * right[0][k][j]
            ii = row[1][k] * right[1][k][j]
            ri = row[0][k] * right[1][k][j]
            ir = row[1][k] * right[0][k][j]
            new_real = rr - ii if row_sign * right_sign > 0 else rr + ii
            if row_sign > 0 and right_sign > 0:
                new_imag = ri + ir
            elif row_sign > 0:
                new_imag = ir - ri
            else:
                new_imag = ri - ir
            real = new_real if real is None else real + new_real
            imag = new_imag if imag is None else imag + new_imag
        result[0].append(real)
        result[1].append(imag)
    return result


def main_kernel(names, where, t_size, near_ref, far_ref, weight_ref, xl_ref, ul_ref, *rest):
    received = rest[: len(names)]
    out_ref, x_tiles, u_tiles, acc = rest[len(names) :]
    buffers = {("local", "x"): xl_ref, ("local", "u"): ul_ref}
    buffers.update(zip(names, received))
    build_fields(buffers, where, t_size, x_tiles, u_tiles)
    near = [near_ref[p] for p in range(NP)]
    far = [far_ref[p] for p in range(NP)]
    upper = lax.broadcasted_iota(jnp.int32, (8, LANES), 0) < 4

    def term(step, first):
        group = step // 3
        for side in range(2):
            base = (step * 2 + side) * 2 * TILE
            force = pole_sum(x_tiles, base, base + TILE, near)
            left = matrix_tiles(u_tiles, base)
            right = matrix_tiles(u_tiles, base + TILE)
            if side == 1:
                left = conj(left)
            else:
                right = conj(right)
            for i in range(3):
                row = [left[0][i], left[1][i]]
                if side == 0:
                    row = row_times(row_times(row, force, 1, 1), right, 1, -1)
                else:
                    row = row_times(row_times(row, force, -1, 1), right, 1, 1)
                for part in range(2):
                    for j in range(3):
                        at = pl.ds((group * MAT + part * 9 + i * 3 + j) * 8, 8)
                        acc[at, :] = acc[at, :] + row[part][j]

    acc[...] = jnp.zeros_like(acc)
    lax.fori_loop(0, 6, lambda step, _: (term(step, False), 0)[1], 0)
    own = 24 * TILE
    for group, (top, bottom) in enumerate(PAIRS):
        near_sum = pole_sum(x_tiles, own, own + (1 + 2 * group) * TILE, near)
        far_sum = pole_sum(x_tiles, own, own + (2 + 2 * group) * TILE, far)
        weight = jnp.where(upper, weight_ref[top], weight_ref[bottom])
        done = []
        for c in range(MAT):
            part, i, j = c // 9, c // 3 % 3, c % 3
            staple = acc[pl.ds((group * MAT + c) * 8, 8), :]
            done.append(near_sum[part][i][j] + far_sum[part][i][j] + weight * staple)
        for c in range(0, MAT, 2):
            first, second = done[c], done[c + 1]
            out_ref[pl.ds((top * MAT + c) * 4, 8), :] = jnp.where(upper, first, pltpu.roll(second, 4, 0))
            out_ref[pl.ds((bottom * MAT + c) * 4, 8), :] = jnp.where(upper, pltpu.roll(first, 4, 0), second)


def on_device(pole_vectors, gauge_links, pole_coeff, naik_coeff, staple_weight):
    t_size = lax.axis_size("ta")
    z_size = lax.axis_size("gz") * lax.axis_size("gy")
    plan = halo_plan(t_size)
    vmem = pl.BlockSpec(memory_space=pltpu.VMEM)
    smem = pl.BlockSpec(memory_space=pltpu.SMEM)
    sizes = [block_rows(items)[1] for _, items in plan]
    packed = pl.pallas_call(
        functools.partial(pack_kernel, plan),
        out_shape=[
            jax.ShapeDtypeStruct((rows, LANES), F32) for rows in [4 * VEC, 16 * SLOT] + sizes
        ],
        in_specs=[vmem] * 2,
        out_specs=[vmem] * (2 + len(plan)),
        scratch_shapes=[pltpu.VMEM((4 * 4 * MAT, LANES), F32)],
        name="pack_halos",
    )(pole_vectors.reshape((4 * VEC, LANES)), gauge_links.reshape((16 * MAT, LANES)))
    local, sends = packed[:2], packed[2:]
    received = []
    for ((dt, dz), _), value in zip(plan, sends):
        if dt == 0:
            axes = ("gz", "gy")
            pairs = [((i + dz) % z_size, i) for i in range(z_size)]
        elif dz == 0:
            axes = "ta"
            pairs = [((j + dt) % t_size, j) for j in range(t_size)]
        else:
            axes = ("gz", "ta", "gy")
            halves = lax.axis_size("gy")

            def index(j, i):
                return ((i // halves) * t_size + j) * halves + i % halves

            pairs = [
                (index((j + dt) % t_size, (i + dz) % z_size), index(j, i))
                for j in range(t_size)
                for i in range(z_size)
            ]
        received.append(lax.ppermute(value, axes, pairs))
    names = [to for to, _ in plan]
    where = {to: block_rows(items)[0] for to, items in plan}
    x_fields, u_fields = tile_fields()
    force = pl.pallas_call(
        functools.partial(main_kernel, names, where, t_size),
        out_shape=jax.ShapeDtypeStruct((16 * MAT, LANES), F32),
        in_specs=[smem] * 3 + [vmem] * (2 + len(plan)),
        out_specs=vmem,
        scratch_shapes=[
            pltpu.VMEM((len(x_fields) * TILE, LANES), F32),
            pltpu.VMEM((len(u_fields) * TILE, LANES), F32),
            pltpu.VMEM((2 * MAT * 8, LANES), F32),
        ],
        compiler_params=pltpu.CompilerParams(vmem_limit_bytes=32 * 1024 * 1024),
        name="force",
    )(pole_coeff, naik_coeff, staple_weight, *local, *received)
    return force.reshape(gauge_links.shape)


def solution(mesh):
    return jax.shard_map(
        on_device,
        mesh=mesh,
        in_specs=(
            P("ens", None, None, "ta", ("gz", "gy"), None),
            P("ens", None, None, None, "ta", ("gz", "gy"), None),
            P(),
            P(),
            P(),
        ),
        out_specs=P("ens", None, None, None, "ta", ("gz", "gy"), None),
        check_vma=False,
    )
```

```python
import collections
import functools

import jax
import jax.numpy as jnp
from jax import lax
from jax.experimental import pallas as pl
from jax.experimental.pallas import tpu as pltpu
from jax.sharding import PartitionSpec as P

NX = 8
NY = 16
LANES = NX * NY
NP = 4
VEC = NP * 6
MAT = 18
SLOT = 24
TILE = 8 * SLOT
PAIRS = ((0, 1), (2, 3))
CROSS = (((1, 0), (2, 2), (3, 3)), ((0, 0), (1, 1), (3, 2)))
UNIT = ((1, 0, 0, 0), (0, 1, 0, 0), (0, 0, 1, 0), (0, 0, 0, 1))
CHUNKS = {"x": (8, 8, 8), "u": (8, 8, 2)}
F32 = jnp.float32


def plus(left, right, scale=1):
    return tuple(a + scale * b for a, b in zip(left, right))


def halo_plan(t_size):
    both = ((0, 0), (0, 1), (1, 0), (1, 1))
    t_low, t_high = ((0, 0), (0, 1)), ((1, 0), (1, 1))
    z_low, z_high = ((0, 0), (1, 0)), ((0, 1), (1, 1))

    def blocks(vec_at, links, link_at):
        found = [("x", 0) + at for at in vec_at]
        return found + [("u", n) + at for n in links for at in link_at]

    wanted = {
        (0, 1): blocks(both, (0, 1, 3), z_low),
        (0, 2): blocks(z_low, (), ()),
        (0, -1): blocks(z_high, (2,), z_high),
        (1, 0): blocks(both, (0, 1, 2), t_low),
        (2, 0): blocks(t_low, (), ()),
        (-1, 0): blocks(t_high, (3,), t_high),
        (1, 1): blocks(((0, 0),), (), ()),
        (-1, 1): blocks(((1, 0),), (3,), ((1, 0),)),
        (1, -1): blocks(((0, 1),), (2,), ((0, 1),)),
    }
    sends = collections.OrderedDict()
    for (dt, dz), items in wanted.items():
        to = (dt % t_size, dz)
        if to == (0, 0):
            continue
        held = sends.setdefault(to, [])
        held.extend(item for item in items if item not in held)
    return [(to, items) for to, items in sends.items()]


def block_rows(items):
    offsets, row = {}, 0
    for item in items:
        offsets[item] = row
        row += VEC if item[0] == "x" else MAT
    return offsets, -(-row // 8) * 8


def local_row(item):
    kind, n, t, z = item
    r = 2 * t + z
    return r * VEC if kind == "x" else (r * 4 + n) * SLOT


def copy_block(kind, src, src_row, dst, dst_rows, change=None):
    done = 0
    for size in CHUNKS[kind]:
        value = src[pl.ds(src_row + done, size), :]
        if change is not None:
            value = change(value)
        for dst_row in dst_rows:
            dst[pl.ds(dst_row + done, size), :] = value
        done += size


def pack_kernel(plan, near_ref, far_ref, weight_ref, x_ref, u_ref, scale_ref, xl_ref, ul_ref, *rest):
    outs, wide = rest[:-1], rest[-1]
    upper = lax.broadcasted_iota(jnp.int32, (8, LANES), 0) < 4
    for p in range(NP):
        scale_ref[pl.ds(8 * p, 8), :] = jnp.full((8, LANES), near_ref[p], F32)
        scale_ref[pl.ds(8 * (NP + p), 8), :] = jnp.full((8, LANES), far_ref[p], F32)
    for group, (top, bottom) in enumerate(PAIRS):
        scale_ref[pl.ds(8 * (2 * NP + group), 8), :] = jnp.where(upper, weight_ref[top], weight_ref[bottom])
    wide[...] = u_ref[...].astype(F32)
    for r in range(4):
        for k in range(3):
            xl_ref[pl.ds(r * VEC + 8 * k, 8), :] = x_ref[pl.ds(r + 32 * k, 8, stride=4), :]
        for n in range(4):
            done = 0
            for size in CHUNKS["u"]:
                value = wide[pl.ds((MAT * n + done) * 4 + r, size, stride=4), :]
                ul_ref[pl.ds((r * 4 + n) * SLOT + done, size), :] = value
                done += size
    for out, (_, items) in zip(outs, plan):
        offsets, _ = block_rows(items)
        for item, row in offsets.items():
            copy_block(item[0], xl_ref if item[0] == "x" else ul_ref, local_row(item), out, (row,))


def tile_fields():
    x_fields, u_fields = [], []
    zero = (0, 0, 0, 0)
    for pair, crosses in zip(PAIRS, CROSS):
        for cross in crosses:
            for sign in (1, -1):
                start = [plus(zero, UNIT[n], sign) for n in cross]
                x_fields.append([("x", 0, start[h]) for h in range(2)])
                x_fields.append([("x", 0, plus(start[h], UNIT[pair[h]])) for h in range(2)])
                base = [zero if sign > 0 else start[h] for h in range(2)]
                u_fields.append([("u", cross[h], base[h]) for h in range(2)])
                u_fields.append([("u", cross[h], plus(base[h], UNIT[pair[h]])) for h in range(2)])
    x_fields.append([("x", 0, zero)] * 2)
    for pair in PAIRS:
        x_fields.append([("x", 0, UNIT[m]) for m in pair])
        x_fields.append([("x", 0, plus(zero, UNIT[m], 3)) for m in pair])
    return x_fields, u_fields


def find_block(where, t_size, kind, n, t, z):
    dt, t_in = divmod(t, 2)
    dz, z_in = divmod(z, 2)
    to = (dt % t_size, dz)
    item = (kind, n, t_in, z_in)
    if to == (0, 0):
        return ("local", kind), local_row(item)
    return to, where[to][item]


def lane_shifted(value, dx, dy):
    if dx != 0:
        x_at = lax.broadcasted_iota(jnp.int32, value.shape, 1) % NX
        beyond = (x_at + dx >= NX) | (x_at + dx < 0)
        main = pltpu.roll(value, (-dx) % LANES, 1)
        wrapped = pltpu.roll(value, (NX - dx if dx > 0 else -NX - dx) % LANES, 1)
        value = jnp.where(beyond, wrapped, main)
    if dy != 0:
        value = pltpu.roll(value, (-dy * NX) % LANES, 1)
    return value


def build_fields(buffers, where, t_size, x_tiles, u_tiles):
    x_fields, u_fields = tile_fields()
    copies = collections.OrderedDict()
    for target, fields in ((0, x_fields), (1, u_fields)):
        for index, halves in enumerate(fields):
            for half, (kind, n, disp) in enumerate(halves):
                for r in range(4):
                    source = find_block(where, t_size, kind, n, r // 2 + disp[3], r % 2 + disp[2])
                    row = index * TILE + (4 * half + r) * SLOT
                    group = copies.setdefault((kind,) + source, collections.OrderedDict())
                    group.setdefault((disp[0], disp[1]), []).append(row)
    for (kind, name, src_row), shifts in copies.items():
        target = x_tiles if kind == "x" else u_tiles
        for (dx, dy), rows in shifts.items():
            change = functools.partial(lane_shifted, dx=dx, dy=dy)
            copy_block(kind, buffers[name], src_row, target, rows, change)


def tile_of(ref, base, component):
    return ref[pl.ds(base + component, 8, stride=SLOT), :]


def vector_tiles(ref, base, pole):
    return [[tile_of(ref, base, pole * 6 + part * 3 + i) for i in range(3)] for part in range(2)]


def pole_sum(ref, here, ahead, scales):
    total = None
    for pole in range(NP):
        h = [[scales[pole] * v for v in part] for part in vector_tiles(ref, here, pole)]
        a = vector_tiles(ref, ahead, pole)
        real = [[a[0][i] * h[0][j] + a[1][i] * h[1][j] for j in range(3)] for i in range(3)]
        imag = [[a[1][i] * h[0][j] - a[0][i] * h[1][j] for j in range(3)] for i in range(3)]
        if total is None:
            total = [real, imag]
        else:
            total = [
                [[total[c][i][j] + new[i][j] for j in range(3)] for i in range(3)]
                for c, new in enumerate((real, imag))
            ]
    return total


def matrix_tiles(ref, base):
    return [
        [[tile_of(ref, base, part * 9 + i * 3 + j) for j in range(3)] for i in range(3)]
        for part in range(2)
    ]


def conj(matrix, transposed=True):
    return [[[matrix[part][j][i] for j in range(3)] for i in range(3)] for part in range(2)]


def row_times(row, right, row_sign, right_sign):
    result = [[], []]
    for j in range(3):
        real = imag = None
        for k in range(3):
            rr = row[0][k] * right[0][k][j]
            ii = row[1][k] * right[1][k][j]
            ri = row[0][k] * right[1][k][j]
            ir = row[1][k] * right[0][k][j]
            new_real = rr - ii if row_sign * right_sign > 0 else rr + ii
            if row_sign > 0 and right_sign > 0:
                new_imag = ri + ir
            elif row_sign > 0:
                new_imag = ir - ri
            else:
                new_imag = ri - ir
            real = new_real if real is None else real + new_real
            imag = new_imag if imag is None else imag + new_imag
        result[0].append(real)
        result[1].append(imag)
    return result


def main_kernel(names, where, t_size, scale_ref, xl_ref, ul_ref, *rest):
    received = rest[: len(names)]
    out_ref, x_tiles, u_tiles, acc = rest[len(names) :]
    buffers = {("local", "x"): xl_ref, ("local", "u"): ul_ref}
    buffers.update(zip(names, received))
    build_fields(buffers, where, t_size, x_tiles, u_tiles)
    near = [scale_ref[pl.ds(8 * p, 8), :] for p in range(NP)]
    far = [scale_ref[pl.ds(8 * (NP + p), 8), :] for p in range(NP)]
    upper = lax.broadcasted_iota(jnp.int32, (8, LANES), 0) < 4

    def term(step, first):
        group = step // 3
        for side in range(2):
            base = (step * 2 + side) * 2 * TILE
            force = pole_sum(x_tiles, base, base + TILE, near)
            left = matrix_tiles(u_tiles, base)
            right = matrix_tiles(u_tiles, base + TILE)
            if side == 1:
                left = conj(left)
            else:
                right = conj(right)
            for i in range(3):
                row = [left[0][i], left[1][i]]
                if side == 0:
                    row = row_times(row_times(row, force, 1, 1), right, 1, -1)
                else:
                    row = row_times(row_times(row, force, -1, 1), right, 1, 1)
                for part in range(2):
                    for j in range(3):
                        at = pl.ds((group * MAT + part * 9 + i * 3 + j) * 8, 8)
                        acc[at, :] = acc[at, :] + row[part][j]

    acc[...] = jnp.zeros_like(acc)
    lax.fori_loop(0, 6, lambda step, _: (term(step, False), 0)[1], 0)
    own = 24 * TILE
    for group, (top, bottom) in enumerate(PAIRS):
        near_sum = pole_sum(x_tiles, own, own + (1 + 2 * group) * TILE, near)
        far_sum = pole_sum(x_tiles, own, own + (2 + 2 * group) * TILE, far)
        weight = scale_ref[pl.ds(8 * (2 * NP + group), 8), :]
        done = []
        for c in range(MAT):
            part, i, j = c // 9, c // 3 % 3, c % 3
            staple = acc[pl.ds((group * MAT + c) * 8, 8), :]
            done.append(near_sum[part][i][j] + far_sum[part][i][j] + weight * staple)
        for c in range(0, MAT, 2):
            first, second = done[c], done[c + 1]
            out_ref[pl.ds((top * MAT + c) * 4, 8), :] = jnp.where(upper, first, pltpu.roll(second, 4, 0))
            out_ref[pl.ds((bottom * MAT + c) * 4, 8), :] = jnp.where(upper, pltpu.roll(first, 4, 0), second)


def on_device(pole_vectors, gauge_links, pole_coeff, naik_coeff, staple_weight):
    t_size = lax.axis_size("ta")
    z_size = lax.axis_size("gz") * lax.axis_size("gy")
    plan = halo_plan(t_size)
    vmem = pl.BlockSpec(memory_space=pltpu.VMEM)
    smem = pl.BlockSpec(memory_space=pltpu.SMEM)
    sizes = [block_rows(items)[1] for _, items in plan]
    packed = pl.pallas_call(
        functools.partial(pack_kernel, plan),
        out_shape=[
            jax.ShapeDtypeStruct((rows, LANES), F32) for rows in [8 * (2 * NP + 2), 4 * VEC, 16 * SLOT] + sizes
        ],
        in_specs=[smem] * 3 + [vmem] * 2,
        out_specs=[vmem] * (3 + len(plan)),
        scratch_shapes=[pltpu.VMEM((4 * 4 * MAT, LANES), F32)],
        compiler_params=pltpu.CompilerParams(vmem_limit_bytes=4 * 1024 * 1024),
        name="pack_halos",
    )(pole_coeff, naik_coeff, staple_weight, pole_vectors.reshape((4 * VEC, LANES)), gauge_links.reshape((16 * MAT, LANES)))
    local, sends = packed[:3], packed[3:]
    received = []
    for ((dt, dz), _), value in zip(plan, sends):
        if dt == 0:
            axes = ("gz", "gy")
            pairs = [((i + dz) % z_size, i) for i in range(z_size)]
        elif dz == 0:
            axes = "ta"
            pairs = [((j + dt) % t_size, j) for j in range(t_size)]
        else:
            axes = ("gz", "ta", "gy")
            halves = lax.axis_size("gy")

            def index(j, i):
                return ((i // halves) * t_size + j) * halves + i % halves

            pairs = [
                (index((j + dt) % t_size, (i + dz) % z_size), index(j, i))
                for j in range(t_size)
                for i in range(z_size)
            ]
        received.append(lax.ppermute(value, axes, pairs))
    names = [to for to, _ in plan]
    where = {to: block_rows(items)[0] for to, items in plan}
    x_fields, u_fields = tile_fields()
    force = pl.pallas_call(
        functools.partial(main_kernel, names, where, t_size),
        out_shape=jax.ShapeDtypeStruct((16 * MAT, LANES), F32),
        in_specs=[vmem] * (3 + len(plan)),
        out_specs=vmem,
        scratch_shapes=[
            pltpu.VMEM((len(x_fields) * TILE, LANES), F32),
            pltpu.VMEM((len(u_fields) * TILE, LANES), F32),
            pltpu.VMEM((2 * MAT * 8, LANES), F32),
        ],
        compiler_params=pltpu.CompilerParams(vmem_limit_bytes=12 * 1024 * 1024),
        name="force",
    )(*local, *received)
    return force.reshape(gauge_links.shape)


def solution(mesh):
    return jax.shard_map(
        on_device,
        mesh=mesh,
        in_specs=(
            P("ens", None, None, "ta", ("gz", "gy"), None),
            P("ens", None, None, None, "ta", ("gz", "gy"), None),
            P(),
            P(),
            P(),
        ),
        out_specs=P("ens", None, None, None, "ta", ("gz", "gy"), None),
        check_vma=False,
    )
```

```python
import collections
import functools

import jax
import jax.numpy as jnp
from jax import lax
from jax.experimental import pallas as pl
from jax.experimental.pallas import tpu as pltpu
from jax.sharding import PartitionSpec as P

NX = 8
NY = 16
LANES = NX * NY
NP = 4
F32 = jnp.float32
REGS = {"x": NP * 3, "u": 9}
UNIT = ((1, 0, 0, 0), (0, 1, 0, 0), (0, 0, 1, 0), (0, 0, 0, 1))
ZERO = (0, 0, 0, 0)
SITES = ((0, 0), (0, 1), (1, 0), (1, 1))
NEAR_TERMS = ((0, ((0, 1), (1, 0))), (0, ((0, 2), (1, 2))), (1, ((2, 0), (2, 1))))
FAR_TERMS = ((0, ((0, 3), (1, 3))), (1, ((3, 0), (3, 1))), (2, ((2, 3), (3, 2))))


def plus(left, right, scale=1):
    return tuple(a + scale * b for a, b in zip(left, right))


class Message:
    def __init__(self):
        self.places = collections.OrderedDict()
        self.count = 0

    def add_full(self, kind, n):
        for k in range(REGS[kind]):
            for t, z in SITES:
                self.places[0, kind, n, k, t, z] = (self.count, 2 * t + z)
            self.count += 1

    def add_halves(self, entries, axis):
        half = -(-len(entries) // 2)
        for index, (kind, n, k, layer) in enumerate(entries):
            reg, part = self.count + index % half, index // half
            for other in range(2):
                t, z = (layer, other) if axis == "t" else (other, layer)
                slot = 2 * part + other if axis == "t" else 2 * other + part
                self.places[0, kind, n, k, t, z] = (reg, slot)
        self.count += half

    def add_single(self, entries):
        quarter = -(-len(entries) // 4)
        for index, entry in enumerate(entries):
            self.places[entry] = (self.count + index % quarter, index // quarter)
        self.count += quarter

    def by_register(self):
        found = [[None] * 4 for _ in range(self.count)]
        for item, (reg, slot) in self.places.items():
            found[reg][slot] = item
        return found


def regs_of(kind, directions, layer):
    return [(kind, n, k, layer) for n in directions for k in range(REGS[kind])]


def message_plan(t_size):
    plan = collections.OrderedDict()
    ahead = plan["z", 1] = Message()
    ahead.add_full("x", 0)
    ahead.add_halves(regs_of("u", (0, 1, 3), 0), "z")
    behind = plan["z", -1] = Message()
    behind.add_halves(regs_of("x", (0,), 1) + regs_of("u", (2,), 1), "z")
    second = plan["z", 2] = Message()
    second.add_halves(regs_of("x", (0,), 0), "z")
    halves, corners = collections.OrderedDict(), collections.OrderedDict()
    for dt, entries in (
        (1, regs_of("u", (0, 1, 2), 0)),
        (-1, regs_of("x", (0,), 1) + regs_of("u", (3,), 1)),
        (2, regs_of("x", (0,), 0)),
    ):
        if dt % t_size != 0:
            halves.setdefault(dt % t_size, []).extend(entries)
    for dt, entries in halves.items():
        message = plan["t", dt] = Message()
        if dt == 1:
            message.add_full("x", 0)
        held = {item[1:4] for item in message.places}
        message.add_halves([e for e in entries if e[:3] not in held], "t")
    for dt, entries in (
        (1, [(1, "x", 0, k, 0, 0) for k in range(REGS["x"])]),
        (1, [(-1, "x", 0, k, 0, 1) for k in range(REGS["x"])]),
        (1, [(-1, "u", 2, k, 0, 1) for k in range(REGS["u"])]),
        (-1, [(1, "x", 0, k, 1, 0) for k in range(REGS["x"])]),
        (-1, [(1, "u", 3, k, 1, 0) for k in range(REGS["u"])]),
    ):
        corners.setdefault(dt % t_size, []).extend(entries)
    for dt, entries in corners.items():
        plan["c", dt] = Message()
        plan["c", dt].add_single(entries)
    return plan


class Locator:
    def __init__(self, plan, t_size, buffers):
        self.plan, self.t_size, self.buffers = plan, t_size, buffers

    def local(self, kind, n, k, t, z):
        return ("own", kind), n * REGS[kind] + k, 2 * t + z

    def find(self, kind, n, k, t_at, z_at):
        (dt, t), (dz, z) = divmod(t_at, 2), divmod(z_at, 2)
        dt %= self.t_size
        if (dt, dz) == (0, 0):
            return self.local(kind, n, k, t, z)
        name = ("z", dz) if dt == 0 else ("t", dt) if dz == 0 else ("c", dt)
        item = (dz if name[0] == "c" else 0, kind, n, k, t, z)
        return (name,) + self.plan[name].places[item]

    def load(self, name, reg):
        return self.buffers[name][pl.ds(8 * reg, 8), :]

    def assemble(self, spots):
        groups = collections.OrderedDict()
        for r, spot in enumerate(spots):
            if spot is not None:
                groups.setdefault((spot[0], spot[1], r - spot[2]), []).append(r)
        row = lax.broadcasted_iota(jnp.int32, (8, LANES), 0) % 4
        result = None
        for (name, reg, move), rows in groups.items():
            value = self.load(name, reg)
            if move != 0:
                value = pltpu.roll(value, move % 8, 0)
            if result is None:
                result = value
            else:
                mask = functools.reduce(jnp.logical_or, [row == r for r in rows])
                result = jnp.where(mask, value, result)
        return result

    def field_register(self, kind, n, k, dt, dz):
        return self.assemble([self.find(kind, n, k, t + dt, z + dz) for t, z in SITES])


def lane_shifted(value, dx, dy):
    if dx != 0:
        x_at = lax.broadcasted_iota(jnp.int32, value.shape, 1) % NX
        beyond = (x_at + dx >= NX) | (x_at + dx < 0)
        main = pltpu.roll(value, (-dx) % LANES, 1)
        wrapped = pltpu.roll(value, (NX - dx if dx > 0 else -NX - dx) % LANES, 1)
        value = jnp.where(beyond, wrapped, main)
    if dy != 0:
        value = pltpu.roll(value, (-dy * NX) % LANES, 1)
    return value


def term_fields(halves, sign):
    here, ahead, left, right = [], [], [], []
    for m, n in halves:
        start = plus(ZERO, UNIT[n], sign)
        base = ZERO if sign > 0 else start
        here.append(("x", 0, start))
        ahead.append(("x", 0, plus(start, UNIT[m])))
        left.append(("u", n, base))
        right.append(("u", n, plus(base, UNIT[m])))
    return here, ahead, left, right


def needed_fields(terms, own):
    keys = collections.OrderedDict()
    for _, halves in terms:
        for sign in (1, -1):
            for pair in term_fields(halves, sign):
                keys.update((key, None) for key in pair)
    for m in own:
        for scale in (1, 3):
            keys["x", 0, plus(ZERO, UNIT[m], scale)] = None
    return [key for key in keys if key[2] != ZERO]


def lay_out(keys):
    rows, total = collections.OrderedDict(), 0
    for key in keys:
        rows[key] = total
        total += 8 * REGS[key[0]]
    return rows, total


def field_split():
    near = needed_fields(NEAR_TERMS, (0, 1, 2))
    far = needed_fields(FAR_TERMS, (3,))
    still = [key for key in far if key[2][3] == 0]
    shared = lay_out(still)
    first = lay_out([key for key in near if key not in shared[0]])
    second = lay_out([key for key in far if key not in shared[0]])
    return shared, first, second


def build_fields(locator, stores):
    groups = collections.OrderedDict()
    for ref, rows in stores:
        for (kind, n, disp), row in rows.items():
            shifts = groups.setdefault((kind, n, disp[3], disp[2]), collections.OrderedDict())
            shifts[disp[0], disp[1]] = (ref, row)
    for (kind, n, dt, dz), shifts in groups.items():
        for k in range(REGS[kind]):
            value = locator.field_register(kind, n, k, dt, dz)
            by_x = {0: value}
            for (dx, dy), (ref, row) in shifts.items():
                if dx not in by_x:
                    by_x[dx] = lane_shifted(value, dx, 0)
                ref[pl.ds(row + 8 * k, 8), :] = lane_shifted(by_x[dx], 0, dy)


class Fields:
    def __init__(self, own_x, own_u, stores):
        self.place = {("x", 0, ZERO): (own_x, 0)}
        for n in range(4):
            self.place["u", n, ZERO] = (own_u, 8 * REGS["u"] * n)
        for ref, rows in stores:
            for key, row in rows.items():
                self.place[key] = (ref, row)
        self.upper = lax.broadcasted_iota(jnp.int32, (8, LANES), 0) < 4

    def reg(self, key, k):
        ref, row = self.place[key]
        return ref[pl.ds(row + 8 * k, 8), :]

    def two_tiles(self, keys, k):
        top = self.reg(keys[0], k)
        turned_top = pltpu.roll(top, 4, 0)
        if keys[0] == keys[1]:
            low, turned_low = top, turned_top
        else:
            low = self.reg(keys[1], k)
            turned_low = pltpu.roll(low, 4, 0)
        return [jnp.where(self.upper, top, turned_low), jnp.where(self.upper, turned_top, low)]

    def vector(self, keys, pole):
        flat = [tile for k in range(3) for tile in self.two_tiles(keys, 3 * pole + k)]
        return [flat[:3], flat[3:]]

    def matrix(self, keys):
        flat = [tile for k in range(9) for tile in self.two_tiles(keys, k)]
        return [[flat[9 * c + 3 * i : 9 * c + 3 * i + 3] for i in range(3)] for c in range(2)]

    def compact_halves(self, first, second):
        top = jnp.where(self.upper, first, pltpu.roll(second, 4, 0))
        return top, jnp.where(self.upper, pltpu.roll(first, 4, 0), second)

    def compact_sum(self, first, second):
        kept = jnp.where(self.upper, first, second)
        return kept + pltpu.roll(jnp.where(self.upper, second, first), 4, 0)


def pole_sum(fields, here, ahead, scales):
    total = None
    for pole in range(NP):
        h = [[scales[pole] * v for v in part] for part in fields.vector(here, pole)]
        a = fields.vector(ahead, pole)
        real = [[a[0][i] * h[0][j] + a[1][i] * h[1][j] for j in range(3)] for i in range(3)]
        imag = [[a[1][i] * h[0][j] - a[0][i] * h[1][j] for j in range(3)] for i in range(3)]
        if total is None:
            total = [real, imag]
        else:
            total = [
                [[total[c][i][j] + new[i][j] for j in range(3)] for i in range(3)]
                for c, new in enumerate((real, imag))
            ]
    return total


def transposed(matrix):
    return [[[part[j][i] for j in range(3)] for i in range(3)] for part in matrix]


def row_times(row, right, row_sign, right_sign):
    result = [[], []]
    for j in range(3):
        real = imag = None
        for k in range(3):
            rr = row[0][k] * right[0][k][j]
            ii = row[1][k] * right[1][k][j]
            ri = row[0][k] * right[1][k][j]
            ir = row[1][k] * right[0][k][j]
            new_real = rr - ii if row_sign * right_sign > 0 else rr + ii
            if row_sign > 0 and right_sign > 0:
                new_imag = ri + ir
            elif row_sign > 0:
                new_imag = ir - ri
            else:
                new_imag = ri - ir
            real = new_real if real is None else real + new_real
            imag = new_imag if imag is None else imag + new_imag
        result[0].append(real)
        result[1].append(imag)
    return result


def add_terms(fields, terms, near, acc):
    started = set()
    for target, halves in terms:
        for sign in (1, -1):
            here, ahead, left, right = term_fields(halves, sign)
            force = pole_sum(fields, here, ahead, near)
            left = fields.matrix(left)
            right = fields.matrix(right)
            if sign > 0:
                right = transposed(right)
            else:
                left = transposed(left)
            rows = [row_times([left[0][i], left[1][i]], force, sign, 1) for i in range(3)]
            for i in range(3):
                row = row_times(rows[i], right, 1, -sign)
                for part in range(2):
                    for j in range(3):
                        at = pl.ds((target * 18 + part * 9 + i * 3 + j) * 8, 8)
                        new = row[part][j]
                        acc[at, :] = acc[at, :] + new if target in started else new
            started.add(target)


def acc_tile(acc, target, c):
    return acc[pl.ds((target * 18 + c) * 8, 8), :]


def scale_tiles(scale_ref):
    tiles = [scale_ref[pl.ds(8 * p, 8), :] for p in range(3 * NP)]
    return tiles[:NP], tiles[NP : 2 * NP], tiles[2 * NP :]


def own_force(fields, m, both):
    total = pole_sum(
        fields,
        [("x", 0, ZERO)] * 2,
        [("x", 0, UNIT[m]), ("x", 0, plus(ZERO, UNIT[m], 3))],
        both,
    )
    flat = [total[c][i][j] for c in range(2) for i in range(3) for j in range(3)]
    return [fields.compact_sum(flat[2 * k], flat[2 * k + 1]) for k in range(9)]


def pack_kernel(plan, names, near_in, far_in, weight_in, x_in, u_in, *rest):
    outs = rest[: len(names)]
    scale_ref, x_ref, u_ref, near_ref, far_ref, weight_ref, u_held, sems = rest[len(names) :]
    copies = [
        pltpu.make_async_copy(source, target, sems.at[index])
        for index, (source, target) in enumerate(
            ((u_in, u_held), (x_in, x_ref), (near_in, near_ref), (far_in, far_ref), (weight_in, weight_ref))
        )
    ]
    for copy in copies:
        copy.start()
    for copy in copies:
        copy.wait()
    u_ref[...] = u_held[...].astype(F32)
    locator = Locator(plan, 1, {("own", "x"): x_ref, ("own", "u"): u_ref})
    for name, out in zip(names, outs):
        for reg, items in enumerate(plan[name].by_register()):
            spots = [item and locator.local(*item[1:]) for item in items]
            out[pl.ds(8 * reg, 8), :] = locator.assemble(spots)
    upper = lax.broadcasted_iota(jnp.int32, (8, LANES), 0) < 4
    for p in range(NP):
        scale_ref[pl.ds(8 * p, 8), :] = jnp.full((8, LANES), near_ref[p], F32)
        scale_ref[pl.ds(8 * (NP + p), 8), :] = jnp.where(upper, near_ref[p], far_ref[p])
        scale_ref[pl.ds(8 * (2 * NP + p), 8), :] = jnp.full((8, LANES), weight_ref[p], F32)


def corner_kernel(plan, names, ahead_ref, behind_ref, *outs):
    locator = Locator(plan, 1, {("z", 1): ahead_ref, ("z", -1): behind_ref})
    for name, out in zip(names, outs):
        for reg, items in enumerate(plan[name].by_register()):
            spots = [
                item and (("z", item[0]),) + plan["z", item[0]].places[(0,) + item[1:]] for item in items
            ]
            out[pl.ds(8 * reg, 8), :] = locator.assemble(spots)


def near_kernel(plan, t_size, names, scale_ref, x_ref, u_ref, *rest):
    received = rest[: len(names)]
    shared_ref, part_ref, first_ref, acc = rest[len(names) :]
    buffers = {("own", "x"): x_ref, ("own", "u"): u_ref}
    buffers.update(zip(names, received))
    shared, first, _ = field_split()
    stores = [(shared_ref, shared[0]), (first_ref, first[0])]
    build_fields(Locator(plan, t_size, buffers), stores)
    fields = Fields(x_ref, u_ref, stores)
    near, both, weight = scale_tiles(scale_ref)
    add_terms(fields, NEAR_TERMS, near, acc)
    own = [own_force(fields, m, both) for m in range(3)]
    for k in range(9):
        staples = list(fields.compact_halves(acc_tile(acc, 0, 2 * k), acc_tile(acc, 0, 2 * k + 1)))
        staples.append(fields.compact_sum(acc_tile(acc, 1, 2 * k), acc_tile(acc, 1, 2 * k + 1)))
        for m in range(3):
            part_ref[pl.ds((9 * m + k) * 8, 8), :] = own[m][k] + weight[m] * staples[m]


def far_kernel(plan, t_size, names, scale_ref, x_ref, u_ref, shared_ref, part_ref, *rest):
    received = rest[: len(names)]
    out_ref, second_ref, acc = rest[len(names) :]
    buffers = {("own", "x"): x_ref, ("own", "u"): u_ref}
    buffers.update(zip(names, received))
    shared, _, second = field_split()
    build_fields(Locator(plan, t_size, buffers), [(second_ref, second[0])])
    fields = Fields(x_ref, u_ref, [(shared_ref, shared[0]), (second_ref, second[0])])
    near, both, weight = scale_tiles(scale_ref)
    add_terms(fields, FAR_TERMS, near, acc)
    own = own_force(fields, 3, both)
    for k in range(9):
        pairs = [[acc_tile(acc, target, 2 * k + c) for c in range(2)] for target in range(3)]
        in_x, in_y = fields.compact_halves(*pairs[0])
        in_z, in_t = fields.compact_halves(*pairs[2])
        in_t = in_t + fields.compact_sum(*pairs[1])
        for m, staple in enumerate((in_x, in_y, in_z, in_t)):
            start = own[k] if m == 3 else part_ref[pl.ds((9 * m + k) * 8, 8), :]
            out_ref[pl.ds((9 * m + k) * 8, 8), :] = start + weight[m] * staple


def rows_of(count):
    return jax.ShapeDtypeStruct((count, LANES), F32)


def on_device(pole_vectors, gauge_links, pole_coeff, naik_coeff, staple_weight):
    t_size = lax.axis_size("ta")
    z_size = lax.axis_size("gz") * lax.axis_size("gy")
    plan = message_plan(t_size)
    x_rows, u_rows = 8 * REGS["x"], 4 * 8 * REGS["u"]
    vmem = pl.BlockSpec(memory_space=pltpu.VMEM)
    hbm = pl.BlockSpec(memory_space=pltpu.HBM)
    limit = pltpu.CompilerParams(vmem_limit_bytes=4 * 1024 * 1024)

    def moved(name, value):
        kind, step = name
        if kind == "z":
            return lax.ppermute(value, ("gz", "gy"), [((i + step) % z_size, i) for i in range(z_size)])
        return lax.ppermute(value, "ta", [((j + step) % t_size, j) for j in range(t_size)])

    first_names = [name for name in plan if name[0] != "c"]
    corner_names = [name for name in plan if name[0] == "c"]
    z_names = [name for name in first_names if name[0] == "z"]
    packed = pl.pallas_call(
        functools.partial(pack_kernel, plan, first_names),
        out_shape=[rows_of(8 * plan[name].count) for name in first_names]
        + [rows_of(8 * 3 * NP), rows_of(x_rows), rows_of(u_rows)],
        in_specs=[hbm] * 5,
        out_specs=[vmem] * (len(first_names) + 3),
        scratch_shapes=[pltpu.SMEM((NP,), F32)] * 3
        + [pltpu.VMEM((u_rows, LANES), jnp.bfloat16), pltpu.SemaphoreType.DMA((5,))],
        compiler_params=limit,
        name="pack_halos",
    )(
        pole_coeff,
        naik_coeff,
        staple_weight,
        pole_vectors.reshape((x_rows, LANES)),
        gauge_links.reshape((u_rows, LANES)),
    )
    local = packed[len(first_names) :]
    received = {name: moved(name, value) for name, value in zip(first_names, packed)}
    corners = pl.pallas_call(
        functools.partial(corner_kernel, plan, corner_names),
        out_shape=[rows_of(8 * plan[name].count) for name in corner_names],
        in_specs=[vmem] * 2,
        out_specs=[vmem] * len(corner_names),
        compiler_params=limit,
        name="pack_corners",
    )(received["z", 1], received["z", -1])
    received.update({name: moved(name, value) for name, value in zip(corner_names, corners)})
    shared, first, second = field_split()
    shared_values, part = pl.pallas_call(
        functools.partial(near_kernel, plan, t_size, z_names),
        out_shape=[rows_of(shared[1]), rows_of(3 * 8 * REGS["u"])],
        in_specs=[vmem] * (3 + len(z_names)),
        out_specs=[vmem] * 2,
        scratch_shapes=[pltpu.VMEM((first[1], LANES), F32), pltpu.VMEM((2 * 18 * 8, LANES), F32)],
        cost_estimate=pl.CostEstimate(flops=4 * 10**6, bytes_accessed=4 * 10**6, transcendentals=0),
        compiler_params=pltpu.CompilerParams(vmem_limit_bytes=8 * 1024 * 1024),
        name="force_without_t",
    )(*local, *[received[name] for name in z_names])
    far_names = [name for name in received if name != ("z", 2)]
    force = pl.pallas_call(
        functools.partial(far_kernel, plan, t_size, far_names),
        out_shape=rows_of(u_rows),
        in_specs=[vmem] * (5 + len(far_names)),
        out_specs=vmem,
        scratch_shapes=[pltpu.VMEM((second[1], LANES), F32), pltpu.VMEM((3 * 18 * 8, LANES), F32)],
        compiler_params=pltpu.CompilerParams(vmem_limit_bytes=8 * 1024 * 1024),
        name="force_with_t",
    )(*local, shared_values, part, *[received[name] for name in far_names])
    return force.reshape(gauge_links.shape)


def solution(mesh):
    return jax.shard_map(
        on_device,
        mesh=mesh,
        in_specs=(
            P("ens", None, None, "ta", ("gz", "gy"), None),
            P("ens", None, None, None, "ta", ("gz", "gy"), None),
            P(),
            P(),
            P(),
        ),
        out_specs=P("ens", None, None, None, "ta", ("gz", "gy"), None),
        check_vma=False,
    )
```

```python
import collections
import functools

import jax
import jax.numpy as jnp
from jax import lax
from jax.experimental import pallas as pl
from jax.experimental.pallas import tpu as pltpu
from jax.sharding import PartitionSpec as P

NX = 8
NY = 16
LANES = NX * NY
NP = 4
F32 = jnp.float32
REGS = {"x": NP * 3, "u": 9}
UNIT = ((1, 0, 0, 0), (0, 1, 0, 0), (0, 0, 1, 0), (0, 0, 0, 1))
ZERO = (0, 0, 0, 0)
SITES = ((0, 0), (0, 1), (1, 0), (1, 1))
NEAR_TERMS = ((0, ((0, 1), (1, 0))), (0, ((0, 2), (1, 2))), (1, ((2, 0), (2, 1))))
FAR_TERMS = ((0, ((0, 3), (1, 3))), (1, ((3, 0), (3, 1))), (2, ((2, 3), (3, 2))))


def plus(left, right, scale=1):
    return tuple(a + scale * b for a, b in zip(left, right))


class Message:
    def __init__(self):
        self.places = collections.OrderedDict()
        self.count = 0

    def add_full(self, kind, n):
        for k in range(REGS[kind]):
            for t, z in SITES:
                self.places[0, kind, n, k, t, z] = (self.count, 2 * t + z)
            self.count += 1

    def add_halves(self, entries, axis):
        half = -(-len(entries) // 2)
        for index, (kind, n, k, layer) in enumerate(entries):
            reg, part = self.count + index % half, index // half
            for other in range(2):
                t, z = (layer, other) if axis == "t" else (other, layer)
                slot = 2 * part + other if axis == "t" else 2 * other + part
                self.places[0, kind, n, k, t, z] = (reg, slot)
        self.count += half

    def add_single(self, entries):
        quarter = -(-len(entries) // 4)
        for index, entry in enumerate(entries):
            self.places[entry] = (self.count + index % quarter, index // quarter)
        self.count += quarter

    def by_register(self):
        found = [[None] * 4 for _ in range(self.count)]
        for item, (reg, slot) in self.places.items():
            found[reg][slot] = item
        return found


def regs_of(kind, directions, layer):
    return [(kind, n, k, layer) for n in directions for k in range(REGS[kind])]


def message_plan(t_size):
    plan = collections.OrderedDict()
    ahead = plan["z", 1] = Message()
    ahead.add_full("x", 0)
    ahead.add_halves(regs_of("u", (0, 1, 3), 0), "z")
    behind = plan["z", -1] = Message()
    behind.add_halves(regs_of("x", (0,), 1) + regs_of("u", (2,), 1), "z")
    second = plan["z", 2] = Message()
    second.add_halves(regs_of("x", (0,), 0), "z")
    halves, corners = collections.OrderedDict(), collections.OrderedDict()
    for dt, entries in (
        (1, regs_of("u", (0, 1, 2), 0)),
        (-1, regs_of("x", (0,), 1) + regs_of("u", (3,), 1)),
        (2, regs_of("x", (0,), 0)),
    ):
        if dt % t_size != 0:
            halves.setdefault(dt % t_size, []).extend(entries)
    for dt, entries in halves.items():
        message = plan["t", dt] = Message()
        if dt == 1:
            message.add_full("x", 0)
        held = {item[1:4] for item in message.places}
        message.add_halves([e for e in entries if e[:3] not in held], "t")
    for dt, entries in (
        (1, [(1, "x", 0, k, 0, 0) for k in range(REGS["x"])]),
        (1, [(-1, "x", 0, k, 0, 1) for k in range(REGS["x"])]),
        (1, [(-1, "u", 2, k, 0, 1) for k in range(REGS["u"])]),
        (-1, [(1, "x", 0, k, 1, 0) for k in range(REGS["x"])]),
        (-1, [(1, "u", 3, k, 1, 0) for k in range(REGS["u"])]),
    ):
        corners.setdefault(dt % t_size, []).extend(entries)
    for dt, entries in corners.items():
        plan["c", dt] = Message()
        plan["c", dt].add_single(entries)
    return plan


class Locator:
    def __init__(self, plan, t_size, buffers):
        self.plan, self.t_size, self.buffers = plan, t_size, buffers

    def local(self, kind, n, k, t, z):
        return ("own", kind), n * REGS[kind] + k, 2 * t + z

    def find(self, kind, n, k, t_at, z_at):
        (dt, t), (dz, z) = divmod(t_at, 2), divmod(z_at, 2)
        dt %= self.t_size
        if (dt, dz) == (0, 0):
            return self.local(kind, n, k, t, z)
        name = ("z", dz) if dt == 0 else ("t", dt) if dz == 0 else ("c", dt)
        item = (dz if name[0] == "c" else 0, kind, n, k, t, z)
        return (name,) + self.plan[name].places[item]

    def load(self, name, reg):
        return self.buffers[name][pl.ds(8 * reg, 8), :]

    def assemble(self, spots):
        groups = collections.OrderedDict()
        for r, spot in enumerate(spots):
            if spot is not None:
                groups.setdefault((spot[0], spot[1], r - spot[2]), []).append(r)
        row = lax.broadcasted_iota(jnp.int32, (8, LANES), 0) % 4
        result = None
        for (name, reg, move), rows in groups.items():
            value = self.load(name, reg)
            if move != 0:
                value = pltpu.roll(value, move % 8, 0)
            if result is None:
                result = value
            else:
                mask = functools.reduce(jnp.logical_or, [row == r for r in rows])
                result = jnp.where(mask, value, result)
        return result

    def field_register(self, kind, n, k, dt, dz):
        return self.assemble([self.find(kind, n, k, t + dt, z + dz) for t, z in SITES])


def lane_shifted(value, dx, dy):
    if dx != 0:
        x_at = lax.broadcasted_iota(jnp.int32, value.shape, 1) % NX
        beyond = (x_at + dx >= NX) | (x_at + dx < 0)
        main = pltpu.roll(value, (-dx) % LANES, 1)
        wrapped = pltpu.roll(value, (NX - dx if dx > 0 else -NX - dx) % LANES, 1)
        value = jnp.where(beyond, wrapped, main)
    if dy != 0:
        value = pltpu.roll(value, (-dy * NX) % LANES, 1)
    return value


def term_fields(halves, sign):
    here, ahead, left, right = [], [], [], []
    for m, n in halves:
        start = plus(ZERO, UNIT[n], sign)
        base = ZERO if sign > 0 else start
        here.append(("x", 0, start))
        ahead.append(("x", 0, plus(start, UNIT[m])))
        left.append(("u", n, base))
        right.append(("u", n, plus(base, UNIT[m])))
    return here, ahead, left, right


def needed_fields(terms, own):
    keys = collections.OrderedDict()
    for _, halves in terms:
        for sign in (1, -1):
            for pair in term_fields(halves, sign):
                keys.update((key, None) for key in pair)
    for m in own:
        for scale in (1, 3):
            keys["x", 0, plus(ZERO, UNIT[m], scale)] = None
    return [key for key in keys if key[2] != ZERO]


def lay_out(keys):
    rows, total = collections.OrderedDict(), 0
    for key in keys:
        rows[key] = total
        total += 8 * REGS[key[0]]
    return rows, total


def field_split():
    near = needed_fields(NEAR_TERMS, (0, 1))
    far = needed_fields(FAR_TERMS, (2, 3))
    still = [key for key in far if key[2][3] == 0 and abs(key[2][2]) < 3]
    shared = lay_out(still)
    first = lay_out([key for key in near if key not in shared[0]])
    second = lay_out([key for key in far if key not in shared[0]])
    return shared, first, second


def build_fields(locator, stores):
    groups = collections.OrderedDict()
    for ref, rows in stores:
        for (kind, n, disp), row in rows.items():
            shifts = groups.setdefault((kind, n, disp[3], disp[2]), collections.OrderedDict())
            shifts[disp[0], disp[1]] = (ref, row)
    for (kind, n, dt, dz), shifts in groups.items():
        for k in range(REGS[kind]):
            value = locator.field_register(kind, n, k, dt, dz)
            by_x = {0: value}
            for (dx, dy), (ref, row) in shifts.items():
                if dx not in by_x:
                    by_x[dx] = lane_shifted(value, dx, 0)
                ref[pl.ds(row + 8 * k, 8), :] = lane_shifted(by_x[dx], 0, dy)


class Fields:
    def __init__(self, own_x, own_u, stores):
        self.place = {("x", 0, ZERO): (own_x, 0)}
        for n in range(4):
            self.place["u", n, ZERO] = (own_u, 8 * REGS["u"] * n)
        for ref, rows in stores:
            for key, row in rows.items():
                self.place[key] = (ref, row)
        self.upper = lax.broadcasted_iota(jnp.int32, (8, LANES), 0) < 4

    def reg(self, key, k):
        ref, row = self.place[key]
        return ref[pl.ds(row + 8 * k, 8), :]

    def two_tiles(self, keys, k):
        top = self.reg(keys[0], k)
        turned_top = pltpu.roll(top, 4, 0)
        if keys[0] == keys[1]:
            low, turned_low = top, turned_top
        else:
            low = self.reg(keys[1], k)
            turned_low = pltpu.roll(low, 4, 0)
        return [jnp.where(self.upper, top, turned_low), jnp.where(self.upper, turned_top, low)]

    def vector(self, keys, pole):
        flat = [tile for k in range(3) for tile in self.two_tiles(keys, 3 * pole + k)]
        return [flat[:3], flat[3:]]

    def matrix(self, keys):
        flat = [tile for k in range(9) for tile in self.two_tiles(keys, k)]
        return [[flat[9 * c + 3 * i : 9 * c + 3 * i + 3] for i in range(3)] for c in range(2)]

    def compact_halves(self, first, second):
        top = jnp.where(self.upper, first, pltpu.roll(second, 4, 0))
        return top, jnp.where(self.upper, pltpu.roll(first, 4, 0), second)

    def compact_sum(self, first, second):
        kept = jnp.where(self.upper, first, second)
        return kept + pltpu.roll(jnp.where(self.upper, second, first), 4, 0)


def pole_sum(fields, here, ahead, scales):
    total = None
    for pole in range(NP):
        h = [[scales[pole] * v for v in part] for part in fields.vector(here, pole)]
        a = fields.vector(ahead, pole)
        real = [[a[0][i] * h[0][j] + a[1][i] * h[1][j] for j in range(3)] for i in range(3)]
        imag = [[a[1][i] * h[0][j] - a[0][i] * h[1][j] for j in range(3)] for i in range(3)]
        if total is None:
            total = [real, imag]
        else:
            total = [
                [[total[c][i][j] + new[i][j] for j in range(3)] for i in range(3)]
                for c, new in enumerate((real, imag))
            ]
    return total


def transposed(matrix):
    return [[[part[j][i] for j in range(3)] for i in range(3)] for part in matrix]


def row_times(row, right, row_sign, right_sign):
    result = [[], []]
    for j in range(3):
        real = imag = None
        for k in range(3):
            rr = row[0][k] * right[0][k][j]
            ii = row[1][k] * right[1][k][j]
            ri = row[0][k] * right[1][k][j]
            ir = row[1][k] * right[0][k][j]
            new_real = rr - ii if row_sign * right_sign > 0 else rr + ii
            if row_sign > 0 and right_sign > 0:
                new_imag = ri + ir
            elif row_sign > 0:
                new_imag = ir - ri
            else:
                new_imag = ri - ir
            real = new_real if real is None else real + new_real
            imag = new_imag if imag is None else imag + new_imag
        result[0].append(real)
        result[1].append(imag)
    return result


def add_terms(fields, terms, near, acc):
    started = set()
    for target, halves in terms:
        for sign in (1, -1):
            here, ahead, left, right = term_fields(halves, sign)
            force = pole_sum(fields, here, ahead, near)
            left = fields.matrix(left)
            right = fields.matrix(right)
            if sign > 0:
                right = transposed(right)
            else:
                left = transposed(left)
            rows = [row_times([left[0][i], left[1][i]], force, sign, 1) for i in range(3)]
            for i in range(3):
                row = row_times(rows[i], right, 1, -sign)
                for part in range(2):
                    for j in range(3):
                        at = pl.ds((target * 18 + part * 9 + i * 3 + j) * 8, 8)
                        new = row[part][j]
                        acc[at, :] = acc[at, :] + new if target in started else new
            started.add(target)


def acc_tile(acc, target, c):
    return acc[pl.ds((target * 18 + c) * 8, 8), :]


def scale_tiles(scale_ref):
    tiles = [scale_ref[pl.ds(8 * p, 8), :] for p in range(3 * NP)]
    return tiles[:NP], tiles[NP : 2 * NP], tiles[2 * NP :]


def own_force(fields, m, both):
    total = pole_sum(
        fields,
        [("x", 0, ZERO)] * 2,
        [("x", 0, UNIT[m]), ("x", 0, plus(ZERO, UNIT[m], 3))],
        both,
    )
    flat = [total[c][i][j] for c in range(2) for i in range(3) for j in range(3)]
    return [fields.compact_sum(flat[2 * k], flat[2 * k + 1]) for k in range(9)]


def write_messages(locator, plan, names, outs):
    for name, out in zip(names, outs):
        for reg, items in enumerate(plan[name].by_register()):
            spots = [item and locator.local(*item[1:]) for item in items]
            out[pl.ds(8 * reg, 8), :] = locator.assemble(spots)


def pack_z_kernel(plan, names, x_in, u_in, *rest):
    outs = rest[: len(names)]
    x_ref, u_ref, u_held, sems = rest[len(names) :]
    copies = [
        pltpu.make_async_copy(u_in, u_held, sems.at[0]),
        pltpu.make_async_copy(x_in, x_ref, sems.at[1]),
    ]
    for copy in copies:
        copy.start()
    for copy in copies:
        copy.wait()
    u_ref[...] = u_held[...].astype(F32)
    write_messages(Locator(plan, 1, {("own", "x"): x_ref, ("own", "u"): u_ref}), plan, names, outs)


def pack_t_kernel(plan, names, near_in, far_in, weight_in, x_ref, u_ref, *rest):
    outs = rest[: len(names)]
    scale_ref, near_ref, far_ref, weight_ref, sems = rest[len(names) :]
    copies = [
        pltpu.make_async_copy(source, target, sems.at[index])
        for index, (source, target) in enumerate(
            ((near_in, near_ref), (far_in, far_ref), (weight_in, weight_ref))
        )
    ]
    for copy in copies:
        copy.start()
    write_messages(Locator(plan, 1, {("own", "x"): x_ref, ("own", "u"): u_ref}), plan, names, outs)
    for copy in copies:
        copy.wait()
    upper = lax.broadcasted_iota(jnp.int32, (8, LANES), 0) < 4
    for p in range(NP):
        scale_ref[pl.ds(8 * p, 8), :] = jnp.full((8, LANES), near_ref[p], F32)
        scale_ref[pl.ds(8 * (NP + p), 8), :] = jnp.where(upper, near_ref[p], far_ref[p])
        scale_ref[pl.ds(8 * (2 * NP + p), 8), :] = jnp.full((8, LANES), weight_ref[p], F32)


def corner_kernel(plan, names, ahead_ref, behind_ref, *outs):
    locator = Locator(plan, 1, {("z", 1): ahead_ref, ("z", -1): behind_ref})
    for name, out in zip(names, outs):
        for reg, items in enumerate(plan[name].by_register()):
            spots = [
                item and (("z", item[0]),) + plan["z", item[0]].places[(0,) + item[1:]] for item in items
            ]
            out[pl.ds(8 * reg, 8), :] = locator.assemble(spots)


def near_kernel(plan, t_size, names, scale_ref, x_ref, u_ref, *rest):
    received = rest[: len(names)]
    shared_ref, part_ref, first_ref, acc = rest[len(names) :]
    buffers = {("own", "x"): x_ref, ("own", "u"): u_ref}
    buffers.update(zip(names, received))
    shared, first, _ = field_split()
    stores = [(shared_ref, shared[0]), (first_ref, first[0])]
    build_fields(Locator(plan, t_size, buffers), stores)
    fields = Fields(x_ref, u_ref, stores)
    near, both, weight = scale_tiles(scale_ref)
    add_terms(fields, NEAR_TERMS, near, acc)
    own = [own_force(fields, m, both) for m in range(2)]
    for k in range(9):
        staples = list(fields.compact_halves(acc_tile(acc, 0, 2 * k), acc_tile(acc, 0, 2 * k + 1)))
        staples.append(fields.compact_sum(acc_tile(acc, 1, 2 * k), acc_tile(acc, 1, 2 * k + 1)))
        for m in range(3):
            value = weight[m] * staples[m]
            part_ref[pl.ds((9 * m + k) * 8, 8), :] = own[m][k] + value if m < 2 else value


def far_kernel(plan, t_size, names, scale_ref, x_ref, u_ref, shared_ref, part_ref, *rest):
    received = rest[: len(names)]
    out_ref, second_ref, acc = rest[len(names) :]
    buffers = {("own", "x"): x_ref, ("own", "u"): u_ref}
    buffers.update(zip(names, received))
    shared, _, second = field_split()
    build_fields(Locator(plan, t_size, buffers), [(second_ref, second[0])])
    fields = Fields(x_ref, u_ref, [(shared_ref, shared[0]), (second_ref, second[0])])
    near, both, weight = scale_tiles(scale_ref)
    add_terms(fields, FAR_TERMS, near, acc)
    own = [own_force(fields, m, both) for m in (2, 3)]
    for k in range(9):
        pairs = [[acc_tile(acc, target, 2 * k + c) for c in range(2)] for target in range(3)]
        in_x, in_y = fields.compact_halves(*pairs[0])
        in_z, in_t = fields.compact_halves(*pairs[2])
        in_t = in_t + fields.compact_sum(*pairs[1])
        for m, staple in enumerate((in_x, in_y, in_z, in_t)):
            value = weight[m] * staple
            if m < 3:
                value = value + part_ref[pl.ds((9 * m + k) * 8, 8), :]
            if m > 1:
                value = value + own[m - 2][k]
            out_ref[pl.ds((9 * m + k) * 8, 8), :] = value


def rows_of(count):
    return jax.ShapeDtypeStruct((count, LANES), F32)


def on_device(pole_vectors, gauge_links, pole_coeff, naik_coeff, staple_weight):
    t_size = lax.axis_size("ta")
    z_size = lax.axis_size("gz") * lax.axis_size("gy")
    plan = message_plan(t_size)
    x_rows, u_rows = 8 * REGS["x"], 4 * 8 * REGS["u"]
    vmem = pl.BlockSpec(memory_space=pltpu.VMEM)
    hbm = pl.BlockSpec(memory_space=pltpu.HBM)
    limit = pltpu.CompilerParams(vmem_limit_bytes=4 * 1024 * 1024)

    def moved(name, value):
        kind, step = name
        if kind == "z":
            return lax.ppermute(value, ("gz", "gy"), [((i + step) % z_size, i) for i in range(z_size)])
        return lax.ppermute(value, "ta", [((j + step) % t_size, j) for j in range(t_size)])

    first_names = [name for name in plan if name[0] != "c"]
    corner_names = [name for name in plan if name[0] == "c"]
    z_names = [name for name in first_names if name[0] == "z"]
    t_names = [name for name in first_names if name[0] == "t"]
    in_hbm = functools.partial(pltpu.with_memory_space_constraint, memory_space=pltpu.HBM)
    packed = pl.pallas_call(
        functools.partial(pack_z_kernel, plan, z_names),
        out_shape=[rows_of(8 * plan[name].count) for name in z_names] + [rows_of(x_rows), rows_of(u_rows)],
        in_specs=[hbm] * 2,
        out_specs=[vmem] * (len(z_names) + 2),
        scratch_shapes=[pltpu.VMEM((u_rows, LANES), jnp.bfloat16), pltpu.SemaphoreType.DMA((2,))],
        compiler_params=limit,
        name="pack_z",
    )(in_hbm(pole_vectors.reshape((x_rows, LANES))), in_hbm(gauge_links.reshape((u_rows, LANES))))
    own = packed[len(z_names) :]
    received = {name: moved(name, value) for name, value in zip(z_names, packed)}
    packed = pl.pallas_call(
        functools.partial(pack_t_kernel, plan, t_names),
        out_shape=[rows_of(8 * plan[name].count) for name in t_names] + [rows_of(8 * 3 * NP)],
        in_specs=[hbm] * 3 + [vmem] * 2,
        out_specs=[vmem] * (len(t_names) + 1),
        scratch_shapes=[pltpu.SMEM((NP,), F32)] * 3 + [pltpu.SemaphoreType.DMA((3,))],
        compiler_params=limit,
        name="pack_t",
    )(in_hbm(pole_coeff), in_hbm(naik_coeff), in_hbm(staple_weight), *own)
    received.update({name: moved(name, value) for name, value in zip(t_names, packed)})
    local = [packed[len(t_names)], *own]
    corners = pl.pallas_call(
        functools.partial(corner_kernel, plan, corner_names),
        out_shape=[rows_of(8 * plan[name].count) for name in corner_names],
        in_specs=[vmem] * 2,
        out_specs=[vmem] * len(corner_names),
        compiler_params=limit,
        name="pack_corners",
    )(received["z", 1], received["z", -1])
    received.update({name: moved(name, value) for name, value in zip(corner_names, corners)})
    shared, first, second = field_split()
    near_names = [name for name in z_names if name != ("z", 2)]
    shared_values, part = pl.pallas_call(
        functools.partial(near_kernel, plan, t_size, near_names),
        out_shape=[rows_of(shared[1]), rows_of(3 * 8 * REGS["u"])],
        in_specs=[vmem] * (3 + len(near_names)),
        out_specs=[vmem] * 2,
        scratch_shapes=[pltpu.VMEM((first[1], LANES), F32), pltpu.VMEM((2 * 18 * 8, LANES), F32)],
        cost_estimate=pl.CostEstimate(flops=4 * 10**6, bytes_accessed=4 * 10**6, transcendentals=0),
        compiler_params=pltpu.CompilerParams(vmem_limit_bytes=8 * 1024 * 1024),
        name="force_without_t",
    )(*local, *[received[name] for name in near_names])
    far_names = list(received)
    force = pl.pallas_call(
        functools.partial(far_kernel, plan, t_size, far_names),
        out_shape=rows_of(u_rows),
        in_specs=[vmem] * (5 + len(far_names)),
        out_specs=vmem,
        scratch_shapes=[pltpu.VMEM((second[1], LANES), F32), pltpu.VMEM((3 * 18 * 8, LANES), F32)],
        compiler_params=pltpu.CompilerParams(vmem_limit_bytes=8 * 1024 * 1024),
        name="force_with_t",
    )(*local, shared_values, part, *[received[name] for name in far_names])
    return force.reshape(gauge_links.shape)


def solution(mesh):
    return jax.shard_map(
        on_device,
        mesh=mesh,
        in_specs=(
            P("ens", None, None, "ta", ("gz", "gy"), None),
            P("ens", None, None, None, "ta", ("gz", "gy"), None),
            P(),
            P(),
            P(),
        ),
        out_specs=P("ens", None, None, None, "ta", ("gz", "gy"), None),
        check_vma=False,
    )
```

```python
import collections
import functools

import jax
import jax.numpy as jnp
from jax import lax
from jax.experimental import pallas as pl
from jax.experimental.pallas import tpu as pltpu
from jax.sharding import PartitionSpec as P

NX = 8
NY = 16
LANES = NX * NY
NP = 4
F32 = jnp.float32
REGS = {"x": NP * 3, "u": 9}
UNIT = ((1, 0, 0, 0), (0, 1, 0, 0), (0, 0, 1, 0), (0, 0, 0, 1))
ZERO = (0, 0, 0, 0)
SITES = ((0, 0), (0, 1), (1, 0), (1, 1))
NEAR_TERMS = ((0, ((0, 1), (1, 0))), (0, ((0, 2), (1, 2))), (1, ((2, 0), (2, 1))))
FAR_TERMS = ((0, ((0, 3), (1, 3))), (1, ((3, 0), (3, 1))), (2, ((2, 3), (3, 2))))


def plus(left, right, scale=1):
    return tuple(a + scale * b for a, b in zip(left, right))


class Message:
    def __init__(self):
        self.places = collections.OrderedDict()
        self.count = 0

    def add_full(self, kind, n):
        for k in range(REGS[kind]):
            for t, z in SITES:
                self.places[0, kind, n, k, t, z] = (self.count, 2 * t + z)
            self.count += 1

    def add_halves(self, entries, axis):
        half = -(-len(entries) // 2)
        for index, (kind, n, k, layer) in enumerate(entries):
            reg, part = self.count + index % half, index // half
            for other in range(2):
                t, z = (layer, other) if axis == "t" else (other, layer)
                slot = 2 * part + other if axis == "t" else 2 * other + part
                self.places[0, kind, n, k, t, z] = (reg, slot)
        self.count += half

    def add_single(self, entries):
        quarter = -(-len(entries) // 4)
        for index, entry in enumerate(entries):
            self.places[entry] = (self.count + index % quarter, index // quarter)
        self.count += quarter

    def by_register(self):
        found = [[None] * 4 for _ in range(self.count)]
        for item, (reg, slot) in self.places.items():
            found[reg][slot] = item
        return found


def regs_of(kind, directions, layer):
    return [(kind, n, k, layer) for n in directions for k in range(REGS[kind])]


def message_plan(t_size):
    plan = collections.OrderedDict()
    ahead = plan["z", 1] = Message()
    ahead.add_full("x", 0)
    ahead.add_halves(regs_of("u", (0, 1, 3), 0), "z")
    behind = plan["z", -1] = Message()
    behind.add_halves(regs_of("x", (0,), 1) + regs_of("u", (2,), 1), "z")
    second = plan["z", 2] = Message()
    second.add_halves(regs_of("x", (0,), 0), "z")
    halves, corners = collections.OrderedDict(), collections.OrderedDict()
    for dt, entries in (
        (1, regs_of("u", (0, 1, 2), 0)),
        (-1, regs_of("x", (0,), 1) + regs_of("u", (3,), 1)),
        (2, regs_of("x", (0,), 0)),
    ):
        if dt % t_size != 0:
            halves.setdefault(dt % t_size, []).extend(entries)
    for dt, entries in halves.items():
        message = plan["t", dt] = Message()
        if dt == 1:
            message.add_full("x", 0)
        held = {item[1:4] for item in message.places}
        message.add_halves([e for e in entries if e[:3] not in held], "t")
    for dt, entries in (
        (1, [(1, "x", 0, k, 0, 0) for k in range(REGS["x"])]),
        (1, [(-1, "x", 0, k, 0, 1) for k in range(REGS["x"])]),
        (1, [(-1, "u", 2, k, 0, 1) for k in range(REGS["u"])]),
        (-1, [(1, "x", 0, k, 1, 0) for k in range(REGS["x"])]),
        (-1, [(1, "u", 3, k, 1, 0) for k in range(REGS["u"])]),
    ):
        corners.setdefault(dt % t_size, []).extend(entries)
    for dt, entries in corners.items():
        plan["c", dt] = Message()
        plan["c", dt].add_single(entries)
    return plan


class Locator:
    def __init__(self, plan, t_size, buffers):
        self.plan, self.t_size, self.buffers = plan, t_size, buffers

    def local(self, kind, n, k, t, z):
        return ("own", kind), n * REGS[kind] + k, 2 * t + z

    def find(self, kind, n, k, t_at, z_at):
        (dt, t), (dz, z) = divmod(t_at, 2), divmod(z_at, 2)
        dt %= self.t_size
        if (dt, dz) == (0, 0):
            return self.local(kind, n, k, t, z)
        name = ("z", dz) if dt == 0 else ("t", dt) if dz == 0 else ("c", dt)
        item = (dz if name[0] == "c" else 0, kind, n, k, t, z)
        return (name,) + self.plan[name].places[item]

    def load(self, name, reg):
        return self.buffers[name][pl.ds(8 * reg, 8), :]

    def assemble(self, spots):
        groups = collections.OrderedDict()
        for r, spot in enumerate(spots):
            if spot is not None:
                groups.setdefault((spot[0], spot[1], r - spot[2]), []).append(r)
        row = lax.broadcasted_iota(jnp.int32, (8, LANES), 0) % 4
        result = None
        for (name, reg, move), rows in groups.items():
            value = self.load(name, reg)
            if move != 0:
                value = pltpu.roll(value, move % 8, 0)
            if result is None:
                result = value
            else:
                mask = functools.reduce(jnp.logical_or, [row == r for r in rows])
                result = jnp.where(mask, value, result)
        return result

    def field_register(self, kind, n, k, dt, dz):
        return self.assemble([self.find(kind, n, k, t + dt, z + dz) for t, z in SITES])


def lane_shifted(value, dx, dy):
    if dx != 0:
        x_at = lax.broadcasted_iota(jnp.int32, value.shape, 1) % NX
        beyond = (x_at + dx >= NX) | (x_at + dx < 0)
        main = pltpu.roll(value, (-dx) % LANES, 1)
        wrapped = pltpu.roll(value, (NX - dx if dx > 0 else -NX - dx) % LANES, 1)
        value = jnp.where(beyond, wrapped, main)
    if dy != 0:
        value = pltpu.roll(value, (-dy * NX) % LANES, 1)
    return value


def term_fields(halves, sign):
    here, ahead, left, right = [], [], [], []
    for m, n in halves:
        start = plus(ZERO, UNIT[n], sign)
        base = ZERO if sign > 0 else start
        here.append(("x", 0, start))
        ahead.append(("x", 0, plus(start, UNIT[m])))
        left.append(("u", n, base))
        right.append(("u", n, plus(base, UNIT[m])))
    return here, ahead, left, right


def needed_fields(terms, own):
    keys = collections.OrderedDict()
    for _, halves in terms:
        for sign in (1, -1):
            for pair in term_fields(halves, sign):
                keys.update((key, None) for key in pair)
    for m in own:
        for scale in (1, 3):
            keys["x", 0, plus(ZERO, UNIT[m], scale)] = None
    return [key for key in keys if key[2] != ZERO]


def lay_out(keys):
    rows, total = collections.OrderedDict(), 0
    for key in keys:
        rows[key] = total
        total += 8 * REGS[key[0]]
    return rows, total


def field_split():
    near = needed_fields(NEAR_TERMS, (0, 1))
    far = needed_fields(FAR_TERMS, (2, 3))
    still = [key for key in far if key[2][3] == 0 and abs(key[2][2]) < 3]
    shared = lay_out(still)
    first = lay_out([key for key in near if key not in shared[0]])
    second = lay_out([key for key in far if key not in shared[0]])
    return shared, first, second


def build_fields(locator, stores):
    groups = collections.OrderedDict()
    for ref, rows in stores:
        for (kind, n, disp), row in rows.items():
            shifts = groups.setdefault((kind, n, disp[3], disp[2]), collections.OrderedDict())
            shifts[disp[0], disp[1]] = (ref, row)
    for (kind, n, dt, dz), shifts in groups.items():
        for k in range(REGS[kind]):
            value = locator.field_register(kind, n, k, dt, dz)
            by_x = {0: value}
            for (dx, dy), (ref, row) in shifts.items():
                if dx not in by_x:
                    by_x[dx] = lane_shifted(value, dx, 0)
                ref[pl.ds(row + 8 * k, 8), :] = lane_shifted(by_x[dx], 0, dy)


class Fields:
    def __init__(self, own_x, own_u, stores):
        self.place = {("x", 0, ZERO): (own_x, 0)}
        for n in range(4):
            self.place["u", n, ZERO] = (own_u, 8 * REGS["u"] * n)
        for ref, rows in stores:
            for key, row in rows.items():
                self.place[key] = (ref, row)
        self.upper = lax.broadcasted_iota(jnp.int32, (8, LANES), 0) < 4

    def reg(self, key, k):
        ref, row = self.place[key]
        return ref[pl.ds(row + 8 * k, 8), :]

    def two_tiles(self, keys, k):
        top = self.reg(keys[0], k)
        turned_top = pltpu.roll(top, 4, 0)
        if keys[0] == keys[1]:
            low, turned_low = top, turned_top
        else:
            low = self.reg(keys[1], k)
            turned_low = pltpu.roll(low, 4, 0)
        return [jnp.where(self.upper, top, turned_low), jnp.where(self.upper, turned_top, low)]

    def vector(self, keys, pole):
        flat = [tile for k in range(3) for tile in self.two_tiles(keys, 3 * pole + k)]
        return [flat[:3], flat[3:]]

    def matrix(self, keys):
        flat = [tile for k in range(9) for tile in self.two_tiles(keys, k)]
        return [[flat[9 * c + 3 * i : 9 * c + 3 * i + 3] for i in range(3)] for c in range(2)]

    def compact_halves(self, first, second):
        top = jnp.where(self.upper, first, pltpu.roll(second, 4, 0))
        return top, jnp.where(self.upper, pltpu.roll(first, 4, 0), second)

    def compact_sum(self, first, second):
        kept = jnp.where(self.upper, first, second)
        return kept + pltpu.roll(jnp.where(self.upper, second, first), 4, 0)


def pole_sum(fields, here, ahead, scales):
    total = None
    for pole in range(NP):
        h = [[scales[pole] * v for v in part] for part in fields.vector(here, pole)]
        a = fields.vector(ahead, pole)
        real = [[a[0][i] * h[0][j] + a[1][i] * h[1][j] for j in range(3)] for i in range(3)]
        imag = [[a[1][i] * h[0][j] - a[0][i] * h[1][j] for j in range(3)] for i in range(3)]
        if total is None:
            total = [real, imag]
        else:
            total = [
                [[total[c][i][j] + new[i][j] for j in range(3)] for i in range(3)]
                for c, new in enumerate((real, imag))
            ]
    return total


def transposed(matrix):
    return [[[part[j][i] for j in range(3)] for i in range(3)] for part in matrix]


def row_times(row, right, row_sign, right_sign):
    result = [[], []]
    for j in range(3):
        real = imag = None
        for k in range(3):
            rr = row[0][k] * right[0][k][j]
            ii = row[1][k] * right[1][k][j]
            ri = row[0][k] * right[1][k][j]
            ir = row[1][k] * right[0][k][j]
            new_real = rr - ii if row_sign * right_sign > 0 else rr + ii
            if row_sign > 0 and right_sign > 0:
                new_imag = ri + ir
            elif row_sign > 0:
                new_imag = ir - ri
            else:
                new_imag = ri - ir
            real = new_real if real is None else real + new_real
            imag = new_imag if imag is None else imag + new_imag
        result[0].append(real)
        result[1].append(imag)
    return result


def add_terms(fields, terms, near, acc):
    started = set()
    for target, halves in terms:
        for sign in (1, -1):
            here, ahead, left, right = term_fields(halves, sign)
            force = pole_sum(fields, here, ahead, near)
            left = fields.matrix(left)
            right = fields.matrix(right)
            if sign > 0:
                right = transposed(right)
            else:
                left = transposed(left)
            rows = [row_times([left[0][i], left[1][i]], force, sign, 1) for i in range(3)]
            for i in range(3):
                row = row_times(rows[i], right, 1, -sign)
                for part in range(2):
                    for j in range(3):
                        at = pl.ds((target * 18 + part * 9 + i * 3 + j) * 8, 8)
                        new = row[part][j]
                        acc[at, :] = acc[at, :] + new if target in started else new
            started.add(target)


def acc_tile(acc, target, c):
    return acc[pl.ds((target * 18 + c) * 8, 8), :]


def scale_tiles(scale_ref):
    tiles = [scale_ref[pl.ds(8 * p, 8), :] for p in range(3 * NP)]
    return tiles[:NP], tiles[NP : 2 * NP], tiles[2 * NP :]


def own_force(fields, m, both):
    total = pole_sum(
        fields,
        [("x", 0, ZERO)] * 2,
        [("x", 0, UNIT[m]), ("x", 0, plus(ZERO, UNIT[m], 3))],
        both,
    )
    flat = [total[c][i][j] for c in range(2) for i in range(3) for j in range(3)]
    return [fields.compact_sum(flat[2 * k], flat[2 * k + 1]) for k in range(9)]


def write_messages(locator, plan, names, outs):
    for name, out in zip(names, outs):
        for reg, items in enumerate(plan[name].by_register()):
            spots = [item and locator.local(*item[1:]) for item in items]
            out[pl.ds(8 * reg, 8), :] = locator.assemble(spots)


def odd_in_z():
    return (lax.axis_index("gz") * lax.axis_size("gy") + lax.axis_index("gy")) % 2 == 1


def pack_z_kernel(plan, x_in, u_in, within_ref, between_ref, second_ref, x_ref, u_ref, u_held, sems):
    copies = [
        pltpu.make_async_copy(u_in, u_held, sems.at[0]),
        pltpu.make_async_copy(x_in, x_ref, sems.at[1]),
    ]
    for copy in copies:
        copy.start()
    for copy in copies:
        copy.wait()
    u_ref[...] = u_held[...].astype(F32)
    locator = Locator(plan, 1, {("own", "x"): x_ref, ("own", "u"): u_ref})
    names = [("z", 1), ("z", -1)]

    @pl.when(odd_in_z())
    def _():
        write_messages(locator, plan, names, (within_ref, between_ref))

    @pl.when(jnp.logical_not(odd_in_z()))
    def _():
        write_messages(locator, plan, names, (between_ref, within_ref))

    write_messages(locator, plan, [("z", 2)], [second_ref])


def pack_t_kernel(plan, names, near_in, far_in, weight_in, x_ref, u_ref, *rest):
    outs = rest[: len(names)]
    scale_ref, near_ref, far_ref, weight_ref, sems = rest[len(names) :]
    copies = [
        pltpu.make_async_copy(source, target, sems.at[index])
        for index, (source, target) in enumerate(
            ((near_in, near_ref), (far_in, far_ref), (weight_in, weight_ref))
        )
    ]
    for copy in copies:
        copy.start()
    write_messages(Locator(plan, 1, {("own", "x"): x_ref, ("own", "u"): u_ref}), plan, names, outs)
    for copy in copies:
        copy.wait()
    upper = lax.broadcasted_iota(jnp.int32, (8, LANES), 0) < 4
    for p in range(NP):
        scale_ref[pl.ds(8 * p, 8), :] = jnp.full((8, LANES), near_ref[p], F32)
        scale_ref[pl.ds(8 * (NP + p), 8), :] = jnp.where(upper, near_ref[p], far_ref[p])
        scale_ref[pl.ds(8 * (2 * NP + p), 8), :] = jnp.full((8, LANES), weight_ref[p], F32)


def corner_kernel(plan, names, within_ref, between_ref, second_ref, ahead_ref, behind_ref, *outs):
    def split(from_ahead, from_behind):
        ahead_ref[...] = from_ahead[pl.ds(0, ahead_ref.shape[0]), :]
        behind_ref[...] = from_behind[pl.ds(0, behind_ref.shape[0]), :]

    @pl.when(odd_in_z())
    def _():
        split(between_ref, within_ref)

    @pl.when(jnp.logical_not(odd_in_z()))
    def _():
        split(within_ref, between_ref)

    locator = Locator(plan, 1, {("z", 1): ahead_ref, ("z", -1): behind_ref})
    for name, out in zip(names, outs):
        for reg, items in enumerate(plan[name].by_register()):
            spots = [
                item and (("z", item[0]),) + plan["z", item[0]].places[(0,) + item[1:]] for item in items
            ]
            out[pl.ds(8 * reg, 8), :] = locator.assemble(spots)


def near_kernel(plan, t_size, names, scale_ref, x_ref, u_ref, *rest):
    received = rest[: len(names)]
    shared_ref, part_ref, first_ref, acc = rest[len(names) :]
    buffers = {("own", "x"): x_ref, ("own", "u"): u_ref}
    buffers.update(zip(names, received))
    shared, first, _ = field_split()
    stores = [(shared_ref, shared[0]), (first_ref, first[0])]
    build_fields(Locator(plan, t_size, buffers), stores)
    fields = Fields(x_ref, u_ref, stores)
    near, both, weight = scale_tiles(scale_ref)
    add_terms(fields, NEAR_TERMS, near, acc)
    own = [own_force(fields, m, both) for m in range(2)]
    for k in range(9):
        staples = list(fields.compact_halves(acc_tile(acc, 0, 2 * k), acc_tile(acc, 0, 2 * k + 1)))
        staples.append(fields.compact_sum(acc_tile(acc, 1, 2 * k), acc_tile(acc, 1, 2 * k + 1)))
        for m in range(3):
            value = weight[m] * staples[m]
            part_ref[pl.ds((9 * m + k) * 8, 8), :] = own[m][k] + value if m < 2 else value


def far_kernel(plan, t_size, names, scale_ref, x_ref, u_ref, shared_ref, part_ref, *rest):
    received = rest[: len(names)]
    out_ref, second_ref, acc = rest[len(names) :]
    buffers = {("own", "x"): x_ref, ("own", "u"): u_ref}
    buffers.update(zip(names, received))
    shared, _, second = field_split()
    build_fields(Locator(plan, t_size, buffers), [(second_ref, second[0])])
    fields = Fields(x_ref, u_ref, [(shared_ref, shared[0]), (second_ref, second[0])])
    near, both, weight = scale_tiles(scale_ref)
    add_terms(fields, FAR_TERMS, near, acc)
    own = [own_force(fields, m, both) for m in (2, 3)]
    for k in range(9):
        pairs = [[acc_tile(acc, target, 2 * k + c) for c in range(2)] for target in range(3)]
        in_x, in_y = fields.compact_halves(*pairs[0])
        in_z, in_t = fields.compact_halves(*pairs[2])
        in_t = in_t + fields.compact_sum(*pairs[1])
        for m, staple in enumerate((in_x, in_y, in_z, in_t)):
            value = weight[m] * staple
            if m < 3:
                value = value + part_ref[pl.ds((9 * m + k) * 8, 8), :]
            if m > 1:
                value = value + own[m - 2][k]
            out_ref[pl.ds((9 * m + k) * 8, 8), :] = value


def rows_of(count):
    return jax.ShapeDtypeStruct((count, LANES), F32)


def on_device(pole_vectors, gauge_links, pole_coeff, naik_coeff, staple_weight):
    t_size = lax.axis_size("ta")
    z_size = lax.axis_size("gz") * lax.axis_size("gy")
    plan = message_plan(t_size)
    x_rows, u_rows = 8 * REGS["x"], 4 * 8 * REGS["u"]
    vmem = pl.BlockSpec(memory_space=pltpu.VMEM)
    hbm = pl.BlockSpec(memory_space=pltpu.HBM)
    limit = pltpu.CompilerParams(vmem_limit_bytes=4 * 1024 * 1024)

    def moved(name, value):
        kind, step = name
        if kind == "z":
            return lax.ppermute(value, ("gz", "gy"), [((i + step) % z_size, i) for i in range(z_size)])
        return lax.ppermute(value, "ta", [((j + step) % t_size, j) for j in range(t_size)])

    def exchanged(value, first):
        pairs = [(i, (i + 1) % z_size) for i in range(first, z_size, 2)]
        return lax.ppermute(value, ("gz", "gy"), pairs + [(j, i) for i, j in pairs])

    first_names = [name for name in plan if name[0] != "c"]
    corner_names = [name for name in plan if name[0] == "c"]
    t_names = [name for name in first_names if name[0] == "t"]
    in_hbm = functools.partial(pltpu.with_memory_space_constraint, memory_space=pltpu.HBM)
    ahead_rows, behind_rows = [8 * plan["z", step].count for step in (1, -1)]
    shared_rows = max(ahead_rows, behind_rows)
    within, between, beyond, *own = pl.pallas_call(
        functools.partial(pack_z_kernel, plan),
        out_shape=[rows_of(shared_rows), rows_of(shared_rows + 8), rows_of(8 * plan["z", 2].count)]
        + [rows_of(x_rows), rows_of(u_rows)],
        in_specs=[hbm] * 2,
        out_specs=[vmem] * 5,
        scratch_shapes=[pltpu.VMEM((u_rows, LANES), jnp.bfloat16), pltpu.SemaphoreType.DMA((2,))],
        compiler_params=limit,
        name="pack_z",
    )(in_hbm(pole_vectors.reshape((x_rows, LANES))), in_hbm(gauge_links.reshape((u_rows, LANES))))
    between, within = exchanged(between, 1), exchanged(within, 0)
    received = {("z", 2): moved(("z", 2), beyond)}
    packed = pl.pallas_call(
        functools.partial(pack_t_kernel, plan, t_names),
        out_shape=[rows_of(8 * plan[name].count) for name in t_names] + [rows_of(8 * 3 * NP)],
        in_specs=[hbm] * 3 + [vmem] * 2,
        out_specs=[vmem] * (len(t_names) + 1),
        scratch_shapes=[pltpu.SMEM((NP,), F32)] * 3 + [pltpu.SemaphoreType.DMA((3,))],
        compiler_params=limit,
        name="pack_t",
    )(in_hbm(pole_coeff), in_hbm(naik_coeff), in_hbm(staple_weight), *own)
    received.update({name: moved(name, value) for name, value in zip(t_names, packed)})
    local = [packed[len(t_names)], *own]
    received["z", 1], received["z", -1], *corners = pl.pallas_call(
        functools.partial(corner_kernel, plan, corner_names),
        out_shape=[rows_of(ahead_rows), rows_of(behind_rows)]
        + [rows_of(8 * plan[name].count) for name in corner_names],
        in_specs=[vmem] * 3,
        out_specs=[vmem] * (2 + len(corner_names)),
        compiler_params=limit,
        name="pack_corners",
    )(within, between, received["z", 2])
    received.update({name: moved(name, value) for name, value in zip(corner_names, corners)})
    shared, first, second = field_split()
    near_names = [("z", 1), ("z", -1)]
    shared_values, part = pl.pallas_call(
        functools.partial(near_kernel, plan, t_size, near_names),
        out_shape=[rows_of(shared[1]), rows_of(3 * 8 * REGS["u"])],
        in_specs=[vmem] * (3 + len(near_names)),
        out_specs=[vmem] * 2,
        scratch_shapes=[pltpu.VMEM((first[1], LANES), F32), pltpu.VMEM((2 * 18 * 8, LANES), F32)],
        cost_estimate=pl.CostEstimate(flops=4 * 10**6, bytes_accessed=4 * 10**6, transcendentals=0),
        compiler_params=pltpu.CompilerParams(vmem_limit_bytes=8 * 1024 * 1024),
        name="force_without_t",
    )(*local, *[received[name] for name in near_names])
    far_names = list(received)
    force = pl.pallas_call(
        functools.partial(far_kernel, plan, t_size, far_names),
        out_shape=rows_of(u_rows),
        in_specs=[vmem] * (5 + len(far_names)),
        out_specs=vmem,
        scratch_shapes=[pltpu.VMEM((second[1], LANES), F32), pltpu.VMEM((3 * 18 * 8, LANES), F32)],
        compiler_params=pltpu.CompilerParams(vmem_limit_bytes=8 * 1024 * 1024),
        name="force_with_t",
    )(*local, shared_values, part, *[received[name] for name in far_names])
    return force.reshape(gauge_links.shape)


def solution(mesh):
    return jax.shard_map(
        on_device,
        mesh=mesh,
        in_specs=(
            P("ens", None, None, "ta", ("gz", "gy"), None),
            P("ens", None, None, None, "ta", ("gz", "gy"), None),
            P(),
            P(),
            P(),
        ),
        out_specs=P("ens", None, None, None, "ta", ("gz", "gy"), None),
        check_vma=False,
    )
```

```python
import collections
import functools

import jax
import jax.numpy as jnp
from jax import lax
from jax.experimental import pallas as pl
from jax.experimental.pallas import tpu as pltpu
from jax.sharding import PartitionSpec as P

NX = 8
NY = 16
LANES = NX * NY
NP = 4
F32 = jnp.float32
REGS = {"x": NP * 3, "u": 9}
UNIT = ((1, 0, 0, 0), (0, 1, 0, 0), (0, 0, 1, 0), (0, 0, 0, 1))
ZERO = (0, 0, 0, 0)
SITES = ((0, 0), (0, 1), (1, 0), (1, 1))
STAGES = ("own", "z", "t", "corner")
TERMS = {
    "own": ((0, ((0, 1), (1, 0))),),
    "z": ((0, ((0, 2), (1, 2))), (1, ((2, 0), (2, 1)))),
    "t": ((0, ((0, 3), (1, 3))), (1, ((3, 0), (3, 1)))),
    "corner": ((0, ((2, 3), (3, 2))),),
}
COSTS = {"own": 2.0, "z": 2.0, "t": 2.0, "corner": 1.0}
DIRECT = {"own": (0, 1), "z": (), "t": (3,), "corner": (2,)}


def plus(left, right, scale=1):
    return tuple(a + scale * b for a, b in zip(left, right))


class Message:
    def __init__(self):
        self.places = collections.OrderedDict()
        self.count = 0

    def add_full(self, kind, n):
        for k in range(REGS[kind]):
            for t, z in SITES:
                self.places[0, kind, n, k, t, z] = (self.count, 2 * t + z)
            self.count += 1

    def add_halves(self, entries, axis):
        half = -(-len(entries) // 2)
        for index, (kind, n, k, layer) in enumerate(entries):
            reg, part = self.count + index % half, index // half
            for other in range(2):
                t, z = (layer, other) if axis == "t" else (other, layer)
                slot = 2 * part + other if axis == "t" else 2 * other + part
                self.places[0, kind, n, k, t, z] = (reg, slot)
        self.count += half

    def add_single(self, entries):
        quarter = -(-len(entries) // 4)
        for index, entry in enumerate(entries):
            self.places[entry] = (self.count + index % quarter, index // quarter)
        self.count += quarter

    def by_register(self):
        found = [[None] * 4 for _ in range(self.count)]
        for item, (reg, slot) in self.places.items():
            found[reg][slot] = item
        return found


def regs_of(kind, directions, layer):
    return [(kind, n, k, layer) for n in directions for k in range(REGS[kind])]


def message_plan(t_size):
    plan = collections.OrderedDict()
    ahead = plan["z", 1] = Message()
    ahead.add_full("x", 0)
    ahead.add_halves(regs_of("u", (0, 1, 3), 0), "z")
    behind = plan["z", -1] = Message()
    behind.add_halves(regs_of("x", (0,), 1) + regs_of("u", (2,), 1), "z")
    second = plan["z", 2] = Message()
    second.add_halves(regs_of("x", (0,), 0), "z")
    halves, corners = collections.OrderedDict(), collections.OrderedDict()
    for dt, entries in (
        (1, regs_of("u", (0, 1, 2), 0)),
        (-1, regs_of("x", (0,), 1) + regs_of("u", (3,), 1)),
        (2, regs_of("x", (0,), 0)),
    ):
        if dt % t_size != 0:
            halves.setdefault(dt % t_size, []).extend(entries)
    for dt, entries in halves.items():
        message = plan["t", dt] = Message()
        if dt == 1:
            message.add_full("x", 0)
        held = {item[1:4] for item in message.places}
        message.add_halves([e for e in entries if e[:3] not in held], "t")
    for dt, entries in (
        (1, [(1, "x", 0, k, 0, 0) for k in range(REGS["x"])]),
        (1, [(-1, "x", 0, k, 0, 1) for k in range(REGS["x"])]),
        (1, [(-1, "u", 2, k, 0, 1) for k in range(REGS["u"])]),
        (-1, [(1, "x", 0, k, 1, 0) for k in range(REGS["x"])]),
        (-1, [(1, "u", 3, k, 1, 0) for k in range(REGS["u"])]),
    ):
        corners.setdefault(dt % t_size, []).extend(entries)
    for dt, entries in corners.items():
        plan["c", dt] = Message()
        plan["c", dt].add_single(entries)
    return plan


class Locator:
    def __init__(self, plan, t_size, buffers):
        self.plan, self.t_size, self.buffers = plan, t_size, buffers

    def local(self, kind, n, k, t, z):
        return ("own", kind), n * REGS[kind] + k, 2 * t + z

    def find(self, kind, n, k, t_at, z_at):
        (dt, t), (dz, z) = divmod(t_at, 2), divmod(z_at, 2)
        dt %= self.t_size
        if (dt, dz) == (0, 0):
            return self.local(kind, n, k, t, z)
        name = ("z", dz) if dt == 0 else ("t", dt) if dz == 0 else ("c", dt)
        item = (dz if name[0] == "c" else 0, kind, n, k, t, z)
        return (name,) + self.plan[name].places[item]

    def load(self, name, reg):
        return self.buffers[name][pl.ds(8 * reg, 8), :]

    def assemble(self, spots):
        groups = collections.OrderedDict()
        for r, spot in enumerate(spots):
            if spot is not None:
                groups.setdefault((spot[0], spot[1], r - spot[2]), []).append(r)
        row = lax.broadcasted_iota(jnp.int32, (8, LANES), 0) % 4
        result = None
        for (name, reg, move), rows in groups.items():
            value = self.load(name, reg)
            if move != 0:
                value = pltpu.roll(value, move % 8, 0)
            if result is None:
                result = value
            else:
                mask = functools.reduce(jnp.logical_or, [row == r for r in rows])
                result = jnp.where(mask, value, result)
        return result

    def field_register(self, kind, n, k, dt, dz):
        return self.assemble([self.find(kind, n, k, t + dt, z + dz) for t, z in SITES])


def lane_shifted(value, dx, dy):
    if dx != 0:
        x_at = lax.broadcasted_iota(jnp.int32, value.shape, 1) % NX
        beyond = (x_at + dx >= NX) | (x_at + dx < 0)
        main = pltpu.roll(value, (-dx) % LANES, 1)
        wrapped = pltpu.roll(value, (NX - dx if dx > 0 else -NX - dx) % LANES, 1)
        value = jnp.where(beyond, wrapped, main)
    if dy != 0:
        value = pltpu.roll(value, (-dy * NX) % LANES, 1)
    return value


def term_fields(halves, sign):
    here, ahead, left, right = [], [], [], []
    for m, n in halves:
        start = plus(ZERO, UNIT[n], sign)
        base = ZERO if sign > 0 else start
        here.append(("x", 0, start))
        ahead.append(("x", 0, plus(start, UNIT[m])))
        left.append(("u", n, base))
        right.append(("u", n, plus(base, UNIT[m])))
    return here, ahead, left, right


def needed_fields(stage):
    keys = collections.OrderedDict()
    for _, halves in TERMS[stage]:
        for sign in (1, -1):
            for pair in term_fields(halves, sign):
                keys.update((key, None) for key in pair)
    for m in DIRECT[stage]:
        for scale in (1, 3):
            keys["x", 0, plus(ZERO, UNIT[m], scale)] = None
    return [key for key in keys if key[2] != ZERO]


def stage_of(key):
    dz, dt = key[2][2:]
    if abs(dz) == 3 or (dz != 0 and dt != 0):
        return "corner"
    return "t" if dt != 0 else "z" if dz != 0 else "own"


def lay_out(keys):
    rows, total = collections.OrderedDict(), 0
    for key in keys:
        rows[key] = total
        total += 8 * REGS[key[0]]
    return rows, total


def field_split():
    uses = collections.OrderedDict()
    for stage in STAGES:
        for key in needed_fields(stage):
            uses.setdefault(key, []).append(stage)
    shared, alone = {}, {}
    for stage in STAGES:
        built = [key for key in uses if stage_of(key) == stage]
        shared[stage] = lay_out([key for key in built if uses[key] != [stage]])
        alone[stage] = lay_out([key for key in built if uses[key] == [stage]])
    return shared, alone


def build_fields(locator, stores):
    groups = collections.OrderedDict()
    for ref, rows in stores:
        for (kind, n, disp), row in rows.items():
            shifts = groups.setdefault((kind, n, disp[3], disp[2]), collections.OrderedDict())
            shifts[disp[0], disp[1]] = (ref, row)
    for (kind, n, dt, dz), shifts in groups.items():
        for k in range(REGS[kind]):
            value = locator.field_register(kind, n, k, dt, dz)
            by_x = {0: value}
            for (dx, dy), (ref, row) in shifts.items():
                if dx not in by_x:
                    by_x[dx] = lane_shifted(value, dx, 0)
                ref[pl.ds(row + 8 * k, 8), :] = lane_shifted(by_x[dx], 0, dy)


class Fields:
    def __init__(self, own_x, own_u, stores):
        self.place = {("x", 0, ZERO): (own_x, 0)}
        for n in range(4):
            self.place["u", n, ZERO] = (own_u, 8 * REGS["u"] * n)
        for ref, rows in stores:
            for key, row in rows.items():
                self.place[key] = (ref, row)
        self.upper = lax.broadcasted_iota(jnp.int32, (8, LANES), 0) < 4

    def reg(self, key, k):
        ref, row = self.place[key]
        return ref[pl.ds(row + 8 * k, 8), :]

    def two_tiles(self, keys, k):
        top = self.reg(keys[0], k)
        turned_top = pltpu.roll(top, 4, 0)
        if keys[0] == keys[1]:
            low, turned_low = top, turned_top
        else:
            low = self.reg(keys[1], k)
            turned_low = pltpu.roll(low, 4, 0)
        return [jnp.where(self.upper, top, turned_low), jnp.where(self.upper, turned_top, low)]

    def vector(self, keys, pole):
        flat = [tile for k in range(3) for tile in self.two_tiles(keys, 3 * pole + k)]
        return [flat[:3], flat[3:]]

    def matrix(self, keys):
        flat = [tile for k in range(9) for tile in self.two_tiles(keys, k)]
        return [[flat[9 * c + 3 * i : 9 * c + 3 * i + 3] for i in range(3)] for c in range(2)]

    def compact_halves(self, first, second):
        top = jnp.where(self.upper, first, pltpu.roll(second, 4, 0))
        return top, jnp.where(self.upper, pltpu.roll(first, 4, 0), second)

    def compact_sum(self, first, second):
        kept = jnp.where(self.upper, first, second)
        return kept + pltpu.roll(jnp.where(self.upper, second, first), 4, 0)


def pole_sum(fields, here, ahead, scales):
    total = None
    for pole in range(NP):
        h = [[scales[pole] * v for v in part] for part in fields.vector(here, pole)]
        a = fields.vector(ahead, pole)
        real = [[a[0][i] * h[0][j] + a[1][i] * h[1][j] for j in range(3)] for i in range(3)]
        imag = [[a[1][i] * h[0][j] - a[0][i] * h[1][j] for j in range(3)] for i in range(3)]
        if total is None:
            total = [real, imag]
        else:
            total = [
                [[total[c][i][j] + new[i][j] for j in range(3)] for i in range(3)]
                for c, new in enumerate((real, imag))
            ]
    return total


def transposed(matrix):
    return [[[part[j][i] for j in range(3)] for i in range(3)] for part in matrix]


def row_times(row, right, row_sign, right_sign):
    result = [[], []]
    for j in range(3):
        real = imag = None
        for k in range(3):
            rr = row[0][k] * right[0][k][j]
            ii = row[1][k] * right[1][k][j]
            ri = row[0][k] * right[1][k][j]
            ir = row[1][k] * right[0][k][j]
            new_real = rr - ii if row_sign * right_sign > 0 else rr + ii
            if row_sign > 0 and right_sign > 0:
                new_imag = ri + ir
            elif row_sign > 0:
                new_imag = ir - ri
            else:
                new_imag = ri - ir
            real = new_real if real is None else real + new_real
            imag = new_imag if imag is None else imag + new_imag
        result[0].append(real)
        result[1].append(imag)
    return result


def add_terms(fields, stage, near, acc):
    started = set()
    for target, halves in TERMS[stage]:
        for sign in (1, -1):
            here, ahead, left, right = term_fields(halves, sign)
            force = pole_sum(fields, here, ahead, near)
            left = fields.matrix(left)
            right = fields.matrix(right)
            if sign > 0:
                right = transposed(right)
            else:
                left = transposed(left)
            rows = [row_times([left[0][i], left[1][i]], force, sign, 1) for i in range(3)]
            for i in range(3):
                row = row_times(rows[i], right, 1, -sign)
                for part in range(2):
                    for j in range(3):
                        at = pl.ds((target * 18 + part * 9 + i * 3 + j) * 8, 8)
                        new = row[part][j]
                        acc[at, :] = acc[at, :] + new if target in started else new
            started.add(target)


def acc_tile(acc, target, c):
    return acc[pl.ds((target * 18 + c) * 8, 8), :]


def scale_tiles(scale_ref):
    tiles = [scale_ref[pl.ds(8 * p, 8), :] for p in range(3 * NP)]
    return tiles[:NP], tiles[NP : 2 * NP], tiles[2 * NP :]


def own_force(fields, m, both):
    total = pole_sum(
        fields,
        [("x", 0, ZERO)] * 2,
        [("x", 0, UNIT[m]), ("x", 0, plus(ZERO, UNIT[m], 3))],
        both,
    )
    flat = [total[c][i][j] for c in range(2) for i in range(3) for j in range(3)]
    return [fields.compact_sum(flat[2 * k], flat[2 * k + 1]) for k in range(9)]


def write_messages(locator, plan, names, outs):
    for name, out in zip(names, outs):
        for reg, items in enumerate(plan[name].by_register()):
            spots = [item and locator.local(*item[1:]) for item in items]
            out[pl.ds(8 * reg, 8), :] = locator.assemble(spots)


def odd_in_z():
    return (lax.axis_index("gz") * lax.axis_size("gy") + lax.axis_index("gy")) % 2 == 1


def pack_z_kernel(plan, x_in, u_in, within_ref, between_ref, second_ref, x_ref, u_ref, u_held, sems):
    copies = [
        pltpu.make_async_copy(u_in, u_held, sems.at[0]),
        pltpu.make_async_copy(x_in, x_ref, sems.at[1]),
    ]
    for copy in copies:
        copy.start()
    for copy in copies:
        copy.wait()
    u_ref[...] = u_held[...].astype(F32)
    locator = Locator(plan, 1, {("own", "x"): x_ref, ("own", "u"): u_ref})
    names = [("z", 1), ("z", -1)]

    @pl.when(odd_in_z())
    def _():
        write_messages(locator, plan, names, (within_ref, between_ref))

    @pl.when(jnp.logical_not(odd_in_z()))
    def _():
        write_messages(locator, plan, names, (between_ref, within_ref))

    write_messages(locator, plan, [("z", 2)], [second_ref])


def pack_t_kernel(plan, names, x_ref, u_ref, *outs):
    write_messages(Locator(plan, 1, {("own", "x"): x_ref, ("own", "u"): u_ref}), plan, names, outs)


def corner_kernel(plan, names, within_ref, between_ref, _, ahead_ref, behind_ref, *outs):
    def split(from_ahead, from_behind):
        ahead_ref[...] = from_ahead[pl.ds(0, ahead_ref.shape[0]), :]
        behind_ref[...] = from_behind[pl.ds(0, behind_ref.shape[0]), :]

    @pl.when(odd_in_z())
    def _():
        split(between_ref, within_ref)

    @pl.when(jnp.logical_not(odd_in_z()))
    def _():
        split(within_ref, between_ref)

    locator = Locator(plan, 1, {("z", 1): ahead_ref, ("z", -1): behind_ref})
    for name, out in zip(names, outs):
        for reg, items in enumerate(plan[name].by_register()):
            spots = [
                item and (("z", item[0]),) + plan["z", item[0]].places[(0,) + item[1:]] for item in items
            ]
            out[pl.ds(8 * reg, 8), :] = locator.assemble(spots)


def part_reg(ref, index, k):
    return ref[pl.ds((9 * index + k) * 8, 8), :]


def write_scales(near_ref, far_ref, weight_ref, scale_ref):
    upper = lax.broadcasted_iota(jnp.int32, (8, LANES), 0) < 4
    for p in range(NP):
        scale_ref[pl.ds(8 * p, 8), :] = jnp.full((8, LANES), near_ref[p], F32)
        scale_ref[pl.ds(8 * (NP + p), 8), :] = jnp.where(upper, near_ref[p], far_ref[p])
        scale_ref[pl.ds(8 * (2 * NP + p), 8), :] = jnp.full((8, LANES), weight_ref[p], F32)


def own_kernel(plan, t_size, near_in, far_in, weight_in, x_ref, u_ref, scale_ref, shared_ref, part_ref, *rest):
    near_ref, far_ref, weight_ref, sems, alone_ref, acc = rest
    copies = [
        pltpu.make_async_copy(source, target, sems.at[index])
        for index, (source, target) in enumerate(
            ((near_in, near_ref), (far_in, far_ref), (weight_in, weight_ref))
        )
    ]
    for copy in copies:
        copy.start()
    shared, alone = field_split()
    stores = [(shared_ref, shared["own"][0]), (alone_ref, alone["own"][0])]
    build_fields(Locator(plan, t_size, {("own", "x"): x_ref, ("own", "u"): u_ref}), stores)
    for copy in copies:
        copy.wait()
    write_scales(near_ref, far_ref, weight_ref, scale_ref)
    fields = Fields(x_ref, u_ref, stores)
    near, both, weight = scale_tiles(scale_ref)
    add_terms(fields, "own", near, acc)
    direct = [own_force(fields, m, both) for m in DIRECT["own"]]
    for k in range(9):
        staples = fields.compact_halves(acc_tile(acc, 0, 2 * k), acc_tile(acc, 0, 2 * k + 1))
        for m in range(2):
            part_ref[pl.ds((9 * m + k) * 8, 8), :] = direct[m][k] + weight[m] * staples[m]


def stage_setup(stage, plan, t_size, names, received, x_ref, u_ref, shared_refs, shared_ref, alone_ref):
    buffers = {("own", "x"): x_ref, ("own", "u"): u_ref}
    buffers.update(zip(names, received))
    shared, alone = field_split()
    stores = [(alone_ref, alone[stage][0])]
    if shared_ref is not None:
        stores.append((shared_ref, shared[stage][0]))
    build_fields(Locator(plan, t_size, buffers), stores)
    earlier = [(ref, shared[name][0]) for name, ref in zip(STAGES, shared_refs)]
    return Fields(x_ref, u_ref, earlier + stores)


def z_kernel(plan, t_size, names, scale_ref, x_ref, u_ref, own_shared, own_part, *rest):
    received = rest[: len(names)]
    shared_ref, part_ref, alone_ref, acc = rest[len(names) :]
    fields = stage_setup("z", plan, t_size, names, received, x_ref, u_ref, [own_shared], shared_ref, alone_ref)
    near, _, weight = scale_tiles(scale_ref)
    add_terms(fields, "z", near, acc)
    for k in range(9):
        staples = fields.compact_halves(acc_tile(acc, 0, 2 * k), acc_tile(acc, 0, 2 * k + 1))
        for m in range(2):
            part_ref[pl.ds((9 * m + k) * 8, 8), :] = part_reg(own_part, m, k) + weight[m] * staples[m]
        staple = fields.compact_sum(acc_tile(acc, 1, 2 * k), acc_tile(acc, 1, 2 * k + 1))
        part_ref[pl.ds((18 + k) * 8, 8), :] = weight[2] * staple


def t_kernel(plan, t_size, names, scale_ref, x_ref, u_ref, own_shared, z_shared, z_part, *rest):
    received = rest[: len(names)]
    shared_ref, part_ref, out_ref, alone_ref, acc, ready, sem = rest[len(names) :]
    fields = stage_setup(
        "t", plan, t_size, names, received, x_ref, u_ref, [own_shared, z_shared], shared_ref, alone_ref
    )
    near, both, weight = scale_tiles(scale_ref)
    add_terms(fields, "t", near, acc)
    for k in range(9):
        staples = fields.compact_halves(acc_tile(acc, 0, 2 * k), acc_tile(acc, 0, 2 * k + 1))
        for m in range(2):
            ready[pl.ds((9 * m + k) * 8, 8), :] = part_reg(z_part, m, k) + weight[m] * staples[m]
    leaving = pltpu.make_async_copy(ready, out_ref.at[pl.ds(0, ready.shape[0])], sem)
    leaving.start()
    direct = own_force(fields, 3, both)
    for k in range(9):
        staple = fields.compact_sum(acc_tile(acc, 1, 2 * k), acc_tile(acc, 1, 2 * k + 1))
        part_ref[pl.ds(k * 8, 8), :] = direct[k] + weight[3] * staple
    leaving.wait()


def last_kernel(plan, t_size, names, scale_ref, x_ref, u_ref, *rest):
    own_shared, z_shared, t_shared, z_part, t_part, _ = rest[:6]
    received = rest[6 : 6 + len(names)]
    out_ref, alone_ref, acc, ready, sem = rest[6 + len(names) :]
    fields = stage_setup(
        "corner",
        plan,
        t_size,
        names,
        received,
        x_ref,
        u_ref,
        [own_shared, z_shared, t_shared],
        None,
        alone_ref,
    )
    near, both, weight = scale_tiles(scale_ref)
    add_terms(fields, "corner", near, acc)
    direct = own_force(fields, 2, both)
    for k in range(9):
        staples = fields.compact_halves(acc_tile(acc, 0, 2 * k), acc_tile(acc, 0, 2 * k + 1))
        ready[pl.ds(k * 8, 8), :] = part_reg(z_part, 2, k) + direct[k] + weight[2] * staples[0]
        ready[pl.ds((9 + k) * 8, 8), :] = part_reg(t_part, 0, k) + weight[3] * staples[1]
    rows = ready.shape[0]
    leaving = pltpu.make_async_copy(ready, out_ref.at[pl.ds(rows, rows)], sem)
    leaving.start()
    leaving.wait()


def rows_of(count):
    return jax.ShapeDtypeStruct((count, LANES), F32)


def on_device(pole_vectors, gauge_links, pole_coeff, naik_coeff, staple_weight):
    t_size = lax.axis_size("ta")
    z_size = lax.axis_size("gz") * lax.axis_size("gy")
    plan = message_plan(t_size)
    x_rows, u_rows = 8 * REGS["x"], 4 * 8 * REGS["u"]
    vmem = pl.BlockSpec(memory_space=pltpu.VMEM)
    hbm = pl.BlockSpec(memory_space=pltpu.HBM)
    limit = pltpu.CompilerParams(vmem_limit_bytes=4 * 1024 * 1024)

    def moved(name, value):
        kind, step = name
        if kind == "z":
            return lax.ppermute(value, ("gz", "gy"), [((i + step) % z_size, i) for i in range(z_size)])
        return lax.ppermute(value, "ta", [((j + step) % t_size, j) for j in range(t_size)])

    def exchanged(value, first):
        pairs = [(i, (i + 1) % z_size) for i in range(first, z_size, 2)]
        return lax.ppermute(value, ("gz", "gy"), pairs + [(j, i) for i, j in pairs])

    first_names = [name for name in plan if name[0] != "c"]
    corner_names = [name for name in plan if name[0] == "c"]
    t_names = [name for name in first_names if name[0] == "t"]
    in_hbm = functools.partial(pltpu.with_memory_space_constraint, memory_space=pltpu.HBM)
    ahead_rows, behind_rows = [8 * plan["z", step].count for step in (1, -1)]
    shared_rows = max(ahead_rows, behind_rows)
    within, between, beyond, *own = pl.pallas_call(
        functools.partial(pack_z_kernel, plan),
        out_shape=[rows_of(shared_rows), rows_of(shared_rows + 8), rows_of(8 * plan["z", 2].count)]
        + [rows_of(x_rows), rows_of(u_rows)],
        in_specs=[hbm] * 2,
        out_specs=[vmem] * 5,
        scratch_shapes=[pltpu.VMEM((u_rows, LANES), jnp.bfloat16), pltpu.SemaphoreType.DMA((2,))],
        compiler_params=limit,
        name="pack_z",
    )(in_hbm(pole_vectors.reshape((x_rows, LANES))), in_hbm(gauge_links.reshape((u_rows, LANES))))
    between, within = exchanged(between, 1), exchanged(within, 0)
    received = {("z", 2): moved(("z", 2), beyond)}
    packed = pl.pallas_call(
        functools.partial(pack_t_kernel, plan, t_names),
        out_shape=[rows_of(8 * plan[name].count) for name in t_names],
        in_specs=[vmem] * 2,
        out_specs=[vmem] * len(t_names),
        compiler_params=limit,
        name="pack_t",
    )(*own)
    received.update({name: moved(name, value) for name, value in zip(t_names, packed)})
    shared, alone = field_split()
    part_rows = 8 * REGS["u"]

    def scratch(stage):
        sums = 1 + max(target for target, _ in TERMS[stage])
        return [pltpu.VMEM((alone[stage][1], LANES), F32), pltpu.VMEM((sums * 18 * 8, LANES), F32)]

    def cost(micros):
        return pl.CostEstimate(flops=10**6, bytes_accessed=int(3.69e6 * micros), transcendentals=0)

    wide_limit = pltpu.CompilerParams(vmem_limit_bytes=6 * 1024 * 1024)
    scale, own_shared, own_part = pl.pallas_call(
        functools.partial(own_kernel, plan, t_size),
        out_shape=[rows_of(8 * 3 * NP), rows_of(shared["own"][1]), rows_of(2 * part_rows)],
        in_specs=[hbm] * 3 + [vmem] * 2,
        out_specs=[vmem] * 3,
        scratch_shapes=[pltpu.SMEM((NP,), F32)] * 3 + [pltpu.SemaphoreType.DMA((3,))] + scratch("own"),
        cost_estimate=cost(COSTS["own"]),
        compiler_params=wide_limit,
        name="force_own",
    )(in_hbm(pole_coeff), in_hbm(naik_coeff), in_hbm(staple_weight), *own)
    local = [scale, *own]
    received["z", 1], received["z", -1], *corners = pl.pallas_call(
        functools.partial(corner_kernel, plan, corner_names),
        out_shape=[rows_of(ahead_rows), rows_of(behind_rows)]
        + [rows_of(8 * plan[name].count) for name in corner_names],
        in_specs=[vmem] * 3,
        out_specs=[vmem] * (2 + len(corner_names)),
        compiler_params=limit,
        name="pack_corners",
    )(within, between, scale)
    received.update({name: moved(name, value) for name, value in zip(corner_names, corners)})
    names = [("z", 1), ("z", -1)]
    z_shared, z_part = pl.pallas_call(
        functools.partial(z_kernel, plan, t_size, names),
        out_shape=[rows_of(shared["z"][1]), rows_of(3 * part_rows)],
        in_specs=[vmem] * (5 + len(names)),
        out_specs=[vmem] * 2,
        scratch_shapes=scratch("z"),
        cost_estimate=cost(COSTS["z"]),
        compiler_params=wide_limit,
        name="force_z",
    )(*local, own_shared, own_part, *[received[name] for name in names])
    t_shared, t_part, force = pl.pallas_call(
        functools.partial(t_kernel, plan, t_size, t_names),
        out_shape=[rows_of(shared["t"][1]), rows_of(part_rows), rows_of(u_rows)],
        in_specs=[vmem] * (6 + len(t_names)),
        out_specs=[vmem] * 2 + [hbm],
        scratch_shapes=scratch("t") + [pltpu.VMEM((2 * part_rows, LANES), F32), pltpu.SemaphoreType.DMA],
        cost_estimate=cost(COSTS["t"]),
        compiler_params=wide_limit,
        name="force_t",
    )(*local, own_shared, z_shared, z_part, *[received[name] for name in t_names])
    names = list(received)
    force = pl.pallas_call(
        functools.partial(last_kernel, plan, t_size, names),
        out_shape=rows_of(u_rows),
        in_specs=[vmem] * 8 + [hbm] + [vmem] * len(names),
        out_specs=hbm,
        input_output_aliases={8: 0},
        scratch_shapes=scratch("corner")
        + [pltpu.VMEM((2 * part_rows, LANES), F32), pltpu.SemaphoreType.DMA],
        cost_estimate=cost(COSTS["corner"]),
        compiler_params=wide_limit,
        name="force_corner",
    )(
        *local,
        own_shared,
        z_shared,
        t_shared,
        z_part,
        t_part,
        force,
        *[received[name] for name in names],
    )
    return force.reshape(gauge_links.shape)


def solution(mesh):
    return jax.shard_map(
        on_device,
        mesh=mesh,
        in_specs=(
            P("ens", None, None, "ta", ("gz", "gy"), None),
            P("ens", None, None, None, "ta", ("gz", "gy"), None),
            P(),
            P(),
            P(),
        ),
        out_specs=P("ens", None, None, None, "ta", ("gz", "gy"), None),
        check_vma=False,
    )
```

```python
import collections
import functools

import jax
import jax.numpy as jnp
from jax import lax
from jax.experimental import pallas as pl
from jax.experimental.pallas import tpu as pltpu
from jax.sharding import PartitionSpec as P

NX = 8
NY = 16
LANES = NX * NY
NP = 4
F32 = jnp.float32
REGS = {"x": NP * 3, "u": 9}
UNIT = ((1, 0, 0, 0), (0, 1, 0, 0), (0, 0, 1, 0), (0, 0, 0, 1))
ZERO = (0, 0, 0, 0)
SITES = ((0, 0), (0, 1), (1, 0), (1, 1))
STAGES = ("own", "z", "t", "corner")
TERMS = {
    "own": ((0, ((0, 1), (1, 0))),),
    "z": ((0, ((0, 2), (1, 2))), (1, ((2, 0), (2, 1)))),
    "t": ((0, ((0, 3), (1, 3))), (1, ((3, 0), (3, 1)))),
    "corner": ((0, ((2, 3), (3, 2))),),
}
COSTS = {"own": 2.0, "z": 2.0, "t": 2.0, "corner": 1.0}
DIRECT = {"own": (0, 1), "z": (2,), "t": (3,), "corner": ()}


def plus(left, right, scale=1):
    return tuple(a + scale * b for a, b in zip(left, right))


class Message:
    def __init__(self):
        self.places = collections.OrderedDict()
        self.count = 0

    def add_full(self, kind, n):
        for k in range(REGS[kind]):
            for t, z in SITES:
                self.places[0, kind, n, k, t, z] = (self.count, 2 * t + z)
            self.count += 1

    def add_halves(self, entries, axis):
        half = -(-len(entries) // 2)
        for index, (kind, n, k, layer) in enumerate(entries):
            reg, part = self.count + index % half, index // half
            for other in range(2):
                t, z = (layer, other) if axis == "t" else (other, layer)
                slot = 2 * part + other if axis == "t" else 2 * other + part
                self.places[0, kind, n, k, t, z] = (reg, slot)
        self.count += half

    def add_single(self, entries):
        quarter = -(-len(entries) // 4)
        for index, entry in enumerate(entries):
            self.places[entry] = (self.count + index % quarter, index // quarter)
        self.count += quarter

    def by_register(self):
        found = [[None] * 4 for _ in range(self.count)]
        for item, (reg, slot) in self.places.items():
            found[reg][slot] = item
        return found


def regs_of(kind, directions, layer):
    return [(kind, n, k, layer) for n in directions for k in range(REGS[kind])]


def message_plan(t_size):
    plan = collections.OrderedDict()
    ahead = plan["z", 1] = Message()
    ahead.add_full("x", 0)
    ahead.add_halves(regs_of("u", (0, 1, 3), 0), "z")
    behind = plan["z", -1] = Message()
    behind.add_halves(regs_of("x", (0,), 1) + regs_of("u", (2,), 1), "z")
    second = plan["z", 2] = Message()
    second.add_halves(regs_of("x", (0,), 0), "z")
    halves, corners = collections.OrderedDict(), collections.OrderedDict()
    for dt, entries in (
        (1, regs_of("u", (0, 1, 2), 0)),
        (-1, regs_of("x", (0,), 1) + regs_of("u", (3,), 1)),
        (2, regs_of("x", (0,), 0)),
    ):
        if dt % t_size != 0:
            halves.setdefault(dt % t_size, []).extend(entries)
    for dt, entries in halves.items():
        message = plan["t", dt] = Message()
        if dt == 1:
            message.add_full("x", 0)
        held = {item[1:4] for item in message.places}
        message.add_halves([e for e in entries if e[:3] not in held], "t")
    for dt, entries in (
        (1, [(1, "x", 0, k, 0, 0) for k in range(REGS["x"])]),
        (1, [(-1, "x", 0, k, 0, 1) for k in range(REGS["x"])]),
        (1, [(-1, "u", 2, k, 0, 1) for k in range(REGS["u"])]),
        (-1, [(1, "x", 0, k, 1, 0) for k in range(REGS["x"])]),
        (-1, [(1, "u", 3, k, 1, 0) for k in range(REGS["u"])]),
    ):
        corners.setdefault(dt % t_size, []).extend(entries)
    for dt, entries in corners.items():
        plan["c", dt] = Message()
        plan["c", dt].add_single(entries)
    return plan


class Locator:
    def __init__(self, plan, t_size, buffers):
        self.plan, self.t_size, self.buffers = plan, t_size, buffers

    def local(self, kind, n, k, t, z):
        return ("own", kind), n * REGS[kind] + k, 2 * t + z

    def find(self, kind, n, k, t_at, z_at):
        (dt, t), (dz, z) = divmod(t_at, 2), divmod(z_at, 2)
        dt %= self.t_size
        if (dt, dz) == (0, 0):
            return self.local(kind, n, k, t, z)
        name = ("z", dz) if dt == 0 else ("t", dt) if dz == 0 else ("c", dt)
        item = (dz if name[0] == "c" else 0, kind, n, k, t, z)
        return (name,) + self.plan[name].places[item]

    def load(self, name, reg):
        return self.buffers[name][pl.ds(8 * reg, 8), :]

    def assemble(self, spots):
        groups = collections.OrderedDict()
        for r, spot in enumerate(spots):
            if spot is not None:
                groups.setdefault((spot[0], spot[1], r - spot[2]), []).append(r)
        row = lax.broadcasted_iota(jnp.int32, (8, LANES), 0) % 4
        result = None
        for (name, reg, move), rows in groups.items():
            value = self.load(name, reg)
            if move != 0:
                value = pltpu.roll(value, move % 8, 0)
            if result is None:
                result = value
            else:
                mask = functools.reduce(jnp.logical_or, [row == r for r in rows])
                result = jnp.where(mask, value, result)
        return result

    def field_register(self, kind, n, k, dt, dz):
        return self.assemble([self.find(kind, n, k, t + dt, z + dz) for t, z in SITES])


def lane_shifted(value, dx, dy):
    if dx != 0:
        x_at = lax.broadcasted_iota(jnp.int32, value.shape, 1) % NX
        beyond = (x_at + dx >= NX) | (x_at + dx < 0)
        main = pltpu.roll(value, (-dx) % LANES, 1)
        wrapped = pltpu.roll(value, (NX - dx if dx > 0 else -NX - dx) % LANES, 1)
        value = jnp.where(beyond, wrapped, main)
    if dy != 0:
        value = pltpu.roll(value, (-dy * NX) % LANES, 1)
    return value


def term_fields(halves, sign):
    here, ahead, left, right = [], [], [], []
    for m, n in halves:
        start = plus(ZERO, UNIT[n], sign)
        base = ZERO if sign > 0 else start
        here.append(("x", 0, start))
        ahead.append(("x", 0, plus(start, UNIT[m])))
        left.append(("u", n, base))
        right.append(("u", n, plus(base, UNIT[m])))
    return here, ahead, left, right


def needed_fields(stage):
    keys = collections.OrderedDict()
    for _, halves in TERMS[stage]:
        for sign in (1, -1):
            for pair in term_fields(halves, sign):
                keys.update((key, None) for key in pair)
    for m in DIRECT[stage]:
        for scale in (1, 3):
            keys["x", 0, plus(ZERO, UNIT[m], scale)] = None
    return [key for key in keys if key[2] != ZERO]


def stage_of(key):
    dz, dt = key[2][2:]
    if dz != 0 and dt != 0:
        return "corner"
    return "t" if dt != 0 else "z" if dz != 0 else "own"


def lay_out(keys):
    rows, total = collections.OrderedDict(), 0
    for key in keys:
        rows[key] = total
        total += 8 * REGS[key[0]]
    return rows, total


def field_split():
    uses = collections.OrderedDict()
    for stage in STAGES:
        for key in needed_fields(stage):
            uses.setdefault(key, []).append(stage)
    shared, alone = {}, {}
    for stage in STAGES:
        built = [key for key in uses if stage_of(key) == stage]
        shared[stage] = lay_out([key for key in built if uses[key] != [stage]])
        alone[stage] = lay_out([key for key in built if uses[key] == [stage]])
    return shared, alone


def build_fields(locator, stores):
    groups = collections.OrderedDict()
    for ref, rows in stores:
        for (kind, n, disp), row in rows.items():
            shifts = groups.setdefault((kind, n, disp[3], disp[2]), collections.OrderedDict())
            shifts[disp[0], disp[1]] = (ref, row)
    for (kind, n, dt, dz), shifts in groups.items():
        for k in range(REGS[kind]):
            value = locator.field_register(kind, n, k, dt, dz)
            by_x = {0: value}
            for (dx, dy), (ref, row) in shifts.items():
                if dx not in by_x:
                    by_x[dx] = lane_shifted(value, dx, 0)
                ref[pl.ds(row + 8 * k, 8), :] = lane_shifted(by_x[dx], 0, dy)


class Fields:
    def __init__(self, own_x, own_u, stores):
        self.place = {("x", 0, ZERO): (own_x, 0)}
        for n in range(4):
            self.place["u", n, ZERO] = (own_u, 8 * REGS["u"] * n)
        for ref, rows in stores:
            for key, row in rows.items():
                self.place[key] = (ref, row)
        self.upper = lax.broadcasted_iota(jnp.int32, (8, LANES), 0) < 4

    def reg(self, key, k):
        ref, row = self.place[key]
        return ref[pl.ds(row + 8 * k, 8), :]

    def two_tiles(self, keys, k):
        top = self.reg(keys[0], k)
        turned_top = pltpu.roll(top, 4, 0)
        if keys[0] == keys[1]:
            low, turned_low = top, turned_top
        else:
            low = self.reg(keys[1], k)
            turned_low = pltpu.roll(low, 4, 0)
        return [jnp.where(self.upper, top, turned_low), jnp.where(self.upper, turned_top, low)]

    def vector(self, keys, pole):
        flat = [tile for k in range(3) for tile in self.two_tiles(keys, 3 * pole + k)]
        return [flat[:3], flat[3:]]

    def matrix(self, keys):
        flat = [tile for k in range(9) for tile in self.two_tiles(keys, k)]
        return [[flat[9 * c + 3 * i : 9 * c + 3 * i + 3] for i in range(3)] for c in range(2)]

    def compact_halves(self, first, second):
        top = jnp.where(self.upper, first, pltpu.roll(second, 4, 0))
        return top, jnp.where(self.upper, pltpu.roll(first, 4, 0), second)

    def compact_sum(self, first, second):
        kept = jnp.where(self.upper, first, second)
        return kept + pltpu.roll(jnp.where(self.upper, second, first), 4, 0)


def pole_sum(fields, here, ahead, scales):
    total = None
    for pole in range(NP):
        h = [[scales[pole] * v for v in part] for part in fields.vector(here, pole)]
        a = fields.vector(ahead, pole)
        real = [[a[0][i] * h[0][j] + a[1][i] * h[1][j] for j in range(3)] for i in range(3)]
        imag = [[a[1][i] * h[0][j] - a[0][i] * h[1][j] for j in range(3)] for i in range(3)]
        if total is None:
            total = [real, imag]
        else:
            total = [
                [[total[c][i][j] + new[i][j] for j in range(3)] for i in range(3)]
                for c, new in enumerate((real, imag))
            ]
    return total


def transposed(matrix):
    return [[[part[j][i] for j in range(3)] for i in range(3)] for part in matrix]


def row_times(row, right, row_sign, right_sign):
    result = [[], []]
    for j in range(3):
        real = imag = None
        for k in range(3):
            rr = row[0][k] * right[0][k][j]
            ii = row[1][k] * right[1][k][j]
            ri = row[0][k] * right[1][k][j]
            ir = row[1][k] * right[0][k][j]
            new_real = rr - ii if row_sign * right_sign > 0 else rr + ii
            if row_sign > 0 and right_sign > 0:
                new_imag = ri + ir
            elif row_sign > 0:
                new_imag = ir - ri
            else:
                new_imag = ri - ir
            real = new_real if real is None else real + new_real
            imag = new_imag if imag is None else imag + new_imag
        result[0].append(real)
        result[1].append(imag)
    return result


def add_terms(fields, stage, near, acc):
    started = set()
    for target, halves in TERMS[stage]:
        for sign in (1, -1):
            here, ahead, left, right = term_fields(halves, sign)
            force = pole_sum(fields, here, ahead, near)
            left = fields.matrix(left)
            right = fields.matrix(right)
            if sign > 0:
                right = transposed(right)
            else:
                left = transposed(left)
            rows = [row_times([left[0][i], left[1][i]], force, sign, 1) for i in range(3)]
            for i in range(3):
                row = row_times(rows[i], right, 1, -sign)
                for part in range(2):
                    for j in range(3):
                        at = pl.ds((target * 18 + part * 9 + i * 3 + j) * 8, 8)
                        new = row[part][j]
                        acc[at, :] = acc[at, :] + new if target in started else new
            started.add(target)


def acc_tile(acc, target, c):
    return acc[pl.ds((target * 18 + c) * 8, 8), :]


def scale_tiles(scale_ref):
    tiles = [scale_ref[pl.ds(8 * p, 8), :] for p in range(3 * NP)]
    return tiles[:NP], tiles[NP : 2 * NP], tiles[2 * NP :]


def own_force(fields, m, both):
    total = pole_sum(
        fields,
        [("x", 0, ZERO)] * 2,
        [("x", 0, UNIT[m]), ("x", 0, plus(ZERO, UNIT[m], 3))],
        both,
    )
    flat = [total[c][i][j] for c in range(2) for i in range(3) for j in range(3)]
    return [fields.compact_sum(flat[2 * k], flat[2 * k + 1]) for k in range(9)]


def write_messages(locator, plan, names, outs):
    for name, out in zip(names, outs):
        for reg, items in enumerate(plan[name].by_register()):
            spots = [item and locator.local(*item[1:]) for item in items]
            out[pl.ds(8 * reg, 8), :] = locator.assemble(spots)


def odd_in_z():
    return (lax.axis_index("gz") * lax.axis_size("gy") + lax.axis_index("gy")) % 2 == 1


def pack_z_kernel(plan, x_in, u_in, within_ref, between_ref, second_ref, x_ref, u_ref, u_held, sems):
    copies = [
        pltpu.make_async_copy(u_in, u_held, sems.at[0]),
        pltpu.make_async_copy(x_in, x_ref, sems.at[1]),
    ]
    for copy in copies:
        copy.start()
    for copy in copies:
        copy.wait()
    u_ref[...] = u_held[...].astype(F32)
    locator = Locator(plan, 1, {("own", "x"): x_ref, ("own", "u"): u_ref})
    names = [("z", 1), ("z", -1)]

    @pl.when(odd_in_z())
    def _():
        write_messages(locator, plan, names, (within_ref, between_ref))

    @pl.when(jnp.logical_not(odd_in_z()))
    def _():
        write_messages(locator, plan, names, (between_ref, within_ref))

    write_messages(locator, plan, [("z", 2)], [second_ref])


def pack_t_kernel(plan, names, x_ref, u_ref, *outs):
    write_messages(Locator(plan, 1, {("own", "x"): x_ref, ("own", "u"): u_ref}), plan, names, outs)


def corner_kernel(plan, names, within_ref, between_ref, _, ahead_ref, behind_ref, *outs):
    def split(from_ahead, from_behind):
        ahead_ref[...] = from_ahead[pl.ds(0, ahead_ref.shape[0]), :]
        behind_ref[...] = from_behind[pl.ds(0, behind_ref.shape[0]), :]

    @pl.when(odd_in_z())
    def _():
        split(between_ref, within_ref)

    @pl.when(jnp.logical_not(odd_in_z()))
    def _():
        split(within_ref, between_ref)

    locator = Locator(plan, 1, {("z", 1): ahead_ref, ("z", -1): behind_ref})
    for name, out in zip(names, outs):
        for reg, items in enumerate(plan[name].by_register()):
            spots = [
                item and (("z", item[0]),) + plan["z", item[0]].places[(0,) + item[1:]] for item in items
            ]
            out[pl.ds(8 * reg, 8), :] = locator.assemble(spots)


def part_reg(ref, index, k):
    return ref[pl.ds((9 * index + k) * 8, 8), :]


def write_scales(near_ref, far_ref, weight_ref, scale_ref):
    upper = lax.broadcasted_iota(jnp.int32, (8, LANES), 0) < 4
    for p in range(NP):
        scale_ref[pl.ds(8 * p, 8), :] = jnp.full((8, LANES), near_ref[p], F32)
        scale_ref[pl.ds(8 * (NP + p), 8), :] = jnp.where(upper, near_ref[p], far_ref[p])
        scale_ref[pl.ds(8 * (2 * NP + p), 8), :] = jnp.full((8, LANES), weight_ref[p], F32)


def own_fields_kernel(plan, t_size, near_in, far_in, weight_in, x_ref, u_ref, scale_ref, shared_ref, alone_ref, *rest):
    near_ref, far_ref, weight_ref, sems = rest
    copies = [
        pltpu.make_async_copy(source, target, sems.at[index])
        for index, (source, target) in enumerate(
            ((near_in, near_ref), (far_in, far_ref), (weight_in, weight_ref))
        )
    ]
    for copy in copies:
        copy.start()
    shared, alone = field_split()
    stores = [(shared_ref, shared["own"][0]), (alone_ref, alone["own"][0])]
    build_fields(Locator(plan, t_size, {("own", "x"): x_ref, ("own", "u"): u_ref}), stores)
    for copy in copies:
        copy.wait()
    write_scales(near_ref, far_ref, weight_ref, scale_ref)


def own_kernel(scale_ref, x_ref, u_ref, shared_ref, alone_ref, part_ref, acc):
    shared, alone = field_split()
    fields = Fields(x_ref, u_ref, [(shared_ref, shared["own"][0]), (alone_ref, alone["own"][0])])
    near, both, weight = scale_tiles(scale_ref)
    add_terms(fields, "own", near, acc)
    direct = [own_force(fields, m, both) for m in DIRECT["own"]]
    for k in range(9):
        staples = fields.compact_halves(acc_tile(acc, 0, 2 * k), acc_tile(acc, 0, 2 * k + 1))
        for m in range(2):
            part_ref[pl.ds((9 * m + k) * 8, 8), :] = direct[m][k] + weight[m] * staples[m]


def stage_setup(stage, plan, t_size, names, received, x_ref, u_ref, shared_refs, shared_ref, alone_ref):
    buffers = {("own", "x"): x_ref, ("own", "u"): u_ref}
    buffers.update(zip(names, received))
    shared, alone = field_split()
    stores = [(alone_ref, alone[stage][0])]
    if shared_ref is not None:
        stores.append((shared_ref, shared[stage][0]))
    build_fields(Locator(plan, t_size, buffers), stores)
    earlier = [(ref, shared[name][0]) for name, ref in zip(STAGES, shared_refs)]
    return Fields(x_ref, u_ref, earlier + stores)


def z_kernel(plan, t_size, names, scale_ref, x_ref, u_ref, own_shared, own_part, *rest):
    received = rest[: len(names)]
    shared_ref, part_ref, alone_ref, acc = rest[len(names) :]
    fields = stage_setup("z", plan, t_size, names, received, x_ref, u_ref, [own_shared], shared_ref, alone_ref)
    near, both, weight = scale_tiles(scale_ref)
    add_terms(fields, "z", near, acc)
    direct = own_force(fields, 2, both)
    for k in range(9):
        staples = fields.compact_halves(acc_tile(acc, 0, 2 * k), acc_tile(acc, 0, 2 * k + 1))
        for m in range(2):
            part_ref[pl.ds((9 * m + k) * 8, 8), :] = part_reg(own_part, m, k) + weight[m] * staples[m]
        staple = fields.compact_sum(acc_tile(acc, 1, 2 * k), acc_tile(acc, 1, 2 * k + 1))
        part_ref[pl.ds((18 + k) * 8, 8), :] = direct[k] + weight[2] * staple


def t_kernel(plan, t_size, names, scale_ref, x_ref, u_ref, own_shared, z_shared, z_part, *rest):
    received = rest[: len(names)]
    shared_ref, part_ref, out_ref, alone_ref, acc, ready, sem = rest[len(names) :]
    fields = stage_setup(
        "t", plan, t_size, names, received, x_ref, u_ref, [own_shared, z_shared], shared_ref, alone_ref
    )
    near, both, weight = scale_tiles(scale_ref)
    add_terms(fields, "t", near, acc)
    for k in range(9):
        staples = fields.compact_halves(acc_tile(acc, 0, 2 * k), acc_tile(acc, 0, 2 * k + 1))
        for m in range(2):
            ready[pl.ds((9 * m + k) * 8, 8), :] = part_reg(z_part, m, k) + weight[m] * staples[m]
    leaving = pltpu.make_async_copy(ready, out_ref.at[pl.ds(0, ready.shape[0])], sem)
    leaving.start()
    direct = own_force(fields, 3, both)
    for k in range(9):
        staple = fields.compact_sum(acc_tile(acc, 1, 2 * k), acc_tile(acc, 1, 2 * k + 1))
        part_ref[pl.ds(k * 8, 8), :] = direct[k] + weight[3] * staple
    leaving.wait()


def last_kernel(plan, t_size, names, scale_ref, x_ref, u_ref, *rest):
    own_shared, z_shared, t_shared, z_part, t_part, _ = rest[:6]
    received = rest[6 : 6 + len(names)]
    out_ref, alone_ref, acc, ready, sem = rest[6 + len(names) :]
    fields = stage_setup(
        "corner",
        plan,
        t_size,
        names,
        received,
        x_ref,
        u_ref,
        [own_shared, z_shared, t_shared],
        None,
        alone_ref,
    )
    near, _, weight = scale_tiles(scale_ref)
    add_terms(fields, "corner", near, acc)
    for k in range(9):
        staples = fields.compact_halves(acc_tile(acc, 0, 2 * k), acc_tile(acc, 0, 2 * k + 1))
        ready[pl.ds(k * 8, 8), :] = part_reg(z_part, 2, k) + weight[2] * staples[0]
        ready[pl.ds((9 + k) * 8, 8), :] = part_reg(t_part, 0, k) + weight[3] * staples[1]
    rows = ready.shape[0]
    leaving = pltpu.make_async_copy(ready, out_ref.at[pl.ds(rows, rows)], sem)
    leaving.start()
    leaving.wait()


def rows_of(count):
    return jax.ShapeDtypeStruct((count, LANES), F32)


def on_device(pole_vectors, gauge_links, pole_coeff, naik_coeff, staple_weight):
    t_size = lax.axis_size("ta")
    z_size = lax.axis_size("gz") * lax.axis_size("gy")
    plan = message_plan(t_size)
    x_rows, u_rows = 8 * REGS["x"], 4 * 8 * REGS["u"]
    vmem = pl.BlockSpec(memory_space=pltpu.VMEM)
    hbm = pl.BlockSpec(memory_space=pltpu.HBM)
    limit = pltpu.CompilerParams(vmem_limit_bytes=4 * 1024 * 1024)

    def moved(name, value):
        kind, step = name
        if kind == "z":
            return lax.ppermute(value, ("gz", "gy"), [((i + step) % z_size, i) for i in range(z_size)])
        return lax.ppermute(value, "ta", [((j + step) % t_size, j) for j in range(t_size)])

    def exchanged(value, first):
        pairs = [(i, (i + 1) % z_size) for i in range(first, z_size, 2)]
        return lax.ppermute(value, ("gz", "gy"), pairs + [(j, i) for i, j in pairs])

    first_names = [name for name in plan if name[0] != "c"]
    corner_names = [name for name in plan if name[0] == "c"]
    t_names = [name for name in first_names if name[0] == "t"]
    in_hbm = functools.partial(pltpu.with_memory_space_constraint, memory_space=pltpu.HBM)
    beyond_rows = 8 * max([plan["z", 2].count] + [plan[name].count for name in corner_names])
    ahead_rows, behind_rows = [8 * plan["z", step].count for step in (1, -1)]
    shared_rows = max(ahead_rows, behind_rows)
    within, between, beyond, *own = pl.pallas_call(
        functools.partial(pack_z_kernel, plan),
        out_shape=[rows_of(shared_rows), rows_of(shared_rows + 8), rows_of(beyond_rows)]
        + [rows_of(x_rows), rows_of(u_rows)],
        in_specs=[hbm] * 2,
        out_specs=[vmem] * 5,
        scratch_shapes=[pltpu.VMEM((u_rows, LANES), jnp.bfloat16), pltpu.SemaphoreType.DMA((2,))],
        compiler_params=limit,
        name="pack_z",
    )(in_hbm(pole_vectors.reshape((x_rows, LANES))), in_hbm(gauge_links.reshape((u_rows, LANES))))
    between, within = exchanged(between, 1), exchanged(within, 0)
    received = {("z", 2): moved(("z", 2), beyond)}
    packed = pl.pallas_call(
        functools.partial(pack_t_kernel, plan, t_names),
        out_shape=[rows_of(8 * plan[name].count) for name in t_names],
        in_specs=[vmem] * 2,
        out_specs=[vmem] * len(t_names),
        compiler_params=limit,
        name="pack_t",
    )(*own)
    received.update({name: moved(name, value) for name, value in zip(t_names, packed)})
    shared, alone = field_split()
    part_rows = 8 * REGS["u"]

    def scratch(stage):
        sums = 1 + max(target for target, _ in TERMS[stage])
        return [pltpu.VMEM((alone[stage][1], LANES), F32), pltpu.VMEM((sums * 18 * 8, LANES), F32)]

    def cost(micros):
        return pl.CostEstimate(flops=10**6, bytes_accessed=int(3.69e6 * micros), transcendentals=0)

    wide_limit = pltpu.CompilerParams(vmem_limit_bytes=6 * 1024 * 1024)
    scale, own_shared, own_alone = pl.pallas_call(
        functools.partial(own_fields_kernel, plan, t_size),
        out_shape=[rows_of(8 * 3 * NP), rows_of(shared["own"][1]), rows_of(alone["own"][1])],
        in_specs=[hbm] * 3 + [vmem] * 2,
        out_specs=[vmem] * 3,
        scratch_shapes=[pltpu.SMEM((NP,), F32)] * 3 + [pltpu.SemaphoreType.DMA((3,))],
        compiler_params=wide_limit,
        name="fields_own",
    )(in_hbm(pole_coeff), in_hbm(naik_coeff), in_hbm(staple_weight), *own)
    own_part = pl.pallas_call(
        own_kernel,
        out_shape=rows_of(2 * part_rows),
        in_specs=[vmem] * 5,
        out_specs=vmem,
        scratch_shapes=scratch("own")[1:],
        cost_estimate=cost(COSTS["own"]),
        compiler_params=wide_limit,
        name="force_own",
    )(scale, *own, own_shared, own_alone)
    local = [scale, *own]
    received["z", 1], received["z", -1], *corners = pl.pallas_call(
        functools.partial(corner_kernel, plan, corner_names),
        out_shape=[rows_of(ahead_rows), rows_of(behind_rows)]
        + [rows_of(8 * plan[name].count) for name in corner_names],
        in_specs=[vmem] * 3,
        out_specs=[vmem] * (2 + len(corner_names)),
        compiler_params=limit,
        name="pack_corners",
    )(within, between, own_part)
    received.update({name: moved(name, value) for name, value in zip(corner_names, corners)})
    names = [("z", 1), ("z", -1), ("z", 2)]
    z_shared, z_part = pl.pallas_call(
        functools.partial(z_kernel, plan, t_size, names),
        out_shape=[rows_of(shared["z"][1]), rows_of(3 * part_rows)],
        in_specs=[vmem] * (5 + len(names)),
        out_specs=[vmem] * 2,
        scratch_shapes=scratch("z"),
        cost_estimate=cost(COSTS["z"]),
        compiler_params=wide_limit,
        name="force_z",
    )(*local, own_shared, own_part, *[received[name] for name in names])
    t_shared, t_part, force = pl.pallas_call(
        functools.partial(t_kernel, plan, t_size, t_names),
        out_shape=[rows_of(shared["t"][1]), rows_of(part_rows), rows_of(u_rows)],
        in_specs=[vmem] * (6 + len(t_names)),
        out_specs=[vmem] * 2 + [hbm],
        scratch_shapes=scratch("t") + [pltpu.VMEM((2 * part_rows, LANES), F32), pltpu.SemaphoreType.DMA],
        cost_estimate=cost(COSTS["t"]),
        compiler_params=wide_limit,
        name="force_t",
    )(*local, own_shared, z_shared, z_part, *[received[name] for name in t_names])
    names = [name for name in received if name != ("z", 2)]
    force = pl.pallas_call(
        functools.partial(last_kernel, plan, t_size, names),
        out_shape=rows_of(u_rows),
        in_specs=[vmem] * 8 + [hbm] + [vmem] * len(names),
        out_specs=hbm,
        input_output_aliases={8: 0},
        scratch_shapes=scratch("corner")
        + [pltpu.VMEM((2 * part_rows, LANES), F32), pltpu.SemaphoreType.DMA],
        cost_estimate=cost(COSTS["corner"]),
        compiler_params=wide_limit,
        name="force_corner",
    )(
        *local,
        own_shared,
        z_shared,
        t_shared,
        z_part,
        t_part,
        force,
        *[received[name] for name in names],
    )
    return force.reshape(gauge_links.shape)


def solution(mesh):
    return jax.shard_map(
        on_device,
        mesh=mesh,
        in_specs=(
            P("ens", None, None, "ta", ("gz", "gy"), None),
            P("ens", None, None, None, "ta", ("gz", "gy"), None),
            P(),
            P(),
            P(),
        ),
        out_specs=P("ens", None, None, None, "ta", ("gz", "gy"), None),
        check_vma=False,
    )
```

```python
import collections
import functools

import jax
import jax.numpy as jnp
from jax import lax
from jax.experimental import pallas as pl
from jax.experimental.pallas import tpu as pltpu
from jax.sharding import PartitionSpec as P

NX = 8
NY = 16
LANES = NX * NY
NP = 4
F32 = jnp.float32
REGS = {"x": NP * 3, "u": 9}
UNIT = ((1, 0, 0, 0), (0, 1, 0, 0), (0, 0, 1, 0), (0, 0, 0, 1))
ZERO = (0, 0, 0, 0)
SITES = ((0, 0), (0, 1), (1, 0), (1, 1))
STAGES = ("own", "z", "t", "corner")
TERMS = {
    "own": ((0, ((0, 1), (1, 0))),),
    "z": ((0, ((0, 2), (1, 2))), (1, ((2, 0), (2, 1)))),
    "t": ((0, ((0, 3), (1, 3))), (1, ((3, 0), (3, 1)))),
    "corner": ((0, ((2, 3), (3, 2))),),
}
COSTS = {"own": 2.0, "z": 2.0, "t": 2.0, "corner": 1.0}
DIRECT = {"own": (0, 1), "z": (2,), "t": (3,), "corner": ()}


def plus(left, right, scale=1):
    return tuple(a + scale * b for a, b in zip(left, right))


class Message:
    def __init__(self):
        self.places = collections.OrderedDict()
        self.count = 0

    def add_full(self, kind, n):
        for k in range(REGS[kind]):
            for t, z in SITES:
                self.places[0, kind, n, k, t, z] = (self.count, 2 * t + z)
            self.count += 1

    def add_halves(self, entries, axis):
        half = -(-len(entries) // 2)
        for index, (kind, n, k, layer) in enumerate(entries):
            reg, part = self.count + index % half, index // half
            for other in range(2):
                t, z = (layer, other) if axis == "t" else (other, layer)
                slot = 2 * part + other if axis == "t" else 2 * other + part
                self.places[0, kind, n, k, t, z] = (reg, slot)
        self.count += half

    def add_single(self, entries):
        quarter = -(-len(entries) // 4)
        for index, entry in enumerate(entries):
            self.places[entry] = (self.count + index % quarter, index // quarter)
        self.count += quarter

    def by_register(self):
        found = [[None] * 4 for _ in range(self.count)]
        for item, (reg, slot) in self.places.items():
            found[reg][slot] = item
        return found


def regs_of(kind, directions, layer):
    return [(kind, n, k, layer) for n in directions for k in range(REGS[kind])]


def message_plan(t_size):
    plan = collections.OrderedDict()
    ahead = plan["z", 1] = Message()
    ahead.add_full("x", 0)
    ahead.add_halves(regs_of("u", (0, 1, 3), 0), "z")
    behind = plan["z", -1] = Message()
    behind.add_halves(regs_of("x", (0,), 1) + regs_of("u", (2,), 1), "z")
    second = plan["z", 2] = Message()
    second.add_halves(regs_of("x", (0,), 0), "z")
    halves, corners = collections.OrderedDict(), collections.OrderedDict()
    for dt, entries in (
        (1, regs_of("u", (0, 1, 2), 0)),
        (-1, regs_of("x", (0,), 1) + regs_of("u", (3,), 1)),
        (2, regs_of("x", (0,), 0)),
    ):
        if dt % t_size != 0:
            halves.setdefault(dt % t_size, []).extend(entries)
    for dt, entries in halves.items():
        message = plan["t", dt] = Message()
        if dt == 1:
            message.add_full("x", 0)
        held = {item[1:4] for item in message.places}
        message.add_halves([e for e in entries if e[:3] not in held], "t")
    for dt, entries in (
        (1, [(1, "x", 0, k, 0, 0) for k in range(REGS["x"])]),
        (1, [(-1, "x", 0, k, 0, 1) for k in range(REGS["x"])]),
        (1, [(-1, "u", 2, k, 0, 1) for k in range(REGS["u"])]),
        (-1, [(1, "x", 0, k, 1, 0) for k in range(REGS["x"])]),
        (-1, [(1, "u", 3, k, 1, 0) for k in range(REGS["u"])]),
    ):
        corners.setdefault(dt % t_size, []).extend(entries)
    for dt, entries in corners.items():
        plan["c", dt] = Message()
        plan["c", dt].add_single(entries)
    return plan


class Locator:
    def __init__(self, plan, t_size, buffers):
        self.plan, self.t_size, self.buffers = plan, t_size, buffers

    def local(self, kind, n, k, t, z):
        return ("own", kind), n * REGS[kind] + k, 2 * t + z

    def find(self, kind, n, k, t_at, z_at):
        (dt, t), (dz, z) = divmod(t_at, 2), divmod(z_at, 2)
        dt %= self.t_size
        if (dt, dz) == (0, 0):
            return self.local(kind, n, k, t, z)
        name = ("z", dz) if dt == 0 else ("t", dt) if dz == 0 else ("c", dt)
        item = (dz if name[0] == "c" else 0, kind, n, k, t, z)
        return (name,) + self.plan[name].places[item]

    def load(self, name, reg):
        return self.buffers[name][pl.ds(8 * reg, 8), :]

    def assemble(self, spots):
        groups = collections.OrderedDict()
        for r, spot in enumerate(spots):
            if spot is not None:
                groups.setdefault((spot[0], spot[1], r - spot[2]), []).append(r)
        row = lax.broadcasted_iota(jnp.int32, (8, LANES), 0) % 4
        result = None
        for (name, reg, move), rows in groups.items():
            value = self.load(name, reg)
            if move != 0:
                value = pltpu.roll(value, move % 8, 0)
            if result is None:
                result = value
            else:
                mask = functools.reduce(jnp.logical_or, [row == r for r in rows])
                result = jnp.where(mask, value, result)
        return result

    def field_register(self, kind, n, k, dt, dz):
        return self.assemble([self.find(kind, n, k, t + dt, z + dz) for t, z in SITES])


def lane_shifted(value, dx, dy):
    if dx != 0:
        x_at = lax.broadcasted_iota(jnp.int32, value.shape, 1) % NX
        beyond = (x_at + dx >= NX) | (x_at + dx < 0)
        main = pltpu.roll(value, (-dx) % LANES, 1)
        wrapped = pltpu.roll(value, (NX - dx if dx > 0 else -NX - dx) % LANES, 1)
        value = jnp.where(beyond, wrapped, main)
    if dy != 0:
        value = pltpu.roll(value, (-dy * NX) % LANES, 1)
    return value


def term_fields(halves, sign):
    here, ahead, left, right = [], [], [], []
    for m, n in halves:
        start = plus(ZERO, UNIT[n], sign)
        base = ZERO if sign > 0 else start
        here.append(("x", 0, start))
        ahead.append(("x", 0, plus(start, UNIT[m])))
        left.append(("u", n, base))
        right.append(("u", n, plus(base, UNIT[m])))
    return here, ahead, left, right


def needed_fields(stage):
    keys = collections.OrderedDict()
    for _, halves in TERMS[stage]:
        for sign in (1, -1):
            for pair in term_fields(halves, sign):
                keys.update((key, None) for key in pair)
    for m in DIRECT[stage]:
        for scale in (1, 3):
            keys["x", 0, plus(ZERO, UNIT[m], scale)] = None
    return [key for key in keys if key[2] != ZERO]


def stage_of(key):
    dz, dt = key[2][2:]
    if dz != 0 and dt != 0:
        return "corner"
    return "t" if dt != 0 else "z" if dz != 0 else "own"


def lay_out(keys):
    rows, total = collections.OrderedDict(), 0
    for key in keys:
        rows[key] = total
        total += 8 * REGS[key[0]]
    return rows, total


def field_split():
    uses = collections.OrderedDict()
    for stage in STAGES:
        for key in needed_fields(stage):
            uses.setdefault(key, []).append(stage)
    shared, alone = {}, {}
    for stage in STAGES:
        built = [key for key in uses if stage_of(key) == stage]
        shared[stage] = lay_out([key for key in built if uses[key] != [stage]])
        alone[stage] = lay_out([key for key in built if uses[key] == [stage]])
    return shared, alone


def build_fields(locator, stores):
    groups = collections.OrderedDict()
    for ref, rows in stores:
        for (kind, n, disp), row in rows.items():
            shifts = groups.setdefault((kind, n, disp[3], disp[2]), collections.OrderedDict())
            shifts[disp[0], disp[1]] = (ref, row)
    for (kind, n, dt, dz), shifts in groups.items():
        for k in range(REGS[kind]):
            value = locator.field_register(kind, n, k, dt, dz)
            by_x = {0: value}
            for (dx, dy), (ref, row) in shifts.items():
                if dx not in by_x:
                    by_x[dx] = lane_shifted(value, dx, 0)
                ref[pl.ds(row + 8 * k, 8), :] = lane_shifted(by_x[dx], 0, dy)


class Fields:
    def __init__(self, own_x, own_u, stores):
        self.place = {("x", 0, ZERO): (own_x, 0)}
        for n in range(4):
            self.place["u", n, ZERO] = (own_u, 8 * REGS["u"] * n)
        for ref, rows in stores:
            for key, row in rows.items():
                self.place[key] = (ref, row)
        self.upper = lax.broadcasted_iota(jnp.int32, (8, LANES), 0) < 4

    def reg(self, key, k):
        ref, row = self.place[key]
        return ref[pl.ds(row + 8 * k, 8), :]

    def two_tiles(self, keys, k):
        top = self.reg(keys[0], k)
        turned_top = pltpu.roll(top, 4, 0)
        if keys[0] == keys[1]:
            low, turned_low = top, turned_top
        else:
            low = self.reg(keys[1], k)
            turned_low = pltpu.roll(low, 4, 0)
        return [jnp.where(self.upper, top, turned_low), jnp.where(self.upper, turned_top, low)]

    def vector(self, keys, pole):
        flat = [tile for k in range(3) for tile in self.two_tiles(keys, 3 * pole + k)]
        return [flat[:3], flat[3:]]

    def matrix(self, keys):
        flat = [tile for k in range(9) for tile in self.two_tiles(keys, k)]
        return [[flat[9 * c + 3 * i : 9 * c + 3 * i + 3] for i in range(3)] for c in range(2)]

    def compact_halves(self, first, second):
        top = jnp.where(self.upper, first, pltpu.roll(second, 4, 0))
        return top, jnp.where(self.upper, pltpu.roll(first, 4, 0), second)

    def compact_sum(self, first, second):
        kept = jnp.where(self.upper, first, second)
        return kept + pltpu.roll(jnp.where(self.upper, second, first), 4, 0)


def pole_sum(fields, here, ahead, scales):
    total = None
    for pole in range(NP):
        h = [[scales[pole] * v for v in part] for part in fields.vector(here, pole)]
        a = fields.vector(ahead, pole)
        real = [[a[0][i] * h[0][j] + a[1][i] * h[1][j] for j in range(3)] for i in range(3)]
        imag = [[a[1][i] * h[0][j] - a[0][i] * h[1][j] for j in range(3)] for i in range(3)]
        if total is None:
            total = [real, imag]
        else:
            total = [
                [[total[c][i][j] + new[i][j] for j in range(3)] for i in range(3)]
                for c, new in enumerate((real, imag))
            ]
    return total


def transposed(matrix):
    return [[[part[j][i] for j in range(3)] for i in range(3)] for part in matrix]


def row_times(row, right, row_sign, right_sign):
    result = [[], []]
    for j in range(3):
        real = imag = None
        for k in range(3):
            rr = row[0][k] * right[0][k][j]
            ii = row[1][k] * right[1][k][j]
            ri = row[0][k] * right[1][k][j]
            ir = row[1][k] * right[0][k][j]
            new_real = rr - ii if row_sign * right_sign > 0 else rr + ii
            if row_sign > 0 and right_sign > 0:
                new_imag = ri + ir
            elif row_sign > 0:
                new_imag = ir - ri
            else:
                new_imag = ri - ir
            real = new_real if real is None else real + new_real
            imag = new_imag if imag is None else imag + new_imag
        result[0].append(real)
        result[1].append(imag)
    return result


def add_terms(fields, stage, near, acc):
    started = set()
    for target, halves in TERMS[stage]:
        for sign in (1, -1):
            here, ahead, left, right = term_fields(halves, sign)
            force = pole_sum(fields, here, ahead, near)
            left = fields.matrix(left)
            right = fields.matrix(right)
            if sign > 0:
                right = transposed(right)
            else:
                left = transposed(left)
            rows = [row_times([left[0][i], left[1][i]], force, sign, 1) for i in range(3)]
            for i in range(3):
                row = row_times(rows[i], right, 1, -sign)
                for part in range(2):
                    for j in range(3):
                        at = pl.ds((target * 18 + part * 9 + i * 3 + j) * 8, 8)
                        new = row[part][j]
                        acc[at, :] = acc[at, :] + new if target in started else new
            started.add(target)


def acc_tile(acc, target, c):
    return acc[pl.ds((target * 18 + c) * 8, 8), :]


def scale_tiles(scale_ref):
    tiles = [scale_ref[pl.ds(8 * p, 8), :] for p in range(3 * NP)]
    return tiles[:NP], tiles[NP : 2 * NP], tiles[2 * NP :]


def own_force(fields, m, both):
    total = pole_sum(
        fields,
        [("x", 0, ZERO)] * 2,
        [("x", 0, UNIT[m]), ("x", 0, plus(ZERO, UNIT[m], 3))],
        both,
    )
    flat = [total[c][i][j] for c in range(2) for i in range(3) for j in range(3)]
    return [fields.compact_sum(flat[2 * k], flat[2 * k + 1]) for k in range(9)]


def write_messages(locator, plan, names, outs):
    for name, out in zip(names, outs):
        for reg, items in enumerate(plan[name].by_register()):
            spots = [item and locator.local(*item[1:]) for item in items]
            out[pl.ds(8 * reg, 8), :] = locator.assemble(spots)


def odd_in_z():
    return (lax.axis_index("gz") * lax.axis_size("gy") + lax.axis_index("gy")) % 2 == 1


def pack_z_kernel(plan, near_in, far_in, weight_in, x_in, u_in, *rest):
    within_ref, between_ref, second_ref, scale_ref, x_ref, u_ref = rest[:6]
    near_ref, far_ref, weight_ref, u_held, sems = rest[6:]
    copies = [
        pltpu.make_async_copy(source, target, sems.at[index])
        for index, (source, target) in enumerate(
            ((u_in, u_held), (x_in, x_ref), (near_in, near_ref), (far_in, far_ref), (weight_in, weight_ref))
        )
    ]
    for copy in copies:
        copy.start()
    for copy in copies:
        copy.wait()
    u_ref[...] = u_held[...].astype(F32)
    locator = Locator(plan, 1, {("own", "x"): x_ref, ("own", "u"): u_ref})
    names = [("z", 1), ("z", -1)]

    @pl.when(odd_in_z())
    def _():
        write_messages(locator, plan, names, (within_ref, between_ref))

    @pl.when(jnp.logical_not(odd_in_z()))
    def _():
        write_messages(locator, plan, names, (between_ref, within_ref))

    write_messages(locator, plan, [("z", 2)], [second_ref])
    write_scales(near_ref, far_ref, weight_ref, scale_ref)


def pack_t_kernel(plan, names, x_ref, u_ref, *outs):
    write_messages(Locator(plan, 1, {("own", "x"): x_ref, ("own", "u"): u_ref}), plan, names, outs)


def corner_kernel(plan, names, within_ref, between_ref, _, ahead_ref, behind_ref, *outs):
    def split(from_ahead, from_behind):
        ahead_ref[...] = from_ahead[pl.ds(0, ahead_ref.shape[0]), :]
        behind_ref[...] = from_behind[pl.ds(0, behind_ref.shape[0]), :]

    @pl.when(odd_in_z())
    def _():
        split(between_ref, within_ref)

    @pl.when(jnp.logical_not(odd_in_z()))
    def _():
        split(within_ref, between_ref)

    locator = Locator(plan, 1, {("z", 1): ahead_ref, ("z", -1): behind_ref})
    for name, out in zip(names, outs):
        for reg, items in enumerate(plan[name].by_register()):
            spots = [
                item and (("z", item[0]),) + plan["z", item[0]].places[(0,) + item[1:]] for item in items
            ]
            out[pl.ds(8 * reg, 8), :] = locator.assemble(spots)


def part_reg(ref, index, k):
    return ref[pl.ds((9 * index + k) * 8, 8), :]


def write_scales(near_ref, far_ref, weight_ref, scale_ref):
    upper = lax.broadcasted_iota(jnp.int32, (8, LANES), 0) < 4
    for p in range(NP):
        scale_ref[pl.ds(8 * p, 8), :] = jnp.full((8, LANES), near_ref[p], F32)
        scale_ref[pl.ds(8 * (NP + p), 8), :] = jnp.where(upper, near_ref[p], far_ref[p])
        scale_ref[pl.ds(8 * (2 * NP + p), 8), :] = jnp.full((8, LANES), weight_ref[p], F32)


def own_fields_kernel(plan, t_size, x_ref, u_ref, shared_ref, alone_ref):
    shared, alone = field_split()
    stores = [(shared_ref, shared["own"][0]), (alone_ref, alone["own"][0])]
    build_fields(Locator(plan, t_size, {("own", "x"): x_ref, ("own", "u"): u_ref}), stores)


def own_kernel(scale_ref, x_ref, u_ref, shared_ref, alone_ref, part_ref, acc):
    shared, alone = field_split()
    fields = Fields(x_ref, u_ref, [(shared_ref, shared["own"][0]), (alone_ref, alone["own"][0])])
    near, both, weight = scale_tiles(scale_ref)
    add_terms(fields, "own", near, acc)
    direct = [own_force(fields, m, both) for m in DIRECT["own"]]
    for k in range(9):
        staples = fields.compact_halves(acc_tile(acc, 0, 2 * k), acc_tile(acc, 0, 2 * k + 1))
        for m in range(2):
            part_ref[pl.ds((9 * m + k) * 8, 8), :] = direct[m][k] + weight[m] * staples[m]


def stage_setup(stage, plan, t_size, names, received, x_ref, u_ref, shared_refs, shared_ref, alone_ref):
    buffers = {("own", "x"): x_ref, ("own", "u"): u_ref}
    buffers.update(zip(names, received))
    shared, alone = field_split()
    stores = [(alone_ref, alone[stage][0])]
    if shared_ref is not None:
        stores.append((shared_ref, shared[stage][0]))
    build_fields(Locator(plan, t_size, buffers), stores)
    earlier = [(ref, shared[name][0]) for name, ref in zip(STAGES, shared_refs)]
    return Fields(x_ref, u_ref, earlier + stores)


def z_kernel(plan, t_size, names, scale_ref, x_ref, u_ref, own_shared, own_part, *rest):
    received = rest[: len(names)]
    shared_ref, part_ref, alone_ref, acc = rest[len(names) :]
    fields = stage_setup("z", plan, t_size, names, received, x_ref, u_ref, [own_shared], shared_ref, alone_ref)
    near, both, weight = scale_tiles(scale_ref)
    add_terms(fields, "z", near, acc)
    direct = own_force(fields, 2, both)
    for k in range(9):
        staples = fields.compact_halves(acc_tile(acc, 0, 2 * k), acc_tile(acc, 0, 2 * k + 1))
        for m in range(2):
            part_ref[pl.ds((9 * m + k) * 8, 8), :] = part_reg(own_part, m, k) + weight[m] * staples[m]
        staple = fields.compact_sum(acc_tile(acc, 1, 2 * k), acc_tile(acc, 1, 2 * k + 1))
        part_ref[pl.ds((18 + k) * 8, 8), :] = direct[k] + weight[2] * staple


def t_kernel(plan, t_size, names, scale_ref, x_ref, u_ref, own_shared, z_shared, z_part, *rest):
    received = rest[: len(names)]
    shared_ref, part_ref, out_ref, alone_ref, acc, ready, sem = rest[len(names) :]
    fields = stage_setup(
        "t", plan, t_size, names, received, x_ref, u_ref, [own_shared, z_shared], shared_ref, alone_ref
    )
    near, both, weight = scale_tiles(scale_ref)
    add_terms(fields, "t", near, acc)
    for k in range(9):
        staples = fields.compact_halves(acc_tile(acc, 0, 2 * k), acc_tile(acc, 0, 2 * k + 1))
        for m in range(2):
            ready[pl.ds((9 * m + k) * 8, 8), :] = part_reg(z_part, m, k) + weight[m] * staples[m]
    leaving = pltpu.make_async_copy(ready, out_ref.at[pl.ds(0, ready.shape[0])], sem)
    leaving.start()
    direct = own_force(fields, 3, both)
    for k in range(9):
        staple = fields.compact_sum(acc_tile(acc, 1, 2 * k), acc_tile(acc, 1, 2 * k + 1))
        part_ref[pl.ds(k * 8, 8), :] = direct[k] + weight[3] * staple
    leaving.wait()


def last_kernel(plan, t_size, names, scale_ref, x_ref, u_ref, *rest):
    own_shared, z_shared, t_shared, z_part, t_part, _ = rest[:6]
    received = rest[6 : 6 + len(names)]
    out_ref, alone_ref, acc, ready, sem = rest[6 + len(names) :]
    fields = stage_setup(
        "corner",
        plan,
        t_size,
        names,
        received,
        x_ref,
        u_ref,
        [own_shared, z_shared, t_shared],
        None,
        alone_ref,
    )
    near, _, weight = scale_tiles(scale_ref)
    add_terms(fields, "corner", near, acc)
    for k in range(9):
        staples = fields.compact_halves(acc_tile(acc, 0, 2 * k), acc_tile(acc, 0, 2 * k + 1))
        ready[pl.ds(k * 8, 8), :] = part_reg(z_part, 2, k) + weight[2] * staples[0]
        ready[pl.ds((9 + k) * 8, 8), :] = part_reg(t_part, 0, k) + weight[3] * staples[1]
    rows = ready.shape[0]
    leaving = pltpu.make_async_copy(ready, out_ref.at[pl.ds(rows, rows)], sem)
    leaving.start()
    leaving.wait()


def rows_of(count):
    return jax.ShapeDtypeStruct((count, LANES), F32)


def on_device(pole_vectors, gauge_links, pole_coeff, naik_coeff, staple_weight):
    t_size = lax.axis_size("ta")
    z_size = lax.axis_size("gz") * lax.axis_size("gy")
    plan = message_plan(t_size)
    x_rows, u_rows = 8 * REGS["x"], 4 * 8 * REGS["u"]
    vmem = pl.BlockSpec(memory_space=pltpu.VMEM)
    hbm = pl.BlockSpec(memory_space=pltpu.HBM)
    limit = pltpu.CompilerParams(vmem_limit_bytes=4 * 1024 * 1024)

    def moved(name, value):
        kind, step = name
        if kind == "z":
            return lax.ppermute(value, ("gz", "gy"), [((i + step) % z_size, i) for i in range(z_size)])
        return lax.ppermute(value, "ta", [((j + step) % t_size, j) for j in range(t_size)])

    def exchanged(value, first):
        pairs = [(i, (i + 1) % z_size) for i in range(first, z_size, 2)]
        return lax.ppermute(value, ("gz", "gy"), pairs + [(j, i) for i, j in pairs])

    first_names = [name for name in plan if name[0] != "c"]
    corner_names = [name for name in plan if name[0] == "c"]
    t_names = [name for name in first_names if name[0] == "t"]
    in_hbm = functools.partial(pltpu.with_memory_space_constraint, memory_space=pltpu.HBM)
    beyond_rows = 8 * max([plan["z", 2].count] + [plan[name].count for name in corner_names])
    ahead_rows, behind_rows = [8 * plan["z", step].count for step in (1, -1)]
    shared_rows = max(ahead_rows, behind_rows)
    within, between, beyond, scale, *own = pl.pallas_call(
        functools.partial(pack_z_kernel, plan),
        out_shape=[rows_of(shared_rows), rows_of(shared_rows + 8), rows_of(beyond_rows)]
        + [rows_of(8 * 3 * NP), rows_of(x_rows), rows_of(u_rows)],
        in_specs=[hbm] * 5,
        out_specs=[vmem] * 6,
        scratch_shapes=[pltpu.SMEM((NP,), F32)] * 3
        + [pltpu.VMEM((u_rows, LANES), jnp.bfloat16), pltpu.SemaphoreType.DMA((5,))],
        compiler_params=limit,
        name="pack_z",
    )(
        in_hbm(pole_coeff),
        in_hbm(naik_coeff),
        in_hbm(staple_weight),
        in_hbm(pole_vectors.reshape((x_rows, LANES))),
        in_hbm(gauge_links.reshape((u_rows, LANES))),
    )
    between, within = exchanged(between, 1), exchanged(within, 0)
    received = {("z", 2): moved(("z", 2), beyond)}
    packed = pl.pallas_call(
        functools.partial(pack_t_kernel, plan, t_names),
        out_shape=[rows_of(8 * plan[name].count) for name in t_names],
        in_specs=[vmem] * 2,
        out_specs=[vmem] * len(t_names),
        compiler_params=limit,
        name="pack_t",
    )(*own)
    received.update({name: moved(name, value) for name, value in zip(t_names, packed)})
    shared, alone = field_split()
    part_rows = 8 * REGS["u"]

    def scratch(stage):
        sums = 1 + max(target for target, _ in TERMS[stage])
        return [pltpu.VMEM((alone[stage][1], LANES), F32), pltpu.VMEM((sums * 18 * 8, LANES), F32)]

    def cost(micros):
        return pl.CostEstimate(flops=10**6, bytes_accessed=int(3.69e6 * micros), transcendentals=0)

    wide_limit = pltpu.CompilerParams(vmem_limit_bytes=6 * 1024 * 1024)
    own_shared, own_alone = pl.pallas_call(
        functools.partial(own_fields_kernel, plan, t_size),
        out_shape=[rows_of(shared["own"][1]), rows_of(alone["own"][1])],
        in_specs=[vmem] * 2,
        out_specs=[vmem] * 2,
        compiler_params=wide_limit,
        name="fields_own",
    )(*own)
    own_part = pl.pallas_call(
        own_kernel,
        out_shape=rows_of(2 * part_rows),
        in_specs=[vmem] * 5,
        out_specs=vmem,
        scratch_shapes=scratch("own")[1:],
        cost_estimate=cost(COSTS["own"]),
        compiler_params=wide_limit,
        name="force_own",
    )(scale, *own, own_shared, own_alone)
    local = [scale, *own]
    received["z", 1], received["z", -1], *corners = pl.pallas_call(
        functools.partial(corner_kernel, plan, corner_names),
        out_shape=[rows_of(ahead_rows), rows_of(behind_rows)]
        + [rows_of(8 * plan[name].count) for name in corner_names],
        in_specs=[vmem] * 3,
        out_specs=[vmem] * (2 + len(corner_names)),
        compiler_params=limit,
        name="pack_corners",
    )(within, between, own_part)
    received.update({name: moved(name, value) for name, value in zip(corner_names, corners)})
    names = [("z", 1), ("z", -1), ("z", 2)]
    z_shared, z_part = pl.pallas_call(
        functools.partial(z_kernel, plan, t_size, names),
        out_shape=[rows_of(shared["z"][1]), rows_of(3 * part_rows)],
        in_specs=[vmem] * (5 + len(names)),
        out_specs=[vmem] * 2,
        scratch_shapes=scratch("z"),
        cost_estimate=cost(COSTS["z"]),
        compiler_params=wide_limit,
        name="force_z",
    )(*local, own_shared, own_part, *[received[name] for name in names])
    t_shared, t_part, force = pl.pallas_call(
        functools.partial(t_kernel, plan, t_size, t_names),
        out_shape=[rows_of(shared["t"][1]), rows_of(part_rows), rows_of(u_rows)],
        in_specs=[vmem] * (6 + len(t_names)),
        out_specs=[vmem] * 2 + [hbm],
        scratch_shapes=scratch("t") + [pltpu.VMEM((2 * part_rows, LANES), F32), pltpu.SemaphoreType.DMA],
        cost_estimate=cost(COSTS["t"]),
        compiler_params=wide_limit,
        name="force_t",
    )(*local, own_shared, z_shared, z_part, *[received[name] for name in t_names])
    names = [name for name in received if name != ("z", 2)]
    force = pl.pallas_call(
        functools.partial(last_kernel, plan, t_size, names),
        out_shape=rows_of(u_rows),
        in_specs=[vmem] * 8 + [hbm] + [vmem] * len(names),
        out_specs=hbm,
        input_output_aliases={8: 0},
        scratch_shapes=scratch("corner")
        + [pltpu.VMEM((2 * part_rows, LANES), F32), pltpu.SemaphoreType.DMA],
        cost_estimate=cost(COSTS["corner"]),
        compiler_params=wide_limit,
        name="force_corner",
    )(
        *local,
        own_shared,
        z_shared,
        t_shared,
        z_part,
        t_part,
        force,
        *[received[name] for name in names],
    )
    return force.reshape(gauge_links.shape)


def solution(mesh):
    return jax.shard_map(
        on_device,
        mesh=mesh,
        in_specs=(
            P("ens", None, None, "ta", ("gz", "gy"), None),
            P("ens", None, None, None, "ta", ("gz", "gy"), None),
            P(),
            P(),
            P(),
        ),
        out_specs=P("ens", None, None, None, "ta", ("gz", "gy"), None),
        check_vma=False,
    )
```

```python
import collections
import functools

import jax
import jax.numpy as jnp
from jax import lax
from jax.experimental import pallas as pl
from jax.experimental.pallas import tpu as pltpu
from jax.sharding import PartitionSpec as P

NX = 8
NY = 16
LANES = NX * NY
NP = 4
F32 = jnp.float32
REGS = {"x": NP * 3, "u": 9}
UNIT = ((1, 0, 0, 0), (0, 1, 0, 0), (0, 0, 1, 0), (0, 0, 0, 1))
ZERO = (0, 0, 0, 0)
SITES = ((0, 0), (0, 1), (1, 0), (1, 1))
STAGES = ("own", "z", "t", "corner")
TERMS = {
    "own": ((0, ((0, 1), (1, 0))),),
    "z": ((0, ((0, 2), (1, 2))), (1, ((2, 0), (2, 1)))),
    "t": ((0, ((0, 3), (1, 3))), (1, ((3, 0), (3, 1)))),
    "corner": ((0, ((2, 3), (3, 2))),),
}
COSTS = {"own": 2.0, "z": 2.0, "t": 2.0, "corner": 1.0}
DIRECT = {"own": (0, 1), "z": (2,), "t": (3,), "corner": ()}


def plus(left, right, scale=1):
    return tuple(a + scale * b for a, b in zip(left, right))


class Message:
    def __init__(self):
        self.places = collections.OrderedDict()
        self.count = 0

    def add_full(self, kind, n):
        for k in range(REGS[kind]):
            for t, z in SITES:
                self.places[0, kind, n, k, t, z] = (self.count, 2 * t + z)
            self.count += 1

    def add_halves(self, entries, axis):
        half = -(-len(entries) // 2)
        for index, (kind, n, k, layer) in enumerate(entries):
            reg, part = self.count + index % half, index // half
            for other in range(2):
                t, z = (layer, other) if axis == "t" else (other, layer)
                slot = 2 * part + other if axis == "t" else 2 * other + part
                self.places[0, kind, n, k, t, z] = (reg, slot)
        self.count += half

    def add_single(self, entries):
        quarter = -(-len(entries) // 4)
        for index, entry in enumerate(entries):
            self.places[entry] = (self.count + index % quarter, index // quarter)
        self.count += quarter

    def by_register(self):
        found = [[None] * 4 for _ in range(self.count)]
        for item, (reg, slot) in self.places.items():
            found[reg][slot] = item
        return found


def regs_of(kind, directions, layer):
    return [(kind, n, k, layer) for n in directions for k in range(REGS[kind])]


def message_plan(t_size):
    plan = collections.OrderedDict()
    ahead = plan["z", 1] = Message()
    ahead.add_full("x", 0)
    ahead.add_halves(regs_of("u", (0, 1, 3), 0), "z")
    behind = plan["z", -1] = Message()
    behind.add_halves(regs_of("x", (0,), 1) + regs_of("u", (2,), 1), "z")
    second = plan["z", 2] = Message()
    second.add_halves(regs_of("x", (0,), 0), "z")
    halves, corners = collections.OrderedDict(), collections.OrderedDict()
    for dt, entries in (
        (1, regs_of("u", (0, 1, 2), 0)),
        (-1, regs_of("x", (0,), 1) + regs_of("u", (3,), 1)),
        (2, regs_of("x", (0,), 0)),
    ):
        if dt % t_size != 0:
            halves.setdefault(dt % t_size, []).extend(entries)
    for dt, entries in halves.items():
        message = plan["t", dt] = Message()
        if dt == 1:
            message.add_full("x", 0)
        held = {item[1:4] for item in message.places}
        message.add_halves([e for e in entries if e[:3] not in held], "t")
    for dt, entries in (
        (1, [(1, "x", 0, k, 0, 0) for k in range(REGS["x"])]),
        (1, [(-1, "x", 0, k, 0, 1) for k in range(REGS["x"])]),
        (1, [(-1, "u", 2, k, 0, 1) for k in range(REGS["u"])]),
        (-1, [(1, "x", 0, k, 1, 0) for k in range(REGS["x"])]),
        (-1, [(1, "u", 3, k, 1, 0) for k in range(REGS["u"])]),
    ):
        corners.setdefault(dt % t_size, []).extend(entries)
    for dt, entries in corners.items():
        plan["c", dt] = Message()
        plan["c", dt].add_single(entries)
    return plan


class Locator:
    def __init__(self, plan, t_size, buffers):
        self.plan, self.t_size, self.buffers = plan, t_size, buffers

    def local(self, kind, n, k, t, z):
        return ("own", kind), n * REGS[kind] + k, 2 * t + z

    def find(self, kind, n, k, t_at, z_at):
        (dt, t), (dz, z) = divmod(t_at, 2), divmod(z_at, 2)
        dt %= self.t_size
        if (dt, dz) == (0, 0):
            return self.local(kind, n, k, t, z)
        name = ("z", dz) if dt == 0 else ("t", dt) if dz == 0 else ("c", dt)
        item = (dz if name[0] == "c" else 0, kind, n, k, t, z)
        return (name,) + self.plan[name].places[item]

    def load(self, name, reg):
        return self.buffers[name][pl.ds(8 * reg, 8), :]

    def assemble(self, spots):
        groups = collections.OrderedDict()
        for r, spot in enumerate(spots):
            if spot is not None:
                groups.setdefault((spot[0], spot[1], r - spot[2]), []).append(r)
        row = lax.broadcasted_iota(jnp.int32, (8, LANES), 0) % 4
        result = None
        for (name, reg, move), rows in groups.items():
            value = self.load(name, reg)
            if move != 0:
                value = pltpu.roll(value, move % 8, 0)
            if result is None:
                result = value
            else:
                mask = functools.reduce(jnp.logical_or, [row == r for r in rows])
                result = jnp.where(mask, value, result)
        return result

    def field_register(self, kind, n, k, dt, dz):
        return self.assemble([self.find(kind, n, k, t + dt, z + dz) for t, z in SITES])


def term_fields(halves, sign):
    here, ahead, left, right = [], [], [], []
    for m, n in halves:
        start = plus(ZERO, UNIT[n], sign)
        base = ZERO if sign > 0 else start
        here.append(("x", 0, start))
        ahead.append(("x", 0, plus(start, UNIT[m])))
        left.append(("u", n, base))
        right.append(("u", n, plus(base, UNIT[m])))
    return here, ahead, left, right


def needed_fields(stage):
    keys = collections.OrderedDict()
    for _, halves in TERMS[stage]:
        for sign in (1, -1):
            for pair in term_fields(halves, sign):
                keys.update((key, None) for key in pair)
    for m in DIRECT[stage]:
        for scale in (1, 3):
            keys["x", 0, plus(ZERO, UNIT[m], scale)] = None
    return [key for key in keys if key[2] != ZERO]


def stage_of(key):
    dz, dt = key[2][2:]
    if dz != 0 and dt != 0:
        return "corner"
    return "t" if dt != 0 else "z" if dz != 0 else "own"


def lay_out(keys):
    rows, total = collections.OrderedDict(), 0
    for key in keys:
        rows[key] = total
        total += 8 * REGS[key[0]]
    return rows, total


def field_split():
    uses = collections.OrderedDict()
    for stage in STAGES:
        for key in needed_fields(stage):
            uses.setdefault(key, []).append(stage)
    shared, alone = {}, {}
    for stage in STAGES:
        built = [key for key in uses if stage_of(key) == stage]
        shared[stage] = lay_out([key for key in built if uses[key] != [stage]])
        alone[stage] = lay_out([key for key in built if uses[key] == [stage]])
    return shared, alone


def all_shifts():
    found = collections.OrderedDict()
    for stage in STAGES:
        for _, _, (dx, dy, _, _) in needed_fields(stage):
            if (dx, dy) != (0, 0):
                found[dx, dy] = None
    return list(found)


def write_shifts(perm_ref):
    lane = lax.broadcasted_iota(jnp.int32, (LANES, LANES), 1)
    source = lax.broadcasted_iota(jnp.int32, (LANES, LANES), 0)
    for index, (dx, dy) in enumerate(all_shifts()):
        wanted = (lane // NX + dy + NY) % NY * NX + (lane + dx + NX) % NX
        perm_ref[pl.ds(index * LANES, LANES), :] = (source == wanted).astype(F32).astype(jnp.bfloat16)


def parts_of(kind, value):
    if kind == "u":
        return [value.astype(jnp.bfloat16)]
    high = value.astype(jnp.bfloat16)
    rest = value - high.astype(F32)
    middle = rest.astype(jnp.bfloat16)
    return [high, middle, (rest - middle.astype(F32)).astype(jnp.bfloat16)]


def build_fields(locator, perm_ref, stores):
    groups = collections.OrderedDict()
    for ref, rows in stores:
        for (kind, n, disp), row in rows.items():
            shifts = groups.setdefault((kind, n, disp[3], disp[2]), collections.OrderedDict())
            shifts[disp[0], disp[1]] = (ref, row)
    order = all_shifts()
    for (kind, n, dt, dz), shifts in groups.items():
        regs = [locator.field_register(kind, n, k, dt, dz) for k in range(REGS[kind])]
        if (0, 0) in shifts:
            ref, row = shifts[0, 0]
            for k, value in enumerate(regs):
                ref[pl.ds(row + 8 * k, 8), :] = value
        parts = parts_of(kind, jnp.concatenate(regs, axis=0))
        for shift, (ref, row) in shifts.items():
            if shift != (0, 0):
                perm = perm_ref[pl.ds(order.index(shift) * LANES, LANES), :]
                moved = [jnp.dot(part, perm, preferred_element_type=F32) for part in parts]
                ref[pl.ds(row, 8 * REGS[kind]), :] = functools.reduce(jnp.add, moved)


class Fields:
    def __init__(self, own_x, own_u, stores):
        self.place = {("x", 0, ZERO): (own_x, 0)}
        for n in range(4):
            self.place["u", n, ZERO] = (own_u, 8 * REGS["u"] * n)
        for ref, rows in stores:
            for key, row in rows.items():
                self.place[key] = (ref, row)
        self.upper = lax.broadcasted_iota(jnp.int32, (8, LANES), 0) < 4

    def reg(self, key, k):
        ref, row = self.place[key]
        return ref[pl.ds(row + 8 * k, 8), :]

    def two_tiles(self, keys, k):
        top = self.reg(keys[0], k)
        turned_top = pltpu.roll(top, 4, 0)
        if keys[0] == keys[1]:
            low, turned_low = top, turned_top
        else:
            low = self.reg(keys[1], k)
            turned_low = pltpu.roll(low, 4, 0)
        return [jnp.where(self.upper, top, turned_low), jnp.where(self.upper, turned_top, low)]

    def vector(self, keys, pole):
        flat = [tile for k in range(3) for tile in self.two_tiles(keys, 3 * pole + k)]
        return [flat[:3], flat[3:]]

    def matrix(self, keys):
        flat = [tile for k in range(9) for tile in self.two_tiles(keys, k)]
        return [[flat[9 * c + 3 * i : 9 * c + 3 * i + 3] for i in range(3)] for c in range(2)]

    def compact_halves(self, first, second):
        top = jnp.where(self.upper, first, pltpu.roll(second, 4, 0))
        return top, jnp.where(self.upper, pltpu.roll(first, 4, 0), second)

    def compact_sum(self, first, second):
        kept = jnp.where(self.upper, first, second)
        return kept + pltpu.roll(jnp.where(self.upper, second, first), 4, 0)


def pole_sum(fields, here, ahead, scales):
    total = None
    for pole in range(NP):
        h = [[scales[pole] * v for v in part] for part in fields.vector(here, pole)]
        a = fields.vector(ahead, pole)
        real = [[a[0][i] * h[0][j] + a[1][i] * h[1][j] for j in range(3)] for i in range(3)]
        imag = [[a[1][i] * h[0][j] - a[0][i] * h[1][j] for j in range(3)] for i in range(3)]
        if total is None:
            total = [real, imag]
        else:
            total = [
                [[total[c][i][j] + new[i][j] for j in range(3)] for i in range(3)]
                for c, new in enumerate((real, imag))
            ]
    return total


def transposed(matrix):
    return [[[part[j][i] for j in range(3)] for i in range(3)] for part in matrix]


def row_times(row, right, row_sign, right_sign):
    result = [[], []]
    for j in range(3):
        real = imag = None
        for k in range(3):
            rr = row[0][k] * right[0][k][j]
            ii = row[1][k] * right[1][k][j]
            ri = row[0][k] * right[1][k][j]
            ir = row[1][k] * right[0][k][j]
            new_real = rr - ii if row_sign * right_sign > 0 else rr + ii
            if row_sign > 0 and right_sign > 0:
                new_imag = ri + ir
            elif row_sign > 0:
                new_imag = ir - ri
            else:
                new_imag = ri - ir
            real = new_real if real is None else real + new_real
            imag = new_imag if imag is None else imag + new_imag
        result[0].append(real)
        result[1].append(imag)
    return result


def add_terms(fields, stage, near, acc):
    started = set()
    for target, halves in TERMS[stage]:
        for sign in (1, -1):
            here, ahead, left, right = term_fields(halves, sign)
            force = pole_sum(fields, here, ahead, near)
            left = fields.matrix(left)
            right = fields.matrix(right)
            if sign > 0:
                right = transposed(right)
            else:
                left = transposed(left)
            rows = [row_times([left[0][i], left[1][i]], force, sign, 1) for i in range(3)]
            for i in range(3):
                row = row_times(rows[i], right, 1, -sign)
                for part in range(2):
                    for j in range(3):
                        at = pl.ds((target * 18 + part * 9 + i * 3 + j) * 8, 8)
                        new = row[part][j]
                        acc[at, :] = acc[at, :] + new if target in started else new
            started.add(target)


def acc_tile(acc, target, c):
    return acc[pl.ds((target * 18 + c) * 8, 8), :]


def scale_tiles(scale_ref):
    tiles = [scale_ref[pl.ds(8 * p, 8), :] for p in range(3 * NP)]
    return tiles[:NP], tiles[NP : 2 * NP], tiles[2 * NP :]


def own_force(fields, m, both):
    total = pole_sum(
        fields,
        [("x", 0, ZERO)] * 2,
        [("x", 0, UNIT[m]), ("x", 0, plus(ZERO, UNIT[m], 3))],
        both,
    )
    flat = [total[c][i][j] for c in range(2) for i in range(3) for j in range(3)]
    return [fields.compact_sum(flat[2 * k], flat[2 * k + 1]) for k in range(9)]


def write_messages(locator, plan, names, outs):
    for name, out in zip(names, outs):
        for reg, items in enumerate(plan[name].by_register()):
            spots = [item and locator.local(*item[1:]) for item in items]
            out[pl.ds(8 * reg, 8), :] = locator.assemble(spots)


def odd_in_z():
    return (lax.axis_index("gz") * lax.axis_size("gy") + lax.axis_index("gy")) % 2 == 1


def pack_z_kernel(plan, near_in, far_in, weight_in, x_in, u_in, *rest):
    within_ref, between_ref, second_ref, scale_ref, perm_ref, x_ref, u_ref = rest[:7]
    near_ref, far_ref, weight_ref, u_held, sems = rest[7:]
    copies = [
        pltpu.make_async_copy(source, target, sems.at[index])
        for index, (source, target) in enumerate(
            ((u_in, u_held), (x_in, x_ref), (near_in, near_ref), (far_in, far_ref), (weight_in, weight_ref))
        )
    ]
    for copy in copies:
        copy.start()
    write_shifts(perm_ref)
    for copy in copies:
        copy.wait()
    u_ref[...] = u_held[...].astype(F32)
    locator = Locator(plan, 1, {("own", "x"): x_ref, ("own", "u"): u_ref})
    names = [("z", 1), ("z", -1)]

    @pl.when(odd_in_z())
    def _():
        write_messages(locator, plan, names, (within_ref, between_ref))

    @pl.when(jnp.logical_not(odd_in_z()))
    def _():
        write_messages(locator, plan, names, (between_ref, within_ref))

    write_messages(locator, plan, [("z", 2)], [second_ref])
    write_scales(near_ref, far_ref, weight_ref, scale_ref)


def pack_t_kernel(plan, names, x_ref, u_ref, *outs):
    write_messages(Locator(plan, 1, {("own", "x"): x_ref, ("own", "u"): u_ref}), plan, names, outs)


def corner_kernel(plan, names, within_ref, between_ref, _, ahead_ref, behind_ref, *outs):
    def split(from_ahead, from_behind):
        ahead_ref[...] = from_ahead[pl.ds(0, ahead_ref.shape[0]), :]
        behind_ref[...] = from_behind[pl.ds(0, behind_ref.shape[0]), :]

    @pl.when(odd_in_z())
    def _():
        split(between_ref, within_ref)

    @pl.when(jnp.logical_not(odd_in_z()))
    def _():
        split(within_ref, between_ref)

    locator = Locator(plan, 1, {("z", 1): ahead_ref, ("z", -1): behind_ref})
    for name, out in zip(names, outs):
        for reg, items in enumerate(plan[name].by_register()):
            spots = [
                item and (("z", item[0]),) + plan["z", item[0]].places[(0,) + item[1:]] for item in items
            ]
            out[pl.ds(8 * reg, 8), :] = locator.assemble(spots)


def part_reg(ref, index, k):
    return ref[pl.ds((9 * index + k) * 8, 8), :]


def write_scales(near_ref, far_ref, weight_ref, scale_ref):
    upper = lax.broadcasted_iota(jnp.int32, (8, LANES), 0) < 4
    for p in range(NP):
        scale_ref[pl.ds(8 * p, 8), :] = jnp.full((8, LANES), near_ref[p], F32)
        scale_ref[pl.ds(8 * (NP + p), 8), :] = jnp.where(upper, near_ref[p], far_ref[p])
        scale_ref[pl.ds(8 * (2 * NP + p), 8), :] = jnp.full((8, LANES), weight_ref[p], F32)


def own_fields_kernel(plan, t_size, perm_ref, x_ref, u_ref, shared_ref, alone_ref):
    shared, alone = field_split()
    stores = [(shared_ref, shared["own"][0]), (alone_ref, alone["own"][0])]
    build_fields(Locator(plan, t_size, {("own", "x"): x_ref, ("own", "u"): u_ref}), perm_ref, stores)


def own_kernel(scale_ref, x_ref, u_ref, shared_ref, alone_ref, part_ref, acc):
    shared, alone = field_split()
    fields = Fields(x_ref, u_ref, [(shared_ref, shared["own"][0]), (alone_ref, alone["own"][0])])
    near, both, weight = scale_tiles(scale_ref)
    add_terms(fields, "own", near, acc)
    direct = [own_force(fields, m, both) for m in DIRECT["own"]]
    for k in range(9):
        staples = fields.compact_halves(acc_tile(acc, 0, 2 * k), acc_tile(acc, 0, 2 * k + 1))
        for m in range(2):
            part_ref[pl.ds((9 * m + k) * 8, 8), :] = direct[m][k] + weight[m] * staples[m]


def stage_setup(stage, plan, t_size, names, received, perm_ref, x_ref, u_ref, shared_refs, shared_ref, alone_ref):
    buffers = {("own", "x"): x_ref, ("own", "u"): u_ref}
    buffers.update(zip(names, received))
    shared, alone = field_split()
    stores = [(alone_ref, alone[stage][0])]
    if shared_ref is not None:
        stores.append((shared_ref, shared[stage][0]))
    build_fields(Locator(plan, t_size, buffers), perm_ref, stores)
    earlier = [(ref, shared[name][0]) for name, ref in zip(STAGES, shared_refs)]
    return Fields(x_ref, u_ref, earlier + stores)


def z_kernel(plan, t_size, names, scale_ref, perm_ref, x_ref, u_ref, own_shared, own_part, *rest):
    received = rest[: len(names)]
    shared_ref, part_ref, alone_ref, acc = rest[len(names) :]
    fields = stage_setup(
        "z", plan, t_size, names, received, perm_ref, x_ref, u_ref, [own_shared], shared_ref, alone_ref
    )
    near, both, weight = scale_tiles(scale_ref)
    add_terms(fields, "z", near, acc)
    direct = own_force(fields, 2, both)
    for k in range(9):
        staples = fields.compact_halves(acc_tile(acc, 0, 2 * k), acc_tile(acc, 0, 2 * k + 1))
        for m in range(2):
            part_ref[pl.ds((9 * m + k) * 8, 8), :] = part_reg(own_part, m, k) + weight[m] * staples[m]
        staple = fields.compact_sum(acc_tile(acc, 1, 2 * k), acc_tile(acc, 1, 2 * k + 1))
        part_ref[pl.ds((18 + k) * 8, 8), :] = direct[k] + weight[2] * staple


def t_kernel(plan, t_size, names, scale_ref, perm_ref, x_ref, u_ref, own_shared, z_shared, z_part, *rest):
    received = rest[: len(names)]
    shared_ref, part_ref, out_ref, alone_ref, acc, ready, sem = rest[len(names) :]
    fields = stage_setup(
        "t", plan, t_size, names, received, perm_ref, x_ref, u_ref, [own_shared, z_shared], shared_ref, alone_ref
    )
    near, both, weight = scale_tiles(scale_ref)
    add_terms(fields, "t", near, acc)
    for k in range(9):
        staples = fields.compact_halves(acc_tile(acc, 0, 2 * k), acc_tile(acc, 0, 2 * k + 1))
        for m in range(2):
            ready[pl.ds((9 * m + k) * 8, 8), :] = part_reg(z_part, m, k) + weight[m] * staples[m]
    leaving = pltpu.make_async_copy(ready, out_ref.at[pl.ds(0, ready.shape[0])], sem)
    leaving.start()
    direct = own_force(fields, 3, both)
    for k in range(9):
        staple = fields.compact_sum(acc_tile(acc, 1, 2 * k), acc_tile(acc, 1, 2 * k + 1))
        part_ref[pl.ds(k * 8, 8), :] = direct[k] + weight[3] * staple
    leaving.wait()


def last_kernel(plan, t_size, names, scale_ref, perm_ref, x_ref, u_ref, *rest):
    own_shared, z_shared, t_shared, z_part, t_part, _ = rest[:6]
    received = rest[6 : 6 + len(names)]
    out_ref, alone_ref, acc, ready, sem = rest[6 + len(names) :]
    fields = stage_setup(
        "corner",
        plan,
        t_size,
        names,
        received,
        perm_ref,
        x_ref,
        u_ref,
        [own_shared, z_shared, t_shared],
        None,
        alone_ref,
    )
    near, _, weight = scale_tiles(scale_ref)
    add_terms(fields, "corner", near, acc)
    for k in range(9):
        staples = fields.compact_halves(acc_tile(acc, 0, 2 * k), acc_tile(acc, 0, 2 * k + 1))
        ready[pl.ds(k * 8, 8), :] = part_reg(z_part, 2, k) + weight[2] * staples[0]
        ready[pl.ds((9 + k) * 8, 8), :] = part_reg(t_part, 0, k) + weight[3] * staples[1]
    rows = ready.shape[0]
    leaving = pltpu.make_async_copy(ready, out_ref.at[pl.ds(rows, rows)], sem)
    leaving.start()
    leaving.wait()


def rows_of(count):
    return jax.ShapeDtypeStruct((count, LANES), F32)


def on_device(pole_vectors, gauge_links, pole_coeff, naik_coeff, staple_weight):
    t_size = lax.axis_size("ta")
    z_size = lax.axis_size("gz") * lax.axis_size("gy")
    plan = message_plan(t_size)
    x_rows, u_rows = 8 * REGS["x"], 4 * 8 * REGS["u"]
    vmem = pl.BlockSpec(memory_space=pltpu.VMEM)
    hbm = pl.BlockSpec(memory_space=pltpu.HBM)
    limit = pltpu.CompilerParams(vmem_limit_bytes=4 * 1024 * 1024)

    def moved(name, value):
        kind, step = name
        if kind == "z":
            return lax.ppermute(value, ("gz", "gy"), [((i + step) % z_size, i) for i in range(z_size)])
        return lax.ppermute(value, "ta", [((j + step) % t_size, j) for j in range(t_size)])

    def exchanged(value, first):
        pairs = [(i, (i + 1) % z_size) for i in range(first, z_size, 2)]
        return lax.ppermute(value, ("gz", "gy"), pairs + [(j, i) for i, j in pairs])

    first_names = [name for name in plan if name[0] != "c"]
    corner_names = [name for name in plan if name[0] == "c"]
    t_names = [name for name in first_names if name[0] == "t"]
    in_hbm = functools.partial(pltpu.with_memory_space_constraint, memory_space=pltpu.HBM)
    beyond_rows = 8 * max([plan["z", 2].count] + [plan[name].count for name in corner_names])
    ahead_rows, behind_rows = [8 * plan["z", step].count for step in (1, -1)]
    shared_rows = max(ahead_rows, behind_rows)
    within, between, beyond, scale, perm, *own = pl.pallas_call(
        functools.partial(pack_z_kernel, plan),
        out_shape=[rows_of(shared_rows), rows_of(shared_rows + 8), rows_of(beyond_rows)]
        + [
            rows_of(8 * 3 * NP),
            jax.ShapeDtypeStruct((len(all_shifts()) * LANES, LANES), jnp.bfloat16),
            rows_of(x_rows),
            rows_of(u_rows),
        ],
        in_specs=[hbm] * 5,
        out_specs=[vmem] * 7,
        scratch_shapes=[pltpu.SMEM((NP,), F32)] * 3
        + [pltpu.VMEM((u_rows, LANES), jnp.bfloat16), pltpu.SemaphoreType.DMA((5,))],
        compiler_params=limit,
        name="pack_z",
    )(
        in_hbm(pole_coeff),
        in_hbm(naik_coeff),
        in_hbm(staple_weight),
        in_hbm(pole_vectors.reshape((x_rows, LANES))),
        in_hbm(gauge_links.reshape((u_rows, LANES))),
    )
    between, within = exchanged(between, 1), exchanged(within, 0)
    received = {("z", 2): moved(("z", 2), beyond)}
    packed = pl.pallas_call(
        functools.partial(pack_t_kernel, plan, t_names),
        out_shape=[rows_of(8 * plan[name].count) for name in t_names],
        in_specs=[vmem] * 2,
        out_specs=[vmem] * len(t_names),
        compiler_params=limit,
        name="pack_t",
    )(*own)
    received.update({name: moved(name, value) for name, value in zip(t_names, packed)})
    shared, alone = field_split()
    part_rows = 8 * REGS["u"]

    def scratch(stage):
        sums = 1 + max(target for target, _ in TERMS[stage])
        return [pltpu.VMEM((alone[stage][1], LANES), F32), pltpu.VMEM((sums * 18 * 8, LANES), F32)]

    def cost(micros):
        return pl.CostEstimate(flops=10**6, bytes_accessed=int(3.69e6 * micros), transcendentals=0)

    wide_limit = pltpu.CompilerParams(vmem_limit_bytes=6 * 1024 * 1024)
    own_shared, own_alone = pl.pallas_call(
        functools.partial(own_fields_kernel, plan, t_size),
        out_shape=[rows_of(shared["own"][1]), rows_of(alone["own"][1])],
        in_specs=[vmem] * 3,
        out_specs=[vmem] * 2,
        compiler_params=wide_limit,
        name="fields_own",
    )(perm, *own)
    own_part = pl.pallas_call(
        own_kernel,
        out_shape=rows_of(2 * part_rows),
        in_specs=[vmem] * 5,
        out_specs=vmem,
        scratch_shapes=scratch("own")[1:],
        cost_estimate=cost(COSTS["own"]),
        compiler_params=wide_limit,
        name="force_own",
    )(scale, *own, own_shared, own_alone)
    local = [scale, perm, *own]
    received["z", 1], received["z", -1], *corners = pl.pallas_call(
        functools.partial(corner_kernel, plan, corner_names),
        out_shape=[rows_of(ahead_rows), rows_of(behind_rows)]
        + [rows_of(8 * plan[name].count) for name in corner_names],
        in_specs=[vmem] * 3,
        out_specs=[vmem] * (2 + len(corner_names)),
        compiler_params=limit,
        name="pack_corners",
    )(within, between, own_part)
    received.update({name: moved(name, value) for name, value in zip(corner_names, corners)})
    names = [("z", 1), ("z", -1), ("z", 2)]
    z_shared, z_part = pl.pallas_call(
        functools.partial(z_kernel, plan, t_size, names),
        out_shape=[rows_of(shared["z"][1]), rows_of(3 * part_rows)],
        in_specs=[vmem] * (6 + len(names)),
        out_specs=[vmem] * 2,
        scratch_shapes=scratch("z"),
        cost_estimate=cost(COSTS["z"]),
        compiler_params=wide_limit,
        name="force_z",
    )(*local, own_shared, own_part, *[received[name] for name in names])
    t_shared, t_part, force = pl.pallas_call(
        functools.partial(t_kernel, plan, t_size, t_names),
        out_shape=[rows_of(shared["t"][1]), rows_of(part_rows), rows_of(u_rows)],
        in_specs=[vmem] * (7 + len(t_names)),
        out_specs=[vmem] * 2 + [hbm],
        scratch_shapes=scratch("t") + [pltpu.VMEM((2 * part_rows, LANES), F32), pltpu.SemaphoreType.DMA],
        cost_estimate=cost(COSTS["t"]),
        compiler_params=wide_limit,
        name="force_t",
    )(*local, own_shared, z_shared, z_part, *[received[name] for name in t_names])
    names = [name for name in received if name != ("z", 2)]
    force = pl.pallas_call(
        functools.partial(last_kernel, plan, t_size, names),
        out_shape=rows_of(u_rows),
        in_specs=[vmem] * 9 + [hbm] + [vmem] * len(names),
        out_specs=hbm,
        input_output_aliases={9: 0},
        scratch_shapes=scratch("corner")
        + [pltpu.VMEM((2 * part_rows, LANES), F32), pltpu.SemaphoreType.DMA],
        cost_estimate=cost(COSTS["corner"]),
        compiler_params=wide_limit,
        name="force_corner",
    )(
        *local,
        own_shared,
        z_shared,
        t_shared,
        z_part,
        t_part,
        force,
        *[received[name] for name in names],
    )
    return force.reshape(gauge_links.shape)


def solution(mesh):
    return jax.shard_map(
        on_device,
        mesh=mesh,
        in_specs=(
            P("ens", None, None, "ta", ("gz", "gy"), None),
            P("ens", None, None, None, "ta", ("gz", "gy"), None),
            P(),
            P(),
            P(),
        ),
        out_specs=P("ens", None, None, None, "ta", ("gz", "gy"), None),
        check_vma=False,
    )
```

```python
import collections
import functools

import jax
import jax.numpy as jnp
from jax import lax
from jax.experimental import pallas as pl
from jax.experimental.pallas import tpu as pltpu
from jax.sharding import PartitionSpec as P

NX = 8
NY = 16
LANES = NX * NY
NP = 4
F32 = jnp.float32
REGS = {"x": NP * 3, "u": 9}
UNIT = ((1, 0, 0, 0), (0, 1, 0, 0), (0, 0, 1, 0), (0, 0, 0, 1))
ZERO = (0, 0, 0, 0)
SITES = ((0, 0), (0, 1), (1, 0), (1, 1))
STAGES = ("own", "z", "t", "corner")
TERMS = {
    "own": ((0, ((0, 1), (1, 0))),),
    "z": ((0, ((0, 2), (1, 2))), (1, ((2, 0), (2, 1)))),
    "t": ((0, ((0, 3), (1, 3))), (1, ((3, 0), (3, 1)))),
    "corner": ((0, ((2, 3), (3, 2))),),
}
COSTS = {"own": 2.0, "z": 2.0, "t": 2.0, "corner": 1.0}
DIRECT = {"own": (0, 1), "z": (), "t": (3,), "corner": (2,)}


def plus(left, right, scale=1):
    return tuple(a + scale * b for a, b in zip(left, right))


class Message:
    def __init__(self):
        self.places = collections.OrderedDict()
        self.count = 0

    def add_full(self, kind, n):
        for k in range(REGS[kind]):
            for t, z in SITES:
                self.places[0, kind, n, k, t, z] = (self.count, 2 * t + z)
            self.count += 1

    def add_halves(self, entries, axis):
        half = -(-len(entries) // 2)
        for index, (kind, n, k, layer) in enumerate(entries):
            reg, part = self.count + index % half, index // half
            for other in range(2):
                t, z = (layer, other) if axis == "t" else (other, layer)
                slot = 2 * part + other if axis == "t" else 2 * other + part
                self.places[0, kind, n, k, t, z] = (reg, slot)
        self.count += half

    def add_single(self, entries):
        quarter = -(-len(entries) // 4)
        for index, entry in enumerate(entries):
            self.places[entry] = (self.count + index % quarter, index // quarter)
        self.count += quarter

    def by_register(self):
        found = [[None] * 4 for _ in range(self.count)]
        for item, (reg, slot) in self.places.items():
            found[reg][slot] = item
        return found


def regs_of(kind, directions, layer):
    return [(kind, n, k, layer) for n in directions for k in range(REGS[kind])]


def message_plan(t_size):
    plan = collections.OrderedDict()
    ahead = plan["z", 1] = Message()
    ahead.add_full("x", 0)
    ahead.add_halves(regs_of("u", (0, 1, 3), 0), "z")
    behind = plan["z", -1] = Message()
    behind.add_halves(regs_of("x", (0,), 1) + regs_of("u", (2,), 1), "z")
    second = plan["z", 2] = Message()
    second.add_halves(regs_of("x", (0,), 0), "z")
    halves, corners = collections.OrderedDict(), collections.OrderedDict()
    for dt, entries in (
        (1, regs_of("u", (0, 1, 2), 0)),
        (-1, regs_of("x", (0,), 1) + regs_of("u", (3,), 1)),
        (2, regs_of("x", (0,), 0)),
    ):
        if dt % t_size != 0:
            halves.setdefault(dt % t_size, []).extend(entries)
    for dt, entries in halves.items():
        message = plan["t", dt] = Message()
        if dt == 1:
            message.add_full("x", 0)
        held = {item[1:4] for item in message.places}
        message.add_halves([e for e in entries if e[:3] not in held], "t")
    for dt, entries in (
        (1, [(1, "x", 0, k, 0, 0) for k in range(REGS["x"])]),
        (1, [(-1, "x", 0, k, 0, 1) for k in range(REGS["x"])]),
        (1, [(-1, "u", 2, k, 0, 1) for k in range(REGS["u"])]),
        (-1, [(1, "x", 0, k, 1, 0) for k in range(REGS["x"])]),
        (-1, [(1, "u", 3, k, 1, 0) for k in range(REGS["u"])]),
    ):
        corners.setdefault(dt % t_size, []).extend(entries)
    for dt, entries in corners.items():
        plan["c", dt] = Message()
        plan["c", dt].add_single(entries)
    return plan


class Locator:
    def __init__(self, plan, t_size, buffers):
        self.plan, self.t_size, self.buffers = plan, t_size, buffers

    def local(self, kind, n, k, t, z):
        return ("own", kind), n * REGS[kind] + k, 2 * t + z

    def find(self, kind, n, k, t_at, z_at):
        (dt, t), (dz, z) = divmod(t_at, 2), divmod(z_at, 2)
        dt %= self.t_size
        if (dt, dz) == (0, 0):
            return self.local(kind, n, k, t, z)
        name = ("z", dz) if dt == 0 else ("t", dt) if dz == 0 else ("c", dt)
        item = (dz if name[0] == "c" else 0, kind, n, k, t, z)
        return (name,) + self.plan[name].places[item]

    def load(self, name, reg):
        return self.buffers[name][pl.ds(8 * reg, 8), :]

    def assemble(self, spots):
        groups = collections.OrderedDict()
        for r, spot in enumerate(spots):
            if spot is not None:
                groups.setdefault((spot[0], spot[1], r - spot[2]), []).append(r)
        row = lax.broadcasted_iota(jnp.int32, (8, LANES), 0) % 4
        result = None
        for (name, reg, move), rows in groups.items():
            value = self.load(name, reg)
            if move != 0:
                value = pltpu.roll(value, move % 8, 0)
            if result is None:
                result = value
            else:
                mask = functools.reduce(jnp.logical_or, [row == r for r in rows])
                result = jnp.where(mask, value, result)
        return result

    def field_register(self, kind, n, k, dt, dz):
        return self.assemble([self.find(kind, n, k, t + dt, z + dz) for t, z in SITES])


def term_fields(halves, sign):
    here, ahead, left, right = [], [], [], []
    for m, n in halves:
        start = plus(ZERO, UNIT[n], sign)
        base = ZERO if sign > 0 else start
        here.append(("x", 0, start))
        ahead.append(("x", 0, plus(start, UNIT[m])))
        left.append(("u", n, base))
        right.append(("u", n, plus(base, UNIT[m])))
    return here, ahead, left, right


def needed_fields(stage):
    keys = collections.OrderedDict()
    for _, halves in TERMS[stage]:
        for sign in (1, -1):
            for pair in term_fields(halves, sign):
                keys.update((key, None) for key in pair)
    for m in DIRECT[stage]:
        for scale in (1, 3):
            keys["x", 0, plus(ZERO, UNIT[m], scale)] = None
    return [key for key in keys if key[2] != ZERO]


def stage_of(key):
    dz, dt = key[2][2:]
    if abs(dz) == 3 or (dz != 0 and dt != 0):
        return "corner"
    return "t" if dt != 0 else "z" if dz != 0 else "own"


def lay_out(keys):
    rows, total = collections.OrderedDict(), 0
    for key in keys:
        rows[key] = total
        total += 8 * REGS[key[0]]
    return rows, total


def field_split():
    uses = collections.OrderedDict()
    for stage in STAGES:
        for key in needed_fields(stage):
            uses.setdefault(key, []).append(stage)
    shared, alone = {}, {}
    for stage in STAGES:
        built = [key for key in uses if stage_of(key) == stage]
        shared[stage] = lay_out([key for key in built if uses[key] != [stage]])
        alone[stage] = lay_out([key for key in built if uses[key] == [stage]])
    return shared, alone


def all_shifts():
    found = collections.OrderedDict()
    for stage in STAGES:
        for _, _, (dx, dy, _, _) in needed_fields(stage):
            if (dx, dy) != (0, 0):
                found[dx, dy] = None
    return list(found)


def write_shifts(perm_ref):
    lane = lax.broadcasted_iota(jnp.int32, (LANES, LANES), 1)
    source = lax.broadcasted_iota(jnp.int32, (LANES, LANES), 0)
    for index, (dx, dy) in enumerate(all_shifts()):
        wanted = (lane // NX + dy + NY) % NY * NX + (lane + dx + NX) % NX
        perm_ref[pl.ds(index * LANES, LANES), :] = (source == wanted).astype(F32).astype(jnp.bfloat16)


def parts_of(kind, value):
    if kind == "u":
        return [value.astype(jnp.bfloat16)]
    high = value.astype(jnp.bfloat16)
    rest = value - high.astype(F32)
    middle = rest.astype(jnp.bfloat16)
    return [high, middle, (rest - middle.astype(F32)).astype(jnp.bfloat16)]


def build_fields(locator, perm_ref, stores):
    groups = collections.OrderedDict()
    for ref, rows in stores:
        for (kind, n, disp), row in rows.items():
            shifts = groups.setdefault((kind, n, disp[3], disp[2]), collections.OrderedDict())
            shifts[disp[0], disp[1]] = (ref, row)
    order = all_shifts()
    for (kind, n, dt, dz), shifts in groups.items():
        regs = [locator.field_register(kind, n, k, dt, dz) for k in range(REGS[kind])]
        if (0, 0) in shifts:
            ref, row = shifts[0, 0]
            for k, value in enumerate(regs):
                ref[pl.ds(row + 8 * k, 8), :] = value
        parts = parts_of(kind, jnp.concatenate(regs, axis=0))
        for shift, (ref, row) in shifts.items():
            if shift != (0, 0):
                perm = perm_ref[pl.ds(order.index(shift) * LANES, LANES), :]
                moved = [jnp.dot(part, perm, preferred_element_type=F32) for part in parts]
                ref[pl.ds(row, 8 * REGS[kind]), :] = functools.reduce(jnp.add, moved)


class Fields:
    def __init__(self, own_x, own_u, stores):
        self.place = {("x", 0, ZERO): (own_x, 0)}
        for n in range(4):
            self.place["u", n, ZERO] = (own_u, 8 * REGS["u"] * n)
        for ref, rows in stores:
            for key, row in rows.items():
                self.place[key] = (ref, row)
        self.upper = lax.broadcasted_iota(jnp.int32, (8, LANES), 0) < 4

    def reg(self, key, k):
        ref, row = self.place[key]
        return ref[pl.ds(row + 8 * k, 8), :]

    def two_tiles(self, keys, k):
        top = self.reg(keys[0], k)
        turned_top = pltpu.roll(top, 4, 0)
        if keys[0] == keys[1]:
            low, turned_low = top, turned_top
        else:
            low = self.reg(keys[1], k)
            turned_low = pltpu.roll(low, 4, 0)
        return [jnp.where(self.upper, top, turned_low), jnp.where(self.upper, turned_top, low)]

    def vector(self, keys, pole):
        flat = [tile for k in range(3) for tile in self.two_tiles(keys, 3 * pole + k)]
        return [flat[:3], flat[3:]]

    def matrix(self, keys):
        flat = [tile for k in range(9) for tile in self.two_tiles(keys, k)]
        return [[flat[9 * c + 3 * i : 9 * c + 3 * i + 3] for i in range(3)] for c in range(2)]

    def compact_halves(self, first, second):
        top = jnp.where(self.upper, first, pltpu.roll(second, 4, 0))
        return top, jnp.where(self.upper, pltpu.roll(first, 4, 0), second)

    def compact_sum(self, first, second):
        kept = jnp.where(self.upper, first, second)
        return kept + pltpu.roll(jnp.where(self.upper, second, first), 4, 0)


def pole_sum(fields, here, ahead, scales):
    total = None
    for pole in range(NP):
        h = [[scales[pole] * v for v in part] for part in fields.vector(here, pole)]
        a = fields.vector(ahead, pole)
        real = [[a[0][i] * h[0][j] + a[1][i] * h[1][j] for j in range(3)] for i in range(3)]
        imag = [[a[1][i] * h[0][j] - a[0][i] * h[1][j] for j in range(3)] for i in range(3)]
        if total is None:
            total = [real, imag]
        else:
            total = [
                [[total[c][i][j] + new[i][j] for j in range(3)] for i in range(3)]
                for c, new in enumerate((real, imag))
            ]
    return total


def transposed(matrix):
    return [[[part[j][i] for j in range(3)] for i in range(3)] for part in matrix]


def row_times(row, right, row_sign, right_sign):
    result = [[], []]
    for j in range(3):
        real = imag = None
        for k in range(3):
            rr = row[0][k] * right[0][k][j]
            ii = row[1][k] * right[1][k][j]
            ri = row[0][k] * right[1][k][j]
            ir = row[1][k] * right[0][k][j]
            new_real = rr - ii if row_sign * right_sign > 0 else rr + ii
            if row_sign > 0 and right_sign > 0:
                new_imag = ri + ir
            elif row_sign > 0:
                new_imag = ir - ri
            else:
                new_imag = ri - ir
            real = new_real if real is None else real + new_real
            imag = new_imag if imag is None else imag + new_imag
        result[0].append(real)
        result[1].append(imag)
    return result


def add_terms(fields, stage, near, acc):
    started = set()
    for target, halves in TERMS[stage]:
        for sign in (1, -1):
            here, ahead, left, right = term_fields(halves, sign)
            force = pole_sum(fields, here, ahead, near)
            left = fields.matrix(left)
            right = fields.matrix(right)
            if sign > 0:
                right = transposed(right)
            else:
                left = transposed(left)
            rows = [row_times([left[0][i], left[1][i]], force, sign, 1) for i in range(3)]
            for i in range(3):
                row = row_times(rows[i], right, 1, -sign)
                for part in range(2):
                    for j in range(3):
                        at = pl.ds((target * 18 + part * 9 + i * 3 + j) * 8, 8)
                        new = row[part][j]
                        acc[at, :] = acc[at, :] + new if target in started else new
            started.add(target)


def acc_tile(acc, target, c):
    return acc[pl.ds((target * 18 + c) * 8, 8), :]


def scale_tiles(scale_ref):
    tiles = [scale_ref[pl.ds(8 * p, 8), :] for p in range(3 * NP)]
    return tiles[:NP], tiles[NP : 2 * NP], tiles[2 * NP :]


def own_force(fields, m, both):
    total = pole_sum(
        fields,
        [("x", 0, ZERO)] * 2,
        [("x", 0, UNIT[m]), ("x", 0, plus(ZERO, UNIT[m], 3))],
        both,
    )
    flat = [total[c][i][j] for c in range(2) for i in range(3) for j in range(3)]
    return [fields.compact_sum(flat[2 * k], flat[2 * k + 1]) for k in range(9)]


def write_messages(locator, plan, names, outs):
    for name, out in zip(names, outs):
        for reg, items in enumerate(plan[name].by_register()):
            spots = [item and locator.local(*item[1:]) for item in items]
            out[pl.ds(8 * reg, 8), :] = locator.assemble(spots)


def odd_in_z():
    return (lax.axis_index("gz") * lax.axis_size("gy") + lax.axis_index("gy")) % 2 == 1


def pack_z_kernel(plan, near_in, far_in, weight_in, x_in, u_in, *rest):
    within_ref, between_ref, second_ref, scale_ref, perm_ref, x_ref, u_ref = rest[:7]
    near_ref, far_ref, weight_ref, u_held, sems = rest[7:]
    copies = [
        pltpu.make_async_copy(source, target, sems.at[index])
        for index, (source, target) in enumerate(
            ((u_in, u_held), (x_in, x_ref), (near_in, near_ref), (far_in, far_ref), (weight_in, weight_ref))
        )
    ]
    for copy in copies:
        copy.start()
    write_shifts(perm_ref)
    for copy in copies:
        copy.wait()
    u_ref[...] = u_held[...].astype(F32)
    locator = Locator(plan, 1, {("own", "x"): x_ref, ("own", "u"): u_ref})
    names = [("z", 1), ("z", -1)]

    @pl.when(odd_in_z())
    def _():
        write_messages(locator, plan, names, (within_ref, between_ref))

    @pl.when(jnp.logical_not(odd_in_z()))
    def _():
        write_messages(locator, plan, names, (between_ref, within_ref))

    write_messages(locator, plan, [("z", 2)], [second_ref])
    write_scales(near_ref, far_ref, weight_ref, scale_ref)


def pack_t_kernel(plan, names, x_ref, u_ref, *outs):
    write_messages(Locator(plan, 1, {("own", "x"): x_ref, ("own", "u"): u_ref}), plan, names, outs)


def corner_kernel(plan, names, within_ref, between_ref, _, ahead_ref, behind_ref, *outs):
    def split(from_ahead, from_behind):
        ahead_ref[...] = from_ahead[pl.ds(0, ahead_ref.shape[0]), :]
        behind_ref[...] = from_behind[pl.ds(0, behind_ref.shape[0]), :]

    @pl.when(odd_in_z())
    def _():
        split(between_ref, within_ref)

    @pl.when(jnp.logical_not(odd_in_z()))
    def _():
        split(within_ref, between_ref)

    locator = Locator(plan, 1, {("z", 1): ahead_ref, ("z", -1): behind_ref})
    for name, out in zip(names, outs):
        for reg, items in enumerate(plan[name].by_register()):
            spots = [
                item and (("z", item[0]),) + plan["z", item[0]].places[(0,) + item[1:]] for item in items
            ]
            out[pl.ds(8 * reg, 8), :] = locator.assemble(spots)


def part_reg(ref, index, k):
    return ref[pl.ds((9 * index + k) * 8, 8), :]


def write_scales(near_ref, far_ref, weight_ref, scale_ref):
    upper = lax.broadcasted_iota(jnp.int32, (8, LANES), 0) < 4
    for p in range(NP):
        scale_ref[pl.ds(8 * p, 8), :] = jnp.full((8, LANES), near_ref[p], F32)
        scale_ref[pl.ds(8 * (NP + p), 8), :] = jnp.where(upper, near_ref[p], far_ref[p])
        scale_ref[pl.ds(8 * (2 * NP + p), 8), :] = jnp.full((8, LANES), weight_ref[p], F32)


def own_fields_kernel(plan, t_size, perm_ref, x_ref, u_ref, shared_ref, alone_ref):
    shared, alone = field_split()
    stores = [(shared_ref, shared["own"][0]), (alone_ref, alone["own"][0])]
    build_fields(Locator(plan, t_size, {("own", "x"): x_ref, ("own", "u"): u_ref}), perm_ref, stores)


def own_kernel(scale_ref, x_ref, u_ref, shared_ref, alone_ref, part_ref, acc):
    shared, alone = field_split()
    fields = Fields(x_ref, u_ref, [(shared_ref, shared["own"][0]), (alone_ref, alone["own"][0])])
    near, both, weight = scale_tiles(scale_ref)
    add_terms(fields, "own", near, acc)
    direct = [own_force(fields, m, both) for m in DIRECT["own"]]
    for k in range(9):
        staples = fields.compact_halves(acc_tile(acc, 0, 2 * k), acc_tile(acc, 0, 2 * k + 1))
        for m in range(2):
            part_ref[pl.ds((9 * m + k) * 8, 8), :] = direct[m][k] + weight[m] * staples[m]


def stage_setup(stage, plan, t_size, names, received, perm_ref, x_ref, u_ref, shared_refs, shared_ref, alone_ref):
    buffers = {("own", "x"): x_ref, ("own", "u"): u_ref}
    buffers.update(zip(names, received))
    shared, alone = field_split()
    stores = [(alone_ref, alone[stage][0])]
    if shared_ref is not None:
        stores.append((shared_ref, shared[stage][0]))
    build_fields(Locator(plan, t_size, buffers), perm_ref, stores)
    earlier = [(ref, shared[name][0]) for name, ref in zip(STAGES, shared_refs)]
    return Fields(x_ref, u_ref, earlier + stores)


def z_kernel(plan, t_size, names, scale_ref, perm_ref, x_ref, u_ref, own_shared, own_part, *rest):
    received = rest[: len(names)]
    shared_ref, part_ref, alone_ref, acc = rest[len(names) :]
    fields = stage_setup(
        "z", plan, t_size, names, received, perm_ref, x_ref, u_ref, [own_shared], shared_ref, alone_ref
    )
    near, _, weight = scale_tiles(scale_ref)
    add_terms(fields, "z", near, acc)
    for k in range(9):
        staples = fields.compact_halves(acc_tile(acc, 0, 2 * k), acc_tile(acc, 0, 2 * k + 1))
        for m in range(2):
            part_ref[pl.ds((9 * m + k) * 8, 8), :] = part_reg(own_part, m, k) + weight[m] * staples[m]
        staple = fields.compact_sum(acc_tile(acc, 1, 2 * k), acc_tile(acc, 1, 2 * k + 1))
        part_ref[pl.ds((18 + k) * 8, 8), :] = weight[2] * staple


def t_kernel(plan, t_size, names, scale_ref, perm_ref, x_ref, u_ref, own_shared, z_shared, z_part, *rest):
    received = rest[: len(names)]
    shared_ref, part_ref, ready, alone_ref, acc = rest[len(names) :]
    fields = stage_setup(
        "t", plan, t_size, names, received, perm_ref, x_ref, u_ref, [own_shared, z_shared], shared_ref, alone_ref
    )
    near, both, weight = scale_tiles(scale_ref)
    add_terms(fields, "t", near, acc)
    for k in range(9):
        staples = fields.compact_halves(acc_tile(acc, 0, 2 * k), acc_tile(acc, 0, 2 * k + 1))
        for m in range(2):
            ready[pl.ds((9 * m + k) * 8, 8), :] = part_reg(z_part, m, k) + weight[m] * staples[m]
    direct = own_force(fields, 3, both)
    for k in range(9):
        staple = fields.compact_sum(acc_tile(acc, 1, 2 * k), acc_tile(acc, 1, 2 * k + 1))
        part_ref[pl.ds(k * 8, 8), :] = direct[k] + weight[3] * staple


def last_kernel(plan, t_size, names, scale_ref, perm_ref, x_ref, u_ref, *rest):
    own_shared, z_shared, t_shared, z_part, t_part, earlier = rest[:6]
    received = rest[6 : 6 + len(names)]
    out_ref, alone_ref, acc, ready, sems = rest[6 + len(names) :]
    rows = ready.shape[0]
    first = pltpu.make_async_copy(earlier, out_ref.at[pl.ds(0, rows)], sems.at[0])
    first.start()
    fields = stage_setup(
        "corner",
        plan,
        t_size,
        names,
        received,
        perm_ref,
        x_ref,
        u_ref,
        [own_shared, z_shared, t_shared],
        None,
        alone_ref,
    )
    near, both, weight = scale_tiles(scale_ref)
    add_terms(fields, "corner", near, acc)
    direct = own_force(fields, 2, both)
    for k in range(9):
        staples = fields.compact_halves(acc_tile(acc, 0, 2 * k), acc_tile(acc, 0, 2 * k + 1))
        ready[pl.ds(k * 8, 8), :] = part_reg(z_part, 2, k) + direct[k] + weight[2] * staples[0]
        ready[pl.ds((9 + k) * 8, 8), :] = part_reg(t_part, 0, k) + weight[3] * staples[1]
    second = pltpu.make_async_copy(ready, out_ref.at[pl.ds(rows, rows)], sems.at[1])
    second.start()
    first.wait()
    second.wait()


def rows_of(count):
    return jax.ShapeDtypeStruct((count, LANES), F32)


def on_device(pole_vectors, gauge_links, pole_coeff, naik_coeff, staple_weight):
    t_size = lax.axis_size("ta")
    z_size = lax.axis_size("gz") * lax.axis_size("gy")
    plan = message_plan(t_size)
    x_rows, u_rows = 8 * REGS["x"], 4 * 8 * REGS["u"]
    vmem = pl.BlockSpec(memory_space=pltpu.VMEM)
    hbm = pl.BlockSpec(memory_space=pltpu.HBM)
    limit = pltpu.CompilerParams(vmem_limit_bytes=4 * 1024 * 1024)

    def moved(name, value):
        kind, step = name
        if kind == "z":
            return lax.ppermute(value, ("gz", "gy"), [((i + step) % z_size, i) for i in range(z_size)])
        return lax.ppermute(value, "ta", [((j + step) % t_size, j) for j in range(t_size)])

    def exchanged(value, first):
        pairs = [(i, (i + 1) % z_size) for i in range(first, z_size, 2)]
        return lax.ppermute(value, ("gz", "gy"), pairs + [(j, i) for i, j in pairs])

    first_names = [name for name in plan if name[0] != "c"]
    corner_names = [name for name in plan if name[0] == "c"]
    t_names = [name for name in first_names if name[0] == "t"]
    in_hbm = functools.partial(pltpu.with_memory_space_constraint, memory_space=pltpu.HBM)
    beyond_rows = 8 * max([plan["z", 2].count] + [plan[name].count for name in corner_names])
    ahead_rows, behind_rows = [8 * plan["z", step].count for step in (1, -1)]
    shared_rows = max(ahead_rows, behind_rows)
    within, between, beyond, scale, perm, *own = pl.pallas_call(
        functools.partial(pack_z_kernel, plan),
        out_shape=[rows_of(shared_rows), rows_of(shared_rows + 8), rows_of(beyond_rows)]
        + [
            rows_of(8 * 3 * NP),
            jax.ShapeDtypeStruct((len(all_shifts()) * LANES, LANES), jnp.bfloat16),
            rows_of(x_rows),
            rows_of(u_rows),
        ],
        in_specs=[hbm] * 5,
        out_specs=[vmem] * 7,
        scratch_shapes=[pltpu.SMEM((NP,), F32)] * 3
        + [pltpu.VMEM((u_rows, LANES), jnp.bfloat16), pltpu.SemaphoreType.DMA((5,))],
        compiler_params=limit,
        name="pack_z",
    )(
        in_hbm(pole_coeff),
        in_hbm(naik_coeff),
        in_hbm(staple_weight),
        in_hbm(pole_vectors.reshape((x_rows, LANES))),
        in_hbm(gauge_links.reshape((u_rows, LANES))),
    )
    between, within = exchanged(between, 1), exchanged(within, 0)
    received = {("z", 2): moved(("z", 2), beyond)}
    packed = pl.pallas_call(
        functools.partial(pack_t_kernel, plan, t_names),
        out_shape=[rows_of(8 * plan[name].count) for name in t_names],
        in_specs=[vmem] * 2,
        out_specs=[vmem] * len(t_names),
        compiler_params=limit,
        name="pack_t",
    )(*own)
    received.update({name: moved(name, value) for name, value in zip(t_names, packed)})
    shared, alone = field_split()
    part_rows = 8 * REGS["u"]

    def scratch(stage):
        sums = 1 + max(target for target, _ in TERMS[stage])
        return [pltpu.VMEM((alone[stage][1], LANES), F32), pltpu.VMEM((sums * 18 * 8, LANES), F32)]

    def cost(micros):
        return pl.CostEstimate(flops=10**6, bytes_accessed=int(3.69e6 * micros), transcendentals=0)

    wide_limit = pltpu.CompilerParams(vmem_limit_bytes=6 * 1024 * 1024)
    own_shared, own_alone = pl.pallas_call(
        functools.partial(own_fields_kernel, plan, t_size),
        out_shape=[rows_of(shared["own"][1]), rows_of(alone["own"][1])],
        in_specs=[vmem] * 3,
        out_specs=[vmem] * 2,
        compiler_params=wide_limit,
        name="fields_own",
    )(perm, *own)
    own_part = pl.pallas_call(
        own_kernel,
        out_shape=rows_of(2 * part_rows),
        in_specs=[vmem] * 5,
        out_specs=vmem,
        scratch_shapes=scratch("own")[1:],
        cost_estimate=cost(COSTS["own"]),
        compiler_params=wide_limit,
        name="force_own",
    )(scale, *own, own_shared, own_alone)
    local = [scale, perm, *own]
    received["z", 1], received["z", -1], *corners = pl.pallas_call(
        functools.partial(corner_kernel, plan, corner_names),
        out_shape=[rows_of(ahead_rows), rows_of(behind_rows)]
        + [rows_of(8 * plan[name].count) for name in corner_names],
        in_specs=[vmem] * 3,
        out_specs=[vmem] * (2 + len(corner_names)),
        compiler_params=limit,
        name="pack_corners",
    )(within, between, own_part)
    received.update({name: moved(name, value) for name, value in zip(corner_names, corners)})
    names = [("z", 1), ("z", -1)]
    z_shared, z_part = pl.pallas_call(
        functools.partial(z_kernel, plan, t_size, names),
        out_shape=[rows_of(shared["z"][1]), rows_of(3 * part_rows)],
        in_specs=[vmem] * (6 + len(names)),
        out_specs=[vmem] * 2,
        scratch_shapes=scratch("z"),
        cost_estimate=cost(COSTS["z"]),
        compiler_params=wide_limit,
        name="force_z",
    )(*local, own_shared, own_part, *[received[name] for name in names])
    t_shared, t_part, earlier = pl.pallas_call(
        functools.partial(t_kernel, plan, t_size, t_names),
        out_shape=[rows_of(shared["t"][1]), rows_of(part_rows), rows_of(2 * part_rows)],
        in_specs=[vmem] * (7 + len(t_names)),
        out_specs=[vmem] * 3,
        scratch_shapes=scratch("t"),
        cost_estimate=cost(COSTS["t"]),
        compiler_params=wide_limit,
        name="force_t",
    )(*local, own_shared, z_shared, z_part, *[received[name] for name in t_names])
    names = list(received)
    force = pl.pallas_call(
        functools.partial(last_kernel, plan, t_size, names),
        out_shape=rows_of(u_rows),
        in_specs=[vmem] * (10 + len(names)),
        out_specs=hbm,
        scratch_shapes=scratch("corner")
        + [pltpu.VMEM((2 * part_rows, LANES), F32), pltpu.SemaphoreType.DMA((2,))],
        cost_estimate=cost(COSTS["corner"]),
        compiler_params=wide_limit,
        name="force_corner",
    )(
        *local,
        own_shared,
        z_shared,
        t_shared,
        z_part,
        t_part,
        earlier,
        *[received[name] for name in names],
    )
    return force.reshape(gauge_links.shape)


def solution(mesh):
    return jax.shard_map(
        on_device,
        mesh=mesh,
        in_specs=(
            P("ens", None, None, "ta", ("gz", "gy"), None),
            P("ens", None, None, None, "ta", ("gz", "gy"), None),
            P(),
            P(),
            P(),
        ),
        out_specs=P("ens", None, None, None, "ta", ("gz", "gy"), None),
        check_vma=False,
    )
```

```python
import collections
import functools

import jax
import jax.numpy as jnp
from jax import lax
from jax.experimental import pallas as pl
from jax.experimental.pallas import tpu as pltpu
from jax.sharding import PartitionSpec as P

NX = 8
NY = 16
LANES = NX * NY
NP = 4
F32 = jnp.float32
REGS = {"x": NP * 3, "u": 9}
UNIT = ((1, 0, 0, 0), (0, 1, 0, 0), (0, 0, 1, 0), (0, 0, 0, 1))
ZERO = (0, 0, 0, 0)
SITES = ((0, 0), (0, 1), (1, 0), (1, 1))
STAGES = ("own", "z", "t", "corner")
TERMS = {
    "own": ((0, ((0, 1), (1, 0))),),
    "z": ((0, ((0, 2), (1, 2))), (1, ((2, 0), (2, 1)))),
    "t": ((0, ((0, 3), (1, 3))), (1, ((3, 0), (3, 1)))),
    "corner": ((0, ((2, 3), (3, 2))),),
}
COSTS = {"own": 2.0, "z": 2.0, "t": 2.0, "corner": 1.0}
DIRECT = {"own": (0, 1), "z": (), "t": (3,), "corner": (2,)}


def plus(left, right, scale=1):
    return tuple(a + scale * b for a, b in zip(left, right))


class Message:
    def __init__(self):
        self.places = collections.OrderedDict()
        self.count = 0

    def add_full(self, kind, n):
        for k in range(REGS[kind]):
            for t, z in SITES:
                self.places[0, kind, n, k, t, z] = (self.count, 2 * t + z)
            self.count += 1

    def add_halves(self, entries, axis):
        half = -(-len(entries) // 2)
        for index, (kind, n, k, layer) in enumerate(entries):
            reg, part = self.count + index % half, index // half
            for other in range(2):
                t, z = (layer, other) if axis == "t" else (other, layer)
                slot = 2 * part + other if axis == "t" else 2 * other + part
                self.places[0, kind, n, k, t, z] = (reg, slot)
        self.count += half

    def add_single(self, entries):
        quarter = -(-len(entries) // 4)
        for index, entry in enumerate(entries):
            self.places[entry] = (self.count + index % quarter, index // quarter)
        self.count += quarter

    def by_register(self):
        found = [[None] * 4 for _ in range(self.count)]
        for item, (reg, slot) in self.places.items():
            found[reg][slot] = item
        return found


def regs_of(kind, directions, layer):
    return [(kind, n, k, layer) for n in directions for k in range(REGS[kind])]


def message_plan(t_size):
    plan = collections.OrderedDict()
    ahead = plan["z", 1] = Message()
    ahead.add_full("x", 0)
    ahead.add_halves(regs_of("u", (0, 1, 3), 0), "z")
    behind = plan["z", -1] = Message()
    behind.add_halves(regs_of("x", (0,), 1) + regs_of("u", (2,), 1), "z")
    second = plan["z", 2] = Message()
    second.add_halves(regs_of("x", (0,), 0), "z")
    halves, corners = collections.OrderedDict(), collections.OrderedDict()
    for dt, entries in (
        (1, regs_of("u", (0, 1, 2), 0)),
        (-1, regs_of("x", (0,), 1) + regs_of("u", (3,), 1)),
        (2, regs_of("x", (0,), 0)),
    ):
        if dt % t_size != 0:
            halves.setdefault(dt % t_size, []).extend(entries)
    for dt, entries in halves.items():
        message = plan["t", dt] = Message()
        if dt == 1:
            message.add_full("x", 0)
        held = {item[1:4] for item in message.places}
        message.add_halves([e for e in entries if e[:3] not in held], "t")
    for dt, entries in (
        (1, [(1, "x", 0, k, 0, 0) for k in range(REGS["x"])]),
        (1, [(-1, "x", 0, k, 0, 1) for k in range(REGS["x"])]),
        (1, [(-1, "u", 2, k, 0, 1) for k in range(REGS["u"])]),
        (-1, [(1, "x", 0, k, 1, 0) for k in range(REGS["x"])]),
        (-1, [(1, "u", 3, k, 1, 0) for k in range(REGS["u"])]),
    ):
        corners.setdefault(dt % t_size, []).extend(entries)
    for dt, entries in corners.items():
        plan["c", dt] = Message()
        plan["c", dt].add_single(entries)
    return plan


class Locator:
    def __init__(self, plan, t_size, buffers):
        self.plan, self.t_size, self.buffers = plan, t_size, buffers

    def local(self, kind, n, k, t, z):
        return ("own", kind), n * REGS[kind] + k, 2 * t + z

    def find(self, kind, n, k, t_at, z_at):
        (dt, t), (dz, z) = divmod(t_at, 2), divmod(z_at, 2)
        dt %= self.t_size
        if (dt, dz) == (0, 0):
            return self.local(kind, n, k, t, z)
        name = ("z", dz) if dt == 0 else ("t", dt) if dz == 0 else ("c", dt)
        item = (dz if name[0] == "c" else 0, kind, n, k, t, z)
        return (name,) + self.plan[name].places[item]

    def load(self, name, reg):
        return self.buffers[name][pl.ds(8 * reg, 8), :]

    def assemble(self, spots):
        groups = collections.OrderedDict()
        for r, spot in enumerate(spots):
            if spot is not None:
                groups.setdefault((spot[0], spot[1], r - spot[2]), []).append(r)
        row = lax.broadcasted_iota(jnp.int32, (8, LANES), 0) % 4
        result = None
        for (name, reg, move), rows in groups.items():
            value = self.load(name, reg)
            if move != 0:
                value = pltpu.roll(value, move % 8, 0)
            if result is None:
                result = value
            else:
                mask = functools.reduce(jnp.logical_or, [row == r for r in rows])
                result = jnp.where(mask, value, result)
        return result

    def field_register(self, kind, n, k, dt, dz):
        return self.assemble([self.find(kind, n, k, t + dt, z + dz) for t, z in SITES])


def term_fields(halves, sign):
    here, ahead, left, right = [], [], [], []
    for m, n in halves:
        start = plus(ZERO, UNIT[n], sign)
        base = ZERO if sign > 0 else start
        here.append(("x", 0, start))
        ahead.append(("x", 0, plus(start, UNIT[m])))
        left.append(("u", n, base))
        right.append(("u", n, plus(base, UNIT[m])))
    return here, ahead, left, right


def needed_fields(stage):
    keys = collections.OrderedDict()
    for _, halves in TERMS[stage]:
        for sign in (1, -1):
            for pair in term_fields(halves, sign):
                keys.update((key, None) for key in pair)
    for m in DIRECT[stage]:
        for scale in (1, 3):
            keys["x", 0, plus(ZERO, UNIT[m], scale)] = None
    return [key for key in keys if key[2] != ZERO]


def stage_of(key):
    dz, dt = key[2][2:]
    if abs(dz) == 3 or (dz != 0 and dt != 0):
        return "corner"
    return "t" if dt != 0 else "z" if dz != 0 else "own"


def lay_out(keys):
    rows, total = collections.OrderedDict(), 0
    for key in keys:
        rows[key] = total
        total += 8 * REGS[key[0]]
    return rows, total


def field_split():
    uses = collections.OrderedDict()
    for stage in STAGES:
        for key in needed_fields(stage):
            uses.setdefault(key, []).append(stage)
    shared, alone = {}, {}
    for stage in STAGES:
        built = [key for key in uses if stage_of(key) == stage]
        shared[stage] = lay_out([key for key in built if uses[key] != [stage]])
        alone[stage] = lay_out([key for key in built if uses[key] == [stage]])
    return shared, alone


def all_shifts():
    found = collections.OrderedDict()
    for stage in STAGES:
        for _, _, (dx, dy, _, _) in needed_fields(stage):
            if (dx, dy) != (0, 0):
                found[dx, dy] = None
    return list(found)


def write_shifts(perm_ref):
    lane = lax.broadcasted_iota(jnp.int32, (LANES, LANES), 1)
    source = lax.broadcasted_iota(jnp.int32, (LANES, LANES), 0)
    for index, (dx, dy) in enumerate(all_shifts()):
        wanted = (lane // NX + dy + NY) % NY * NX + (lane + dx + NX) % NX
        perm_ref[pl.ds(index * LANES, LANES), :] = (source == wanted).astype(F32).astype(jnp.bfloat16)


def parts_of(kind, value):
    if kind == "u":
        return [value.astype(jnp.bfloat16)]
    high = value.astype(jnp.bfloat16)
    rest = value - high.astype(F32)
    middle = rest.astype(jnp.bfloat16)
    return [high, middle, (rest - middle.astype(F32)).astype(jnp.bfloat16)]


def build_fields(locator, perm_ref, stores):
    groups = collections.OrderedDict()
    for ref, rows in stores:
        for (kind, n, disp), row in rows.items():
            shifts = groups.setdefault((kind, n, disp[3], disp[2]), collections.OrderedDict())
            shifts[disp[0], disp[1]] = (ref, row)
    order = all_shifts()
    for (kind, n, dt, dz), shifts in groups.items():
        regs = [locator.field_register(kind, n, k, dt, dz) for k in range(REGS[kind])]
        if (0, 0) in shifts:
            ref, row = shifts[0, 0]
            for k, value in enumerate(regs):
                ref[pl.ds(row + 8 * k, 8), :] = value
        parts = parts_of(kind, jnp.concatenate(regs, axis=0))
        for shift, (ref, row) in shifts.items():
            if shift != (0, 0):
                perm = perm_ref[pl.ds(order.index(shift) * LANES, LANES), :]
                moved = [jnp.dot(part, perm, preferred_element_type=F32) for part in parts]
                ref[pl.ds(row, 8 * REGS[kind]), :] = functools.reduce(jnp.add, moved)


class Fields:
    def __init__(self, own_x, own_u, stores):
        self.place = {("x", 0, ZERO): (own_x, 0)}
        for n in range(4):
            self.place["u", n, ZERO] = (own_u, 8 * REGS["u"] * n)
        for ref, rows in stores:
            for key, row in rows.items():
                self.place[key] = (ref, row)
        self.upper = lax.broadcasted_iota(jnp.int32, (8, LANES), 0) < 4

    def reg(self, key, k):
        ref, row = self.place[key]
        return ref[pl.ds(row + 8 * k, 8), :]

    def two_tiles(self, keys, k):
        top = self.reg(keys[0], k)
        turned_top = pltpu.roll(top, 4, 0)
        if keys[0] == keys[1]:
            low, turned_low = top, turned_top
        else:
            low = self.reg(keys[1], k)
            turned_low = pltpu.roll(low, 4, 0)
        return [jnp.where(self.upper, top, turned_low), jnp.where(self.upper, turned_top, low)]

    def vector(self, keys, pole):
        flat = [tile for k in range(3) for tile in self.two_tiles(keys, 3 * pole + k)]
        return [flat[:3], flat[3:]]

    def matrix(self, keys):
        flat = [tile for k in range(9) for tile in self.two_tiles(keys, k)]
        return [[flat[9 * c + 3 * i : 9 * c + 3 * i + 3] for i in range(3)] for c in range(2)]

    def compact_halves(self, first, second):
        top = jnp.where(self.upper, first, pltpu.roll(second, 4, 0))
        return top, jnp.where(self.upper, pltpu.roll(first, 4, 0), second)

    def compact_sum(self, first, second):
        kept = jnp.where(self.upper, first, second)
        return kept + pltpu.roll(jnp.where(self.upper, second, first), 4, 0)


def pole_sum(fields, here, ahead, scales):
    total = None
    for pole in range(NP):
        h = [[scales[pole] * v for v in part] for part in fields.vector(here, pole)]
        a = fields.vector(ahead, pole)
        real = [[a[0][i] * h[0][j] + a[1][i] * h[1][j] for j in range(3)] for i in range(3)]
        imag = [[a[1][i] * h[0][j] - a[0][i] * h[1][j] for j in range(3)] for i in range(3)]
        if total is None:
            total = [real, imag]
        else:
            total = [
                [[total[c][i][j] + new[i][j] for j in range(3)] for i in range(3)]
                for c, new in enumerate((real, imag))
            ]
    return total


def transposed(matrix):
    return [[[part[j][i] for j in range(3)] for i in range(3)] for part in matrix]


def row_times(row, right, row_sign, right_sign):
    result = [[], []]
    for j in range(3):
        real = imag = None
        for k in range(3):
            rr = row[0][k] * right[0][k][j]
            ii = row[1][k] * right[1][k][j]
            ri = row[0][k] * right[1][k][j]
            ir = row[1][k] * right[0][k][j]
            new_real = rr - ii if row_sign * right_sign > 0 else rr + ii
            if row_sign > 0 and right_sign > 0:
                new_imag = ri + ir
            elif row_sign > 0:
                new_imag = ir - ri
            else:
                new_imag = ri - ir
            real = new_real if real is None else real + new_real
            imag = new_imag if imag is None else imag + new_imag
        result[0].append(real)
        result[1].append(imag)
    return result


def add_terms(fields, stage, near, acc):
    started = set()
    for target, halves in TERMS[stage]:
        for sign in (1, -1):
            here, ahead, left, right = term_fields(halves, sign)
            force = pole_sum(fields, here, ahead, near)
            left = fields.matrix(left)
            right = fields.matrix(right)
            if sign > 0:
                right = transposed(right)
            else:
                left = transposed(left)
            rows = [row_times([left[0][i], left[1][i]], force, sign, 1) for i in range(3)]
            for i in range(3):
                row = row_times(rows[i], right, 1, -sign)
                for part in range(2):
                    for j in range(3):
                        at = pl.ds((target * 18 + part * 9 + i * 3 + j) * 8, 8)
                        new = row[part][j]
                        acc[at, :] = acc[at, :] + new if target in started else new
            started.add(target)


def acc_tile(acc, target, c):
    return acc[pl.ds((target * 18 + c) * 8, 8), :]


def scale_tiles(scale_ref):
    tiles = [scale_ref[pl.ds(8 * p, 8), :] for p in range(3 * NP)]
    return tiles[:NP], tiles[NP : 2 * NP], tiles[2 * NP :]


def own_force(fields, m, both):
    total = pole_sum(
        fields,
        [("x", 0, ZERO)] * 2,
        [("x", 0, UNIT[m]), ("x", 0, plus(ZERO, UNIT[m], 3))],
        both,
    )
    flat = [total[c][i][j] for c in range(2) for i in range(3) for j in range(3)]
    return [fields.compact_sum(flat[2 * k], flat[2 * k + 1]) for k in range(9)]


def write_messages(locator, plan, names, outs):
    for name, out in zip(names, outs):
        for reg, items in enumerate(plan[name].by_register()):
            spots = [item and locator.local(*item[1:]) for item in items]
            out[pl.ds(8 * reg, 8), :] = locator.assemble(spots)


def odd_in_z():
    return (lax.axis_index("gz") * lax.axis_size("gy") + lax.axis_index("gy")) % 2 == 1


def pack_z_kernel(plan, near_in, far_in, weight_in, x_in, u_in, *rest):
    within_ref, between_ref, second_ref, scale_ref, perm_ref, x_ref, u_ref = rest[:7]
    near_ref, far_ref, weight_ref, u_held, sems = rest[7:]
    copies = [
        pltpu.make_async_copy(source, target, sems.at[index])
        for index, (source, target) in enumerate(
            ((u_in, u_held), (x_in, x_ref), (near_in, near_ref), (far_in, far_ref), (weight_in, weight_ref))
        )
    ]
    for copy in copies:
        copy.start()
    write_shifts(perm_ref)
    for copy in copies:
        copy.wait()
    u_ref[...] = u_held[...].astype(F32)
    locator = Locator(plan, 1, {("own", "x"): x_ref, ("own", "u"): u_ref})
    names = [("z", 1), ("z", -1)]

    @pl.when(odd_in_z())
    def _():
        write_messages(locator, plan, names, (within_ref, between_ref))

    @pl.when(jnp.logical_not(odd_in_z()))
    def _():
        write_messages(locator, plan, names, (between_ref, within_ref))

    write_messages(locator, plan, [("z", 2)], [second_ref])
    write_scales(near_ref, far_ref, weight_ref, scale_ref)


def pack_t_kernel(plan, names, x_ref, u_ref, *outs):
    write_messages(Locator(plan, 1, {("own", "x"): x_ref, ("own", "u"): u_ref}), plan, names, outs)


def corner_kernel(plan, names, within_ref, between_ref, _, ahead_ref, behind_ref, *outs):
    def split(from_ahead, from_behind):
        ahead_ref[...] = from_ahead[pl.ds(0, ahead_ref.shape[0]), :]
        behind_ref[...] = from_behind[pl.ds(0, behind_ref.shape[0]), :]

    @pl.when(odd_in_z())
    def _():
        split(between_ref, within_ref)

    @pl.when(jnp.logical_not(odd_in_z()))
    def _():
        split(within_ref, between_ref)

    locator = Locator(plan, 1, {("z", 1): ahead_ref, ("z", -1): behind_ref})
    for name, out in zip(names, outs):
        for reg, items in enumerate(plan[name].by_register()):
            spots = [
                item and (("z", item[0]),) + plan["z", item[0]].places[(0,) + item[1:]] for item in items
            ]
            out[pl.ds(8 * reg, 8), :] = locator.assemble(spots)


def part_reg(ref, index, k):
    return ref[pl.ds((9 * index + k) * 8, 8), :]


def write_scales(near_ref, far_ref, weight_ref, scale_ref):
    upper = lax.broadcasted_iota(jnp.int32, (8, LANES), 0) < 4
    for p in range(NP):
        scale_ref[pl.ds(8 * p, 8), :] = jnp.full((8, LANES), near_ref[p], F32)
        scale_ref[pl.ds(8 * (NP + p), 8), :] = jnp.where(upper, near_ref[p], far_ref[p])
        scale_ref[pl.ds(8 * (2 * NP + p), 8), :] = jnp.full((8, LANES), weight_ref[p], F32)


def own_fields_kernel(plan, t_size, perm_ref, x_ref, u_ref, shared_ref, alone_ref):
    shared, alone = field_split()
    stores = [(shared_ref, shared["own"][0]), (alone_ref, alone["own"][0])]
    build_fields(Locator(plan, t_size, {("own", "x"): x_ref, ("own", "u"): u_ref}), perm_ref, stores)


def own_kernel(scale_ref, x_ref, u_ref, shared_ref, alone_ref, part_ref, acc):
    shared, alone = field_split()
    fields = Fields(x_ref, u_ref, [(shared_ref, shared["own"][0]), (alone_ref, alone["own"][0])])
    near, both, weight = scale_tiles(scale_ref)
    add_terms(fields, "own", near, acc)
    direct = [own_force(fields, m, both) for m in DIRECT["own"]]
    for k in range(9):
        staples = fields.compact_halves(acc_tile(acc, 0, 2 * k), acc_tile(acc, 0, 2 * k + 1))
        for m in range(2):
            part_ref[pl.ds((9 * m + k) * 8, 8), :] = direct[m][k] + weight[m] * staples[m]


def stage_setup(stage, plan, t_size, names, received, perm_ref, x_ref, u_ref, shared_refs, shared_ref, alone_ref):
    buffers = {("own", "x"): x_ref, ("own", "u"): u_ref}
    buffers.update(zip(names, received))
    shared, alone = field_split()
    stores = [(alone_ref, alone[stage][0])]
    if shared_ref is not None:
        stores.append((shared_ref, shared[stage][0]))
    build_fields(Locator(plan, t_size, buffers), perm_ref, stores)
    earlier = [(ref, shared[name][0]) for name, ref in zip(STAGES, shared_refs)]
    return Fields(x_ref, u_ref, earlier + stores)


def z_kernel(plan, t_size, names, scale_ref, perm_ref, x_ref, u_ref, own_shared, own_part, *rest):
    received = rest[: len(names)]
    shared_ref, part_ref, alone_ref, acc = rest[len(names) :]
    fields = stage_setup(
        "z", plan, t_size, names, received, perm_ref, x_ref, u_ref, [own_shared], shared_ref, alone_ref
    )
    near, _, weight = scale_tiles(scale_ref)
    add_terms(fields, "z", near, acc)
    for k in range(9):
        staples = fields.compact_halves(acc_tile(acc, 0, 2 * k), acc_tile(acc, 0, 2 * k + 1))
        for m in range(2):
            part_ref[pl.ds((9 * m + k) * 8, 8), :] = part_reg(own_part, m, k) + weight[m] * staples[m]
        staple = fields.compact_sum(acc_tile(acc, 1, 2 * k), acc_tile(acc, 1, 2 * k + 1))
        part_ref[pl.ds((18 + k) * 8, 8), :] = weight[2] * staple


def t_kernel(plan, t_size, names, scale_ref, perm_ref, x_ref, u_ref, own_shared, z_shared, z_part, *rest):
    received = rest[: len(names)]
    shared_ref, part_ref, ready, alone_ref, acc = rest[len(names) :]
    fields = stage_setup(
        "t", plan, t_size, names, received, perm_ref, x_ref, u_ref, [own_shared, z_shared], shared_ref, alone_ref
    )
    near, both, weight = scale_tiles(scale_ref)
    add_terms(fields, "t", near, acc)
    for k in range(9):
        staples = fields.compact_halves(acc_tile(acc, 0, 2 * k), acc_tile(acc, 0, 2 * k + 1))
        for m in range(2):
            ready[pl.ds((9 * m + k) * 8, 8), :] = part_reg(z_part, m, k) + weight[m] * staples[m]
    direct = own_force(fields, 3, both)
    for k in range(9):
        staple = fields.compact_sum(acc_tile(acc, 1, 2 * k), acc_tile(acc, 1, 2 * k + 1))
        part_ref[pl.ds(k * 8, 8), :] = direct[k] + weight[3] * staple


def last_kernel(plan, t_size, names, scale_ref, perm_ref, x_ref, u_ref, *rest):
    own_shared, z_shared, t_shared, z_part, t_part, earlier = rest[:6]
    received = rest[6 : 6 + len(names)]
    out_ref, alone_ref, acc, ready, sems = rest[6 + len(names) :]
    rows = ready.shape[0]
    first = pltpu.make_async_copy(earlier, out_ref.at[pl.ds(0, rows)], sems.at[0])
    first.start()
    fields = stage_setup(
        "corner",
        plan,
        t_size,
        names,
        received,
        perm_ref,
        x_ref,
        u_ref,
        [own_shared, z_shared, t_shared],
        None,
        alone_ref,
    )
    near, both, weight = scale_tiles(scale_ref)
    add_terms(fields, "corner", near, acc)
    direct = own_force(fields, 2, both)
    for k in range(9):
        staples = fields.compact_halves(acc_tile(acc, 0, 2 * k), acc_tile(acc, 0, 2 * k + 1))
        ready[pl.ds(k * 8, 8), :] = part_reg(z_part, 2, k) + direct[k] + weight[2] * staples[0]
        ready[pl.ds((9 + k) * 8, 8), :] = part_reg(t_part, 0, k) + weight[3] * staples[1]
    second = pltpu.make_async_copy(ready, out_ref.at[pl.ds(rows, rows)], sems.at[1])
    second.start()
    first.wait()
    second.wait()


def rows_of(count):
    return jax.ShapeDtypeStruct((count, LANES), F32)


def on_device(pole_vectors, gauge_links, pole_coeff, naik_coeff, staple_weight):
    t_size = lax.axis_size("ta")
    z_size = lax.axis_size("gz") * lax.axis_size("gy")
    plan = message_plan(t_size)
    x_rows, u_rows = 8 * REGS["x"], 4 * 8 * REGS["u"]
    vmem = pl.BlockSpec(memory_space=pltpu.VMEM)
    hbm = pl.BlockSpec(memory_space=pltpu.HBM)
    limit = pltpu.CompilerParams(vmem_limit_bytes=4 * 1024 * 1024)

    def moved(name, value):
        kind, step = name
        if kind == "z":
            return lax.ppermute(value, ("gz", "gy"), [((i + step) % z_size, i) for i in range(z_size)])
        return lax.ppermute(value, "ta", [((j + step) % t_size, j) for j in range(t_size)])

    def exchanged(value, first):
        pairs = [(i, (i + 1) % z_size) for i in range(first, z_size, 2)]
        return lax.ppermute(value, ("gz", "gy"), pairs + [(j, i) for i, j in pairs])

    first_names = [name for name in plan if name[0] != "c"]
    corner_names = [name for name in plan if name[0] == "c"]
    t_names = [name for name in first_names if name[0] == "t"]
    in_hbm = functools.partial(pltpu.with_memory_space_constraint, memory_space=pltpu.HBM)
    beyond_rows = 8 * plan["z", 2].count
    ahead_rows, behind_rows = [8 * plan["z", step].count for step in (1, -1)]
    shared_rows = max(ahead_rows, behind_rows)
    within, between, beyond, scale, perm, *own = pl.pallas_call(
        functools.partial(pack_z_kernel, plan),
        out_shape=[rows_of(shared_rows), rows_of(shared_rows + 8), rows_of(beyond_rows)]
        + [
            rows_of(8 * 3 * NP),
            jax.ShapeDtypeStruct((len(all_shifts()) * LANES, LANES), jnp.bfloat16),
            rows_of(x_rows),
            rows_of(u_rows),
        ],
        in_specs=[hbm] * 5,
        out_specs=[vmem] * 7,
        scratch_shapes=[pltpu.SMEM((NP,), F32)] * 3
        + [pltpu.VMEM((u_rows, LANES), jnp.bfloat16), pltpu.SemaphoreType.DMA((5,))],
        compiler_params=limit,
        name="pack_z",
    )(
        in_hbm(pole_coeff),
        in_hbm(naik_coeff),
        in_hbm(staple_weight),
        in_hbm(pole_vectors.reshape((x_rows, LANES))),
        in_hbm(gauge_links.reshape((u_rows, LANES))),
    )
    between, within = exchanged(between, 1), exchanged(within, 0)
    received = {("z", 2): moved(("z", 2), beyond)}
    packed = pl.pallas_call(
        functools.partial(pack_t_kernel, plan, t_names),
        out_shape=[rows_of(8 * plan[name].count) for name in t_names],
        in_specs=[vmem] * 2,
        out_specs=[vmem] * len(t_names),
        compiler_params=limit,
        name="pack_t",
    )(*own)
    received.update({name: moved(name, value) for name, value in zip(t_names, packed)})
    shared, alone = field_split()
    part_rows = 8 * REGS["u"]

    def scratch(stage):
        sums = 1 + max(target for target, _ in TERMS[stage])
        return [pltpu.VMEM((alone[stage][1], LANES), F32), pltpu.VMEM((sums * 18 * 8, LANES), F32)]

    def cost(micros):
        return pl.CostEstimate(flops=10**6, bytes_accessed=int(3.69e6 * micros), transcendentals=0)

    wide_limit = pltpu.CompilerParams(vmem_limit_bytes=6 * 1024 * 1024)
    own_shared, own_alone = pl.pallas_call(
        functools.partial(own_fields_kernel, plan, t_size),
        out_shape=[rows_of(shared["own"][1]), rows_of(alone["own"][1])],
        in_specs=[vmem] * 3,
        out_specs=[vmem] * 2,
        compiler_params=wide_limit,
        name="fields_own",
    )(perm, *own)
    own_part = pl.pallas_call(
        own_kernel,
        out_shape=rows_of(2 * part_rows),
        in_specs=[vmem] * 5,
        out_specs=vmem,
        scratch_shapes=scratch("own")[1:],
        cost_estimate=cost(COSTS["own"]),
        compiler_params=wide_limit,
        name="force_own",
    )(scale, *own, own_shared, own_alone)
    local = [scale, perm, *own]
    received["z", 1], received["z", -1], *corners = pl.pallas_call(
        functools.partial(corner_kernel, plan, corner_names),
        out_shape=[rows_of(ahead_rows), rows_of(behind_rows)]
        + [rows_of(8 * plan[name].count) for name in corner_names],
        in_specs=[vmem] * 3,
        out_specs=[vmem] * (2 + len(corner_names)),
        compiler_params=limit,
        name="pack_corners",
    )(within, between, own_part)
    received.update({name: moved(name, value) for name, value in zip(corner_names, corners)})
    names = [("z", 1), ("z", -1)]
    z_shared, z_part = pl.pallas_call(
        functools.partial(z_kernel, plan, t_size, names),
        out_shape=[rows_of(shared["z"][1]), rows_of(3 * part_rows)],
        in_specs=[vmem] * (6 + len(names)),
        out_specs=[vmem] * 2,
        scratch_shapes=scratch("z"),
        cost_estimate=cost(COSTS["z"]),
        compiler_params=wide_limit,
        name="force_z",
    )(*local, own_shared, own_part, *[received[name] for name in names])
    t_shared, t_part, earlier = pl.pallas_call(
        functools.partial(t_kernel, plan, t_size, t_names),
        out_shape=[rows_of(shared["t"][1]), rows_of(part_rows), rows_of(2 * part_rows)],
        in_specs=[vmem] * (7 + len(t_names)),
        out_specs=[vmem] * 3,
        scratch_shapes=scratch("t"),
        cost_estimate=cost(COSTS["t"]),
        compiler_params=wide_limit,
        name="force_t",
    )(*local, own_shared, z_shared, z_part, *[received[name] for name in t_names])
    names = list(received)
    force = pl.pallas_call(
        functools.partial(last_kernel, plan, t_size, names),
        out_shape=rows_of(u_rows),
        in_specs=[vmem] * (10 + len(names)),
        out_specs=hbm,
        scratch_shapes=scratch("corner")
        + [pltpu.VMEM((2 * part_rows, LANES), F32), pltpu.SemaphoreType.DMA((2,))],
        cost_estimate=cost(COSTS["corner"]),
        compiler_params=wide_limit,
        name="force_corner",
    )(
        *local,
        own_shared,
        z_shared,
        t_shared,
        z_part,
        t_part,
        earlier,
        *[received[name] for name in names],
    )
    return force.reshape(gauge_links.shape)


def solution(mesh):
    return jax.shard_map(
        on_device,
        mesh=mesh,
        in_specs=(
            P("ens", None, None, "ta", ("gz", "gy"), None),
            P("ens", None, None, None, "ta", ("gz", "gy"), None),
            P(),
            P(),
            P(),
        ),
        out_specs=P("ens", None, None, None, "ta", ("gz", "gy"), None),
        check_vma=False,
    )
```

```python
import collections
import functools

import jax
import jax.numpy as jnp
from jax import lax
from jax.experimental import pallas as pl
from jax.experimental.pallas import tpu as pltpu
from jax.sharding import PartitionSpec as P

NX = 8
NY = 16
LANES = NX * NY
NP = 4
F32 = jnp.float32
REGS = {"x": NP * 3, "u": 9}
UNIT = ((1, 0, 0, 0), (0, 1, 0, 0), (0, 0, 1, 0), (0, 0, 0, 1))
ZERO = (0, 0, 0, 0)
SITES = ((0, 0), (0, 1), (1, 0), (1, 1))
STAGES = ("own", "z", "t", "corner")
TERMS = {
    "own": ((0, ((0, 1), (1, 0))),),
    "z": ((0, ((0, 2), (1, 2))),),
    "t": ((0, ((0, 3), (1, 3))), (1, ((3, 0), (3, 1))), (2, ((2, 0), (2, 1)))),
    "corner": ((0, ((2, 3), (3, 2))),),
}
COSTS = {"own": 2.0, "z": 2.0, "t": 2.0, "corner": 1.0}
DIRECT = {"own": (0, 1), "z": (), "t": (3,), "corner": (2,)}


def plus(left, right, scale=1):
    return tuple(a + scale * b for a, b in zip(left, right))


class Message:
    def __init__(self):
        self.places = collections.OrderedDict()
        self.count = 0

    def add_full(self, kind, n):
        for k in range(REGS[kind]):
            for t, z in SITES:
                self.places[0, kind, n, k, t, z] = (self.count, 2 * t + z)
            self.count += 1

    def add_halves(self, entries, axis):
        half = -(-len(entries) // 2)
        for index, (kind, n, k, layer) in enumerate(entries):
            reg, part = self.count + index % half, index // half
            for other in range(2):
                t, z = (layer, other) if axis == "t" else (other, layer)
                slot = 2 * part + other if axis == "t" else 2 * other + part
                self.places[0, kind, n, k, t, z] = (reg, slot)
        self.count += half

    def add_single(self, entries):
        quarter = -(-len(entries) // 4)
        for index, entry in enumerate(entries):
            self.places[entry] = (self.count + index % quarter, index // quarter)
        self.count += quarter

    def by_register(self):
        found = [[None] * 4 for _ in range(self.count)]
        for item, (reg, slot) in self.places.items():
            found[reg][slot] = item
        return found


def regs_of(kind, directions, layer):
    return [(kind, n, k, layer) for n in directions for k in range(REGS[kind])]


def message_plan(t_size):
    plan = collections.OrderedDict()
    ahead = plan["z", 1] = Message()
    ahead.add_halves(regs_of("x", (0,), 0) + regs_of("u", (3,), 0), "z")
    late = plan["b", 1] = Message()
    late.add_halves(regs_of("x", (0,), 1) + regs_of("u", (0, 1), 0), "z")
    behind = plan["z", -1] = Message()
    behind.add_halves(regs_of("x", (0,), 1) + regs_of("u", (2,), 1), "z")
    second = plan["z", 2] = Message()
    second.add_halves(regs_of("x", (0,), 0), "z")
    halves, corners = collections.OrderedDict(), collections.OrderedDict()
    for dt, entries in (
        (1, regs_of("u", (0, 1, 2), 0)),
        (-1, regs_of("x", (0,), 1) + regs_of("u", (3,), 1)),
        (2, regs_of("x", (0,), 0)),
    ):
        if dt % t_size != 0:
            halves.setdefault(dt % t_size, []).extend(entries)
    for dt, entries in halves.items():
        message = plan["t", dt] = Message()
        if dt == 1:
            message.add_full("x", 0)
        held = {item[1:4] for item in message.places}
        message.add_halves([e for e in entries if e[:3] not in held], "t")
    for dt, entries in (
        (1, [(1, "x", 0, k, 0, 0) for k in range(REGS["x"])]),
        (1, [(-1, "x", 0, k, 0, 1) for k in range(REGS["x"])]),
        (1, [(-1, "u", 2, k, 0, 1) for k in range(REGS["u"])]),
        (-1, [(1, "x", 0, k, 1, 0) for k in range(REGS["x"])]),
        (-1, [(1, "u", 3, k, 1, 0) for k in range(REGS["u"])]),
    ):
        corners.setdefault(dt % t_size, []).extend(entries)
    for dt, entries in corners.items():
        plan["c", dt] = Message()
        plan["c", dt].add_single(entries)
    return plan


class Locator:
    def __init__(self, plan, t_size, buffers):
        self.plan, self.t_size, self.buffers = plan, t_size, buffers

    def local(self, kind, n, k, t, z):
        return ("own", kind), n * REGS[kind] + k, 2 * t + z

    def find(self, kind, n, k, t_at, z_at):
        (dt, t), (dz, z) = divmod(t_at, 2), divmod(z_at, 2)
        dt %= self.t_size
        if (dt, dz) == (0, 0):
            return self.local(kind, n, k, t, z)
        name = ("z", dz) if dt == 0 else ("t", dt) if dz == 0 else ("c", dt)
        item = (dz if name[0] == "c" else 0, kind, n, k, t, z)
        if name == ("z", 1) and item not in self.plan[name].places:
            name = ("b", 1)
        return (name,) + self.plan[name].places[item]

    def load(self, name, reg):
        return self.buffers[name][pl.ds(8 * reg, 8), :]

    def assemble(self, spots):
        groups = collections.OrderedDict()
        for r, spot in enumerate(spots):
            if spot is not None:
                groups.setdefault((spot[0], spot[1], r - spot[2]), []).append(r)
        row = lax.broadcasted_iota(jnp.int32, (8, LANES), 0) % 4
        result = None
        for (name, reg, move), rows in groups.items():
            value = self.load(name, reg)
            if move != 0:
                value = pltpu.roll(value, move % 8, 0)
            if result is None:
                result = value
            else:
                mask = functools.reduce(jnp.logical_or, [row == r for r in rows])
                result = jnp.where(mask, value, result)
        return result

    def field_register(self, kind, n, k, dt, dz):
        return self.assemble([self.find(kind, n, k, t + dt, z + dz) for t, z in SITES])


def term_fields(halves, sign):
    here, ahead, left, right = [], [], [], []
    for m, n in halves:
        start = plus(ZERO, UNIT[n], sign)
        base = ZERO if sign > 0 else start
        here.append(("x", 0, start))
        ahead.append(("x", 0, plus(start, UNIT[m])))
        left.append(("u", n, base))
        right.append(("u", n, plus(base, UNIT[m])))
    return here, ahead, left, right


def needed_fields(stage):
    keys = collections.OrderedDict()
    for _, halves in TERMS[stage]:
        for sign in (1, -1):
            for pair in term_fields(halves, sign):
                keys.update((key, None) for key in pair)
    for m in DIRECT[stage]:
        for scale in (1, 3):
            keys["x", 0, plus(ZERO, UNIT[m], scale)] = None
    return [key for key in keys if key[2] != ZERO]


def stage_of(key):
    dz, dt = key[2][2:]
    if key[0] == "u" and key[1] < 2 and dz == 1 and dt == 0:
        return "t"
    if abs(dz) == 3 or (dz != 0 and dt != 0):
        return "corner"
    return "t" if dt != 0 else "z" if dz != 0 else "own"


def lay_out(keys):
    rows, total = collections.OrderedDict(), 0
    for key in keys:
        rows[key] = total
        total += 8 * REGS[key[0]]
    return rows, total


def field_split():
    uses = collections.OrderedDict()
    for stage in STAGES:
        for key in needed_fields(stage):
            uses.setdefault(key, []).append(stage)
    shared, alone = {}, {}
    for stage in STAGES:
        built = [key for key in uses if stage_of(key) == stage]
        shared[stage] = lay_out([key for key in built if uses[key] != [stage]])
        alone[stage] = lay_out([key for key in built if uses[key] == [stage]])
    return shared, alone


def all_shifts():
    found = collections.OrderedDict()
    for stage in STAGES:
        for _, _, (dx, dy, _, _) in needed_fields(stage):
            if (dx, dy) != (0, 0):
                found[dx, dy] = None
    return list(found)


def write_shifts(perm_ref):
    lane = lax.broadcasted_iota(jnp.int32, (LANES, LANES), 1)
    source = lax.broadcasted_iota(jnp.int32, (LANES, LANES), 0)
    for index, (dx, dy) in enumerate(all_shifts()):
        wanted = (lane // NX + dy + NY) % NY * NX + (lane + dx + NX) % NX
        perm_ref[pl.ds(index * LANES, LANES), :] = (source == wanted).astype(F32).astype(jnp.bfloat16)


def parts_of(kind, value):
    if kind == "u":
        return [value.astype(jnp.bfloat16)]
    high = value.astype(jnp.bfloat16)
    rest = value - high.astype(F32)
    middle = rest.astype(jnp.bfloat16)
    return [high, middle, (rest - middle.astype(F32)).astype(jnp.bfloat16)]


def build_fields(locator, perm_ref, stores):
    groups = collections.OrderedDict()
    for ref, rows in stores:
        for (kind, n, disp), row in rows.items():
            shifts = groups.setdefault((kind, n, disp[3], disp[2]), collections.OrderedDict())
            shifts[disp[0], disp[1]] = (ref, row)
    order = all_shifts()
    for (kind, n, dt, dz), shifts in groups.items():
        regs = [locator.field_register(kind, n, k, dt, dz) for k in range(REGS[kind])]
        if (0, 0) in shifts:
            ref, row = shifts[0, 0]
            for k, value in enumerate(regs):
                ref[pl.ds(row + 8 * k, 8), :] = value
        parts = parts_of(kind, jnp.concatenate(regs, axis=0))
        for shift, (ref, row) in shifts.items():
            if shift != (0, 0):
                perm = perm_ref[pl.ds(order.index(shift) * LANES, LANES), :]
                moved = [jnp.dot(part, perm, preferred_element_type=F32) for part in parts]
                ref[pl.ds(row, 8 * REGS[kind]), :] = functools.reduce(jnp.add, moved)


class Fields:
    def __init__(self, own_x, own_u, stores):
        self.place = {("x", 0, ZERO): (own_x, 0)}
        for n in range(4):
            self.place["u", n, ZERO] = (own_u, 8 * REGS["u"] * n)
        for ref, rows in stores:
            for key, row in rows.items():
                self.place[key] = (ref, row)
        self.upper = lax.broadcasted_iota(jnp.int32, (8, LANES), 0) < 4

    def reg(self, key, k):
        ref, row = self.place[key]
        return ref[pl.ds(row + 8 * k, 8), :]

    def two_tiles(self, keys, k):
        top = self.reg(keys[0], k)
        turned_top = pltpu.roll(top, 4, 0)
        if keys[0] == keys[1]:
            low, turned_low = top, turned_top
        else:
            low = self.reg(keys[1], k)
            turned_low = pltpu.roll(low, 4, 0)
        return [jnp.where(self.upper, top, turned_low), jnp.where(self.upper, turned_top, low)]

    def vector(self, keys, pole):
        flat = [tile for k in range(3) for tile in self.two_tiles(keys, 3 * pole + k)]
        return [flat[:3], flat[3:]]

    def matrix(self, keys):
        flat = [tile for k in range(9) for tile in self.two_tiles(keys, k)]
        return [[flat[9 * c + 3 * i : 9 * c + 3 * i + 3] for i in range(3)] for c in range(2)]

    def compact_halves(self, first, second):
        top = jnp.where(self.upper, first, pltpu.roll(second, 4, 0))
        return top, jnp.where(self.upper, pltpu.roll(first, 4, 0), second)

    def compact_sum(self, first, second):
        kept = jnp.where(self.upper, first, second)
        return kept + pltpu.roll(jnp.where(self.upper, second, first), 4, 0)


def pole_sum(fields, here, ahead, scales):
    total = None
    for pole in range(NP):
        h = [[scales[pole] * v for v in part] for part in fields.vector(here, pole)]
        a = fields.vector(ahead, pole)
        real = [[a[0][i] * h[0][j] + a[1][i] * h[1][j] for j in range(3)] for i in range(3)]
        imag = [[a[1][i] * h[0][j] - a[0][i] * h[1][j] for j in range(3)] for i in range(3)]
        if total is None:
            total = [real, imag]
        else:
            total = [
                [[total[c][i][j] + new[i][j] for j in range(3)] for i in range(3)]
                for c, new in enumerate((real, imag))
            ]
    return total


def transposed(matrix):
    return [[[part[j][i] for j in range(3)] for i in range(3)] for part in matrix]


def row_times(row, right, row_sign, right_sign):
    result = [[], []]
    for j in range(3):
        real = imag = None
        for k in range(3):
            rr = row[0][k] * right[0][k][j]
            ii = row[1][k] * right[1][k][j]
            ri = row[0][k] * right[1][k][j]
            ir = row[1][k] * right[0][k][j]
            new_real = rr - ii if row_sign * right_sign > 0 else rr + ii
            if row_sign > 0 and right_sign > 0:
                new_imag = ri + ir
            elif row_sign > 0:
                new_imag = ir - ri
            else:
                new_imag = ri - ir
            real = new_real if real is None else real + new_real
            imag = new_imag if imag is None else imag + new_imag
        result[0].append(real)
        result[1].append(imag)
    return result


def add_terms(fields, stage, near, acc):
    started = set()
    for target, halves in TERMS[stage]:
        for sign in (1, -1):
            here, ahead, left, right = term_fields(halves, sign)
            force = pole_sum(fields, here, ahead, near)
            left = fields.matrix(left)
            right = fields.matrix(right)
            if sign > 0:
                right = transposed(right)
            else:
                left = transposed(left)
            rows = [row_times([left[0][i], left[1][i]], force, sign, 1) for i in range(3)]
            for i in range(3):
                row = row_times(rows[i], right, 1, -sign)
                for part in range(2):
                    for j in range(3):
                        at = pl.ds((target * 18 + part * 9 + i * 3 + j) * 8, 8)
                        new = row[part][j]
                        acc[at, :] = acc[at, :] + new if target in started else new
            started.add(target)


def acc_tile(acc, target, c):
    return acc[pl.ds((target * 18 + c) * 8, 8), :]


def scale_tiles(scale_ref):
    tiles = [scale_ref[pl.ds(8 * p, 8), :] for p in range(3 * NP)]
    return tiles[:NP], tiles[NP : 2 * NP], tiles[2 * NP :]


def own_force(fields, m, both):
    total = pole_sum(
        fields,
        [("x", 0, ZERO)] * 2,
        [("x", 0, UNIT[m]), ("x", 0, plus(ZERO, UNIT[m], 3))],
        both,
    )
    flat = [total[c][i][j] for c in range(2) for i in range(3) for j in range(3)]
    return [fields.compact_sum(flat[2 * k], flat[2 * k + 1]) for k in range(9)]


def write_messages(locator, plan, names, outs):
    for name, out in zip(names, outs):
        for reg, items in enumerate(plan[name].by_register()):
            spots = [item and locator.local(*item[1:]) for item in items]
            out[pl.ds(8 * reg, 8), :] = locator.assemble(spots)


def pack_z_kernel(plan, names, near_in, far_in, weight_in, x_in, u_in, *rest):
    outs = rest[: len(names)]
    scale_ref, perm_ref, x_ref, u_ref, near_ref, far_ref, weight_ref, u_held, sems = rest[len(names) :]
    copies = [
        pltpu.make_async_copy(source, target, sems.at[index])
        for index, (source, target) in enumerate(
            ((u_in, u_held), (x_in, x_ref), (near_in, near_ref), (far_in, far_ref), (weight_in, weight_ref))
        )
    ]
    for copy in copies:
        copy.start()
    write_shifts(perm_ref)
    for copy in copies:
        copy.wait()
    u_ref[...] = u_held[...].astype(F32)
    locator = Locator(plan, 1, {("own", "x"): x_ref, ("own", "u"): u_ref})
    write_messages(locator, plan, names, outs)
    write_scales(near_ref, far_ref, weight_ref, scale_ref)


def pack_t_kernel(plan, names, x_ref, u_ref, *outs):
    write_messages(Locator(plan, 1, {("own", "x"): x_ref, ("own", "u"): u_ref}), plan, names, outs)


def corner_kernel(plan, names, ahead_ref, behind_ref, _, *outs):
    locator = Locator(plan, 1, {("z", 1): ahead_ref, ("z", -1): behind_ref})
    for name, out in zip(names, outs):
        for reg, items in enumerate(plan[name].by_register()):
            spots = [
                item and (("z", item[0]),) + plan["z", item[0]].places[(0,) + item[1:]] for item in items
            ]
            out[pl.ds(8 * reg, 8), :] = locator.assemble(spots)


def part_reg(ref, index, k):
    return ref[pl.ds((9 * index + k) * 8, 8), :]


def write_scales(near_ref, far_ref, weight_ref, scale_ref):
    upper = lax.broadcasted_iota(jnp.int32, (8, LANES), 0) < 4
    for p in range(NP):
        scale_ref[pl.ds(8 * p, 8), :] = jnp.full((8, LANES), near_ref[p], F32)
        scale_ref[pl.ds(8 * (NP + p), 8), :] = jnp.where(upper, near_ref[p], far_ref[p])
        scale_ref[pl.ds(8 * (2 * NP + p), 8), :] = jnp.full((8, LANES), weight_ref[p], F32)


def own_fields_kernel(plan, t_size, perm_ref, x_ref, u_ref, shared_ref, alone_ref):
    shared, alone = field_split()
    stores = [(shared_ref, shared["own"][0]), (alone_ref, alone["own"][0])]
    build_fields(Locator(plan, t_size, {("own", "x"): x_ref, ("own", "u"): u_ref}), perm_ref, stores)


def own_kernel(scale_ref, x_ref, u_ref, shared_ref, alone_ref, part_ref, acc):
    shared, alone = field_split()
    fields = Fields(x_ref, u_ref, [(shared_ref, shared["own"][0]), (alone_ref, alone["own"][0])])
    near, both, weight = scale_tiles(scale_ref)
    add_terms(fields, "own", near, acc)
    direct = [own_force(fields, m, both) for m in DIRECT["own"]]
    for k in range(9):
        staples = fields.compact_halves(acc_tile(acc, 0, 2 * k), acc_tile(acc, 0, 2 * k + 1))
        for m in range(2):
            part_ref[pl.ds((9 * m + k) * 8, 8), :] = direct[m][k] + weight[m] * staples[m]


def stage_setup(stage, plan, t_size, names, received, perm_ref, x_ref, u_ref, shared_refs, shared_ref, alone_ref):
    buffers = {("own", "x"): x_ref, ("own", "u"): u_ref}
    buffers.update(zip(names, received))
    shared, alone = field_split()
    stores = [(alone_ref, alone[stage][0])]
    if shared_ref is not None:
        stores.append((shared_ref, shared[stage][0]))
    build_fields(Locator(plan, t_size, buffers), perm_ref, stores)
    earlier = [(ref, shared[name][0]) for name, ref in zip(STAGES, shared_refs)]
    return Fields(x_ref, u_ref, earlier + stores)


def z_kernel(plan, t_size, names, scale_ref, perm_ref, x_ref, u_ref, own_shared, own_part, *rest):
    received = rest[: len(names)]
    shared_ref, part_ref, alone_ref, acc = rest[len(names) :]
    fields = stage_setup(
        "z", plan, t_size, names, received, perm_ref, x_ref, u_ref, [own_shared], shared_ref, alone_ref
    )
    near, _, weight = scale_tiles(scale_ref)
    add_terms(fields, "z", near, acc)
    for k in range(9):
        staples = fields.compact_halves(acc_tile(acc, 0, 2 * k), acc_tile(acc, 0, 2 * k + 1))
        for m in range(2):
            part_ref[pl.ds((9 * m + k) * 8, 8), :] = part_reg(own_part, m, k) + weight[m] * staples[m]


def t_kernel(plan, t_size, names, scale_ref, perm_ref, x_ref, u_ref, own_shared, z_shared, z_part, *rest):
    received = rest[: len(names)]
    shared_ref, part_ref, ready, alone_ref, acc = rest[len(names) :]
    fields = stage_setup(
        "t", plan, t_size, names, received, perm_ref, x_ref, u_ref, [own_shared, z_shared], shared_ref, alone_ref
    )
    near, both, weight = scale_tiles(scale_ref)
    add_terms(fields, "t", near, acc)
    for k in range(9):
        staples = fields.compact_halves(acc_tile(acc, 0, 2 * k), acc_tile(acc, 0, 2 * k + 1))
        for m in range(2):
            ready[pl.ds((9 * m + k) * 8, 8), :] = part_reg(z_part, m, k) + weight[m] * staples[m]
    direct = own_force(fields, 3, both)
    for k in range(9):
        staple = fields.compact_sum(acc_tile(acc, 1, 2 * k), acc_tile(acc, 1, 2 * k + 1))
        part_ref[pl.ds(k * 8, 8), :] = direct[k] + weight[3] * staple
        staple = fields.compact_sum(acc_tile(acc, 2, 2 * k), acc_tile(acc, 2, 2 * k + 1))
        part_ref[pl.ds((9 + k) * 8, 8), :] = weight[2] * staple


def last_kernel(plan, t_size, names, scale_ref, perm_ref, x_ref, u_ref, *rest):
    own_shared, z_shared, t_shared, t_part, earlier = rest[:5]
    received = rest[5 : 5 + len(names)]
    out_ref, alone_ref, acc, ready, sems = rest[5 + len(names) :]
    rows = ready.shape[0]
    first = pltpu.make_async_copy(earlier, out_ref.at[pl.ds(0, rows)], sems.at[0])
    first.start()
    fields = stage_setup(
        "corner",
        plan,
        t_size,
        names,
        received,
        perm_ref,
        x_ref,
        u_ref,
        [own_shared, z_shared, t_shared],
        None,
        alone_ref,
    )
    near, both, weight = scale_tiles(scale_ref)
    add_terms(fields, "corner", near, acc)
    direct = own_force(fields, 2, both)
    for k in range(9):
        staples = fields.compact_halves(acc_tile(acc, 0, 2 * k), acc_tile(acc, 0, 2 * k + 1))
        ready[pl.ds(k * 8, 8), :] = part_reg(t_part, 1, k) + direct[k] + weight[2] * staples[0]
        ready[pl.ds((9 + k) * 8, 8), :] = part_reg(t_part, 0, k) + weight[3] * staples[1]
    second = pltpu.make_async_copy(ready, out_ref.at[pl.ds(rows, rows)], sems.at[1])
    second.start()
    first.wait()
    second.wait()


def rows_of(count):
    return jax.ShapeDtypeStruct((count, LANES), F32)


def on_device(pole_vectors, gauge_links, pole_coeff, naik_coeff, staple_weight):
    t_size = lax.axis_size("ta")
    z_size = lax.axis_size("gz") * lax.axis_size("gy")
    plan = message_plan(t_size)
    x_rows, u_rows = 8 * REGS["x"], 4 * 8 * REGS["u"]
    vmem = pl.BlockSpec(memory_space=pltpu.VMEM)
    hbm = pl.BlockSpec(memory_space=pltpu.HBM)
    limit = pltpu.CompilerParams(vmem_limit_bytes=4 * 1024 * 1024)

    def moved(name, value):
        kind, step = name
        if kind in ("z", "b"):
            return lax.ppermute(value, ("gz", "gy"), [((i + step) % z_size, i) for i in range(z_size)])
        return lax.ppermute(value, "ta", [((j + step) % t_size, j) for j in range(t_size)])

    first_names = [name for name in plan if name[0] != "c"]
    corner_names = [name for name in plan if name[0] == "c"]
    t_names = [name for name in first_names if name[0] == "t"]
    in_hbm = functools.partial(pltpu.with_memory_space_constraint, memory_space=pltpu.HBM)
    z_names = [name for name in first_names if name[0] != "t"]
    least = {
        ("z", 2): max(plan[name].count for name in corner_names),
        ("z", -1): plan["z", 1].count + 1,
    }
    *sends, scale, perm, x_own, u_own = pl.pallas_call(
        functools.partial(pack_z_kernel, plan, z_names),
        out_shape=[rows_of(8 * max(plan[name].count, least.get(name, 0))) for name in z_names]
        + [
            rows_of(8 * 3 * NP),
            jax.ShapeDtypeStruct((len(all_shifts()) * LANES, LANES), jnp.bfloat16),
            rows_of(x_rows),
            rows_of(u_rows),
        ],
        in_specs=[hbm] * 5,
        out_specs=[vmem] * (len(z_names) + 4),
        scratch_shapes=[pltpu.SMEM((NP,), F32)] * 3
        + [pltpu.VMEM((u_rows, LANES), jnp.bfloat16), pltpu.SemaphoreType.DMA((5,))],
        compiler_params=limit,
        name="pack_z",
    )(
        in_hbm(pole_coeff),
        in_hbm(naik_coeff),
        in_hbm(staple_weight),
        in_hbm(pole_vectors.reshape((x_rows, LANES))),
        in_hbm(gauge_links.reshape((u_rows, LANES))),
    )
    own = [x_own, u_own]
    received = {name: moved(name, value) for name, value in zip(z_names, sends)}
    packed = pl.pallas_call(
        functools.partial(pack_t_kernel, plan, t_names),
        out_shape=[rows_of(8 * plan[name].count) for name in t_names],
        in_specs=[vmem] * 2,
        out_specs=[vmem] * len(t_names),
        compiler_params=limit,
        name="pack_t",
    )(*own)
    received.update({name: moved(name, value) for name, value in zip(t_names, packed)})
    shared, alone = field_split()
    part_rows = 8 * REGS["u"]

    def scratch(stage):
        sums = 1 + max(target for target, _ in TERMS[stage])
        return [pltpu.VMEM((alone[stage][1], LANES), F32), pltpu.VMEM((sums * 18 * 8, LANES), F32)]

    def cost(micros):
        return pl.CostEstimate(flops=10**6, bytes_accessed=int(3.69e6 * micros), transcendentals=0)

    wide_limit = pltpu.CompilerParams(vmem_limit_bytes=6 * 1024 * 1024)
    own_shared, own_alone = pl.pallas_call(
        functools.partial(own_fields_kernel, plan, t_size),
        out_shape=[rows_of(shared["own"][1]), rows_of(alone["own"][1])],
        in_specs=[vmem] * 3,
        out_specs=[vmem] * 2,
        compiler_params=wide_limit,
        name="fields_own",
    )(perm, *own)
    own_part = pl.pallas_call(
        own_kernel,
        out_shape=rows_of(2 * part_rows),
        in_specs=[vmem] * 5,
        out_specs=vmem,
        scratch_shapes=scratch("own")[1:],
        cost_estimate=cost(COSTS["own"]),
        compiler_params=wide_limit,
        name="force_own",
    )(scale, *own, own_shared, own_alone)
    local = [scale, perm, *own]
    corners = pl.pallas_call(
        functools.partial(corner_kernel, plan, corner_names),
        out_shape=[rows_of(8 * plan[name].count) for name in corner_names],
        in_specs=[vmem] * 3,
        out_specs=[vmem] * len(corner_names),
        compiler_params=limit,
        name="pack_corners",
    )(received["z", 1], received["z", -1], own_part)
    received.update({name: moved(name, value) for name, value in zip(corner_names, corners)})
    names = [("z", 1), ("z", -1)]
    z_shared, z_part = pl.pallas_call(
        functools.partial(z_kernel, plan, t_size, names),
        out_shape=[rows_of(shared["z"][1]), rows_of(2 * part_rows)],
        in_specs=[vmem] * (6 + len(names)),
        out_specs=[vmem] * 2,
        scratch_shapes=scratch("z"),
        cost_estimate=cost(COSTS["z"]),
        compiler_params=wide_limit,
        name="force_z",
    )(*local, own_shared, own_part, *[received[name] for name in names])
    far_names = t_names + [("b", 1)]
    t_shared, t_part, earlier = pl.pallas_call(
        functools.partial(t_kernel, plan, t_size, far_names),
        out_shape=[rows_of(shared["t"][1]), rows_of(2 * part_rows), rows_of(2 * part_rows)],
        in_specs=[vmem] * (7 + len(far_names)),
        out_specs=[vmem] * 3,
        scratch_shapes=scratch("t"),
        cost_estimate=cost(COSTS["t"]),
        compiler_params=wide_limit,
        name="force_t",
    )(*local, own_shared, z_shared, z_part, *[received[name] for name in far_names])
    names = list(received)
    force = pl.pallas_call(
        functools.partial(last_kernel, plan, t_size, names),
        out_shape=rows_of(u_rows),
        in_specs=[vmem] * (9 + len(names)),
        out_specs=hbm,
        scratch_shapes=scratch("corner")
        + [pltpu.VMEM((2 * part_rows, LANES), F32), pltpu.SemaphoreType.DMA((2,))],
        cost_estimate=cost(COSTS["corner"]),
        compiler_params=wide_limit,
        name="force_corner",
    )(
        *local,
        own_shared,
        z_shared,
        t_shared,
        t_part,
        earlier,
        *[received[name] for name in names],
    )
    return force.reshape(gauge_links.shape)


def solution(mesh):
    return jax.shard_map(
        on_device,
        mesh=mesh,
        in_specs=(
            P("ens", None, None, "ta", ("gz", "gy"), None),
            P("ens", None, None, None, "ta", ("gz", "gy"), None),
            P(),
            P(),
            P(),
        ),
        out_specs=P("ens", None, None, None, "ta", ("gz", "gy"), None),
        check_vma=False,
    )
```

```python
import collections
import functools

import jax
import jax.numpy as jnp
from jax import lax
from jax.experimental import pallas as pl
from jax.experimental.pallas import tpu as pltpu
from jax.sharding import PartitionSpec as P

NX = 8
NY = 16
LANES = NX * NY
NP = 4
F32 = jnp.float32
REGS = {"x": NP * 3, "u": 9}
UNIT = ((1, 0, 0, 0), (0, 1, 0, 0), (0, 0, 1, 0), (0, 0, 0, 1))
ZERO = (0, 0, 0, 0)
SITES = ((0, 0), (0, 1), (1, 0), (1, 1))
STAGES = ("own", "z", "t", "corner")
TERMS = {
    "own": ((0, ((0, 1), (1, 0))),),
    "z": ((0, ((0, 2), (1, 2))),),
    "t": ((0, ((0, 3), (1, 3))), (1, ((3, 0), (3, 1))), (2, ((2, 0), (2, 1)))),
    "corner": ((0, ((2, 3), (3, 2))),),
}
COSTS = {"own": 2.0, "z": 2.0, "t": 2.0, "corner": 1.0}
DIRECT = {"own": (0, 1), "z": (), "t": (3,), "corner": (2,)}


def plus(left, right, scale=1):
    return tuple(a + scale * b for a, b in zip(left, right))


class Message:
    def __init__(self):
        self.places = collections.OrderedDict()
        self.count = 0

    def add_full(self, kind, n):
        for k in range(REGS[kind]):
            for t, z in SITES:
                self.places[0, kind, n, k, t, z] = (self.count, 2 * t + z)
            self.count += 1

    def add_halves(self, entries, axis):
        half = -(-len(entries) // 2)
        for index, (kind, n, k, layer) in enumerate(entries):
            reg, part = self.count + index % half, index // half
            for other in range(2):
                t, z = (layer, other) if axis == "t" else (other, layer)
                slot = 2 * part + other if axis == "t" else 2 * other + part
                self.places[0, kind, n, k, t, z] = (reg, slot)
        self.count += half

    def add_single(self, entries):
        quarter = -(-len(entries) // 4)
        for index, entry in enumerate(entries):
            self.places[entry] = (self.count + index % quarter, index // quarter)
        self.count += quarter

    def by_register(self):
        found = [[None] * 4 for _ in range(self.count)]
        for item, (reg, slot) in self.places.items():
            found[reg][slot] = item
        return found


def regs_of(kind, directions, layer):
    return [(kind, n, k, layer) for n in directions for k in range(REGS[kind])]


def message_plan(t_size):
    plan = collections.OrderedDict()
    ahead = plan["z", 1] = Message()
    ahead.add_halves(regs_of("x", (0,), 0) + regs_of("u", (3,), 0), "z")
    late = plan["b", 1] = Message()
    late.add_halves(regs_of("x", (0,), 1) + regs_of("u", (0, 1), 0), "z")
    behind = plan["z", -1] = Message()
    behind.add_halves(regs_of("x", (0,), 1) + regs_of("u", (2,), 1), "z")
    second = plan["z", 2] = Message()
    second.add_halves(regs_of("x", (0,), 0), "z")
    halves, corners = collections.OrderedDict(), collections.OrderedDict()
    for dt, entries in (
        (1, regs_of("u", (0, 1, 2), 0)),
        (-1, regs_of("x", (0,), 1) + regs_of("u", (3,), 1)),
        (2, regs_of("x", (0,), 0)),
    ):
        if dt % t_size != 0:
            halves.setdefault(dt % t_size, []).extend(entries)
    for dt, entries in halves.items():
        message = plan["t", dt] = Message()
        if dt == 1:
            message.add_full("x", 0)
        held = {item[1:4] for item in message.places}
        message.add_halves([e for e in entries if e[:3] not in held], "t")
    for dt, entries in (
        (1, [(1, "x", 0, k, 0, 0) for k in range(REGS["x"])]),
        (1, [(-1, "x", 0, k, 0, 1) for k in range(REGS["x"])]),
        (1, [(-1, "u", 2, k, 0, 1) for k in range(REGS["u"])]),
        (-1, [(1, "x", 0, k, 1, 0) for k in range(REGS["x"])]),
        (-1, [(1, "u", 3, k, 1, 0) for k in range(REGS["u"])]),
    ):
        corners.setdefault(dt % t_size, []).extend(entries)
    for dt, entries in corners.items():
        plan["c", dt] = Message()
        plan["c", dt].add_single(entries)
    return plan


class Locator:
    def __init__(self, plan, t_size, buffers):
        self.plan, self.t_size, self.buffers = plan, t_size, buffers

    def local(self, kind, n, k, t, z):
        return ("own", kind), n * REGS[kind] + k, 2 * t + z

    def find(self, kind, n, k, t_at, z_at):
        (dt, t), (dz, z) = divmod(t_at, 2), divmod(z_at, 2)
        dt %= self.t_size
        if (dt, dz) == (0, 0):
            return self.local(kind, n, k, t, z)
        name = ("z", dz) if dt == 0 else ("t", dt) if dz == 0 else ("c", dt)
        item = (dz if name[0] == "c" else 0, kind, n, k, t, z)
        if name == ("z", 1) and item not in self.plan[name].places:
            name = ("b", 1)
        return (name,) + self.plan[name].places[item]

    def load(self, name, reg):
        return self.buffers[name][pl.ds(8 * reg, 8), :]

    def assemble(self, spots):
        groups = collections.OrderedDict()
        for r, spot in enumerate(spots):
            if spot is not None:
                groups.setdefault((spot[0], spot[1], r - spot[2]), []).append(r)
        row = lax.broadcasted_iota(jnp.int32, (8, LANES), 0) % 4
        result = None
        for (name, reg, move), rows in groups.items():
            value = self.load(name, reg)
            if move != 0:
                value = pltpu.roll(value, move % 8, 0)
            if result is None:
                result = value
            else:
                mask = functools.reduce(jnp.logical_or, [row == r for r in rows])
                result = jnp.where(mask, value, result)
        return result

    def field_register(self, kind, n, k, dt, dz):
        return self.assemble([self.find(kind, n, k, t + dt, z + dz) for t, z in SITES])


def term_fields(halves, sign):
    here, ahead, left, right = [], [], [], []
    for m, n in halves:
        start = plus(ZERO, UNIT[n], sign)
        base = ZERO if sign > 0 else start
        here.append(("x", 0, start))
        ahead.append(("x", 0, plus(start, UNIT[m])))
        left.append(("u", n, base))
        right.append(("u", n, plus(base, UNIT[m])))
    return here, ahead, left, right


def needed_fields(stage):
    keys = collections.OrderedDict()
    for _, halves in TERMS[stage]:
        for sign in (1, -1):
            for pair in term_fields(halves, sign):
                keys.update((key, None) for key in pair)
    for m in DIRECT[stage]:
        for scale in (1, 3):
            keys["x", 0, plus(ZERO, UNIT[m], scale)] = None
    return [key for key in keys if key[2] != ZERO]


def stage_of(key):
    dz, dt = key[2][2:]
    if key[0] == "u" and key[1] < 2 and dz == 1 and dt == 0:
        return "t"
    if abs(dz) == 3 or (dz != 0 and dt != 0):
        return "corner"
    return "t" if dt != 0 else "z" if dz != 0 else "own"


def lay_out(keys):
    rows, total = collections.OrderedDict(), 0
    for key in keys:
        rows[key] = total
        total += 8 * REGS[key[0]]
    return rows, total


def field_split():
    uses = collections.OrderedDict()
    for stage in STAGES:
        for key in needed_fields(stage):
            uses.setdefault(key, []).append(stage)
    shared, alone = {}, {}
    for stage in STAGES:
        built = [key for key in uses if stage_of(key) == stage]
        shared[stage] = lay_out([key for key in built if uses[key] != [stage]])
        alone[stage] = lay_out([key for key in built if uses[key] == [stage]])
    return shared, alone


def all_shifts():
    found = collections.OrderedDict()
    for stage in STAGES:
        for _, _, (dx, dy, _, _) in needed_fields(stage):
            if (dx, dy) != (0, 0):
                found[dx, dy] = None
    return list(found)


def write_shifts(perm_ref):
    lane = lax.broadcasted_iota(jnp.int32, (LANES, LANES), 1)
    source = lax.broadcasted_iota(jnp.int32, (LANES, LANES), 0)
    for index, (dx, dy) in enumerate(all_shifts()):
        wanted = (lane // NX + dy + NY) % NY * NX + (lane + dx + NX) % NX
        perm_ref[pl.ds(index * LANES, LANES), :] = (source == wanted).astype(F32).astype(jnp.bfloat16)


def parts_of(kind, value):
    if kind == "u":
        return [value.astype(jnp.bfloat16)]
    high = value.astype(jnp.bfloat16)
    rest = value - high.astype(F32)
    middle = rest.astype(jnp.bfloat16)
    return [high, middle, (rest - middle.astype(F32)).astype(jnp.bfloat16)]


def build_fields(locator, perm_ref, stores):
    groups = collections.OrderedDict()
    for ref, rows in stores:
        for (kind, n, disp), row in rows.items():
            shifts = groups.setdefault((kind, n, disp[3], disp[2]), collections.OrderedDict())
            shifts[disp[0], disp[1]] = (ref, row)
    order = all_shifts()
    for (kind, n, dt, dz), shifts in groups.items():
        regs = [locator.field_register(kind, n, k, dt, dz) for k in range(REGS[kind])]
        if (0, 0) in shifts:
            ref, row = shifts[0, 0]
            for k, value in enumerate(regs):
                ref[pl.ds(row + 8 * k, 8), :] = value
        parts = parts_of(kind, jnp.concatenate(regs, axis=0))
        for shift, (ref, row) in shifts.items():
            if shift != (0, 0):
                perm = perm_ref[pl.ds(order.index(shift) * LANES, LANES), :]
                moved = [jnp.dot(part, perm, preferred_element_type=F32) for part in parts]
                ref[pl.ds(row, 8 * REGS[kind]), :] = functools.reduce(jnp.add, moved)


class Fields:
    def __init__(self, own_x, own_u, stores):
        self.place = {("x", 0, ZERO): (own_x, 0)}
        for n in range(4):
            self.place["u", n, ZERO] = (own_u, 8 * REGS["u"] * n)
        for ref, rows in stores:
            for key, row in rows.items():
                self.place[key] = (ref, row)
        self.upper = lax.broadcasted_iota(jnp.int32, (8, LANES), 0) < 4

    def reg(self, key, k):
        ref, row = self.place[key]
        return ref[pl.ds(row + 8 * k, 8), :]

    def two_tiles(self, keys, k):
        top = self.reg(keys[0], k)
        turned_top = pltpu.roll(top, 4, 0)
        if keys[0] == keys[1]:
            low, turned_low = top, turned_top
        else:
            low = self.reg(keys[1], k)
            turned_low = pltpu.roll(low, 4, 0)
        return [jnp.where(self.upper, top, turned_low), jnp.where(self.upper, turned_top, low)]

    def vector(self, keys, pole):
        flat = [tile for k in range(3) for tile in self.two_tiles(keys, 3 * pole + k)]
        return [flat[:3], flat[3:]]

    def matrix(self, keys):
        flat = [tile for k in range(9) for tile in self.two_tiles(keys, k)]
        return [[flat[9 * c + 3 * i : 9 * c + 3 * i + 3] for i in range(3)] for c in range(2)]

    def compact_halves(self, first, second):
        top = jnp.where(self.upper, first, pltpu.roll(second, 4, 0))
        return top, jnp.where(self.upper, pltpu.roll(first, 4, 0), second)

    def compact_sum(self, first, second):
        kept = jnp.where(self.upper, first, second)
        return kept + pltpu.roll(jnp.where(self.upper, second, first), 4, 0)


def pole_sum(fields, here, ahead, scales):
    total = None
    for pole in range(NP):
        h = [[scales[pole] * v for v in part] for part in fields.vector(here, pole)]
        a = fields.vector(ahead, pole)
        real = [[a[0][i] * h[0][j] + a[1][i] * h[1][j] for j in range(3)] for i in range(3)]
        imag = [[a[1][i] * h[0][j] - a[0][i] * h[1][j] for j in range(3)] for i in range(3)]
        if total is None:
            total = [real, imag]
        else:
            total = [
                [[total[c][i][j] + new[i][j] for j in range(3)] for i in range(3)]
                for c, new in enumerate((real, imag))
            ]
    return total


def transposed(matrix):
    return [[[part[j][i] for j in range(3)] for i in range(3)] for part in matrix]


def row_times(row, right, row_sign, right_sign):
    result = [[], []]
    for j in range(3):
        real = imag = None
        for k in range(3):
            rr = row[0][k] * right[0][k][j]
            ii = row[1][k] * right[1][k][j]
            ri = row[0][k] * right[1][k][j]
            ir = row[1][k] * right[0][k][j]
            new_real = rr - ii if row_sign * right_sign > 0 else rr + ii
            if row_sign > 0 and right_sign > 0:
                new_imag = ri + ir
            elif row_sign > 0:
                new_imag = ir - ri
            else:
                new_imag = ri - ir
            real = new_real if real is None else real + new_real
            imag = new_imag if imag is None else imag + new_imag
        result[0].append(real)
        result[1].append(imag)
    return result


def add_terms(fields, stage, near, acc):
    started = set()
    for target, halves in TERMS[stage]:
        for sign in (1, -1):
            here, ahead, left, right = term_fields(halves, sign)
            force = pole_sum(fields, here, ahead, near)
            left = fields.matrix(left)
            right = fields.matrix(right)
            if sign > 0:
                right = transposed(right)
            else:
                left = transposed(left)
            rows = [row_times([left[0][i], left[1][i]], force, sign, 1) for i in range(3)]
            for i in range(3):
                row = row_times(rows[i], right, 1, -sign)
                for part in range(2):
                    for j in range(3):
                        at = pl.ds((target * 18 + part * 9 + i * 3 + j) * 8, 8)
                        new = row[part][j]
                        acc[at, :] = acc[at, :] + new if target in started else new
            started.add(target)


def acc_tile(acc, target, c):
    return acc[pl.ds((target * 18 + c) * 8, 8), :]


def scale_tiles(scale_ref):
    tiles = [scale_ref[pl.ds(8 * p, 8), :] for p in range(3 * NP)]
    return tiles[:NP], tiles[NP : 2 * NP], tiles[2 * NP :]


def own_force(fields, m, both):
    total = pole_sum(
        fields,
        [("x", 0, ZERO)] * 2,
        [("x", 0, UNIT[m]), ("x", 0, plus(ZERO, UNIT[m], 3))],
        both,
    )
    flat = [total[c][i][j] for c in range(2) for i in range(3) for j in range(3)]
    return [fields.compact_sum(flat[2 * k], flat[2 * k + 1]) for k in range(9)]


def write_messages(locator, plan, names, outs):
    for name, out in zip(names, outs):
        for reg, items in enumerate(plan[name].by_register()):
            spots = [item and locator.local(*item[1:]) for item in items]
            out[pl.ds(8 * reg, 8), :] = locator.assemble(spots)


def pack_z_kernel(plan, names, near_in, far_in, weight_in, x_in, u_in, *rest):
    outs = rest[: len(names)]
    scale_ref, perm_ref, x_ref, u_ref, near_ref, far_ref, weight_ref, u_held, sems = rest[len(names) :]
    copies = [
        pltpu.make_async_copy(source, target, sems.at[index])
        for index, (source, target) in enumerate(
            ((u_in, u_held), (x_in, x_ref), (near_in, near_ref), (far_in, far_ref), (weight_in, weight_ref))
        )
    ]
    for copy in copies:
        copy.start()
    write_shifts(perm_ref)
    for copy in copies:
        copy.wait()
    u_ref[...] = u_held[...].astype(F32)
    locator = Locator(plan, 1, {("own", "x"): x_ref, ("own", "u"): u_ref})
    write_messages(locator, plan, names, outs)
    write_scales(near_ref, far_ref, weight_ref, scale_ref)


def pack_t_kernel(plan, names, x_ref, u_ref, *outs):
    write_messages(Locator(plan, 1, {("own", "x"): x_ref, ("own", "u"): u_ref}), plan, names, outs)


def corner_kernel(plan, names, ahead_ref, behind_ref, *outs):
    locator = Locator(plan, 1, {("z", 1): ahead_ref, ("z", -1): behind_ref})
    for name, out in zip(names, outs):
        for reg, items in enumerate(plan[name].by_register()):
            spots = [
                item and (("z", item[0]),) + plan["z", item[0]].places[(0,) + item[1:]] for item in items
            ]
            out[pl.ds(8 * reg, 8), :] = locator.assemble(spots)


def part_reg(ref, index, k):
    return ref[pl.ds((9 * index + k) * 8, 8), :]


def write_scales(near_ref, far_ref, weight_ref, scale_ref):
    upper = lax.broadcasted_iota(jnp.int32, (8, LANES), 0) < 4
    for p in range(NP):
        scale_ref[pl.ds(8 * p, 8), :] = jnp.full((8, LANES), near_ref[p], F32)
        scale_ref[pl.ds(8 * (NP + p), 8), :] = jnp.where(upper, near_ref[p], far_ref[p])
        scale_ref[pl.ds(8 * (2 * NP + p), 8), :] = jnp.full((8, LANES), weight_ref[p], F32)


def own_fields_kernel(plan, t_size, perm_ref, x_ref, u_ref, shared_ref, alone_ref):
    shared, alone = field_split()
    stores = [(shared_ref, shared["own"][0]), (alone_ref, alone["own"][0])]
    build_fields(Locator(plan, t_size, {("own", "x"): x_ref, ("own", "u"): u_ref}), perm_ref, stores)


def own_kernel(scale_ref, x_ref, u_ref, shared_ref, alone_ref, part_ref, acc):
    shared, alone = field_split()
    fields = Fields(x_ref, u_ref, [(shared_ref, shared["own"][0]), (alone_ref, alone["own"][0])])
    near, both, weight = scale_tiles(scale_ref)
    add_terms(fields, "own", near, acc)
    direct = [own_force(fields, m, both) for m in DIRECT["own"]]
    for k in range(9):
        staples = fields.compact_halves(acc_tile(acc, 0, 2 * k), acc_tile(acc, 0, 2 * k + 1))
        for m in range(2):
            part_ref[pl.ds((9 * m + k) * 8, 8), :] = direct[m][k] + weight[m] * staples[m]


def stage_setup(stage, plan, t_size, names, received, perm_ref, x_ref, u_ref, shared_refs, shared_ref, alone_ref):
    buffers = {("own", "x"): x_ref, ("own", "u"): u_ref}
    buffers.update(zip(names, received))
    shared, alone = field_split()
    stores = [(alone_ref, alone[stage][0])]
    if shared_ref is not None:
        stores.append((shared_ref, shared[stage][0]))
    build_fields(Locator(plan, t_size, buffers), perm_ref, stores)
    earlier = [(ref, shared[name][0]) for name, ref in zip(STAGES, shared_refs)]
    return Fields(x_ref, u_ref, earlier + stores)


def z_kernel(plan, t_size, names, scale_ref, perm_ref, x_ref, u_ref, own_shared, own_part, *rest):
    received = rest[: len(names)]
    shared_ref, part_ref, alone_ref, acc = rest[len(names) :]
    fields = stage_setup(
        "z", plan, t_size, names, received, perm_ref, x_ref, u_ref, [own_shared], shared_ref, alone_ref
    )
    near, _, weight = scale_tiles(scale_ref)
    add_terms(fields, "z", near, acc)
    for k in range(9):
        staples = fields.compact_halves(acc_tile(acc, 0, 2 * k), acc_tile(acc, 0, 2 * k + 1))
        for m in range(2):
            part_ref[pl.ds((9 * m + k) * 8, 8), :] = part_reg(own_part, m, k) + weight[m] * staples[m]


def t_kernel(plan, t_size, names, scale_ref, perm_ref, x_ref, u_ref, own_shared, z_shared, z_part, *rest):
    received = rest[: len(names)]
    shared_ref, part_ref, ready, alone_ref, acc = rest[len(names) :]
    fields = stage_setup(
        "t", plan, t_size, names, received, perm_ref, x_ref, u_ref, [own_shared, z_shared], shared_ref, alone_ref
    )
    near, both, weight = scale_tiles(scale_ref)
    add_terms(fields, "t", near, acc)
    for k in range(9):
        staples = fields.compact_halves(acc_tile(acc, 0, 2 * k), acc_tile(acc, 0, 2 * k + 1))
        for m in range(2):
            ready[pl.ds((9 * m + k) * 8, 8), :] = part_reg(z_part, m, k) + weight[m] * staples[m]
    direct = own_force(fields, 3, both)
    for k in range(9):
        staple = fields.compact_sum(acc_tile(acc, 1, 2 * k), acc_tile(acc, 1, 2 * k + 1))
        part_ref[pl.ds(k * 8, 8), :] = direct[k] + weight[3] * staple
        staple = fields.compact_sum(acc_tile(acc, 2, 2 * k), acc_tile(acc, 2, 2 * k + 1))
        part_ref[pl.ds((9 + k) * 8, 8), :] = weight[2] * staple


def last_kernel(plan, t_size, names, scale_ref, perm_ref, x_ref, u_ref, *rest):
    own_shared, z_shared, t_shared, t_part, earlier = rest[:5]
    received = rest[5 : 5 + len(names)]
    out_ref, alone_ref, acc, ready, sems = rest[5 + len(names) :]
    rows = ready.shape[0]
    first = pltpu.make_async_copy(earlier, out_ref.at[pl.ds(0, rows)], sems.at[0])
    first.start()
    fields = stage_setup(
        "corner",
        plan,
        t_size,
        names,
        received,
        perm_ref,
        x_ref,
        u_ref,
        [own_shared, z_shared, t_shared],
        None,
        alone_ref,
    )
    near, both, weight = scale_tiles(scale_ref)
    add_terms(fields, "corner", near, acc)
    direct = own_force(fields, 2, both)
    for k in range(9):
        staples = fields.compact_halves(acc_tile(acc, 0, 2 * k), acc_tile(acc, 0, 2 * k + 1))
        ready[pl.ds(k * 8, 8), :] = part_reg(t_part, 1, k) + direct[k] + weight[2] * staples[0]
        ready[pl.ds((9 + k) * 8, 8), :] = part_reg(t_part, 0, k) + weight[3] * staples[1]
    second = pltpu.make_async_copy(ready, out_ref.at[pl.ds(rows, rows)], sems.at[1])
    second.start()
    first.wait()
    second.wait()


def rows_of(count):
    return jax.ShapeDtypeStruct((count, LANES), F32)


def on_device(pole_vectors, gauge_links, pole_coeff, naik_coeff, staple_weight):
    t_size = lax.axis_size("ta")
    z_size = lax.axis_size("gz") * lax.axis_size("gy")
    plan = message_plan(t_size)
    x_rows, u_rows = 8 * REGS["x"], 4 * 8 * REGS["u"]
    vmem = pl.BlockSpec(memory_space=pltpu.VMEM)
    hbm = pl.BlockSpec(memory_space=pltpu.HBM)
    limit = pltpu.CompilerParams(vmem_limit_bytes=4 * 1024 * 1024)

    def moved(name, value):
        kind, step = name
        if kind in ("z", "b"):
            return lax.ppermute(value, ("gz", "gy"), [((i + step) % z_size, i) for i in range(z_size)])
        return lax.ppermute(value, "ta", [((j + step) % t_size, j) for j in range(t_size)])

    first_names = [name for name in plan if name[0] != "c"]
    corner_names = [name for name in plan if name[0] == "c"]
    t_names = [name for name in first_names if name[0] == "t"]
    in_hbm = functools.partial(pltpu.with_memory_space_constraint, memory_space=pltpu.HBM)
    z_names = [name for name in first_names if name[0] != "t"]
    corner_count = max(plan[name].count for name in corner_names)
    ahead_count = max(plan["z", 1].count, plan["t", 1].count - corner_count + 1)
    least = {("z", 2): corner_count, ("z", 1): ahead_count, ("z", -1): ahead_count + 1}
    *sends, scale, perm, x_own, u_own = pl.pallas_call(
        functools.partial(pack_z_kernel, plan, z_names),
        out_shape=[rows_of(8 * max(plan[name].count, least.get(name, 0))) for name in z_names]
        + [
            rows_of(8 * 3 * NP),
            jax.ShapeDtypeStruct((len(all_shifts()) * LANES, LANES), jnp.bfloat16),
            rows_of(x_rows),
            rows_of(u_rows),
        ],
        in_specs=[hbm] * 5,
        out_specs=[vmem] * (len(z_names) + 4),
        scratch_shapes=[pltpu.SMEM((NP,), F32)] * 3
        + [pltpu.VMEM((u_rows, LANES), jnp.bfloat16), pltpu.SemaphoreType.DMA((5,))],
        compiler_params=limit,
        name="pack_z",
    )(
        in_hbm(pole_coeff),
        in_hbm(naik_coeff),
        in_hbm(staple_weight),
        in_hbm(pole_vectors.reshape((x_rows, LANES))),
        in_hbm(gauge_links.reshape((u_rows, LANES))),
    )
    own = [x_own, u_own]
    received = {name: moved(name, value) for name, value in zip(z_names, sends)}
    packed = pl.pallas_call(
        functools.partial(pack_t_kernel, plan, t_names),
        out_shape=[rows_of(8 * plan[name].count) for name in t_names],
        in_specs=[vmem] * 2,
        out_specs=[vmem] * len(t_names),
        compiler_params=limit,
        name="pack_t",
    )(*own)
    received.update({name: moved(name, value) for name, value in zip(t_names, packed)})
    shared, alone = field_split()
    part_rows = 8 * REGS["u"]

    def scratch(stage):
        sums = 1 + max(target for target, _ in TERMS[stage])
        return [pltpu.VMEM((alone[stage][1], LANES), F32), pltpu.VMEM((sums * 18 * 8, LANES), F32)]

    def cost(micros):
        return pl.CostEstimate(flops=10**6, bytes_accessed=int(3.69e6 * micros), transcendentals=0)

    wide_limit = pltpu.CompilerParams(vmem_limit_bytes=6 * 1024 * 1024)
    own_shared, own_alone = pl.pallas_call(
        functools.partial(own_fields_kernel, plan, t_size),
        out_shape=[rows_of(shared["own"][1]), rows_of(alone["own"][1])],
        in_specs=[vmem] * 3,
        out_specs=[vmem] * 2,
        compiler_params=wide_limit,
        name="fields_own",
    )(perm, *own)
    own_part = pl.pallas_call(
        own_kernel,
        out_shape=rows_of(2 * part_rows),
        in_specs=[vmem] * 5,
        out_specs=vmem,
        scratch_shapes=scratch("own")[1:],
        cost_estimate=cost(COSTS["own"]),
        compiler_params=wide_limit,
        name="force_own",
    )(scale, *own, own_shared, own_alone)
    local = [scale, perm, *own]
    corners = pl.pallas_call(
        functools.partial(corner_kernel, plan, corner_names),
        out_shape=[rows_of(8 * plan[name].count) for name in corner_names],
        in_specs=[vmem] * 2,
        out_specs=[vmem] * len(corner_names),
        compiler_params=limit,
        name="pack_corners",
    )(received["z", 1], received["z", -1])
    received.update({name: moved(name, value) for name, value in zip(corner_names, corners)})
    names = [("z", 1), ("z", -1)]
    z_shared, z_part = pl.pallas_call(
        functools.partial(z_kernel, plan, t_size, names),
        out_shape=[rows_of(shared["z"][1]), rows_of(2 * part_rows)],
        in_specs=[vmem] * (6 + len(names)),
        out_specs=[vmem] * 2,
        scratch_shapes=scratch("z"),
        cost_estimate=cost(COSTS["z"]),
        compiler_params=wide_limit,
        name="force_z",
    )(*local, own_shared, own_part, *[received[name] for name in names])
    far_names = t_names + [("b", 1)]
    t_shared, t_part, earlier = pl.pallas_call(
        functools.partial(t_kernel, plan, t_size, far_names),
        out_shape=[rows_of(shared["t"][1]), rows_of(2 * part_rows), rows_of(2 * part_rows)],
        in_specs=[vmem] * (7 + len(far_names)),
        out_specs=[vmem] * 3,
        scratch_shapes=scratch("t"),
        cost_estimate=cost(COSTS["t"]),
        compiler_params=wide_limit,
        name="force_t",
    )(*local, own_shared, z_shared, z_part, *[received[name] for name in far_names])
    names = list(received)
    force = pl.pallas_call(
        functools.partial(last_kernel, plan, t_size, names),
        out_shape=rows_of(u_rows),
        in_specs=[vmem] * (9 + len(names)),
        out_specs=hbm,
        scratch_shapes=scratch("corner")
        + [pltpu.VMEM((2 * part_rows, LANES), F32), pltpu.SemaphoreType.DMA((2,))],
        cost_estimate=cost(COSTS["corner"]),
        compiler_params=wide_limit,
        name="force_corner",
    )(
        *local,
        own_shared,
        z_shared,
        t_shared,
        t_part,
        earlier,
        *[received[name] for name in names],
    )
    return force.reshape(gauge_links.shape)


def solution(mesh):
    return jax.shard_map(
        on_device,
        mesh=mesh,
        in_specs=(
            P("ens", None, None, "ta", ("gz", "gy"), None),
            P("ens", None, None, None, "ta", ("gz", "gy"), None),
            P(),
            P(),
            P(),
        ),
        out_specs=P("ens", None, None, None, "ta", ("gz", "gy"), None),
        check_vma=False,
    )
```

```python
import collections
import functools

import jax
import jax.numpy as jnp
from jax import lax
from jax.experimental import pallas as pl
from jax.experimental.pallas import tpu as pltpu
from jax.sharding import PartitionSpec as P

NX = 8
NY = 16
LANES = NX * NY
NP = 4
F32 = jnp.float32
REGS = {"x": NP * 3, "u": 9}
UNIT = ((1, 0, 0, 0), (0, 1, 0, 0), (0, 0, 1, 0), (0, 0, 0, 1))
ZERO = (0, 0, 0, 0)
SITES = ((0, 0), (0, 1), (1, 0), (1, 1))
STAGES = ("own", "z", "t", "corner")
TERMS = {
    "own": ((0, ((0, 1), (1, 0))),),
    "z": ((0, ((0, 2), (1, 2))),),
    "t": ((0, ((0, 3), (1, 3))), (1, ((3, 0), (3, 1))), (2, ((2, 0), (2, 1)))),
    "corner": ((0, ((2, 3), (3, 2))),),
}
COSTS = {"own": 2.0, "z": 2.0, "t": 2.0, "corner": 1.0}
DIRECT = {"own": (0, 1), "z": (), "t": (3,), "corner": (2,)}


def plus(left, right, scale=1):
    return tuple(a + scale * b for a, b in zip(left, right))


class Message:
    def __init__(self):
        self.places = collections.OrderedDict()
        self.count = 0

    def add_full(self, kind, n):
        for k in range(REGS[kind]):
            for t, z in SITES:
                self.places[0, kind, n, k, t, z] = (self.count, 2 * t + z)
            self.count += 1

    def add_halves(self, entries, axis):
        half = -(-len(entries) // 2)
        for index, (kind, n, k, layer) in enumerate(entries):
            reg, part = self.count + index % half, index // half
            for other in range(2):
                t, z = (layer, other) if axis == "t" else (other, layer)
                slot = 2 * part + other if axis == "t" else 2 * other + part
                self.places[0, kind, n, k, t, z] = (reg, slot)
        self.count += half

    def add_single(self, entries):
        quarter = -(-len(entries) // 4)
        for index, entry in enumerate(entries):
            self.places[entry] = (self.count + index % quarter, index // quarter)
        self.count += quarter

    def by_register(self):
        found = [[None] * 4 for _ in range(self.count)]
        for item, (reg, slot) in self.places.items():
            found[reg][slot] = item
        return found


def regs_of(kind, directions, layer):
    return [(kind, n, k, layer) for n in directions for k in range(REGS[kind])]


def message_plan(t_size):
    plan = collections.OrderedDict()
    ahead = plan["z", 1] = Message()
    ahead.add_halves(regs_of("x", (0,), 0) + regs_of("u", (3,), 0), "z")
    late = plan["b", 1] = Message()
    late.add_halves(regs_of("x", (0,), 1) + regs_of("u", (0, 1), 0), "z")
    behind = plan["z", -1] = Message()
    behind.add_halves(regs_of("x", (0,), 1) + regs_of("u", (2,), 1), "z")
    second = plan["z", 2] = Message()
    second.add_halves(regs_of("x", (0,), 0), "z")
    halves, corners = collections.OrderedDict(), collections.OrderedDict()
    for dt, entries in (
        (1, regs_of("u", (0, 1, 2), 0)),
        (-1, regs_of("x", (0,), 1) + regs_of("u", (3,), 1)),
        (2, regs_of("x", (0,), 0)),
    ):
        if dt % t_size != 0:
            halves.setdefault(dt % t_size, []).extend(entries)
    for dt, entries in halves.items():
        message = plan["t", dt] = Message()
        if dt == 1:
            message.add_full("x", 0)
        held = {item[1:4] for item in message.places}
        message.add_halves([e for e in entries if e[:3] not in held], "t")
    for dt, entries in (
        (1, [(1, "x", 0, k, 0, 0) for k in range(REGS["x"])]),
        (1, [(-1, "x", 0, k, 0, 1) for k in range(REGS["x"])]),
        (1, [(-1, "u", 2, k, 0, 1) for k in range(REGS["u"])]),
        (-1, [(1, "x", 0, k, 1, 0) for k in range(REGS["x"])]),
        (-1, [(1, "u", 3, k, 1, 0) for k in range(REGS["u"])]),
    ):
        corners.setdefault(dt % t_size, []).extend(entries)
    for dt, entries in corners.items():
        plan["c", dt] = Message()
        plan["c", dt].add_single(entries)
    return plan


class Locator:
    def __init__(self, plan, t_size, buffers):
        self.plan, self.t_size, self.buffers = plan, t_size, buffers

    def local(self, kind, n, k, t, z):
        return ("own", kind), n * REGS[kind] + k, 2 * t + z

    def find(self, kind, n, k, t_at, z_at):
        (dt, t), (dz, z) = divmod(t_at, 2), divmod(z_at, 2)
        dt %= self.t_size
        if (dt, dz) == (0, 0):
            return self.local(kind, n, k, t, z)
        name = ("z", dz) if dt == 0 else ("t", dt) if dz == 0 else ("c", dt)
        item = (dz if name[0] == "c" else 0, kind, n, k, t, z)
        if name == ("z", 1) and item not in self.plan[name].places:
            name = ("b", 1)
        return (name,) + self.plan[name].places[item]

    def load(self, name, reg):
        return self.buffers[name][pl.ds(8 * reg, 8), :]

    def assemble(self, spots):
        groups = collections.OrderedDict()
        for r, spot in enumerate(spots):
            if spot is not None:
                groups.setdefault((spot[0], spot[1], r - spot[2]), []).append(r)
        row = lax.broadcasted_iota(jnp.int32, (8, LANES), 0) % 4
        result = None
        for (name, reg, move), rows in groups.items():
            value = self.load(name, reg)
            if move != 0:
                value = pltpu.roll(value, move % 8, 0)
            if result is None:
                result = value
            else:
                mask = functools.reduce(jnp.logical_or, [row == r for r in rows])
                result = jnp.where(mask, value, result)
        return result

    def field_register(self, kind, n, k, dt, dz):
        return self.assemble([self.find(kind, n, k, t + dt, z + dz) for t, z in SITES])


def term_fields(halves, sign):
    here, ahead, left, right = [], [], [], []
    for m, n in halves:
        start = plus(ZERO, UNIT[n], sign)
        base = ZERO if sign > 0 else start
        here.append(("x", 0, start))
        ahead.append(("x", 0, plus(start, UNIT[m])))
        left.append(("u", n, base))
        right.append(("u", n, plus(base, UNIT[m])))
    return here, ahead, left, right


def needed_fields(stage):
    keys = collections.OrderedDict()
    for _, halves in TERMS[stage]:
        for sign in (1, -1):
            for pair in term_fields(halves, sign):
                keys.update((key, None) for key in pair)
    for m in DIRECT[stage]:
        for scale in (1, 3):
            keys["x", 0, plus(ZERO, UNIT[m], scale)] = None
    return [key for key in keys if key[2] != ZERO]


def stage_of(key):
    dz, dt = key[2][2:]
    if key[0] == "u" and key[1] < 2 and dz == 1 and dt == 0:
        return "t"
    if abs(dz) == 3 or (dz != 0 and dt != 0):
        return "corner"
    return "t" if dt != 0 else "z" if dz != 0 else "own"


def lay_out(keys):
    rows, total = collections.OrderedDict(), 0
    for key in keys:
        rows[key] = total
        total += 8 * REGS[key[0]]
    return rows, total


def field_split():
    uses = collections.OrderedDict()
    for stage in STAGES:
        for key in needed_fields(stage):
            uses.setdefault(key, []).append(stage)
    shared, alone = {}, {}
    for stage in STAGES:
        built = [key for key in uses if stage_of(key) == stage]
        shared[stage] = lay_out([key for key in built if uses[key] != [stage]])
        alone[stage] = lay_out([key for key in built if uses[key] == [stage]])
    return shared, alone


def all_shifts():
    found = collections.OrderedDict()
    for stage in STAGES:
        for _, _, (dx, dy, _, _) in needed_fields(stage):
            if (dx, dy) != (0, 0):
                found[dx, dy] = None
    return list(found)


def write_shifts(perm_ref):
    lane = lax.broadcasted_iota(jnp.int32, (LANES, LANES), 1)
    source = lax.broadcasted_iota(jnp.int32, (LANES, LANES), 0)
    for index, (dx, dy) in enumerate(all_shifts()):
        wanted = (lane // NX + dy + NY) % NY * NX + (lane + dx + NX) % NX
        perm_ref[pl.ds(index * LANES, LANES), :] = (source == wanted).astype(F32).astype(jnp.bfloat16)


def parts_of(kind, value):
    if kind == "u":
        return [value.astype(jnp.bfloat16)]
    high = value.astype(jnp.bfloat16)
    rest = value - high.astype(F32)
    middle = rest.astype(jnp.bfloat16)
    return [high, middle, (rest - middle.astype(F32)).astype(jnp.bfloat16)]


def build_fields(locator, perm_ref, stores):
    groups = collections.OrderedDict()
    for ref, rows in stores:
        for (kind, n, disp), row in rows.items():
            shifts = groups.setdefault((kind, n, disp[3], disp[2]), collections.OrderedDict())
            shifts[disp[0], disp[1]] = (ref, row)
    order = all_shifts()
    for (kind, n, dt, dz), shifts in groups.items():
        regs = [locator.field_register(kind, n, k, dt, dz) for k in range(REGS[kind])]
        if (0, 0) in shifts:
            ref, row = shifts[0, 0]
            for k, value in enumerate(regs):
                ref[pl.ds(row + 8 * k, 8), :] = value
        parts = parts_of(kind, jnp.concatenate(regs, axis=0))
        for shift, (ref, row) in shifts.items():
            if shift != (0, 0):
                perm = perm_ref[pl.ds(order.index(shift) * LANES, LANES), :]
                moved = [jnp.dot(part, perm, preferred_element_type=F32) for part in parts]
                ref[pl.ds(row, 8 * REGS[kind]), :] = functools.reduce(jnp.add, moved)


class Fields:
    def __init__(self, own_x, own_u, stores):
        self.place = {("x", 0, ZERO): (own_x, 0)}
        for n in range(4):
            self.place["u", n, ZERO] = (own_u, 8 * REGS["u"] * n)
        for ref, rows in stores:
            for key, row in rows.items():
                self.place[key] = (ref, row)
        self.upper = lax.broadcasted_iota(jnp.int32, (8, LANES), 0) < 4

    def reg(self, key, k):
        ref, row = self.place[key]
        return ref[pl.ds(row + 8 * k, 8), :]

    def two_tiles(self, keys, k):
        top = self.reg(keys[0], k)
        turned_top = pltpu.roll(top, 4, 0)
        if keys[0] == keys[1]:
            low, turned_low = top, turned_top
        else:
            low = self.reg(keys[1], k)
            turned_low = pltpu.roll(low, 4, 0)
        return [jnp.where(self.upper, top, turned_low), jnp.where(self.upper, turned_top, low)]

    def vector(self, keys, pole):
        flat = [tile for k in range(3) for tile in self.two_tiles(keys, 3 * pole + k)]
        return [flat[:3], flat[3:]]

    def matrix(self, keys):
        flat = [tile for k in range(9) for tile in self.two_tiles(keys, k)]
        return [[flat[9 * c + 3 * i : 9 * c + 3 * i + 3] for i in range(3)] for c in range(2)]

    def compact_halves(self, first, second):
        top = jnp.where(self.upper, first, pltpu.roll(second, 4, 0))
        return top, jnp.where(self.upper, pltpu.roll(first, 4, 0), second)

    def compact_sum(self, first, second):
        kept = jnp.where(self.upper, first, second)
        return kept + pltpu.roll(jnp.where(self.upper, second, first), 4, 0)


def pole_sum(fields, here, ahead, scales):
    total = None
    for pole in range(NP):
        h = [[scales[pole] * v for v in part] for part in fields.vector(here, pole)]
        a = fields.vector(ahead, pole)
        real = [[a[0][i] * h[0][j] + a[1][i] * h[1][j] for j in range(3)] for i in range(3)]
        imag = [[a[1][i] * h[0][j] - a[0][i] * h[1][j] for j in range(3)] for i in range(3)]
        if total is None:
            total = [real, imag]
        else:
            total = [
                [[total[c][i][j] + new[i][j] for j in range(3)] for i in range(3)]
                for c, new in enumerate((real, imag))
            ]
    return total


def transposed(matrix):
    return [[[part[j][i] for j in range(3)] for i in range(3)] for part in matrix]


def row_times(row, right, row_sign, right_sign):
    result = [[], []]
    for j in range(3):
        real = imag = None
        for k in range(3):
            rr = row[0][k] * right[0][k][j]
            ii = row[1][k] * right[1][k][j]
            ri = row[0][k] * right[1][k][j]
            ir = row[1][k] * right[0][k][j]
            new_real = rr - ii if row_sign * right_sign > 0 else rr + ii
            if row_sign > 0 and right_sign > 0:
                new_imag = ri + ir
            elif row_sign > 0:
                new_imag = ir - ri
            else:
                new_imag = ri - ir
            real = new_real if real is None else real + new_real
            imag = new_imag if imag is None else imag + new_imag
        result[0].append(real)
        result[1].append(imag)
    return result


def add_terms(fields, stage, near, acc):
    started = set()
    for target, halves in TERMS[stage]:
        for sign in (1, -1):
            here, ahead, left, right = term_fields(halves, sign)
            force = pole_sum(fields, here, ahead, near)
            left = fields.matrix(left)
            right = fields.matrix(right)
            if sign > 0:
                right = transposed(right)
            else:
                left = transposed(left)
            rows = [row_times([left[0][i], left[1][i]], force, sign, 1) for i in range(3)]
            for i in range(3):
                row = row_times(rows[i], right, 1, -sign)
                for part in range(2):
                    for j in range(3):
                        at = pl.ds((target * 18 + part * 9 + i * 3 + j) * 8, 8)
                        new = row[part][j]
                        acc[at, :] = acc[at, :] + new if target in started else new
            started.add(target)


def acc_tile(acc, target, c):
    return acc[pl.ds((target * 18 + c) * 8, 8), :]


def scale_tiles(scale_ref):
    tiles = [scale_ref[pl.ds(8 * p, 8), :] for p in range(3 * NP)]
    return tiles[:NP], tiles[NP : 2 * NP], tiles[2 * NP :]


def own_force(fields, m, both):
    total = pole_sum(
        fields,
        [("x", 0, ZERO)] * 2,
        [("x", 0, UNIT[m]), ("x", 0, plus(ZERO, UNIT[m], 3))],
        both,
    )
    flat = [total[c][i][j] for c in range(2) for i in range(3) for j in range(3)]
    return [fields.compact_sum(flat[2 * k], flat[2 * k + 1]) for k in range(9)]


def write_messages(locator, plan, names, outs):
    for name, out in zip(names, outs):
        for reg, items in enumerate(plan[name].by_register()):
            spots = [item and locator.local(*item[1:]) for item in items]
            out[pl.ds(8 * reg, 8), :] = locator.assemble(spots)


def odd_in_z():
    return (lax.axis_index("gz") * lax.axis_size("gy") + lax.axis_index("gy")) % 2 == 1


def pack_z_kernel(plan, names, near_in, far_in, weight_in, x_in, u_in, *rest):
    within_ref, between_ref = rest[:2]
    outs = rest[2 : 2 + len(names)]
    scale_ref, perm_ref, x_ref, u_ref, near_ref, far_ref, weight_ref, u_held, sems = rest[2 + len(names) :]
    copies = [
        pltpu.make_async_copy(source, target, sems.at[index])
        for index, (source, target) in enumerate(
            ((u_in, u_held), (x_in, x_ref), (near_in, near_ref), (far_in, far_ref), (weight_in, weight_ref))
        )
    ]
    for copy in copies:
        copy.start()
    write_shifts(perm_ref)
    for copy in copies:
        copy.wait()
    u_ref[...] = u_held[...].astype(F32)
    locator = Locator(plan, 1, {("own", "x"): x_ref, ("own", "u"): u_ref})
    both = [("z", 1), ("z", -1)]

    @pl.when(odd_in_z())
    def _():
        write_messages(locator, plan, both, (within_ref, between_ref))

    @pl.when(jnp.logical_not(odd_in_z()))
    def _():
        write_messages(locator, plan, both, (between_ref, within_ref))

    write_messages(locator, plan, names, outs)
    write_scales(near_ref, far_ref, weight_ref, scale_ref)


def pack_t_kernel(plan, names, x_ref, u_ref, *outs):
    write_messages(Locator(plan, 1, {("own", "x"): x_ref, ("own", "u"): u_ref}), plan, names, outs)


def corner_kernel(plan, names, within_ref, between_ref, _, ahead_ref, behind_ref, *outs):
    def split(from_ahead, from_behind):
        ahead_ref[...] = from_ahead[pl.ds(0, ahead_ref.shape[0]), :]
        behind_ref[...] = from_behind[pl.ds(0, behind_ref.shape[0]), :]

    @pl.when(odd_in_z())
    def _():
        split(between_ref, within_ref)

    @pl.when(jnp.logical_not(odd_in_z()))
    def _():
        split(within_ref, between_ref)

    locator = Locator(plan, 1, {("z", 1): ahead_ref, ("z", -1): behind_ref})
    for name, out in zip(names, outs):
        for reg, items in enumerate(plan[name].by_register()):
            spots = [
                item and (("z", item[0]),) + plan["z", item[0]].places[(0,) + item[1:]] for item in items
            ]
            out[pl.ds(8 * reg, 8), :] = locator.assemble(spots)


def part_reg(ref, index, k):
    return ref[pl.ds((9 * index + k) * 8, 8), :]


def write_scales(near_ref, far_ref, weight_ref, scale_ref):
    upper = lax.broadcasted_iota(jnp.int32, (8, LANES), 0) < 4
    for p in range(NP):
        scale_ref[pl.ds(8 * p, 8), :] = jnp.full((8, LANES), near_ref[p], F32)
        scale_ref[pl.ds(8 * (NP + p), 8), :] = jnp.where(upper, near_ref[p], far_ref[p])
        scale_ref[pl.ds(8 * (2 * NP + p), 8), :] = jnp.full((8, LANES), weight_ref[p], F32)


def own_fields_kernel(plan, t_size, perm_ref, x_ref, u_ref, shared_ref, alone_ref):
    shared, alone = field_split()
    stores = [(shared_ref, shared["own"][0]), (alone_ref, alone["own"][0])]
    build_fields(Locator(plan, t_size, {("own", "x"): x_ref, ("own", "u"): u_ref}), perm_ref, stores)


def own_kernel(scale_ref, x_ref, u_ref, shared_ref, alone_ref, part_ref, acc):
    shared, alone = field_split()
    fields = Fields(x_ref, u_ref, [(shared_ref, shared["own"][0]), (alone_ref, alone["own"][0])])
    near, both, weight = scale_tiles(scale_ref)
    add_terms(fields, "own", near, acc)
    direct = [own_force(fields, m, both) for m in DIRECT["own"]]
    for k in range(9):
        staples = fields.compact_halves(acc_tile(acc, 0, 2 * k), acc_tile(acc, 0, 2 * k + 1))
        for m in range(2):
            part_ref[pl.ds((9 * m + k) * 8, 8), :] = direct[m][k] + weight[m] * staples[m]


def stage_setup(stage, plan, t_size, names, received, perm_ref, x_ref, u_ref, shared_refs, shared_ref, alone_ref):
    buffers = {("own", "x"): x_ref, ("own", "u"): u_ref}
    buffers.update(zip(names, received))
    shared, alone = field_split()
    stores = [(alone_ref, alone[stage][0])]
    if shared_ref is not None:
        stores.append((shared_ref, shared[stage][0]))
    build_fields(Locator(plan, t_size, buffers), perm_ref, stores)
    earlier = [(ref, shared[name][0]) for name, ref in zip(STAGES, shared_refs)]
    return Fields(x_ref, u_ref, earlier + stores)


def z_kernel(plan, t_size, names, scale_ref, perm_ref, x_ref, u_ref, own_shared, own_part, *rest):
    received = rest[: len(names)]
    shared_ref, part_ref, alone_ref, acc = rest[len(names) :]
    fields = stage_setup(
        "z", plan, t_size, names, received, perm_ref, x_ref, u_ref, [own_shared], shared_ref, alone_ref
    )
    near, _, weight = scale_tiles(scale_ref)
    add_terms(fields, "z", near, acc)
    for k in range(9):
        staples = fields.compact_halves(acc_tile(acc, 0, 2 * k), acc_tile(acc, 0, 2 * k + 1))
        for m in range(2):
            part_ref[pl.ds((9 * m + k) * 8, 8), :] = part_reg(own_part, m, k) + weight[m] * staples[m]


def t_kernel(plan, t_size, names, scale_ref, perm_ref, x_ref, u_ref, own_shared, z_shared, z_part, *rest):
    received = rest[: len(names)]
    shared_ref, part_ref, ready, alone_ref, acc = rest[len(names) :]
    fields = stage_setup(
        "t", plan, t_size, names, received, perm_ref, x_ref, u_ref, [own_shared, z_shared], shared_ref, alone_ref
    )
    near, both, weight = scale_tiles(scale_ref)
    add_terms(fields, "t", near, acc)
    for k in range(9):
        staples = fields.compact_halves(acc_tile(acc, 0, 2 * k), acc_tile(acc, 0, 2 * k + 1))
        for m in range(2):
            ready[pl.ds((9 * m + k) * 8, 8), :] = part_reg(z_part, m, k) + weight[m] * staples[m]
    direct = own_force(fields, 3, both)
    for k in range(9):
        staple = fields.compact_sum(acc_tile(acc, 1, 2 * k), acc_tile(acc, 1, 2 * k + 1))
        part_ref[pl.ds(k * 8, 8), :] = direct[k] + weight[3] * staple
        staple = fields.compact_sum(acc_tile(acc, 2, 2 * k), acc_tile(acc, 2, 2 * k + 1))
        part_ref[pl.ds((9 + k) * 8, 8), :] = weight[2] * staple


def last_kernel(plan, t_size, names, scale_ref, perm_ref, x_ref, u_ref, *rest):
    own_shared, z_shared, t_shared, t_part, earlier = rest[:5]
    received = rest[5 : 5 + len(names)]
    out_ref, alone_ref, acc, ready, sems = rest[5 + len(names) :]
    rows = ready.shape[0]
    first = pltpu.make_async_copy(earlier, out_ref.at[pl.ds(0, rows)], sems.at[0])
    first.start()
    fields = stage_setup(
        "corner",
        plan,
        t_size,
        names,
        received,
        perm_ref,
        x_ref,
        u_ref,
        [own_shared, z_shared, t_shared],
        None,
        alone_ref,
    )
    near, both, weight = scale_tiles(scale_ref)
    add_terms(fields, "corner", near, acc)
    direct = own_force(fields, 2, both)
    for k in range(9):
        staples = fields.compact_halves(acc_tile(acc, 0, 2 * k), acc_tile(acc, 0, 2 * k + 1))
        ready[pl.ds(k * 8, 8), :] = part_reg(t_part, 1, k) + direct[k] + weight[2] * staples[0]
        ready[pl.ds((9 + k) * 8, 8), :] = part_reg(t_part, 0, k) + weight[3] * staples[1]
    second = pltpu.make_async_copy(ready, out_ref.at[pl.ds(rows, rows)], sems.at[1])
    second.start()
    first.wait()
    second.wait()


def rows_of(count):
    return jax.ShapeDtypeStruct((count, LANES), F32)


def on_device(pole_vectors, gauge_links, pole_coeff, naik_coeff, staple_weight):
    t_size = lax.axis_size("ta")
    z_size = lax.axis_size("gz") * lax.axis_size("gy")
    plan = message_plan(t_size)
    x_rows, u_rows = 8 * REGS["x"], 4 * 8 * REGS["u"]
    vmem = pl.BlockSpec(memory_space=pltpu.VMEM)
    hbm = pl.BlockSpec(memory_space=pltpu.HBM)
    limit = pltpu.CompilerParams(vmem_limit_bytes=4 * 1024 * 1024)

    def moved(name, value):
        kind, step = name
        if kind in ("z", "b"):
            return lax.ppermute(value, ("gz", "gy"), [((i + step) % z_size, i) for i in range(z_size)])
        return lax.ppermute(value, "ta", [((j + step) % t_size, j) for j in range(t_size)])

    def exchanged(value, first):
        pairs = [(i, (i + 1) % z_size) for i in range(first, z_size, 2)]
        return lax.ppermute(value, ("gz", "gy"), pairs + [(j, i) for i, j in pairs])

    first_names = [name for name in plan if name[0] != "c"]
    corner_names = [name for name in plan if name[0] == "c"]
    t_names = [name for name in first_names if name[0] == "t"]
    in_hbm = functools.partial(pltpu.with_memory_space_constraint, memory_space=pltpu.HBM)
    z_names = [("b", 1), ("z", 2)]
    corner_count = max(plan[name].count for name in corner_names)
    exchange_counts = [plan["z", step].count for step in (1, -1)]
    exchange = max(exchange_counts + [plan["t", 1].count - corner_count + 1])
    within, between, *sends, scale, perm, x_own, u_own = pl.pallas_call(
        functools.partial(pack_z_kernel, plan, z_names),
        out_shape=[rows_of(8 * exchange), rows_of(8 * (exchange + 1))]
        + [rows_of(8 * max(plan[name].count, corner_count)) for name in z_names]
        + [
            rows_of(8 * 3 * NP),
            jax.ShapeDtypeStruct((len(all_shifts()) * LANES, LANES), jnp.bfloat16),
            rows_of(x_rows),
            rows_of(u_rows),
        ],
        in_specs=[hbm] * 5,
        out_specs=[vmem] * (len(z_names) + 6),
        scratch_shapes=[pltpu.SMEM((NP,), F32)] * 3
        + [pltpu.VMEM((u_rows, LANES), jnp.bfloat16), pltpu.SemaphoreType.DMA((5,))],
        compiler_params=limit,
        name="pack_z",
    )(
        in_hbm(pole_coeff),
        in_hbm(naik_coeff),
        in_hbm(staple_weight),
        in_hbm(pole_vectors.reshape((x_rows, LANES))),
        in_hbm(gauge_links.reshape((u_rows, LANES))),
    )
    own = [x_own, u_own]
    between, within = exchanged(between, 1), exchanged(within, 0)
    received = {name: moved(name, value) for name, value in zip(z_names, sends)}
    packed = pl.pallas_call(
        functools.partial(pack_t_kernel, plan, t_names),
        out_shape=[rows_of(8 * plan[name].count) for name in t_names],
        in_specs=[vmem] * 2,
        out_specs=[vmem] * len(t_names),
        compiler_params=limit,
        name="pack_t",
    )(*own)
    received.update({name: moved(name, value) for name, value in zip(t_names, packed)})
    shared, alone = field_split()
    part_rows = 8 * REGS["u"]

    def scratch(stage):
        sums = 1 + max(target for target, _ in TERMS[stage])
        return [pltpu.VMEM((alone[stage][1], LANES), F32), pltpu.VMEM((sums * 18 * 8, LANES), F32)]

    def cost(micros):
        return pl.CostEstimate(flops=10**6, bytes_accessed=int(3.69e6 * micros), transcendentals=0)

    wide_limit = pltpu.CompilerParams(vmem_limit_bytes=6 * 1024 * 1024)
    own_shared, own_alone = pl.pallas_call(
        functools.partial(own_fields_kernel, plan, t_size),
        out_shape=[rows_of(shared["own"][1]), rows_of(alone["own"][1])],
        in_specs=[vmem] * 3,
        out_specs=[vmem] * 2,
        compiler_params=wide_limit,
        name="fields_own",
    )(perm, *own)
    own_part = pl.pallas_call(
        own_kernel,
        out_shape=rows_of(2 * part_rows),
        in_specs=[vmem] * 5,
        out_specs=vmem,
        scratch_shapes=scratch("own")[1:],
        cost_estimate=cost(COSTS["own"]),
        compiler_params=wide_limit,
        name="force_own",
    )(scale, *own, own_shared, own_alone)
    local = [scale, perm, *own]
    received["z", 1], received["z", -1], *corners = pl.pallas_call(
        functools.partial(corner_kernel, plan, corner_names),
        out_shape=[rows_of(8 * count) for count in exchange_counts]
        + [rows_of(8 * plan[name].count) for name in corner_names],
        in_specs=[vmem] * 3,
        out_specs=[vmem] * (2 + len(corner_names)),
        compiler_params=limit,
        name="pack_corners",
    )(within, between, own_part)
    received.update({name: moved(name, value) for name, value in zip(corner_names, corners)})
    names = [("z", 1), ("z", -1)]
    z_shared, z_part = pl.pallas_call(
        functools.partial(z_kernel, plan, t_size, names),
        out_shape=[rows_of(shared["z"][1]), rows_of(2 * part_rows)],
        in_specs=[vmem] * (6 + len(names)),
        out_specs=[vmem] * 2,
        scratch_shapes=scratch("z"),
        cost_estimate=cost(COSTS["z"]),
        compiler_params=wide_limit,
        name="force_z",
    )(*local, own_shared, own_part, *[received[name] for name in names])
    far_names = t_names + [("b", 1)]
    t_shared, t_part, earlier = pl.pallas_call(
        functools.partial(t_kernel, plan, t_size, far_names),
        out_shape=[rows_of(shared["t"][1]), rows_of(2 * part_rows), rows_of(2 * part_rows)],
        in_specs=[vmem] * (7 + len(far_names)),
        out_specs=[vmem] * 3,
        scratch_shapes=scratch("t"),
        cost_estimate=cost(COSTS["t"]),
        compiler_params=wide_limit,
        name="force_t",
    )(*local, own_shared, z_shared, z_part, *[received[name] for name in far_names])
    names = list(received)
    force = pl.pallas_call(
        functools.partial(last_kernel, plan, t_size, names),
        out_shape=rows_of(u_rows),
        in_specs=[vmem] * (9 + len(names)),
        out_specs=hbm,
        scratch_shapes=scratch("corner")
        + [pltpu.VMEM((2 * part_rows, LANES), F32), pltpu.SemaphoreType.DMA((2,))],
        cost_estimate=cost(COSTS["corner"]),
        compiler_params=wide_limit,
        name="force_corner",
    )(
        *local,
        own_shared,
        z_shared,
        t_shared,
        t_part,
        earlier,
        *[received[name] for name in names],
    )
    return force.reshape(gauge_links.shape)


def solution(mesh):
    return jax.shard_map(
        on_device,
        mesh=mesh,
        in_specs=(
            P("ens", None, None, "ta", ("gz", "gy"), None),
            P("ens", None, None, None, "ta", ("gz", "gy"), None),
            P(),
            P(),
            P(),
        ),
        out_specs=P("ens", None, None, None, "ta", ("gz", "gy"), None),
        check_vma=False,
    )
```

```python
import collections
import functools

import jax
import jax.numpy as jnp
from jax import lax
from jax.experimental import pallas as pl
from jax.experimental.pallas import tpu as pltpu
from jax.sharding import PartitionSpec as P

NX = 8
NY = 16
LANES = NX * NY
NP = 4
F32 = jnp.float32
REGS = {"x": NP * 3, "u": 9}
UNIT = ((1, 0, 0, 0), (0, 1, 0, 0), (0, 0, 1, 0), (0, 0, 0, 1))
ZERO = (0, 0, 0, 0)
SITES = ((0, 0), (0, 1), (1, 0), (1, 1))
STAGES = ("own", "z", "t", "corner")
TERMS = {
    "own": ((0, ((0, 1), (1, 0))),),
    "z": ((0, ((0, 2), (1, 2))),),
    "t": ((0, ((0, 3), (1, 3))), (1, ((3, 0), (3, 1))), (2, ((2, 0), (2, 1)))),
    "corner": ((0, ((2, 3), (3, 2))),),
}
COSTS = {"own": 2.0, "z": 2.0, "t": 2.0, "corner": 1.0}
DIRECT = {"own": (0, 1), "z": (), "t": (3,), "corner": (2,)}


def plus(left, right, scale=1):
    return tuple(a + scale * b for a, b in zip(left, right))


class Message:
    def __init__(self):
        self.places = collections.OrderedDict()
        self.count = 0

    def add_full(self, kind, n):
        for k in range(REGS[kind]):
            for t, z in SITES:
                self.places[0, kind, n, k, t, z] = (self.count, 2 * t + z)
            self.count += 1

    def add_halves(self, entries, axis):
        half = -(-len(entries) // 2)
        for index, (kind, n, k, layer) in enumerate(entries):
            reg, part = self.count + index % half, index // half
            for other in range(2):
                t, z = (layer, other) if axis == "t" else (other, layer)
                slot = 2 * part + other if axis == "t" else 2 * other + part
                self.places[0, kind, n, k, t, z] = (reg, slot)
        self.count += half

    def add_single(self, entries):
        quarter = -(-len(entries) // 4)
        for index, entry in enumerate(entries):
            self.places[entry] = (self.count + index % quarter, index // quarter)
        self.count += quarter

    def by_register(self):
        found = [[None] * 4 for _ in range(self.count)]
        for item, (reg, slot) in self.places.items():
            found[reg][slot] = item
        return found


def regs_of(kind, directions, layer):
    return [(kind, n, k, layer) for n in directions for k in range(REGS[kind])]


def message_plan(t_size):
    plan = collections.OrderedDict()
    ahead = plan["z", 1] = Message()
    ahead.add_halves(regs_of("x", (0,), 0) + regs_of("u", (3,), 0), "z")
    late = plan["b", 1] = Message()
    late.add_halves(regs_of("x", (0,), 1) + regs_of("u", (0, 1), 0), "z")
    behind = plan["z", -1] = Message()
    behind.add_halves(regs_of("x", (0,), 1) + regs_of("u", (2,), 1), "z")
    second = plan["z", 2] = Message()
    second.add_halves(regs_of("x", (0,), 0), "z")
    halves, corners = collections.OrderedDict(), collections.OrderedDict()
    for dt, entries in (
        (1, regs_of("u", (0, 1, 2), 0)),
        (-1, regs_of("x", (0,), 1) + regs_of("u", (3,), 1)),
        (2, regs_of("x", (0,), 0)),
    ):
        if dt % t_size != 0:
            halves.setdefault(dt % t_size, []).extend(entries)
    for dt, entries in halves.items():
        message = plan["t", dt] = Message()
        if dt == 1:
            message.add_full("x", 0)
        held = {item[1:4] for item in message.places}
        message.add_halves([e for e in entries if e[:3] not in held], "t")
    for dt, entries in (
        (1, [(1, "x", 0, k, 0, 0) for k in range(REGS["x"])]),
        (1, [(-1, "x", 0, k, 0, 1) for k in range(REGS["x"])]),
        (1, [(-1, "u", 2, k, 0, 1) for k in range(REGS["u"])]),
        (-1, [(1, "x", 0, k, 1, 0) for k in range(REGS["x"])]),
        (-1, [(1, "u", 3, k, 1, 0) for k in range(REGS["u"])]),
    ):
        corners.setdefault(dt % t_size, []).extend(entries)
    for dt, entries in corners.items():
        plan["c", dt] = Message()
        plan["c", dt].add_single(entries)
    return plan


class Locator:
    def __init__(self, plan, t_size, buffers):
        self.plan, self.t_size, self.buffers = plan, t_size, buffers

    def local(self, kind, n, k, t, z):
        return ("own", kind), n * REGS[kind] + k, 2 * t + z

    def find(self, kind, n, k, t_at, z_at):
        (dt, t), (dz, z) = divmod(t_at, 2), divmod(z_at, 2)
        dt %= self.t_size
        if (dt, dz) == (0, 0):
            return self.local(kind, n, k, t, z)
        name = ("z", dz) if dt == 0 else ("t", dt) if dz == 0 else ("c", dt)
        item = (dz if name[0] == "c" else 0, kind, n, k, t, z)
        if name == ("z", 1) and item not in self.plan[name].places:
            name = ("b", 1)
        return (name,) + self.plan[name].places[item]

    def load(self, name, reg):
        return self.buffers[name][pl.ds(8 * reg, 8), :]

    def assemble(self, spots):
        groups = collections.OrderedDict()
        for r, spot in enumerate(spots):
            if spot is not None:
                groups.setdefault((spot[0], spot[1], r - spot[2]), []).append(r)
        row = lax.broadcasted_iota(jnp.int32, (8, LANES), 0) % 4
        result = None
        for (name, reg, move), rows in groups.items():
            value = self.load(name, reg)
            if move != 0:
                value = pltpu.roll(value, move % 8, 0)
            if result is None:
                result = value
            else:
                mask = functools.reduce(jnp.logical_or, [row == r for r in rows])
                result = jnp.where(mask, value, result)
        return result

    def field_register(self, kind, n, k, dt, dz):
        return self.assemble([self.find(kind, n, k, t + dt, z + dz) for t, z in SITES])


def term_fields(halves, sign):
    here, ahead, left, right = [], [], [], []
    for m, n in halves:
        start = plus(ZERO, UNIT[n], sign)
        base = ZERO if sign > 0 else start
        here.append(("x", 0, start))
        ahead.append(("x", 0, plus(start, UNIT[m])))
        left.append(("u", n, base))
        right.append(("u", n, plus(base, UNIT[m])))
    return here, ahead, left, right


def needed_fields(stage):
    keys = collections.OrderedDict()
    for _, halves in TERMS[stage]:
        for sign in (1, -1):
            for pair in term_fields(halves, sign):
                keys.update((key, None) for key in pair)
    for m in DIRECT[stage]:
        for scale in (1, 3):
            keys["x", 0, plus(ZERO, UNIT[m], scale)] = None
    return [key for key in keys if key[2] != ZERO]


def stage_of(key):
    dz, dt = key[2][2:]
    if key[0] == "u" and key[1] < 2 and dz == 1 and dt == 0:
        return "t"
    if abs(dz) == 3 or (dz != 0 and dt != 0):
        return "corner"
    return "t" if dt != 0 else "z" if dz != 0 else "own"


def lay_out(keys):
    rows, total = collections.OrderedDict(), 0
    for key in keys:
        rows[key] = total
        total += 8 * REGS[key[0]]
    return rows, total


def field_split():
    uses = collections.OrderedDict()
    for stage in STAGES:
        for key in needed_fields(stage):
            uses.setdefault(key, []).append(stage)
    shared, alone = {}, {}
    for stage in STAGES:
        built = [key for key in uses if stage_of(key) == stage]
        shared[stage] = lay_out([key for key in built if uses[key] != [stage]])
        alone[stage] = lay_out([key for key in built if uses[key] == [stage]])
    return shared, alone


def all_shifts():
    found = collections.OrderedDict()
    for stage in STAGES:
        for _, _, (dx, dy, _, _) in needed_fields(stage):
            if (dx, dy) != (0, 0):
                found[dx, dy] = None
    return list(found)


def write_shifts(perm_ref):
    lane = lax.broadcasted_iota(jnp.int32, (LANES, LANES), 1)
    source = lax.broadcasted_iota(jnp.int32, (LANES, LANES), 0)
    for index, (dx, dy) in enumerate(all_shifts()):
        wanted = (lane // NX + dy + NY) % NY * NX + (lane + dx + NX) % NX
        perm_ref[pl.ds(index * LANES, LANES), :] = (source == wanted).astype(F32).astype(jnp.bfloat16)


def parts_of(kind, value):
    if kind == "u":
        return [value.astype(jnp.bfloat16)]
    high = value.astype(jnp.bfloat16)
    rest = value - high.astype(F32)
    middle = rest.astype(jnp.bfloat16)
    return [high, middle, (rest - middle.astype(F32)).astype(jnp.bfloat16)]


def build_fields(locator, perm_ref, stores):
    groups = collections.OrderedDict()
    for ref, rows in stores:
        for (kind, n, disp), row in rows.items():
            shifts = groups.setdefault((kind, n, disp[3], disp[2]), collections.OrderedDict())
            shifts[disp[0], disp[1]] = (ref, row)
    order = all_shifts()
    for (kind, n, dt, dz), shifts in groups.items():
        regs = [locator.field_register(kind, n, k, dt, dz) for k in range(REGS[kind])]
        if (0, 0) in shifts:
            ref, row = shifts[0, 0]
            for k, value in enumerate(regs):
                ref[pl.ds(row + 8 * k, 8), :] = value
        parts = parts_of(kind, jnp.concatenate(regs, axis=0))
        for shift, (ref, row) in shifts.items():
            if shift != (0, 0):
                perm = perm_ref[pl.ds(order.index(shift) * LANES, LANES), :]
                moved = [jnp.dot(part, perm, preferred_element_type=F32) for part in parts]
                ref[pl.ds(row, 8 * REGS[kind]), :] = functools.reduce(jnp.add, moved)


class Fields:
    def __init__(self, own_x, own_u, stores):
        self.place = {("x", 0, ZERO): (own_x, 0)}
        for n in range(4):
            self.place["u", n, ZERO] = (own_u, 8 * REGS["u"] * n)
        for ref, rows in stores:
            for key, row in rows.items():
                self.place[key] = (ref, row)
        self.upper = lax.broadcasted_iota(jnp.int32, (8, LANES), 0) < 4

    def reg(self, key, k):
        ref, row = self.place[key]
        return ref[pl.ds(row + 8 * k, 8), :]

    def two_tiles(self, keys, k):
        top = self.reg(keys[0], k)
        turned_top = pltpu.roll(top, 4, 0)
        if keys[0] == keys[1]:
            low, turned_low = top, turned_top
        else:
            low = self.reg(keys[1], k)
            turned_low = pltpu.roll(low, 4, 0)
        return [jnp.where(self.upper, top, turned_low), jnp.where(self.upper, turned_top, low)]

    def vector(self, keys, pole):
        flat = [tile for k in range(3) for tile in self.two_tiles(keys, 3 * pole + k)]
        return [flat[:3], flat[3:]]

    def matrix(self, keys):
        flat = [tile for k in range(9) for tile in self.two_tiles(keys, k)]
        return [[flat[9 * c + 3 * i : 9 * c + 3 * i + 3] for i in range(3)] for c in range(2)]

    def compact_halves(self, first, second):
        top = jnp.where(self.upper, first, pltpu.roll(second, 4, 0))
        return top, jnp.where(self.upper, pltpu.roll(first, 4, 0), second)

    def compact_sum(self, first, second):
        kept = jnp.where(self.upper, first, second)
        return kept + pltpu.roll(jnp.where(self.upper, second, first), 4, 0)


def pole_sum(fields, here, ahead, scales):
    total = None
    for pole in range(NP):
        h = [[scales[pole] * v for v in part] for part in fields.vector(here, pole)]
        a = fields.vector(ahead, pole)
        real = [[a[0][i] * h[0][j] + a[1][i] * h[1][j] for j in range(3)] for i in range(3)]
        imag = [[a[1][i] * h[0][j] - a[0][i] * h[1][j] for j in range(3)] for i in range(3)]
        if total is None:
            total = [real, imag]
        else:
            total = [
                [[total[c][i][j] + new[i][j] for j in range(3)] for i in range(3)]
                for c, new in enumerate((real, imag))
            ]
    return total


def transposed(matrix):
    return [[[part[j][i] for j in range(3)] for i in range(3)] for part in matrix]


def row_times(row, right, row_sign, right_sign):
    result = [[], []]
    for j in range(3):
        real = imag = None
        for k in range(3):
            rr = row[0][k] * right[0][k][j]
            ii = row[1][k] * right[1][k][j]
            ri = row[0][k] * right[1][k][j]
            ir = row[1][k] * right[0][k][j]
            new_real = rr - ii if row_sign * right_sign > 0 else rr + ii
            if row_sign > 0 and right_sign > 0:
                new_imag = ri + ir
            elif row_sign > 0:
                new_imag = ir - ri
            else:
                new_imag = ri - ir
            real = new_real if real is None else real + new_real
            imag = new_imag if imag is None else imag + new_imag
        result[0].append(real)
        result[1].append(imag)
    return result


def add_terms(fields, stage, near, acc):
    started = set()
    for target, halves in TERMS[stage]:
        for sign in (1, -1):
            here, ahead, left, right = term_fields(halves, sign)
            force = pole_sum(fields, here, ahead, near)
            left = fields.matrix(left)
            right = fields.matrix(right)
            if sign > 0:
                right = transposed(right)
            else:
                left = transposed(left)
            rows = [row_times([left[0][i], left[1][i]], force, sign, 1) for i in range(3)]
            for i in range(3):
                row = row_times(rows[i], right, 1, -sign)
                for part in range(2):
                    for j in range(3):
                        at = pl.ds((target * 18 + part * 9 + i * 3 + j) * 8, 8)
                        new = row[part][j]
                        acc[at, :] = acc[at, :] + new if target in started else new
            started.add(target)


def acc_tile(acc, target, c):
    return acc[pl.ds((target * 18 + c) * 8, 8), :]


def scale_tiles(scale_ref):
    tiles = [scale_ref[pl.ds(8 * p, 8), :] for p in range(3 * NP)]
    return tiles[:NP], tiles[NP : 2 * NP], tiles[2 * NP :]


def own_force(fields, m, both):
    total = pole_sum(
        fields,
        [("x", 0, ZERO)] * 2,
        [("x", 0, UNIT[m]), ("x", 0, plus(ZERO, UNIT[m], 3))],
        both,
    )
    flat = [total[c][i][j] for c in range(2) for i in range(3) for j in range(3)]
    return [fields.compact_sum(flat[2 * k], flat[2 * k + 1]) for k in range(9)]


def write_messages(locator, plan, names, outs):
    for name, out in zip(names, outs):
        for reg, items in enumerate(plan[name].by_register()):
            spots = [item and locator.local(*item[1:]) for item in items]
            out[pl.ds(8 * reg, 8), :] = locator.assemble(spots)


def odd_in_z():
    return (lax.axis_index("gz") * lax.axis_size("gy") + lax.axis_index("gy")) % 2 == 1


def pack_z_kernel(plan, names, near_in, far_in, weight_in, x_in, u_in, *rest):
    within_ref, between_ref = rest[:2]
    outs = rest[2 : 2 + len(names)]
    scale_ref, perm_ref, x_ref, u_ref, near_ref, far_ref, weight_ref, u_held, sems = rest[2 + len(names) :]
    copies = [
        pltpu.make_async_copy(source, target, sems.at[index])
        for index, (source, target) in enumerate(
            ((u_in, u_held), (x_in, x_ref), (near_in, near_ref), (far_in, far_ref), (weight_in, weight_ref))
        )
    ]
    for copy in copies:
        copy.start()
    write_shifts(perm_ref)
    for copy in copies:
        copy.wait()
    u_ref[...] = u_held[...].astype(F32)
    locator = Locator(plan, 1, {("own", "x"): x_ref, ("own", "u"): u_ref})
    both = [("z", 1), ("z", -1)]

    @pl.when(odd_in_z())
    def _():
        write_messages(locator, plan, both, (within_ref, between_ref))

    @pl.when(jnp.logical_not(odd_in_z()))
    def _():
        write_messages(locator, plan, both, (between_ref, within_ref))

    write_messages(locator, plan, names, outs)
    write_scales(near_ref, far_ref, weight_ref, scale_ref)


def pack_t_kernel(plan, names, x_ref, u_ref, *outs):
    write_messages(Locator(plan, 1, {("own", "x"): x_ref, ("own", "u"): u_ref}), plan, names, outs)


def corner_kernel(plan, names, within_ref, between_ref, ahead_ref, behind_ref, *outs):
    def split(from_ahead, from_behind):
        ahead_ref[...] = from_ahead[pl.ds(0, ahead_ref.shape[0]), :]
        behind_ref[...] = from_behind[pl.ds(0, behind_ref.shape[0]), :]

    @pl.when(odd_in_z())
    def _():
        split(between_ref, within_ref)

    @pl.when(jnp.logical_not(odd_in_z()))
    def _():
        split(within_ref, between_ref)

    locator = Locator(plan, 1, {("z", 1): ahead_ref, ("z", -1): behind_ref})
    for name, out in zip(names, outs):
        for reg, items in enumerate(plan[name].by_register()):
            spots = [
                item and (("z", item[0]),) + plan["z", item[0]].places[(0,) + item[1:]] for item in items
            ]
            out[pl.ds(8 * reg, 8), :] = locator.assemble(spots)


def part_reg(ref, index, k):
    return ref[pl.ds((9 * index + k) * 8, 8), :]


def write_scales(near_ref, far_ref, weight_ref, scale_ref):
    upper = lax.broadcasted_iota(jnp.int32, (8, LANES), 0) < 4
    for p in range(NP):
        scale_ref[pl.ds(8 * p, 8), :] = jnp.full((8, LANES), near_ref[p], F32)
        scale_ref[pl.ds(8 * (NP + p), 8), :] = jnp.where(upper, near_ref[p], far_ref[p])
        scale_ref[pl.ds(8 * (2 * NP + p), 8), :] = jnp.full((8, LANES), weight_ref[p], F32)


def own_fields_kernel(plan, t_size, perm_ref, x_ref, u_ref, shared_ref, alone_ref):
    shared, alone = field_split()
    stores = [(shared_ref, shared["own"][0]), (alone_ref, alone["own"][0])]
    build_fields(Locator(plan, t_size, {("own", "x"): x_ref, ("own", "u"): u_ref}), perm_ref, stores)


def own_kernel(scale_ref, x_ref, u_ref, shared_ref, alone_ref, part_ref, acc):
    shared, alone = field_split()
    fields = Fields(x_ref, u_ref, [(shared_ref, shared["own"][0]), (alone_ref, alone["own"][0])])
    near, both, weight = scale_tiles(scale_ref)
    add_terms(fields, "own", near, acc)
    direct = [own_force(fields, m, both) for m in DIRECT["own"]]
    for k in range(9):
        staples = fields.compact_halves(acc_tile(acc, 0, 2 * k), acc_tile(acc, 0, 2 * k + 1))
        for m in range(2):
            part_ref[pl.ds((9 * m + k) * 8, 8), :] = direct[m][k] + weight[m] * staples[m]


def stage_setup(stage, plan, t_size, names, received, perm_ref, x_ref, u_ref, shared_refs, shared_ref, alone_ref):
    buffers = {("own", "x"): x_ref, ("own", "u"): u_ref}
    buffers.update(zip(names, received))
    shared, alone = field_split()
    stores = [(alone_ref, alone[stage][0])]
    if shared_ref is not None:
        stores.append((shared_ref, shared[stage][0]))
    build_fields(Locator(plan, t_size, buffers), perm_ref, stores)
    earlier = [(ref, shared[name][0]) for name, ref in zip(STAGES, shared_refs)]
    return Fields(x_ref, u_ref, earlier + stores)


def z_kernel(plan, t_size, names, scale_ref, perm_ref, x_ref, u_ref, own_shared, own_part, *rest):
    received = rest[: len(names)]
    shared_ref, part_ref, alone_ref, acc = rest[len(names) :]
    fields = stage_setup(
        "z", plan, t_size, names, received, perm_ref, x_ref, u_ref, [own_shared], shared_ref, alone_ref
    )
    near, _, weight = scale_tiles(scale_ref)
    add_terms(fields, "z", near, acc)
    for k in range(9):
        staples = fields.compact_halves(acc_tile(acc, 0, 2 * k), acc_tile(acc, 0, 2 * k + 1))
        for m in range(2):
            part_ref[pl.ds((9 * m + k) * 8, 8), :] = part_reg(own_part, m, k) + weight[m] * staples[m]


def t_kernel(plan, t_size, names, scale_ref, perm_ref, x_ref, u_ref, own_shared, z_shared, z_part, *rest):
    received = rest[: len(names)]
    shared_ref, part_ref, ready, alone_ref, acc = rest[len(names) :]
    fields = stage_setup(
        "t", plan, t_size, names, received, perm_ref, x_ref, u_ref, [own_shared, z_shared], shared_ref, alone_ref
    )
    near, both, weight = scale_tiles(scale_ref)
    add_terms(fields, "t", near, acc)
    for k in range(9):
        staples = fields.compact_halves(acc_tile(acc, 0, 2 * k), acc_tile(acc, 0, 2 * k + 1))
        for m in range(2):
            ready[pl.ds((9 * m + k) * 8, 8), :] = part_reg(z_part, m, k) + weight[m] * staples[m]
    direct = own_force(fields, 3, both)
    for k in range(9):
        staple = fields.compact_sum(acc_tile(acc, 1, 2 * k), acc_tile(acc, 1, 2 * k + 1))
        part_ref[pl.ds(k * 8, 8), :] = direct[k] + weight[3] * staple
        staple = fields.compact_sum(acc_tile(acc, 2, 2 * k), acc_tile(acc, 2, 2 * k + 1))
        part_ref[pl.ds((9 + k) * 8, 8), :] = weight[2] * staple


def last_kernel(plan, t_size, names, scale_ref, perm_ref, x_ref, u_ref, *rest):
    own_shared, z_shared, t_shared, t_part, earlier = rest[:5]
    received = rest[5 : 5 + len(names)]
    out_ref, alone_ref, acc, ready, sems = rest[5 + len(names) :]
    rows = ready.shape[0]
    first = pltpu.make_async_copy(earlier, out_ref.at[pl.ds(0, rows)], sems.at[0])
    first.start()
    fields = stage_setup(
        "corner",
        plan,
        t_size,
        names,
        received,
        perm_ref,
        x_ref,
        u_ref,
        [own_shared, z_shared, t_shared],
        None,
        alone_ref,
    )
    near, both, weight = scale_tiles(scale_ref)
    add_terms(fields, "corner", near, acc)
    direct = own_force(fields, 2, both)
    for k in range(9):
        staples = fields.compact_halves(acc_tile(acc, 0, 2 * k), acc_tile(acc, 0, 2 * k + 1))
        ready[pl.ds(k * 8, 8), :] = part_reg(t_part, 1, k) + direct[k] + weight[2] * staples[0]
        ready[pl.ds((9 + k) * 8, 8), :] = part_reg(t_part, 0, k) + weight[3] * staples[1]
    second = pltpu.make_async_copy(ready, out_ref.at[pl.ds(rows, rows)], sems.at[1])
    second.start()
    first.wait()
    second.wait()


def rows_of(count):
    return jax.ShapeDtypeStruct((count, LANES), F32)


def on_device(pole_vectors, gauge_links, pole_coeff, naik_coeff, staple_weight):
    t_size = lax.axis_size("ta")
    z_size = lax.axis_size("gz") * lax.axis_size("gy")
    plan = message_plan(t_size)
    x_rows, u_rows = 8 * REGS["x"], 4 * 8 * REGS["u"]
    vmem = pl.BlockSpec(memory_space=pltpu.VMEM)
    hbm = pl.BlockSpec(memory_space=pltpu.HBM)
    limit = pltpu.CompilerParams(vmem_limit_bytes=4 * 1024 * 1024)

    def moved(name, value):
        kind, step = name
        if kind in ("z", "b"):
            return lax.ppermute(value, ("gz", "gy"), [((i + step) % z_size, i) for i in range(z_size)])
        return lax.ppermute(value, "ta", [((j + step) % t_size, j) for j in range(t_size)])

    def exchanged(value, first):
        pairs = [(i, (i + 1) % z_size) for i in range(first, z_size, 2)]
        return lax.ppermute(value, ("gz", "gy"), pairs + [(j, i) for i, j in pairs])

    first_names = [name for name in plan if name[0] != "c"]
    corner_names = [name for name in plan if name[0] == "c"]
    t_names = [name for name in first_names if name[0] == "t"]
    in_hbm = functools.partial(pltpu.with_memory_space_constraint, memory_space=pltpu.HBM)
    z_names = [("b", 1), ("z", 2)]
    corner_count = max(plan[name].count for name in corner_names)
    late = max(plan["b", 1].count, corner_count)
    late_counts = [late, late + 1]
    exchange_counts = [plan["z", step].count for step in (1, -1)]
    exchange = max(exchange_counts + [plan["t", 1].count - corner_count + 1])
    within, between, *sends, scale, perm, x_own, u_own = pl.pallas_call(
        functools.partial(pack_z_kernel, plan, z_names),
        out_shape=[rows_of(8 * exchange), rows_of(8 * (exchange + 1))]
        + [rows_of(8 * max(plan[name].count, least)) for name, least in zip(z_names, late_counts)]
        + [
            rows_of(8 * 3 * NP),
            jax.ShapeDtypeStruct((len(all_shifts()) * LANES, LANES), jnp.bfloat16),
            rows_of(x_rows),
            rows_of(u_rows),
        ],
        in_specs=[hbm] * 5,
        out_specs=[vmem] * (len(z_names) + 6),
        scratch_shapes=[pltpu.SMEM((NP,), F32)] * 3
        + [pltpu.VMEM((u_rows, LANES), jnp.bfloat16), pltpu.SemaphoreType.DMA((5,))],
        compiler_params=limit,
        name="pack_z",
    )(
        in_hbm(pole_coeff),
        in_hbm(naik_coeff),
        in_hbm(staple_weight),
        in_hbm(pole_vectors.reshape((x_rows, LANES))),
        in_hbm(gauge_links.reshape((u_rows, LANES))),
    )
    own = [x_own, u_own]
    between, within = exchanged(between, 1), exchanged(within, 0)
    received = {name: moved(name, value) for name, value in zip(z_names, sends)}
    packed = pl.pallas_call(
        functools.partial(pack_t_kernel, plan, t_names),
        out_shape=[rows_of(8 * plan[name].count) for name in t_names],
        in_specs=[vmem] * 2,
        out_specs=[vmem] * len(t_names),
        compiler_params=limit,
        name="pack_t",
    )(*own)
    received.update({name: moved(name, value) for name, value in zip(t_names, packed)})
    shared, alone = field_split()
    part_rows = 8 * REGS["u"]

    def scratch(stage):
        sums = 1 + max(target for target, _ in TERMS[stage])
        return [pltpu.VMEM((alone[stage][1], LANES), F32), pltpu.VMEM((sums * 18 * 8, LANES), F32)]

    def cost(micros):
        return pl.CostEstimate(flops=10**6, bytes_accessed=int(3.69e6 * micros), transcendentals=0)

    wide_limit = pltpu.CompilerParams(vmem_limit_bytes=6 * 1024 * 1024)
    own_shared, own_alone = pl.pallas_call(
        functools.partial(own_fields_kernel, plan, t_size),
        out_shape=[rows_of(shared["own"][1]), rows_of(alone["own"][1])],
        in_specs=[vmem] * 3,
        out_specs=[vmem] * 2,
        compiler_params=wide_limit,
        name="fields_own",
    )(perm, *own)
    own_part = pl.pallas_call(
        own_kernel,
        out_shape=rows_of(2 * part_rows),
        in_specs=[vmem] * 5,
        out_specs=vmem,
        scratch_shapes=scratch("own")[1:],
        cost_estimate=cost(COSTS["own"]),
        compiler_params=wide_limit,
        name="force_own",
    )(scale, *own, own_shared, own_alone)
    local = [scale, perm, *own]
    received["z", 1], received["z", -1], *corners = pl.pallas_call(
        functools.partial(corner_kernel, plan, corner_names),
        out_shape=[rows_of(8 * count) for count in exchange_counts]
        + [rows_of(8 * plan[name].count) for name in corner_names],
        in_specs=[vmem] * 2,
        out_specs=[vmem] * (2 + len(corner_names)),
        compiler_params=limit,
        name="pack_corners",
    )(within, between)
    received.update({name: moved(name, value) for name, value in zip(corner_names, corners)})
    names = [("z", 1), ("z", -1)]
    z_shared, z_part = pl.pallas_call(
        functools.partial(z_kernel, plan, t_size, names),
        out_shape=[rows_of(shared["z"][1]), rows_of(2 * part_rows)],
        in_specs=[vmem] * (6 + len(names)),
        out_specs=[vmem] * 2,
        scratch_shapes=scratch("z"),
        cost_estimate=cost(COSTS["z"]),
        compiler_params=wide_limit,
        name="force_z",
    )(*local, own_shared, own_part, *[received[name] for name in names])
    far_names = t_names + [("b", 1)]
    t_shared, t_part, earlier = pl.pallas_call(
        functools.partial(t_kernel, plan, t_size, far_names),
        out_shape=[rows_of(shared["t"][1]), rows_of(2 * part_rows), rows_of(2 * part_rows)],
        in_specs=[vmem] * (7 + len(far_names)),
        out_specs=[vmem] * 3,
        scratch_shapes=scratch("t"),
        cost_estimate=cost(COSTS["t"]),
        compiler_params=wide_limit,
        name="force_t",
    )(*local, own_shared, z_shared, z_part, *[received[name] for name in far_names])
    names = list(received)
    force = pl.pallas_call(
        functools.partial(last_kernel, plan, t_size, names),
        out_shape=rows_of(u_rows),
        in_specs=[vmem] * (9 + len(names)),
        out_specs=hbm,
        scratch_shapes=scratch("corner")
        + [pltpu.VMEM((2 * part_rows, LANES), F32), pltpu.SemaphoreType.DMA((2,))],
        cost_estimate=cost(COSTS["corner"]),
        compiler_params=wide_limit,
        name="force_corner",
    )(
        *local,
        own_shared,
        z_shared,
        t_shared,
        t_part,
        earlier,
        *[received[name] for name in names],
    )
    return force.reshape(gauge_links.shape)


def solution(mesh):
    return jax.shard_map(
        on_device,
        mesh=mesh,
        in_specs=(
            P("ens", None, None, "ta", ("gz", "gy"), None),
            P("ens", None, None, None, "ta", ("gz", "gy"), None),
            P(),
            P(),
            P(),
        ),
        out_specs=P("ens", None, None, None, "ta", ("gz", "gy"), None),
        check_vma=False,
    )
```

```python
import collections
import functools

import jax
import jax.numpy as jnp
from jax import lax
from jax.experimental import pallas as pl
from jax.experimental.pallas import tpu as pltpu
from jax.sharding import PartitionSpec as P

NX = 8
NY = 16
LANES = NX * NY
NP = 4
F32 = jnp.float32
REGS = {"x": NP * 3, "u": 9}
UNIT = ((1, 0, 0, 0), (0, 1, 0, 0), (0, 0, 1, 0), (0, 0, 0, 1))
ZERO = (0, 0, 0, 0)
SITES = ((0, 0), (0, 1), (1, 0), (1, 1))
STAGES = ("own", "z", "t", "corner")
TERMS = {
    "own": ((0, ((0, 1), (1, 0))),),
    "z": ((0, ((0, 2), (1, 2))),),
    "t": ((0, ((0, 3), (1, 3))), (1, ((3, 0), (3, 1))), (2, ((2, 0), (2, 1)))),
    "corner": ((0, ((2, 3), (3, 2))),),
}
COSTS = {"own": 2.0, "z": 2.0, "t": 2.0, "corner": 1.0}
DIRECT = {"own": (0, 1), "z": (), "t": (2, 3), "corner": ()}


def plus(left, right, scale=1):
    return tuple(a + scale * b for a, b in zip(left, right))


class Message:
    def __init__(self):
        self.places = collections.OrderedDict()
        self.count = 0

    def add_full(self, kind, n):
        for k in range(REGS[kind]):
            for t, z in SITES:
                self.places[0, kind, n, k, t, z] = (self.count, 2 * t + z)
            self.count += 1

    def add_halves(self, entries, axis):
        half = -(-len(entries) // 2)
        for index, (kind, n, k, layer) in enumerate(entries):
            reg, part = self.count + index % half, index // half
            for other in range(2):
                t, z = (layer, other) if axis == "t" else (other, layer)
                slot = 2 * part + other if axis == "t" else 2 * other + part
                self.places[0, kind, n, k, t, z] = (reg, slot)
        self.count += half

    def add_single(self, entries):
        quarter = -(-len(entries) // 4)
        for index, entry in enumerate(entries):
            self.places[entry] = (self.count + index % quarter, index // quarter)
        self.count += quarter

    def by_register(self):
        found = [[None] * 4 for _ in range(self.count)]
        for item, (reg, slot) in self.places.items():
            found[reg][slot] = item
        return found


def regs_of(kind, directions, layer):
    return [(kind, n, k, layer) for n in directions for k in range(REGS[kind])]


def message_plan(t_size):
    plan = collections.OrderedDict()
    ahead = plan["z", 1] = Message()
    ahead.add_halves(regs_of("x", (0,), 0) + regs_of("u", (3,), 0), "z")
    late = plan["b", 1] = Message()
    late.add_halves(regs_of("x", (0,), 1) + regs_of("u", (0, 1), 0), "z")
    behind = plan["z", -1] = Message()
    behind.add_halves(regs_of("x", (0,), 1) + regs_of("u", (2,), 1), "z")
    second = plan["z", 2] = Message()
    second.add_halves(regs_of("x", (0,), 0), "z")
    halves, corners = collections.OrderedDict(), collections.OrderedDict()
    for dt, entries in (
        (1, regs_of("u", (0, 1, 2), 0)),
        (-1, regs_of("x", (0,), 1) + regs_of("u", (3,), 1)),
        (2, regs_of("x", (0,), 0)),
    ):
        if dt % t_size != 0:
            halves.setdefault(dt % t_size, []).extend(entries)
    for dt, entries in halves.items():
        message = plan["t", dt] = Message()
        if dt == 1:
            message.add_full("x", 0)
        held = {item[1:4] for item in message.places}
        message.add_halves([e for e in entries if e[:3] not in held], "t")
    for dt, entries in (
        (1, [(1, "x", 0, k, 0, 0) for k in range(REGS["x"])]),
        (1, [(-1, "x", 0, k, 0, 1) for k in range(REGS["x"])]),
        (1, [(-1, "u", 2, k, 0, 1) for k in range(REGS["u"])]),
        (-1, [(1, "x", 0, k, 1, 0) for k in range(REGS["x"])]),
        (-1, [(1, "u", 3, k, 1, 0) for k in range(REGS["u"])]),
    ):
        corners.setdefault(dt % t_size, []).extend(entries)
    for dt, entries in corners.items():
        plan["c", dt] = Message()
        plan["c", dt].add_single(entries)
    return plan


class Locator:
    def __init__(self, plan, t_size, buffers):
        self.plan, self.t_size, self.buffers = plan, t_size, buffers

    def local(self, kind, n, k, t, z):
        return ("own", kind), n * REGS[kind] + k, 2 * t + z

    def find(self, kind, n, k, t_at, z_at):
        (dt, t), (dz, z) = divmod(t_at, 2), divmod(z_at, 2)
        dt %= self.t_size
        if (dt, dz) == (0, 0):
            return self.local(kind, n, k, t, z)
        name = ("z", dz) if dt == 0 else ("t", dt) if dz == 0 else ("c", dt)
        item = (dz if name[0] == "c" else 0, kind, n, k, t, z)
        if name == ("z", 1) and item not in self.plan[name].places:
            name = ("b", 1)
        return (name,) + self.plan[name].places[item]

    def load(self, name, reg):
        return self.buffers[name][pl.ds(8 * reg, 8), :]

    def assemble(self, spots):
        groups = collections.OrderedDict()
        for r, spot in enumerate(spots):
            if spot is not None:
                groups.setdefault((spot[0], spot[1], r - spot[2]), []).append(r)
        row = lax.broadcasted_iota(jnp.int32, (8, LANES), 0) % 4
        result = None
        for (name, reg, move), rows in groups.items():
            value = self.load(name, reg)
            if move != 0:
                value = pltpu.roll(value, move % 8, 0)
            if result is None:
                result = value
            else:
                mask = functools.reduce(jnp.logical_or, [row == r for r in rows])
                result = jnp.where(mask, value, result)
        return result

    def field_register(self, kind, n, k, dt, dz):
        return self.assemble([self.find(kind, n, k, t + dt, z + dz) for t, z in SITES])


def term_fields(halves, sign):
    here, ahead, left, right = [], [], [], []
    for m, n in halves:
        start = plus(ZERO, UNIT[n], sign)
        base = ZERO if sign > 0 else start
        here.append(("x", 0, start))
        ahead.append(("x", 0, plus(start, UNIT[m])))
        left.append(("u", n, base))
        right.append(("u", n, plus(base, UNIT[m])))
    return here, ahead, left, right


def needed_fields(stage):
    keys = collections.OrderedDict()
    for _, halves in TERMS[stage]:
        for sign in (1, -1):
            for pair in term_fields(halves, sign):
                keys.update((key, None) for key in pair)
    for m in DIRECT[stage]:
        for scale in (1, 3):
            keys["x", 0, plus(ZERO, UNIT[m], scale)] = None
    return [key for key in keys if key[2] != ZERO]


def stage_of(key):
    dz, dt = key[2][2:]
    if key[0] == "u" and key[1] < 2 and dz == 1 and dt == 0:
        return "t"
    if dz != 0 and dt != 0:
        return "corner"
    return "t" if dt != 0 or abs(dz) == 3 else "z" if dz != 0 else "own"


def lay_out(keys):
    rows, total = collections.OrderedDict(), 0
    for key in keys:
        rows[key] = total
        total += 8 * REGS[key[0]]
    return rows, total


def field_split():
    uses = collections.OrderedDict()
    for stage in STAGES:
        for key in needed_fields(stage):
            uses.setdefault(key, []).append(stage)
    shared, alone = {}, {}
    for stage in STAGES:
        built = [key for key in uses if stage_of(key) == stage]
        shared[stage] = lay_out([key for key in built if uses[key] != [stage]])
        alone[stage] = lay_out([key for key in built if uses[key] == [stage]])
    return shared, alone


def all_shifts():
    found = collections.OrderedDict()
    for stage in STAGES:
        for _, _, (dx, dy, _, _) in needed_fields(stage):
            if (dx, dy) != (0, 0):
                found[dx, dy] = None
    return list(found)


def write_shifts(perm_ref):
    lane = lax.broadcasted_iota(jnp.int32, (LANES, LANES), 1)
    source = lax.broadcasted_iota(jnp.int32, (LANES, LANES), 0)
    for index, (dx, dy) in enumerate(all_shifts()):
        wanted = (lane // NX + dy + NY) % NY * NX + (lane + dx + NX) % NX
        perm_ref[pl.ds(index * LANES, LANES), :] = (source == wanted).astype(F32).astype(jnp.bfloat16)


def parts_of(kind, value):
    if kind == "u":
        return [value.astype(jnp.bfloat16)]
    high = value.astype(jnp.bfloat16)
    rest = value - high.astype(F32)
    middle = rest.astype(jnp.bfloat16)
    return [high, middle, (rest - middle.astype(F32)).astype(jnp.bfloat16)]


def build_fields(locator, perm_ref, stores):
    groups = collections.OrderedDict()
    for ref, rows in stores:
        for (kind, n, disp), row in rows.items():
            shifts = groups.setdefault((kind, n, disp[3], disp[2]), collections.OrderedDict())
            shifts[disp[0], disp[1]] = (ref, row)
    order = all_shifts()
    for (kind, n, dt, dz), shifts in groups.items():
        regs = [locator.field_register(kind, n, k, dt, dz) for k in range(REGS[kind])]
        if (0, 0) in shifts:
            ref, row = shifts[0, 0]
            for k, value in enumerate(regs):
                ref[pl.ds(row + 8 * k, 8), :] = value
        parts = parts_of(kind, jnp.concatenate(regs, axis=0))
        for shift, (ref, row) in shifts.items():
            if shift != (0, 0):
                perm = perm_ref[pl.ds(order.index(shift) * LANES, LANES), :]
                moved = [jnp.dot(part, perm, preferred_element_type=F32) for part in parts]
                ref[pl.ds(row, 8 * REGS[kind]), :] = functools.reduce(jnp.add, moved)


class Fields:
    def __init__(self, own_x, own_u, stores):
        self.place = {("x", 0, ZERO): (own_x, 0)}
        for n in range(4):
            self.place["u", n, ZERO] = (own_u, 8 * REGS["u"] * n)
        for ref, rows in stores:
            for key, row in rows.items():
                self.place[key] = (ref, row)
        self.upper = lax.broadcasted_iota(jnp.int32, (8, LANES), 0) < 4

    def reg(self, key, k):
        ref, row = self.place[key]
        return ref[pl.ds(row + 8 * k, 8), :]

    def two_tiles(self, keys, k):
        top = self.reg(keys[0], k)
        turned_top = pltpu.roll(top, 4, 0)
        if keys[0] == keys[1]:
            low, turned_low = top, turned_top
        else:
            low = self.reg(keys[1], k)
            turned_low = pltpu.roll(low, 4, 0)
        return [jnp.where(self.upper, top, turned_low), jnp.where(self.upper, turned_top, low)]

    def vector(self, keys, pole):
        flat = [tile for k in range(3) for tile in self.two_tiles(keys, 3 * pole + k)]
        return [flat[:3], flat[3:]]

    def matrix(self, keys):
        flat = [tile for k in range(9) for tile in self.two_tiles(keys, k)]
        return [[flat[9 * c + 3 * i : 9 * c + 3 * i + 3] for i in range(3)] for c in range(2)]

    def compact_halves(self, first, second):
        top = jnp.where(self.upper, first, pltpu.roll(second, 4, 0))
        return top, jnp.where(self.upper, pltpu.roll(first, 4, 0), second)

    def compact_sum(self, first, second):
        kept = jnp.where(self.upper, first, second)
        return kept + pltpu.roll(jnp.where(self.upper, second, first), 4, 0)


def pole_sum(fields, here, ahead, scales):
    total = None
    for pole in range(NP):
        h = [[scales[pole] * v for v in part] for part in fields.vector(here, pole)]
        a = fields.vector(ahead, pole)
        real = [[a[0][i] * h[0][j] + a[1][i] * h[1][j] for j in range(3)] for i in range(3)]
        imag = [[a[1][i] * h[0][j] - a[0][i] * h[1][j] for j in range(3)] for i in range(3)]
        if total is None:
            total = [real, imag]
        else:
            total = [
                [[total[c][i][j] + new[i][j] for j in range(3)] for i in range(3)]
                for c, new in enumerate((real, imag))
            ]
    return total


def transposed(matrix):
    return [[[part[j][i] for j in range(3)] for i in range(3)] for part in matrix]


def row_times(row, right, row_sign, right_sign):
    result = [[], []]
    for j in range(3):
        real = imag = None
        for k in range(3):
            rr = row[0][k] * right[0][k][j]
            ii = row[1][k] * right[1][k][j]
            ri = row[0][k] * right[1][k][j]
            ir = row[1][k] * right[0][k][j]
            new_real = rr - ii if row_sign * right_sign > 0 else rr + ii
            if row_sign > 0 and right_sign > 0:
                new_imag = ri + ir
            elif row_sign > 0:
                new_imag = ir - ri
            else:
                new_imag = ri - ir
            real = new_real if real is None else real + new_real
            imag = new_imag if imag is None else imag + new_imag
        result[0].append(real)
        result[1].append(imag)
    return result


def add_terms(fields, stage, near, acc):
    started = set()
    for target, halves in TERMS[stage]:
        for sign in (1, -1):
            here, ahead, left, right = term_fields(halves, sign)
            force = pole_sum(fields, here, ahead, near)
            left = fields.matrix(left)
            right = fields.matrix(right)
            if sign > 0:
                right = transposed(right)
            else:
                left = transposed(left)
            rows = [row_times([left[0][i], left[1][i]], force, sign, 1) for i in range(3)]
            for i in range(3):
                row = row_times(rows[i], right, 1, -sign)
                for part in range(2):
                    for j in range(3):
                        at = pl.ds((target * 18 + part * 9 + i * 3 + j) * 8, 8)
                        new = row[part][j]
                        acc[at, :] = acc[at, :] + new if target in started else new
            started.add(target)


def acc_tile(acc, target, c):
    return acc[pl.ds((target * 18 + c) * 8, 8), :]


def scale_tiles(scale_ref):
    tiles = [scale_ref[pl.ds(8 * p, 8), :] for p in range(3 * NP)]
    return tiles[:NP], tiles[NP : 2 * NP], tiles[2 * NP :]


def own_force(fields, m, both):
    total = pole_sum(
        fields,
        [("x", 0, ZERO)] * 2,
        [("x", 0, UNIT[m]), ("x", 0, plus(ZERO, UNIT[m], 3))],
        both,
    )
    flat = [total[c][i][j] for c in range(2) for i in range(3) for j in range(3)]
    return [fields.compact_sum(flat[2 * k], flat[2 * k + 1]) for k in range(9)]


def write_messages(locator, plan, names, outs):
    for name, out in zip(names, outs):
        for reg, items in enumerate(plan[name].by_register()):
            spots = [item and locator.local(*item[1:]) for item in items]
            out[pl.ds(8 * reg, 8), :] = locator.assemble(spots)


def odd_in_z():
    return (lax.axis_index("gz") * lax.axis_size("gy") + lax.axis_index("gy")) % 2 == 1


def pack_z_kernel(plan, names, near_in, far_in, weight_in, x_in, u_in, *rest):
    within_ref, between_ref = rest[:2]
    outs = rest[2 : 2 + len(names)]
    scale_ref, perm_ref, x_ref, u_ref, near_ref, far_ref, weight_ref, u_held, sems = rest[2 + len(names) :]
    copies = [
        pltpu.make_async_copy(source, target, sems.at[index])
        for index, (source, target) in enumerate(
            ((u_in, u_held), (x_in, x_ref), (near_in, near_ref), (far_in, far_ref), (weight_in, weight_ref))
        )
    ]
    for copy in copies:
        copy.start()
    write_shifts(perm_ref)
    for copy in copies[:2]:
        copy.wait()
    u_ref[...] = u_held[...].astype(F32)
    locator = Locator(plan, 1, {("own", "x"): x_ref, ("own", "u"): u_ref})
    both = [("z", 1), ("z", -1)]

    @pl.when(odd_in_z())
    def _():
        write_messages(locator, plan, both, (within_ref, between_ref))

    @pl.when(jnp.logical_not(odd_in_z()))
    def _():
        write_messages(locator, plan, both, (between_ref, within_ref))

    write_messages(locator, plan, names, outs)
    for copy in copies[2:]:
        copy.wait()
    write_scales(near_ref, far_ref, weight_ref, scale_ref)


def pack_t_kernel(plan, names, x_ref, u_ref, *outs):
    write_messages(Locator(plan, 1, {("own", "x"): x_ref, ("own", "u"): u_ref}), plan, names, outs)


def corner_kernel(plan, names, within_ref, between_ref, ahead_ref, behind_ref, *outs):
    def split(from_ahead, from_behind):
        ahead_ref[...] = from_ahead[pl.ds(0, ahead_ref.shape[0]), :]
        behind_ref[...] = from_behind[pl.ds(0, behind_ref.shape[0]), :]

    @pl.when(odd_in_z())
    def _():
        split(between_ref, within_ref)

    @pl.when(jnp.logical_not(odd_in_z()))
    def _():
        split(within_ref, between_ref)

    locator = Locator(plan, 1, {("z", 1): ahead_ref, ("z", -1): behind_ref})
    for name, out in zip(names, outs):
        for reg, items in enumerate(plan[name].by_register()):
            spots = [
                item and (("z", item[0]),) + plan["z", item[0]].places[(0,) + item[1:]] for item in items
            ]
            out[pl.ds(8 * reg, 8), :] = locator.assemble(spots)


def part_reg(ref, index, k):
    return ref[pl.ds((9 * index + k) * 8, 8), :]


def write_scales(near_ref, far_ref, weight_ref, scale_ref):
    upper = lax.broadcasted_iota(jnp.int32, (8, LANES), 0) < 4
    for p in range(NP):
        scale_ref[pl.ds(8 * p, 8), :] = jnp.full((8, LANES), near_ref[p], F32)
        scale_ref[pl.ds(8 * (NP + p), 8), :] = jnp.where(upper, near_ref[p], far_ref[p])
        scale_ref[pl.ds(8 * (2 * NP + p), 8), :] = jnp.full((8, LANES), weight_ref[p], F32)


def own_fields_kernel(plan, t_size, perm_ref, x_ref, u_ref, shared_ref, alone_ref):
    shared, alone = field_split()
    stores = [(shared_ref, shared["own"][0]), (alone_ref, alone["own"][0])]
    build_fields(Locator(plan, t_size, {("own", "x"): x_ref, ("own", "u"): u_ref}), perm_ref, stores)


def own_kernel(scale_ref, x_ref, u_ref, shared_ref, alone_ref, part_ref, acc):
    shared, alone = field_split()
    fields = Fields(x_ref, u_ref, [(shared_ref, shared["own"][0]), (alone_ref, alone["own"][0])])
    near, both, weight = scale_tiles(scale_ref)
    add_terms(fields, "own", near, acc)
    direct = [own_force(fields, m, both) for m in DIRECT["own"]]
    for k in range(9):
        staples = fields.compact_halves(acc_tile(acc, 0, 2 * k), acc_tile(acc, 0, 2 * k + 1))
        for m in range(2):
            part_ref[pl.ds((9 * m + k) * 8, 8), :] = direct[m][k] + weight[m] * staples[m]


def stage_setup(stage, plan, t_size, names, received, perm_ref, x_ref, u_ref, shared_refs, shared_ref, alone_ref):
    buffers = {("own", "x"): x_ref, ("own", "u"): u_ref}
    buffers.update(zip(names, received))
    shared, alone = field_split()
    stores = [(alone_ref, alone[stage][0])]
    if shared_ref is not None:
        stores.append((shared_ref, shared[stage][0]))
    build_fields(Locator(plan, t_size, buffers), perm_ref, stores)
    earlier = [(ref, shared[name][0]) for name, ref in zip(STAGES, shared_refs)]
    return Fields(x_ref, u_ref, earlier + stores)


def z_kernel(plan, t_size, names, scale_ref, perm_ref, x_ref, u_ref, own_shared, own_part, *rest):
    received = rest[: len(names)]
    shared_ref, part_ref, alone_ref, acc = rest[len(names) :]
    fields = stage_setup(
        "z", plan, t_size, names, received, perm_ref, x_ref, u_ref, [own_shared], shared_ref, alone_ref
    )
    near, _, weight = scale_tiles(scale_ref)
    add_terms(fields, "z", near, acc)
    for k in range(9):
        staples = fields.compact_halves(acc_tile(acc, 0, 2 * k), acc_tile(acc, 0, 2 * k + 1))
        for m in range(2):
            part_ref[pl.ds((9 * m + k) * 8, 8), :] = part_reg(own_part, m, k) + weight[m] * staples[m]


def t_kernel(plan, t_size, names, scale_ref, perm_ref, x_ref, u_ref, own_shared, z_shared, z_part, *rest):
    received = rest[: len(names)]
    shared_ref, part_ref, ready, alone_ref, acc = rest[len(names) :]
    fields = stage_setup(
        "t", plan, t_size, names, received, perm_ref, x_ref, u_ref, [own_shared, z_shared], shared_ref, alone_ref
    )
    near, both, weight = scale_tiles(scale_ref)
    add_terms(fields, "t", near, acc)
    for k in range(9):
        staples = fields.compact_halves(acc_tile(acc, 0, 2 * k), acc_tile(acc, 0, 2 * k + 1))
        for m in range(2):
            ready[pl.ds((9 * m + k) * 8, 8), :] = part_reg(z_part, m, k) + weight[m] * staples[m]
    own_z, own_t = [own_force(fields, m, both) for m in DIRECT["t"]]
    for k in range(9):
        staple = fields.compact_sum(acc_tile(acc, 1, 2 * k), acc_tile(acc, 1, 2 * k + 1))
        part_ref[pl.ds(k * 8, 8), :] = own_t[k] + weight[3] * staple
        staple = fields.compact_sum(acc_tile(acc, 2, 2 * k), acc_tile(acc, 2, 2 * k + 1))
        part_ref[pl.ds((9 + k) * 8, 8), :] = own_z[k] + weight[2] * staple


def last_kernel(plan, t_size, names, scale_ref, perm_ref, x_ref, u_ref, *rest):
    own_shared, z_shared, t_shared, t_part, earlier = rest[:5]
    received = rest[5 : 5 + len(names)]
    out_ref, alone_ref, acc, ready, sems = rest[5 + len(names) :]
    rows = ready.shape[0]
    first = pltpu.make_async_copy(earlier, out_ref.at[pl.ds(0, rows)], sems.at[0])
    first.start()
    fields = stage_setup(
        "corner",
        plan,
        t_size,
        names,
        received,
        perm_ref,
        x_ref,
        u_ref,
        [own_shared, z_shared, t_shared],
        None,
        alone_ref,
    )
    near, _, weight = scale_tiles(scale_ref)
    add_terms(fields, "corner", near, acc)
    for k in range(9):
        staples = fields.compact_halves(acc_tile(acc, 0, 2 * k), acc_tile(acc, 0, 2 * k + 1))
        ready[pl.ds(k * 8, 8), :] = part_reg(t_part, 1, k) + weight[2] * staples[0]
        ready[pl.ds((9 + k) * 8, 8), :] = part_reg(t_part, 0, k) + weight[3] * staples[1]
    second = pltpu.make_async_copy(ready, out_ref.at[pl.ds(rows, rows)], sems.at[1])
    second.start()
    first.wait()
    second.wait()


def rows_of(count):
    return jax.ShapeDtypeStruct((count, LANES), F32)


def on_device(pole_vectors, gauge_links, pole_coeff, naik_coeff, staple_weight):
    t_size = lax.axis_size("ta")
    z_size = lax.axis_size("gz") * lax.axis_size("gy")
    plan = message_plan(t_size)
    x_rows, u_rows = 8 * REGS["x"], 4 * 8 * REGS["u"]
    vmem = pl.BlockSpec(memory_space=pltpu.VMEM)
    hbm = pl.BlockSpec(memory_space=pltpu.HBM)
    limit = pltpu.CompilerParams(vmem_limit_bytes=4 * 1024 * 1024)

    def moved(name, value):
        kind, step = name
        if kind in ("z", "b"):
            return lax.ppermute(value, ("gz", "gy"), [((i + step) % z_size, i) for i in range(z_size)])
        return lax.ppermute(value, "ta", [((j + step) % t_size, j) for j in range(t_size)])

    def exchanged(value, first):
        pairs = [(i, (i + 1) % z_size) for i in range(first, z_size, 2)]
        return lax.ppermute(value, ("gz", "gy"), pairs + [(j, i) for i, j in pairs])

    first_names = [name for name in plan if name[0] != "c"]
    corner_names = [name for name in plan if name[0] == "c"]
    t_names = [name for name in first_names if name[0] == "t"]
    in_hbm = functools.partial(pltpu.with_memory_space_constraint, memory_space=pltpu.HBM)
    z_names = [("b", 1), ("z", 2)]
    corner_count = max(plan[name].count for name in corner_names)
    late = max(plan["b", 1].count, corner_count)
    late_counts = [late, late + 1]
    exchange_counts = [plan["z", step].count for step in (1, -1)]
    exchange = max(exchange_counts + [plan["t", 1].count - corner_count + 1])
    within, between, *sends, scale, perm, x_own, u_own = pl.pallas_call(
        functools.partial(pack_z_kernel, plan, z_names),
        out_shape=[rows_of(8 * exchange), rows_of(8 * (exchange + 1))]
        + [rows_of(8 * max(plan[name].count, least)) for name, least in zip(z_names, late_counts)]
        + [
            rows_of(8 * 3 * NP),
            jax.ShapeDtypeStruct((len(all_shifts()) * LANES, LANES), jnp.bfloat16),
            rows_of(x_rows),
            rows_of(u_rows),
        ],
        in_specs=[hbm] * 5,
        out_specs=[vmem] * (len(z_names) + 6),
        scratch_shapes=[pltpu.SMEM((NP,), F32)] * 3
        + [pltpu.VMEM((u_rows, LANES), jnp.bfloat16), pltpu.SemaphoreType.DMA((5,))],
        compiler_params=limit,
        name="pack_z",
    )(
        in_hbm(pole_coeff),
        in_hbm(naik_coeff),
        in_hbm(staple_weight),
        in_hbm(pole_vectors.reshape((x_rows, LANES))),
        in_hbm(gauge_links.reshape((u_rows, LANES))),
    )
    own = [x_own, u_own]
    between, within = exchanged(between, 1), exchanged(within, 0)
    received = {name: moved(name, value) for name, value in zip(z_names, sends)}
    packed = pl.pallas_call(
        functools.partial(pack_t_kernel, plan, t_names),
        out_shape=[rows_of(8 * plan[name].count) for name in t_names],
        in_specs=[vmem] * 2,
        out_specs=[vmem] * len(t_names),
        compiler_params=limit,
        name="pack_t",
    )(*own)
    received.update({name: moved(name, value) for name, value in zip(t_names, packed)})
    shared, alone = field_split()
    part_rows = 8 * REGS["u"]

    def scratch(stage):
        sums = 1 + max(target for target, _ in TERMS[stage])
        return [pltpu.VMEM((alone[stage][1], LANES), F32), pltpu.VMEM((sums * 18 * 8, LANES), F32)]

    def cost(micros):
        return pl.CostEstimate(flops=10**6, bytes_accessed=int(3.69e6 * micros), transcendentals=0)

    wide_limit = pltpu.CompilerParams(vmem_limit_bytes=6 * 1024 * 1024)
    own_shared, own_alone = pl.pallas_call(
        functools.partial(own_fields_kernel, plan, t_size),
        out_shape=[rows_of(shared["own"][1]), rows_of(alone["own"][1])],
        in_specs=[vmem] * 3,
        out_specs=[vmem] * 2,
        compiler_params=wide_limit,
        name="fields_own",
    )(perm, *own)
    own_part = pl.pallas_call(
        own_kernel,
        out_shape=rows_of(2 * part_rows),
        in_specs=[vmem] * 5,
        out_specs=vmem,
        scratch_shapes=scratch("own")[1:],
        cost_estimate=cost(COSTS["own"]),
        compiler_params=wide_limit,
        name="force_own",
    )(scale, *own, own_shared, own_alone)
    local = [scale, perm, *own]
    received["z", 1], received["z", -1], *corners = pl.pallas_call(
        functools.partial(corner_kernel, plan, corner_names),
        out_shape=[rows_of(8 * count) for count in exchange_counts]
        + [rows_of(8 * plan[name].count) for name in corner_names],
        in_specs=[vmem] * 2,
        out_specs=[vmem] * (2 + len(corner_names)),
        compiler_params=limit,
        name="pack_corners",
    )(within, between)
    received.update({name: moved(name, value) for name, value in zip(corner_names, corners)})
    names = [("z", 1), ("z", -1)]
    z_shared, z_part = pl.pallas_call(
        functools.partial(z_kernel, plan, t_size, names),
        out_shape=[rows_of(shared["z"][1]), rows_of(2 * part_rows)],
        in_specs=[vmem] * (6 + len(names)),
        out_specs=[vmem] * 2,
        scratch_shapes=scratch("z"),
        cost_estimate=cost(COSTS["z"]),
        compiler_params=wide_limit,
        name="force_z",
    )(*local, own_shared, own_part, *[received[name] for name in names])
    far_names = t_names + [("b", 1), ("z", 2)]
    t_shared, t_part, earlier = pl.pallas_call(
        functools.partial(t_kernel, plan, t_size, far_names),
        out_shape=[rows_of(shared["t"][1]), rows_of(2 * part_rows), rows_of(2 * part_rows)],
        in_specs=[vmem] * (7 + len(far_names)),
        out_specs=[vmem] * 3,
        scratch_shapes=scratch("t"),
        cost_estimate=cost(COSTS["t"]),
        compiler_params=wide_limit,
        name="force_t",
    )(*local, own_shared, z_shared, z_part, *[received[name] for name in far_names])
    names = [name for name in received if name not in (("b", 1), ("z", 2))]
    force = pl.pallas_call(
        functools.partial(last_kernel, plan, t_size, names),
        out_shape=rows_of(u_rows),
        in_specs=[vmem] * (9 + len(names)),
        out_specs=hbm,
        scratch_shapes=scratch("corner")
        + [pltpu.VMEM((2 * part_rows, LANES), F32), pltpu.SemaphoreType.DMA((2,))],
        cost_estimate=cost(COSTS["corner"]),
        compiler_params=wide_limit,
        name="force_corner",
    )(
        *local,
        own_shared,
        z_shared,
        t_shared,
        t_part,
        earlier,
        *[received[name] for name in names],
    )
    return force.reshape(gauge_links.shape)


def solution(mesh):
    return jax.shard_map(
        on_device,
        mesh=mesh,
        in_specs=(
            P("ens", None, None, "ta", ("gz", "gy"), None),
            P("ens", None, None, None, "ta", ("gz", "gy"), None),
            P(),
            P(),
            P(),
        ),
        out_specs=P("ens", None, None, None, "ta", ("gz", "gy"), None),
        check_vma=False,
    )
```
